32 devices in a mesh: dp: 8 (over z, y), fsdp: 4 (over x, core).
Axes of the slice: x: 2, y: 2, z: 4, core: 2. Of those that a mesh axis runs over, the one named last changes fastest.
Arguments:
- frames_in: bfloat16 [64, 16, 32, 256], P(('dp', 'fsdp')), may hold values from -40 to 40
- domain: int32 [64], P(('dp', 'fsdp')), may hold values from 0 to 1, as said below
- kernel_one: bfloat16 [2304, 512], P('dp', 'fsdp'), may hold values from -0.125 to 0.125
- kernel_two: bfloat16 [4608, 512], P('dp', 'fsdp'), may hold values from -0.09375 to 0.09375
- kernel_three: bfloat16 [4608, 512], P('dp', 'fsdp'), may hold values from -0.09375 to 0.09375
- attn_enc: bfloat16 [512, 1536], P('dp', 'fsdp'), may hold values from -0.25 to 0.25
- kernel_four: bfloat16 [4608, 512], P('dp', 'fsdp'), may hold values from -0.09375 to 0.09375
- kernel_five: bfloat16 [4608, 512], P('dp', 'fsdp'), may hold values from -0.09375 to 0.09375
- kernel_six: bfloat16 [4608, 256], P('dp', 'fsdp'), may hold values from -0.09375 to 0.09375
- attn_dec: bfloat16 [512, 768], P('dp', 'fsdp'), may hold values from -0.25 to 0.25
- gains: float32 [5120], P(('dp', 'fsdp')), may hold values from 0.5 to 1.5
- biases: float32 [5120], P(('dp', 'fsdp')), may hold values from -3 to 3
- enc_cot: bfloat16 [64, 8, 16, 3, 512], P(('dp', 'fsdp')), may hold values from -40 to 40
- dec_cot: bfloat16 [64, 16, 32, 3, 256], P(('dp', 'fsdp')), may hold values from -40 to 40
Outputs:
- task_features: float32 [64, 8, 16, 3, 512], P(('dp', 'fsdp'))
- task_maps: float32 [64, 16, 32, 3, 256], P(('dp', 'fsdp'))
- frames_grad: float32 [64, 16, 32, 256], P(('dp', 'fsdp'))
- kernel_one_grad: float32 [2304, 512], P('dp', 'fsdp')
- kernel_two_grad: float32 [4608, 512], P('dp', 'fsdp')
- kernel_three_grad: float32 [4608, 512], P('dp', 'fsdp')
- attn_enc_grad: float32 [512, 1536], P('dp', 'fsdp')
- kernel_four_grad: float32 [4608, 512], P('dp', 'fsdp')
- kernel_five_grad: float32 [4608, 512], P('dp', 'fsdp')
- kernel_six_grad: float32 [4608, 256], P('dp', 'fsdp')
- attn_dec_grad: float32 [512, 768], P('dp', 'fsdp')
- gains_grad: float32 [5120], P(('dp', 'fsdp'))
- biases_grad: float32 [5120], P(('dp', 'fsdp'))
The draws below stay inside these ranges and needn't reach their ends.
Inputs may be any that keep to these rules, and one draw needn't show every extreme that they name: Exactly 40 frames have domain 0 and the others domain 1; which frames is drawn.
All inputs are finite; a program needn't handle non-finite values.
Results may differ from the reference program's by a relative error of at most 0.025.
Values may be sent and summed in bfloat16 or wider, within the bound.
No kernel may reach another device: no remote copies, remote signals or barrier semaphores. Data moves between devices by JAX's collectives and lax.ppermute only.
A program may use at most 256 MiB of HBM per device.

```python
from functools import partial
import jax
import jax.numpy as jnp
from jax import lax

C_IN = 256
C_MID = 512
C_DEC = 256
TASKS = 3
ROWS_PX = 16
COLS_PX = 32
FRAMES = 64
CH_ALL = 5120


def frame_scales(key, count, highest):
    ramp = jnp.exp(jnp.log(highest) * jnp.arange(count, dtype=jnp.float32) / (count - 1))
    return ramp * jnp.exp(jax.random.uniform(key, (count,), jnp.float32, -0.35, 0.35))


def draw_frames_in(key, part):
    key = jax.random.fold_in(key, 11)
    base_key, scale_key = jax.random.split(key, 2)
    shape = (FRAMES, ROWS_PX, COLS_PX, C_IN)
    values = jnp.clip(jax.random.normal(base_key, shape, jnp.float32), -5.0, 5.0)
    scales = frame_scales(scale_key, FRAMES, 3.0)
    return (values * scales[:, None, None, None]).astype(jnp.bfloat16)


def draw_domain(key, part):
    key = jax.random.fold_in(key, 5)
    order = jax.random.permutation(key, FRAMES)
    return jnp.where(order < FRAMES * 5 // 8, 0, 1).astype(jnp.int32)


def draw_enc_cot(key, part):
    key = jax.random.fold_in(key, 23)
    base_key, scale_key = jax.random.split(key, 2)
    shape = (FRAMES, ROWS_PX // 2, COLS_PX // 2, TASKS, C_MID)
    values = jnp.clip(jax.random.normal(base_key, shape, jnp.float32), -5.0, 5.0)
    scales = frame_scales(scale_key, FRAMES, 3.0)
    return (values * scales[:, None, None, None, None]).astype(jnp.bfloat16)


def draw_dec_cot(key, part):
    key = jax.random.fold_in(key, 37)
    base_key, scale_key = jax.random.split(key, 2)
    shape = (FRAMES, ROWS_PX, COLS_PX, TASKS, C_DEC)
    values = jnp.clip(jax.random.normal(base_key, shape, jnp.float32), -5.0, 5.0)
    scales = frame_scales(scale_key, FRAMES, 3.0)
    return (values * scales[:, None, None, None, None]).astype(jnp.bfloat16)


def level_of(rng, shape, cuts, least, top_value):
    loudness = 1.0
    for axis_at, blocks in cuts:
        steps = jax.random.uniform(jax.random.fold_in(jax.random.fold_in(rng, 6), axis_at), (blocks,), jnp.float32, least / len(cuts), top_value / len(cuts))
        loudness = loudness * jnp.repeat(jnp.exp(steps), shape[axis_at] // blocks).reshape((-1,) + (1,) * (len(shape) - 1 - axis_at))
    return loudness


def scatter_about(key, shape, width, reach, shards=(), kind=jnp.bfloat16):
    drawn = jax.random.normal(key, shape, jnp.float32) * width
    if len(shards) > 0:
        drawn = level_of(key, shape, shards, -0.22, 0.18) * drawn
    return jnp.clip(drawn, min=-reach, max=reach).astype(kind)


def setup_inputs(seed: int = 0) -> dict:
    seeds = jax.random.split(jax.random.key(seed), 15)
    return {
        "frames_in": draw_frames_in(jax.random.fold_in(seeds[14], 71), 0),
        "domain": draw_domain(jax.random.fold_in(seeds[14], 71), 0),
        "kernel_one": scatter_about(seeds[2], (9 * C_IN, C_MID), (9 * C_IN) ** -0.5, 0.125, ((0, 8), (1, 4))),
        "kernel_two": scatter_about(seeds[3], (9 * C_MID, C_MID), (9 * C_MID) ** -0.5, 0.09375, ((0, 8), (1, 4))),
        "kernel_three": scatter_about(seeds[4], (9 * C_MID, C_MID), (9 * C_MID) ** -0.5, 0.09375, ((0, 8), (1, 4))),
        "attn_enc": scatter_about(seeds[5], (C_MID, TASKS * C_MID), C_MID ** -0.5, 0.25, ((0, 8), (1, 4))),
        "kernel_four": scatter_about(seeds[6], (9 * C_MID, C_MID), (9 * C_MID) ** -0.5, 0.09375, ((0, 8), (1, 4))),
        "kernel_five": scatter_about(seeds[7], (9 * C_MID, C_MID), (9 * C_MID) ** -0.5, 0.09375, ((0, 8), (1, 4))),
        "kernel_six": scatter_about(seeds[8], (9 * C_MID, C_DEC), (9 * C_MID) ** -0.5, 0.09375, ((0, 8), (1, 4))),
        "attn_dec": scatter_about(seeds[9], (C_MID, TASKS * C_DEC), C_MID ** -0.5, 0.25, ((0, 8), (1, 4))),
        "gains": jnp.clip(1.0 + 0.1 * jax.random.normal(seeds[10], (CH_ALL,), jnp.float32), 0.5, 1.5),
        "biases": scatter_about(seeds[11], (CH_ALL,), 0.5, 3.0, ((0, 32),), jnp.float32),
        "enc_cot": draw_enc_cot(jax.random.fold_in(seeds[14], 71), 0),
        "dec_cot": draw_dec_cot(jax.random.fold_in(seeds[14], 71), 0),
    }


eps = 1e-05
HIGH = lax.Precision.HIGHEST

@jax.custom_vjp
def low(v):
    return lax.optimization_barrier(v.astype(jnp.bfloat16)).astype(jnp.float32)

@jax.custom_vjp
def low_back(v):
    return v

def low_keep(v):
    return (low(v), None)

def low_pass(kept, grad):
    return (grad,)

def back_keep(v):
    return (v, None)

def back_low(kept, grad):
    return (low(grad),)
low.defvjp(low_keep, low_pass)
low_back.defvjp(back_keep, back_low)

def layer_params(vector):
    widths_list = [C_MID, C_MID, C_MID, TASKS * C_MID, C_MID, C_MID, C_DEC, TASKS * C_DEC]
    pieces = []
    position = 0
    for extent in widths_list:
        pieces.append(vector[position:position + extent])
        position = position + extent
    return pieces

def conv_apply(source, kernel):
    frame_count, grid_rows, grid_cols, chans_in = source.shape
    padded = jnp.pad(source, ((0, 0), (1, 1), (1, 1), (0, 0)))
    summed = jnp.zeros((frame_count, grid_rows, grid_cols, kernel.shape[1]), jnp.float32)
    for offset in range(9):
        row_at = offset // 3
        col_at = offset % 3
        window = padded[:, row_at:row_at + grid_rows, col_at:col_at + grid_cols, :]
        summed = summed + jnp.einsum('fhwc,cd->fhwd', window, kernel[offset * chans_in:(offset + 1) * chans_in], precision=HIGH)
    return summed

def domain_norm(values, onehot, gain, bias):
    shaped = values.reshape(values.shape[0], -1, values.shape[-1])
    counts = lax.optimization_barrier(jnp.sum(onehot, axis=0)) * shaped.shape[1]
    first_sum = jnp.einsum('fd,fpc->dc', onehot, shaped, precision=HIGH)
    second_sum = jnp.einsum('fd,fpc->dc', onehot, shaped * shaped, precision=HIGH)
    average = first_sum / counts[:, None]
    variance = second_sum / counts[:, None] - average * average
    inverse = lax.rsqrt(variance + eps)
    frame_mean = jnp.dot(onehot, average, precision=HIGH)[:, None, :]
    frame_inverse = jnp.dot(onehot, inverse, precision=HIGH)[:, None, :]
    normed = (shaped - frame_mean) * frame_inverse
    return (normed * gain + bias).reshape(values.shape)

def pool_mask(top, mask):
    frame_count, grid_rows, grid_cols, chans = top.shape
    blocks = top.reshape(frame_count, grid_rows // 2, 2, grid_cols // 2, 2, chans)
    exponent = jnp.exp(blocks)
    weights = exponent / lax.optimization_barrier(jnp.sum(exponent, axis=(2, 4), keepdims=True))
    pooled = lax.optimization_barrier(jnp.sum(weights * blocks, axis=(2, 4)))
    attended = mask.reshape(frame_count, grid_rows // 2, 2, grid_cols // 2, 2, TASKS, chans) * blocks[:, :, :, :, :, None, :]
    task_out = lax.optimization_barrier(jnp.sum(attended * weights[:, :, :, :, :, None, :], axis=(2, 4)))
    unpooled = (weights * pooled[:, :, None, :, None, :]).reshape(top.shape)
    return (task_out, unpooled)

def forward(onehot, frames, kernel_one, kernel_two, kernel_three, attn_enc, kernel_four, kernel_five, kernel_six, attn_dec, gains, biases):
    gain_list = layer_params(gains)
    bias_list = layer_params(biases)
    pre_one = low_back(conv_apply(frames, kernel_one))
    enc_one = low(jax.nn.silu(domain_norm(pre_one, onehot, gain_list[0], bias_list[0])))
    pre_two = low_back(conv_apply(enc_one, kernel_two))
    enc_two = low(jax.nn.silu(domain_norm(pre_two, onehot, gain_list[1], bias_list[1])))
    pre_three = low_back(conv_apply(enc_two, kernel_three))
    top = jax.nn.silu(domain_norm(pre_three, onehot, gain_list[2], bias_list[2]))
    pre_attend = low_back(jnp.einsum('fhwc,cd->fhwd', enc_two, attn_enc, precision=HIGH))
    mask = jax.nn.sigmoid(domain_norm(pre_attend, onehot, gain_list[3], bias_list[3]))
    task_out, unpooled = pool_mask(top, mask)
    unpooled_low = low(unpooled)
    pre_four = low_back(conv_apply(unpooled_low, kernel_four))
    dec_one = low(jax.nn.silu(domain_norm(pre_four, onehot, gain_list[4], bias_list[4])))
    pre_five = low_back(conv_apply(dec_one, kernel_five))
    dec_two = low(jax.nn.silu(domain_norm(pre_five, onehot, gain_list[5], bias_list[5])))
    pre_six = low_back(conv_apply(dec_two, kernel_six))
    bottom = jax.nn.silu(domain_norm(pre_six, onehot, gain_list[6], bias_list[6]))
    pre_gate = low_back(jnp.einsum('fhwc,cd->fhwd', dec_one, attn_dec, precision=HIGH))
    gate = jax.nn.sigmoid(domain_norm(pre_gate, onehot, gain_list[7], bias_list[7]))
    frame_count, grid_rows, grid_cols, chans = bottom.shape
    task_maps = gate.reshape(frame_count, grid_rows, grid_cols, TASKS, chans) * bottom[:, :, :, None, :]
    return (task_out, task_maps)

def reference(frames_in, domain, kernel_one, kernel_two, kernel_three, attn_enc, kernel_four, kernel_five, kernel_six, attn_dec, gains, biases, enc_cot, dec_cot):
    onehot = (domain[:, None] == jnp.arange(2, dtype=jnp.int32)[None, :]).astype(jnp.float32)
    primals = (frames_in.astype(jnp.float32), kernel_one.astype(jnp.float32), kernel_two.astype(jnp.float32), kernel_three.astype(jnp.float32), attn_enc.astype(jnp.float32), kernel_four.astype(jnp.float32), kernel_five.astype(jnp.float32), kernel_six.astype(jnp.float32), attn_dec.astype(jnp.float32), gains.astype(jnp.float32), biases.astype(jnp.float32))
    outputs, pullback = jax.vjp(partial(forward, onehot), *primals)
    grads = pullback((enc_cot.astype(jnp.float32), dec_cot.astype(jnp.float32)))
    return (outputs[0], outputs[1], grads[0], grads[1], grads[2], grads[3], grads[4], grads[5], grads[6], grads[7], grads[8], grads[9], grads[10])
```

```python
import functools

import jax
import jax.numpy as jnp
from jax import lax
from jax.experimental import pallas as pl
from jax.experimental.pallas import tpu as pltpu
from jax.sharding import PartitionSpec as P

C_IN = 256
C_MID = 512
C_DEC = 256
TASKS = 3
EPS = 1e-05
LANES = 128
F32 = jnp.float32
BF16 = jnp.bfloat16
VMEM_LIMIT = 56 * 1024 * 1024


def params(grid_dims=0):
    return pltpu.CompilerParams(
        vmem_limit_bytes=VMEM_LIMIT,
        dimension_semantics=("arbitrary",) * grid_dims if grid_dims else None,
    )


def whole(shape):
    zeros = (0,) * len(shape)
    return pl.BlockSpec(shape, lambda *_: zeros)


SCALARS = pl.BlockSpec(memory_space=pltpu.SMEM)


def sds(shape, dtype):
    return jax.ShapeDtypeStruct(shape, dtype)


def sigmoid(v):
    return 0.5 * jnp.tanh(0.5 * v) + 0.5


def frame_tables(stats, domain_at, counts):
    first = domain_at == 0
    share = jnp.where(first, 1.0 / counts[0], 1.0 / counts[1])
    average = jnp.where(first, stats[0:1], stats[1:2]) * share
    square = jnp.where(first, stats[2:3], stats[3:4]) * share
    return average, lax.rsqrt(square - average * average + EPS)


def grad_tables(sums, domain_at, counts):
    first = domain_at == 0
    share = jnp.where(first, 1.0 / counts[0], 1.0 / counts[1])
    return (
        jnp.where(first, sums[0:1], sums[1:2]) * share,
        jnp.where(first, sums[2:3], sums[3:4]) * share,
    )


def by_domain(first, second, domain_ref):
    rows = []
    for per_frame in (first, second):
        for d in (0, 1):
            total = None
            for f, value in enumerate(per_frame):
                term = jnp.where(domain_ref[f] == d, value, jnp.zeros_like(value))
                total = term if total is None else total + term
            rows.append(total)
    return jnp.concatenate(rows, 0)


def fold(x):
    return jnp.sum(x.reshape(-1, 8, x.shape[-1]), 0)


def put_windows(win_ref, f, row, value, cols):
    col = lax.broadcasted_iota(jnp.int32, value.shape, 0)
    left = jnp.where(col == 0, 0.0, pltpu.roll(value, 1, 0))
    right = jnp.where(col == cols - 1, 0.0, pltpu.roll(value, cols - 1, 0))
    win_ref[0, f, row + 1] = left.astype(BF16)
    win_ref[1, f, row + 1] = value.astype(BF16)
    win_ref[2, f, row + 1] = right.astype(BF16)


def clear_edges(win_ref, rows):
    shape = win_ref.shape
    for b in range(3):
        for f in range(shape[1]):
            win_ref[b, f, 0] = jnp.zeros(shape[3:], BF16)
            win_ref[b, f, rows + 1] = jnp.zeros(shape[3:], BF16)


def window(win_ref, b, row_at, rows):
    part = win_ref[b, :, pl.ds(row_at, rows)]
    return part.reshape(-1, part.shape[-1])


def column_sums(ref, f, pixels, lanes, step=64):
    def add(i, carry):
        part = ref[pl.ds(f * pixels + i * step, step), lanes]
        return carry[0] + fold(part), carry[1] + fold(part * part)

    width = lanes.stop - lanes.start
    zero = jnp.zeros((8, width), F32)
    one, two = lax.fori_loop(0, pixels // step, add, (zero, zero), unroll=2)
    return jnp.sum(one, 0, keepdims=True), jnp.sum(two, 0, keepdims=True)


class Pieces:
    def __init__(self, member, parts, me, sources):
        self.member, self.parts, self.me, self.sources = member, parts, me, sources
        self.shape = member.shape


def span(start, size):
    return pl.ds(start if isinstance(start, int) else pl.multiple_of(start, size & -size), size)


def fetch(member, parts, me_ref, sources, dst_ref, sem):
    me = me_ref[0]
    for (first, size, masks), src in zip(parts, sources):
        for q in range(src.shape[0]):
            d = q if masks is None else me ^ masks[q]
            for at, row, col in member.spots(d >> 2, d & 3):
                low, high = max(at, first), min(at + member.vr, first + size)
                if low < high:
                    pltpu.make_async_copy(
                        src.at[q, pl.ds(low - first, high - low)],
                        dst_ref.at[span(row + (low - at), high - low), span(col, LANES)],
                        sem,
                    ).start()


def arrived(ref, sem):
    pltpu.make_async_copy(ref, ref, sem).wait()


def forward_kernel(geom, normed, pieces, *refs):
    frames, rows, cols, counts = geom
    pixels = rows * cols
    refs = list(refs)
    domain_ref = refs.pop(0)
    source_ref = refs.pop(0)
    if normed:
        stats_ref, gain_ref, bias_ref = refs.pop(0), refs.pop(0), refs.pop(0)
    if pieces:
        me_ref = refs.pop(0)
        sources = [refs.pop(0) for _ in pieces[1]]
    else:
        kernel_ref = refs.pop(0)
    out_ref = refs.pop(0)
    sums_ref = refs.pop(0)
    act_ref = refs.pop(0) if normed else None
    if pieces:
        matrix_ref = refs.pop(0)
    win_ref = refs.pop(0)
    if pieces:
        held_ref, sem = refs.pop(0), refs.pop(0)
    step = pl.program_id(0)
    chans = win_ref.shape[-1]

    @pl.when(step == 0)
    def _():
        if pieces:
            fetch(*pieces, me_ref, sources, held_ref, sem.at[0])
        clear_edges(win_ref, rows)
        for f in range(frames):
            if normed:
                average, inverse = frame_tables(stats_ref[...], domain_ref[f], counts)
                scale = inverse * gain_ref[...]
                shift = bias_ref[...] - average * scale

            def one_row(r, _):
                at = pl.multiple_of(f * pixels + r * cols, cols)
                value = source_ref[pl.ds(at, cols), :].astype(F32)
                if normed:
                    act = value * scale + shift
                    value = act * sigmoid(act)
                    act_ref[pl.ds(at, cols), :] = value.astype(BF16)
                put_windows(win_ref, f, r, value, cols)
                return 0

            lax.fori_loop(0, rows, one_row, 0, unroll=2)
        if pieces:
            arrived(held_ref, sem.at[0])
            pltpu.make_async_copy(held_ref, matrix_ref, sem.at[1]).start()

    source = jnp.concatenate([window(win_ref, b, step, rows) for b in range(3)], 1)
    if pieces:
        matrix = held_ref[pl.ds(pl.multiple_of(step * 3 * chans, 3 * chans), 3 * chans), :]
    else:
        matrix = kernel_ref[...]
    part = jnp.dot(source, matrix, preferred_element_type=F32)

    @pl.when(step == 0)
    def _():
        out_ref[...] = part

    @pl.when(step > 0)
    def _():
        out_ref[...] += part

    @pl.when(step == 2)
    def _():
        for lane in range(0, out_ref.shape[-1], 256):
            lanes = slice(lane, lane + 256)
            pairs = [column_sums(out_ref, f, pixels, lanes) for f in range(frames)]
            sums_ref[:, lanes] = by_domain([p[0] for p in pairs], [p[1] for p in pairs], domain_ref)
        if pieces:
            pltpu.make_async_copy(held_ref, matrix_ref, sem.at[1]).wait()


ANYWHERE = pl.BlockSpec(memory_space=pl.ANY)


def forward_layer(geom, domain, source, kernel, norm=None):
    frames, rows, cols, _ = geom
    pix, chans = source.shape
    width = kernel.shape[1]
    pieces = isinstance(kernel, Pieces)
    args, specs = [domain, source], [SCALARS, whole(source.shape)]
    if norm is not None:
        args += list(norm)
        specs += [whole(x.shape) for x in norm]
    if pieces:
        args += [kernel.me, *kernel.sources]
        specs += [SCALARS] + [ANYWHERE] * len(kernel.sources)
    else:
        args.append(kernel)
        specs.append(pl.BlockSpec((3 * chans, width), lambda a: (a, 0)))
    outs, out_specs = [sds((pix, width), F32)], [whole((pix, width))]
    outs.append(sds((4, width), F32))
    out_specs.append(whole((4, width)))
    if norm is not None:
        outs.append(sds((pix, chans), BF16))
        out_specs.append(whole((pix, chans)))
    scratch = [pltpu.VMEM((3, frames, rows + 2, cols, chans), BF16)]
    if pieces:
        outs.append(sds(kernel.shape, BF16))
        out_specs.append(ANYWHERE)
        scratch += [pltpu.VMEM(kernel.shape, BF16), pltpu.SemaphoreType.DMA((2,))]
    size = kernel.shape[0] * kernel.shape[1]
    return pl.pallas_call(
        functools.partial(forward_kernel, geom, norm is not None, (kernel.member, kernel.parts) if pieces else None),
        grid=(3,),
        in_specs=specs,
        out_specs=out_specs,
        out_shape=outs,
        scratch_shapes=scratch,
        compiler_params=params(1),
        cost_estimate=pl.CostEstimate(flops=2 * pix * size, bytes_accessed=size * 2 + pix * 4096, transcendentals=0),
    )(*args)


def pair_sum(x, cols):
    even = lax.broadcasted_iota(jnp.int32, x.shape, 0) % 2 == 0
    return x + jnp.where(even, pltpu.roll(x, cols - 1, 0), pltpu.roll(x, 1, 0))


def softmax_window(top, cols):
    exps = [jnp.exp(t) for t in top]
    share = 1.0 / pair_sum(exps[0] + exps[1], cols)
    return [e * share for e in exps]


def spread_cols(scr_ref, x):
    half = x.shape[0]
    scr_ref[pl.ds(0, half, stride=2), :] = x
    scr_ref[pl.ds(1, half, stride=2), :] = x
    return scr_ref[...]


def top_rows(top_ref, at, cols, lanes, scale, shift):
    top = []
    for a in at:
        act = top_ref[pl.ds(a, cols), lanes] * scale + shift
        top.append(act * sigmoid(act))
    return top


def pool_kernel(geom, domain_ref, top_ref, top_st, gain_t, bias_t, un_ref):
    frames, rows, cols, counts = geom
    pixels = rows * cols
    for f in range(frames):
        for lane in range(0, top_ref.shape[-1], LANES):
            lanes = slice(lane, lane + LANES)
            average, inverse = frame_tables(top_st[:, lanes], domain_ref[f], counts)
            scale = inverse * gain_t[:, lanes]
            shift = bias_t[:, lanes] - average * scale

            def one(i, _):
                at = [pl.multiple_of(f * pixels + (2 * i + h) * cols, cols) for h in (0, 1)]
                top = top_rows(top_ref, at, cols, lanes, scale, shift)
                weight = softmax_window(top, cols)
                pooled = pair_sum(weight[0] * top[0] + weight[1] * top[1], cols)
                for h in (0, 1):
                    un_ref[pl.ds(at[h], cols), lanes] = (weight[h] * pooled).astype(BF16)
                return 0

            lax.fori_loop(0, rows // 2, one, 0, unroll=2)


def pool_layer(geom, domain, top, top_st, gain_t, bias_t):
    pix, chans = top.shape
    args = (domain, top, top_st, gain_t, bias_t)
    return pl.pallas_call(
        functools.partial(pool_kernel, geom),
        in_specs=[SCALARS] + [whole(x.shape) for x in args[1:]],
        out_specs=whole((pix, chans)),
        out_shape=sds((pix, chans), BF16),
        compiler_params=params(),
        cost_estimate=pl.CostEstimate(flops=pix * chans * 20, bytes_accessed=pix * chans * 6, transcendentals=pix * chans * 2),
    )(*args)


def task_kernel(geom, domain_ref, top_ref, top_st, wide_ref, wide_st, gain_t, bias_t, gain_w, bias_w, task_ref, scr_ref):
    frames, rows, cols, counts = geom
    pixels = rows * cols
    chans = top_ref.shape[-1]
    for f in range(frames):
        for lane in range(0, chans, LANES):
            lanes = slice(lane, lane + LANES)

            def table(st, gain, bias, sl):
                average, inverse = frame_tables(st[:, sl], domain_ref[f], counts)
                scale = inverse * gain[:, sl]
                return scale, bias[:, sl] - average * scale

            t_scale, t_shift = table(top_st, gain_t, bias_t, lanes)
            wide = []
            for k in range(TASKS):
                sl = slice(k * chans + lane, k * chans + lane + LANES)
                wide.append((sl, *table(wide_st, gain_w, bias_w, sl)))

            def one(i, _):
                at = [pl.multiple_of(f * pixels + (2 * i + h) * cols, cols) for h in (0, 1)]
                top = top_rows(top_ref, at, cols, lanes, t_scale, t_shift)
                weight = softmax_window(top, cols)
                held = [w * t for w, t in zip(weight, top)]
                for k in range(TASKS):
                    sl, scale, shift = wide[k]
                    total = None
                    for h in (0, 1):
                        mask = sigmoid(wide_ref[pl.ds(at[h], cols), sl] * scale + shift)
                        term = mask * held[h]
                        total = term if total is None else total + term
                    scr_ref[k] = total
                    even = scr_ref[k, pl.ds(0, cols // 2, stride=2), :]
                    odd = scr_ref[k, pl.ds(1, cols // 2, stride=2), :]
                    task_ref[f, i, k, :, lanes] = even + odd
                return 0

            lax.fori_loop(0, rows // 2, one, 0, unroll=2)


def task_layer(geom, domain, top, top_st, wide, wide_st, gain_t, bias_t, gain_w, bias_w):
    frames, rows, cols, _ = geom
    pix, chans = top.shape
    task_shape = (frames, rows // 2, TASKS, cols // 2, chans)
    args = (domain, top, top_st, wide, wide_st, gain_t, bias_t, gain_w, bias_w)
    return pl.pallas_call(
        functools.partial(task_kernel, geom),
        in_specs=[SCALARS] + [whole(x.shape) for x in args[1:]],
        out_specs=whole(task_shape),
        out_shape=sds(task_shape, F32),
        scratch_shapes=[pltpu.VMEM((TASKS, cols, LANES), F32)],
        compiler_params=params(),
        cost_estimate=pl.CostEstimate(flops=pix * chans * 60, bytes_accessed=pix * chans * 28, transcendentals=pix * chans * 5),
    )(*args)


def pool_early_kernel(geom, domain_ref, top_ref, top_st, wide_ref, wide_st, gain_t, bias_t, gain_w, bias_w, cot_ref,
                      mix_ref, gw_ref, sums_ref, scr_ref):
    frames, rows, cols, counts = geom
    pixels = rows * cols
    chans = top_ref.shape[-1]
    for lane in range(0, chans, LANES):
        lanes = slice(lane, lane + LANES)
        sums = []
        for f in range(frames):
            average, inverse = frame_tables(top_st[:, lanes], domain_ref[f], counts)
            t_scale = inverse * gain_t[:, lanes]
            t_shift = bias_t[:, lanes] - average * t_scale
            wide = []
            for k in range(TASKS):
                sl = slice(k * chans + lane, k * chans + lane + LANES)
                wide.append((sl, *frame_tables(wide_st[:, sl], domain_ref[f], counts)))

            def one(i, carry):
                at = [pl.multiple_of(f * pixels + (2 * i + h) * cols, cols) for h in (0, 1)]
                top = []
                for h in (0, 1):
                    act = top_ref[pl.ds(at[h], cols), lanes] * t_scale + t_shift
                    top.append(act * sigmoid(act))
                weight = softmax_window(top, cols)
                held = [w * t for w, t in zip(weight, top)]
                mix = [None, None]
                new = []
                for k in range(TASKS):
                    sl, average, inverse = wide[k]
                    cot = spread_cols(scr_ref, cot_ref[f, i, k, :, lanes].astype(F32))
                    one_sum, two_sum = carry[2 * k], carry[2 * k + 1]
                    for h in (0, 1):
                        xhat = (wide_ref[pl.ds(at[h], cols), sl] - average) * inverse
                        mask = sigmoid(xhat * gain_w[:, sl] + bias_w[:, sl])
                        part = cot * mask
                        mix[h] = part if mix[h] is None else mix[h] + part
                        g = part * held[h] * (1.0 - mask)
                        gw_ref[pl.ds(at[h], cols), sl] = g
                        one_sum = one_sum + fold(g)
                        two_sum = two_sum + fold(g * xhat)
                    new += [one_sum, two_sum]
                for h in (0, 1):
                    mix_ref[pl.ds(at[h], cols), lanes] = mix[h]
                return tuple(new)

            zero = jnp.zeros((8, LANES), F32)
            sums.append(lax.fori_loop(0, rows // 2, one, (zero,) * (2 * TASKS)))
        for k in range(TASKS):
            first = [jnp.sum(s[2 * k], 0, keepdims=True) for s in sums]
            second = [jnp.sum(s[2 * k + 1], 0, keepdims=True) for s in sums]
            sl = slice(k * chans + lane, k * chans + lane + LANES)
            sums_ref[:, sl] = by_domain(first, second, domain_ref)


def pool_early(geom, domain, top, top_st, wide, wide_st, gain_t, bias_t, gain_w, bias_w, cot):
    _, _, cols, _ = geom
    pix, chans = top.shape
    args = (domain, top, top_st, wide, wide_st, gain_t, bias_t, gain_w, bias_w, cot)
    outs = [sds((pix, chans), F32), sds((pix, TASKS * chans), F32), sds((4, TASKS * chans), F32)]
    return pl.pallas_call(
        functools.partial(pool_early_kernel, geom),
        in_specs=[SCALARS] + [whole(x.shape) for x in args[1:]],
        out_specs=[whole(o.shape) for o in outs],
        out_shape=outs,
        scratch_shapes=[pltpu.VMEM((cols, LANES), F32)],
        compiler_params=params(),
        cost_estimate=pl.CostEstimate(flops=pix * chans * 90, bytes_accessed=pix * chans * 40, transcendentals=pix * chans * 5),
    )(*args)


def head_kernel(geom, domain_ref, bot_ref, bot_st, gate_ref, gate_st, gain_b, bias_b, gain_g, bias_g, cot_ref,
                maps_ref, gb_ref, gg_ref, sums_ref):
    frames, rows, cols, counts = geom
    pixels = rows * cols
    chans = bot_ref.shape[-1]
    for lane in range(0, chans, LANES):
        lanes = slice(lane, lane + LANES)
        sums = []
        for f in range(frames):
            b_mean, b_inv = frame_tables(bot_st[:, lanes], domain_ref[f], counts)
            gate = []
            for k in range(TASKS):
                sl = slice(k * chans + lane, k * chans + lane + LANES)
                gate.append((sl, *frame_tables(gate_st[:, sl], domain_ref[f], counts)))

            def one(r, carry):
                at = pl.multiple_of(f * pixels + r * cols, cols)
                b_hat = (bot_ref[pl.ds(at, cols), lanes] - b_mean) * b_inv
                act = b_hat * gain_b[:, lanes] + bias_b[:, lanes]
                s = sigmoid(act)
                bottom = act * s
                back = None
                new = []
                for k in range(TASKS):
                    sl, mean, inv = gate[k]
                    xhat = (gate_ref[pl.ds(at, cols), sl] - mean) * inv
                    value = sigmoid(xhat * gain_g[:, sl] + bias_g[:, sl])
                    maps_ref[k, pl.ds(at, cols), lanes] = value * bottom
                    cot = cot_ref[k, pl.ds(at, cols), lanes].astype(F32)
                    part = cot * value
                    back = part if back is None else back + part
                    g = part * bottom * (1.0 - value)
                    gg_ref[pl.ds(at, cols), sl] = g
                    new += [carry[2 * k] + fold(g), carry[2 * k + 1] + fold(g * xhat)]
                g = back * (s * (1.0 + act * (1.0 - s)))
                gb_ref[pl.ds(at, cols), lanes] = g
                new += [carry[-2] + fold(g), carry[-1] + fold(g * b_hat)]
                return tuple(new)

            zero = jnp.zeros((8, LANES), F32)
            sums.append(lax.fori_loop(0, rows, one, (zero,) * (2 * TASKS + 2), unroll=2))
        for k in range(TASKS + 1):
            first = [jnp.sum(s[2 * k], 0, keepdims=True) for s in sums]
            second = [jnp.sum(s[2 * k + 1], 0, keepdims=True) for s in sums]
            at = chans + k * chans + lane if k < TASKS else lane
            sums_ref[:, at : at + LANES] = by_domain(first, second, domain_ref)


def head_layer(geom, domain, bot, bot_st, gate, gate_st, gain_b, bias_b, gain_g, bias_g, cot):
    pix, chans = bot.shape
    args = (domain, bot, bot_st, gate, gate_st, gain_b, bias_b, gain_g, bias_g, cot)
    outs = [sds((TASKS, pix, chans), F32), sds((pix, chans), F32), sds((pix, TASKS * chans), F32),
            sds((4, (TASKS + 1) * chans), F32)]
    return pl.pallas_call(
        functools.partial(head_kernel, geom),
        in_specs=[SCALARS] + [whole(x.shape) for x in args[1:]],
        out_specs=[whole(o.shape) for o in outs],
        out_shape=outs,
        compiler_params=params(),
        cost_estimate=pl.CostEstimate(flops=pix * chans * 80, bytes_accessed=pix * chans * 44, transcendentals=pix * chans * 4),
    )(*args)


def norm_back_rows(g, pre, tables):
    mean, inv, scale, g_mean, g_cross = tables
    xhat = (pre - mean) * inv
    return scale * (g - g_mean - xhat * g_cross)


def back_tables(stats_ref, sums_ref, gain_ref, domain_at, counts):
    mean, inv = frame_tables(stats_ref[...], domain_at, counts)
    g_mean, g_cross = grad_tables(sums_ref[...], domain_at, counts)
    return mean, inv, inv * gain_ref[...], g_mean, g_cross


def backward_kernel(geom, added, epilogue, *refs):
    frames, rows, cols, counts = geom
    pixels = rows * cols
    refs = list(refs)
    domain_ref = refs.pop(0)
    g_ref, pre_ref, st_ref, sm_ref, gain_ref = (refs.pop(0) for _ in range(5))
    kernel_ref = refs.pop(0)
    add_ref = refs.pop(0) if added else None
    if epilogue in ("silu", "pool"):
        lpre_ref, lst_ref, lgain_ref, lbias_ref = (refs.pop(0) for _ in range(4))
    if epilogue == "pool":
        mix_ref = refs.pop(0)
    win_ref = refs.pop(0)
    out_ref = refs.pop(0)
    if epilogue != "none":
        sums_ref = refs.pop(0)
    step = pl.program_id(0)
    chans = kernel_ref.shape[0] // 3

    @pl.when(step == 0)
    def _():
        clear_edges(win_ref, rows)
        for f in range(frames):
            tables = back_tables(st_ref, sm_ref, gain_ref, domain_ref[f], counts)

            def one_row(r, _):
                at = pl.multiple_of(f * pixels + r * cols, cols)
                low = norm_back_rows(g_ref[pl.ds(at, cols), :], pre_ref[pl.ds(at, cols), :], tables)
                put_windows(win_ref, f, r, low, cols)
                return 0

            lax.fori_loop(0, rows, one_row, 0, unroll=2)

    source = jnp.concatenate([window(win_ref, 2 - b, 2 - step, rows) for b in range(3)], 1)
    weight = jnp.concatenate([kernel_ref[b * chans : (b + 1) * chans, :] for b in range(3)], 1)
    nt = (((1,), (1,)), ((), ()))
    part = lax.dot_general(source, weight, nt, preferred_element_type=F32)

    @pl.when(step == 0)
    def _():
        out_ref[...] = part + add_ref[...] if added else part

    @pl.when(step > 0)
    def _():
        out_ref[...] += part

    if epilogue == "none":
        return

    @pl.when(step == 2)
    def _():
        for lane in range(0, chans, LANES):
            lanes = slice(lane, lane + LANES)
            sums = []
            for f in range(frames):
                mean, inv = frame_tables(lst_ref[:, lanes], domain_ref[f], counts)

                def slope(at):
                    xhat = (lpre_ref[pl.ds(at, cols), lanes] - mean) * inv
                    act = xhat * lgain_ref[:, lanes] + lbias_ref[:, lanes]
                    s = sigmoid(act)
                    return xhat, act * s, s * (1.0 + act * (1.0 - s))

                def finish(at, g, xhat, carry):
                    out_ref[pl.ds(at, cols), lanes] = g
                    return carry[0] + fold(g), carry[1] + fold(g * xhat)

                def one_row(r, carry):
                    at = pl.multiple_of(f * pixels + r * cols, cols)
                    xhat, _, steep = slope(at)
                    return finish(at, out_ref[pl.ds(at, cols), lanes] * steep, xhat, carry)

                def one_pair(i, carry):
                    at = [pl.multiple_of(f * pixels + (2 * i + h) * cols, cols) for h in (0, 1)]
                    xhat, top, steep = zip(*(slope(a) for a in at))
                    weight = softmax_window(top, cols)
                    up = [out_ref[pl.ds(a, cols), lanes] for a in at]
                    mix = [mix_ref[pl.ds(a, cols), lanes] for a in at]
                    pooled = pair_sum(weight[0] * top[0] + weight[1] * top[1], cols)
                    d_pool = pair_sum(weight[0] * up[0] + weight[1] * up[1], cols)
                    flow = [m + d_pool for m in mix]
                    d_w = [u * pooled + fl * t for u, fl, t in zip(up, flow, top)]
                    centre = pair_sum(weight[0] * d_w[0] + weight[1] * d_w[1], cols)
                    for h in (0, 1):
                        d_top = weight[h] * (flow[h] + d_w[h] - centre)
                        carry = finish(at[h], d_top * steep[h], xhat[h], carry)
                    return carry

                zero = jnp.zeros((8, LANES), F32)
                if epilogue == "silu":
                    sums.append(lax.fori_loop(0, rows, one_row, (zero, zero), unroll=2))
                else:
                    sums.append(lax.fori_loop(0, rows // 2, one_pair, (zero, zero)))
            sums_ref[:, lanes] = by_domain(
                [jnp.sum(s[0], 0, keepdims=True) for s in sums],
                [jnp.sum(s[1], 0, keepdims=True) for s in sums],
                domain_ref,
            )


def backward_layer(geom, domain, top, kernel, added=None, lower=None, mix=None):
    frames, rows, cols, _ = geom
    pix, width = top[0].shape
    chans = kernel.shape[0] // 9
    args = [domain, *top, kernel]
    specs = [SCALARS] + [whole(x.shape) for x in top] + [pl.BlockSpec((3 * chans, width), lambda a: (a, 0))]
    win = (3, frames, rows + 2, cols, width)
    outs = [sds(win, BF16), sds((pix, chans), F32)]
    extra = [] if added is None else [added]
    epilogue = "none"
    if lower is not None:
        epilogue = "silu" if mix is None else "pool"
        extra += list(lower) + ([] if mix is None else [mix])
        outs.append(sds((4, chans), F32))
    return pl.pallas_call(
        functools.partial(backward_kernel, geom, added is not None, epilogue),
        grid=(3,),
        in_specs=specs + [whole(x.shape) for x in extra],
        out_specs=[whole(o.shape) for o in outs],
        out_shape=outs,
        compiler_params=params(1),
        cost_estimate=pl.CostEstimate(flops=2 * pix * kernel.size, bytes_accessed=kernel.size * 2 + pix * 10240, transcendentals=0),
    )(*args, *extra)


class Member:
    def __init__(self, at, shape, dp, fsdp, split=False):
        self.at, self.shape, self.split = at, shape, split
        self.vr = shape[0] // dp // (2 if split else 1)
        self.blocks = shape[1] // fsdp * (2 if split else 1) // LANES
        self.rows = self.vr * self.blocks

    def spots(self, i, j):
        if self.split:
            row, col = i * 2 * self.vr + (j & 1) * self.vr, (j >> 1) * self.blocks * LANES
        else:
            row, col = i * self.vr, j * self.blocks * LANES
        for k in range(self.blocks):
            yield self.at + k * self.vr, row, col + k * LANES


def collect_kernel(member, parts, me_ref, *refs):
    out_ref, sem = refs[-2:]
    fetch(member, parts, me_ref, refs[:-2], out_ref, sem)
    arrived(out_ref, sem)


def collect(pieces):
    return pl.pallas_call(
        functools.partial(collect_kernel, pieces.member, pieces.parts),
        in_specs=[SCALARS] + [ANYWHERE] * len(pieces.sources),
        out_specs=whole(pieces.shape),
        out_shape=sds(pieces.shape, BF16),
        scratch_shapes=[pltpu.SemaphoreType.DMA],
        grid=(1,),
        compiler_params=params(1),
        cost_estimate=pl.CostEstimate(flops=0, bytes_accessed=4 * pieces.shape[0] * pieces.shape[1], transcendentals=0),
    )(pieces.me, *pieces.sources)


def weight_parts(geom, step, act_ref, low_ref, tr_ref):
    rows = geom[1]

    @pl.when(step == 0)
    def _():
        tr_ref[...] = act_ref[...].astype(F32).T.astype(BF16)

    if len(low_ref.shape) == 5:
        for b in range(3):
            yield jnp.dot(tr_ref[...], window(low_ref, 2 - b, 2 - step, rows), preferred_element_type=F32)
    else:
        yield jnp.dot(tr_ref[...], low_ref[...], preferred_element_type=F32)


def weight_kernel(geom, act_ref, low_ref, out_ref, tr_ref):
    chans = tr_ref.shape[0]
    for b, part in enumerate(weight_parts(geom, pl.program_id(0), act_ref, low_ref, tr_ref)):
        out_ref[b * chans : (b + 1) * chans, :] = part.astype(BF16)


def weight_layer(geom, act, low):
    pix, chans = act.shape
    win = low.ndim == 5
    width = low.shape[-1]
    steps = 3 if win else 1
    out = sds((9 * chans if win else chans, width), BF16)
    return pl.pallas_call(
        functools.partial(weight_kernel, geom),
        grid=(steps,),
        in_specs=[whole(act.shape), whole(low.shape)],
        out_specs=pl.BlockSpec((out.shape[0] // steps, width), lambda a: (a, 0)),
        out_shape=out,
        scratch_shapes=[pltpu.VMEM((chans, pix), BF16)],
        compiler_params=params(1),
        cost_estimate=pl.CostEstimate(flops=2 * pix * out.size, bytes_accessed=out.size * 2 + pix * 4096, transcendentals=0),
    )(act, low)


def weight_blocks_kernel(geom, member, steps, far, aliased, *refs):
    refs = list(refs)
    me_ref, act_ref, low_ref = (refs.pop(0) for _ in range(3))
    if aliased:
        refs.pop(0)
    outs = [refs.pop(0) for _ in range(3 if far else 1)]
    scr_ref, tr_ref, sem = refs
    step = pl.program_id(0)
    chans = tr_ref.shape[0]
    for b, part in enumerate(weight_parts(geom, step, act_ref, low_ref, tr_ref)):
        scr_ref[pl.ds(pl.multiple_of(step * 3 * chans, chans) + b * chans, chans), :] = part.astype(BF16)

    def copies(i):
        if not far:
            for j in range(4):
                for at, row, col in member.spots(i, j):
                    yield scr_ref.at[pl.ds(row, member.vr), pl.ds(col, LANES)], outs[0].at[i * 4 + j, pl.ds(at, member.vr)]
            return
        me = me_ref[0]
        e = i ^ (me >> 2)
        q = ((e & 1) << 2) | (e & 2) | (e >> 2)
        for jd in range(4):
            dst = outs[2].at[jd >> 1, q] if jd & 1 else outs[jd >> 1].at[q]
            for at, row, col in member.spots(i, (me & 3) ^ jd):
                yield scr_ref.at[span(row, member.vr), span(col, LANES)], dst.at[pl.ds(at, member.vr)]

    share = member.shape[0] // 8
    done = 0
    for s in range(steps):
        ready = member.shape[0] * (s + 1) // steps // share

        @pl.when(step == s)
        def _(done=done, ready=ready):
            for i in range(done, ready):
                for src, dst in copies(i):
                    pltpu.make_async_copy(src, dst, sem).start()

        done = ready

    @pl.when(step == steps - 1)
    def _():
        pltpu.make_async_copy(scr_ref, scr_ref, sem).wait()


def weight_blocks(geom, me, act, low, member, rows, far, buffer=None):
    pix, chans = act.shape
    win = low.ndim == 5
    steps = 3 if win else 1
    shard = (rows, LANES)
    outs = [sds((8, *shard), BF16)] * 2 + [sds((2, 8, *shard), BF16)] if far else [sds((32, *shard), BF16)]
    args = [me, act, low] + ([] if buffer is None else [buffer])
    size = member.shape[0] * member.shape[1]
    got = pl.pallas_call(
        functools.partial(weight_blocks_kernel, geom, member, steps, far, buffer is not None),
        grid=(steps,),
        in_specs=[SCALARS, whole(act.shape), whole(low.shape)] + [ANYWHERE] * (buffer is not None),
        out_specs=[ANYWHERE] * len(outs),
        out_shape=outs,
        scratch_shapes=[pltpu.VMEM(member.shape, BF16), pltpu.VMEM((chans, pix), BF16), pltpu.SemaphoreType.DMA],
        input_output_aliases={} if buffer is None else {3: 0},
        compiler_params=params(1),
        cost_estimate=pl.CostEstimate(flops=2 * pix * size, bytes_accessed=size * 2 + pix * 4096, transcendentals=0),
    )(*args)
    return got if far else got[0]


def point_kernel(geom, pieces, *refs):
    frames, rows, cols, _ = geom
    pixels = rows * cols
    refs = list(refs)
    domain_ref, act_ref = refs.pop(0), refs.pop(0)
    if pieces:
        out_ref, sums_ref, matrix_ref, sem = refs[-4:]
        fetch(*pieces, refs[0], refs[1:-4], matrix_ref, sem)
        arrived(matrix_ref, sem)
    else:
        matrix_ref, out_ref, sums_ref = refs
    for lane in range(0, out_ref.shape[-1], 256):
        lanes = slice(lane, lane + 256)
        out_ref[:, lanes] = jnp.dot(act_ref[...], matrix_ref[:, lanes], preferred_element_type=F32)
        pairs = [column_sums(out_ref, f, pixels, lanes) for f in range(frames)]
        sums_ref[:, lanes] = by_domain([p[0] for p in pairs], [p[1] for p in pairs], domain_ref)


def point_layer(geom, domain, act, mat):
    pix, chans = act.shape
    width = mat.shape[1]
    pieces = isinstance(mat, Pieces)
    outs = [sds((pix, width), F32), sds((4, width), F32)] + [sds(mat.shape, BF16)] * pieces
    args = [domain, act] + ([mat.me, *mat.sources] if pieces else [mat])
    specs = [SCALARS, whole(act.shape)]
    specs += [SCALARS] + [ANYWHERE] * len(mat.sources) if pieces else [whole(mat.shape)]
    return pl.pallas_call(
        functools.partial(point_kernel, geom, (mat.member, mat.parts) if pieces else None),
        in_specs=specs,
        out_specs=[whole(o.shape) for o in outs],
        out_shape=outs,
        scratch_shapes=[pltpu.SemaphoreType.DMA] * pieces,
        grid=(1,),
        compiler_params=params(1),
        cost_estimate=pl.CostEstimate(flops=2 * pix * chans * width, bytes_accessed=chans * width * 2 + pix * width * 4, transcendentals=0),
    )(*args)


def point_back_kernel(geom, domain_ref, g_ref, pre_ref, st_ref, sm_ref, gain_ref, mat_ref, low_ref, out_ref):
    frames, rows, cols, counts = geom
    pixels = rows * cols
    for f in range(frames):
        tables = back_tables(st_ref, sm_ref, gain_ref, domain_ref[f], counts)

        def one_row(r, _):
            at = pl.multiple_of(f * pixels + r * cols, cols)
            low = norm_back_rows(g_ref[pl.ds(at, cols), :], pre_ref[pl.ds(at, cols), :], tables)
            low_ref[pl.ds(at, cols), :] = low.astype(BF16)
            return 0

        lax.fori_loop(0, rows, one_row, 0, unroll=2)
    part = lax.dot_general(low_ref[...], mat_ref[...], (((1,), (1,)), ((), ())), preferred_element_type=F32)

    @pl.when(pl.program_id(0) == 0)
    def _():
        out_ref[...] = part

    @pl.when(pl.program_id(0) > 0)
    def _():
        out_ref[...] += part


def point_back(geom, domain, g, pre, stats, sums, gain, mat):
    pix, width = g.shape
    chans = mat.shape[0]
    block = min(width, 512)
    while width % block:
        block -= 256
    col = lambda n: (0, n)
    specs = [SCALARS, pl.BlockSpec((pix, block), col), pl.BlockSpec((pix, block), col)]
    specs += [pl.BlockSpec((4, block), col)] * 2 + [pl.BlockSpec((1, block), col), pl.BlockSpec((chans, block), col)]
    outs = [sds((pix, width), BF16), sds((pix, chans), F32)]
    return pl.pallas_call(
        functools.partial(point_back_kernel, geom),
        grid=(width // block,),
        in_specs=specs,
        out_specs=[pl.BlockSpec((pix, block), col), whole((pix, chans))],
        out_shape=outs,
        compiler_params=params(1),
        cost_estimate=pl.CostEstimate(flops=2 * pix * mat.size, bytes_accessed=mat.size * 2 + pix * width * 10, transcendentals=0),
    )(domain, g, pre, stats, sums, gain, mat)


AXES = ("dp", "fsdp")
CORE, X, Y, Z_NEAR, Z_FAR = range(5)


def swap(x, bit):
    n = lax.axis_size(AXES)
    return lax.ppermute(x, AXES, [(i, i ^ (1 << bit)) for i in range(n)])


def bit_of(bit):
    return (lax.axis_index(AXES) >> bit) & 1


def all_bits():
    return range(lax.axis_size(AXES).bit_length() - 1)


def tied(value, to):
    return lax.optimization_barrier((value, to))[0]


class Links:
    def __init__(self):
        self.under_way = {}

    def busy(self, bit, *values):
        self.under_way.setdefault(bit, []).extend(values)

    def total(self, x, after=None):
        for bit in all_bits():
            for value in self.under_way.pop(bit, ()):
                x = tied(x, value)
            x = x + swap(x, bit)
            for start in (after or {}).get(bit, ()):
                start(x)
        return x


def half_rows(rows):
    return rows // 32 * 16


class Gather:
    def __init__(self, links, shard):
        self.links, self.shard, self.cut = links, shard, half_rows(shard.shape[0])

    def far(self, to=None):
        self.z = self.shard if to is None else tied(self.shard, to)
        self.seen = swap(self.z, Z_FAR)

    def near(self, to=None):
        z = jnp.stack([self.z, self.seen])
        z = z if to is None else tied(z, to)
        self.seen = swap(z, Z_NEAR)
        z = jnp.concatenate([z, self.seen])
        self.a, self.b = z[:, : self.cut], z[:, self.cut :]

    def first(self, to=None):
        a, b = (self.a, self.b) if to is None else (tied(self.a, to), tied(self.b, to))
        self.seen = swap(a, Y), swap(b, X)
        self.a, self.b = jnp.concatenate([a, self.seen[0]]), jnp.concatenate([b, self.seen[1]])

    def second(self, to=None):
        a, b = (self.a, self.b) if to is None else (tied(self.a, to), tied(self.b, to))
        self.seen = swap(a, X), swap(b, Y)
        self.held = [a, self.seen[0], b, self.seen[1]]

    def busy(self):
        self.links.busy(X, self.seen[0])
        self.links.busy(Y, self.seen[1])

    def finish(self, to=None):
        rows = self.shard.shape[0]
        self.sources, self.parts = [], []
        for core in (0, 1):
            for n, value in enumerate(self.held):
                z = [8 * (k >> 1) + 16 * (k & 1) for k in range(4)]
                if n < 2:
                    masks = [core + 2 * n + 4 * y + m for y in (0, 1) for m in z]
                else:
                    masks = [core + 4 * (n - 2) + 2 * x + m for x in (0, 1) for m in z]
                self.parts.append((0, self.cut, masks) if n < 2 else (self.cut, rows - self.cut, masks))
                self.sources.append(swap(value, CORE) if core else value)

    def pieces(self, member):
        return Pieces(member, self.parts, number(1), self.sources)


def number(entries):
    return jnp.full((entries,), lax.axis_index(AXES), jnp.int32)


def plus(a, b):
    return (a.astype(F32) + b.astype(F32)).astype(BF16)


class Scatter:
    def __init__(self, links, blocks):
        self.links = links
        near, far, send = blocks
        self.cut = half_rows(near.shape[1])
        got = swap(send, CORE)
        cut = self.cut
        self.a = [plus(near[:, :cut], got[0, :, :cut]), plus(far[:, :cut], got[1, :, :cut])]
        self.b = [
            jnp.stack([plus(near[s, cut:], got[0, s, cut:]), plus(far[s, cut:], got[1, s, cut:])])
            for s in (slice(0, 4), slice(4, 8))
        ]

    def first(self, to=None):
        send_a, send_b = self.a[1], self.b[1]
        if to is not None:
            send_a, send_b = tied(send_a, to), tied(send_b, to)
        got_a, got_b = swap(send_a, X), swap(send_b, Y)
        self.a = [plus(self.a[0][:4], got_a[:4]), plus(self.a[0][4:], got_a[4:])]
        self.b = [plus(self.b[0][0], got_b[0]), plus(self.b[0][1], got_b[1])]

    def second(self):
        got_a, got_b = swap(self.a[1], Y), swap(self.b[1], X)
        self.links.busy(Y, got_a)
        self.links.busy(X, got_b)
        self.z = [
            jnp.concatenate([plus(self.a[0][s], got_a[s]), plus(self.b[0][s], got_b[s])], 1)
            for s in (slice(0, 2), slice(2, 4))
        ]

    def along_z(self, to=None):
        send = self.z[1] if to is None else tied(self.z[1], to)
        got = swap(send, Z_NEAR)
        keep, send = plus(self.z[0][0], got[0]), plus(self.z[0][1], got[1])
        got = swap(send, Z_FAR)
        self.links.busy(Z_NEAR, got)
        self.out = keep.astype(F32) + got.astype(F32)


def rows_of_chip(shard):
    half = shard.shape[0] // 2
    odd = bit_of(CORE) == 1
    mine = jnp.where(odd, shard[half:], shard[:half])
    got = swap(jnp.where(odd, shard[:half], shard[half:]), CORE)
    return jnp.concatenate([jnp.where(odd, got, mine), jnp.where(odd, mine, got)], 1)


def columns_of_core(rows):
    half = rows.shape[1] // 2
    odd = bit_of(CORE) == 1
    mine = jnp.where(odd, rows[:, half:], rows[:, :half])
    got = swap(jnp.where(odd, rows[:, :half], rows[:, half:]), CORE)
    return jnp.concatenate([jnp.where(odd, got, mine), jnp.where(odd, mine, got)], 0)


def pack(x):
    return jnp.concatenate([x[:, k : k + LANES] for k in range(0, x.shape[1], LANES)], 0)


def unpack(x, blocks):
    rows = x.shape[0] // blocks
    return jnp.concatenate([x[k * rows : (k + 1) * rows] for k in range(blocks)], 1)


def in_three(x):
    high = lax.reduce_precision(x, 8, 7)
    middle = lax.reduce_precision(x - high, 8, 7)
    return jnp.stack([high, middle, x - high - middle]).astype(BF16)


def gather(x):
    x = x[None]
    for bit in all_bits():
        other = swap(x, bit)
        high = bit_of(bit) == 1
        x = jnp.concatenate([jnp.where(high, other, x), jnp.where(high, x, other)], 0)
    return x


def scatter(x):
    for bit in reversed(all_bits()):
        half = x.shape[0] // 2
        high = bit_of(bit) == 1
        send = jnp.where(high, x[:half], x[half:])
        keep = jnp.where(high, x[half:], x[:half])
        x = plus(keep, swap(send, bit))
    return x[0]


def gather_matrix(shard):
    dp, fsdp = lax.axis_size("dp"), lax.axis_size("fsdp")
    rows, cols = shard.shape
    full = gather(shard).reshape(dp, fsdp, rows, cols)
    return full.transpose(0, 2, 1, 3).reshape(dp * rows, fsdp * cols)


def scatter_matrix(full):
    dp, fsdp = lax.axis_size("dp"), lax.axis_size("fsdp")
    rows, cols = full.shape[0] // dp, full.shape[1] // fsdp
    parts = full.reshape(dp, rows, fsdp, cols).transpose(0, 2, 1, 3)
    return scatter(parts.reshape(dp * fsdp, rows, cols)).astype(F32)


class AnyMesh:
    def __init__(self, links, geom, weights, gains, biases):
        self.geom = geom
        self.mats = {name: gather_matrix(w) for name, w in weights.items()}
        self.affine = gather(jnp.stack([gains, biases])).transpose(1, 0, 2).reshape(2, 1, -1)
        self.grads = {}

    def get(self, name):
        return self.mats[name]

    def put(self, name, matrix):
        pass

    def during(self, point):
        return {}

    def add(self, name, act, low):
        self.grads[name] = scatter_matrix(weight_layer(self.geom, act, low))

    def step(self, point, value=None):
        pass


class ThisMesh:
    def __init__(self, links, geom, weights, gains, biases):
        self.geom, self.links = geom, links
        self.me = number(1)
        sizes = (8, 4)
        full = {n: (w.shape[0] * 8, w.shape[1] * 4) for n, w in weights.items()}
        at, packed, self.rest = 0, [], {}
        for name in ("six", "gating", "attend", "five", "four"):
            split = name in ("six", "gating")
            member = Member(at, full[name], *sizes, split=split)
            packed.append(pack(rows_of_chip(weights[name]) if split else weights[name]))
            self.rest[name] = member
            at += member.rows
        self.rest_rows = at
        self.rest_packed = jnp.concatenate(packed)
        self.lone = {n: Member(0, full[n], *sizes) for n in ("one", "two", "three")}
        affine = in_three(jnp.stack([gains, biases])).reshape(-1)
        affine = jnp.pad(affine, (0, 2048 - affine.shape[0])).reshape(16, LANES)
        two = self.lone["two"].rows
        self.g1 = Gather(links, weights["one"])
        self.g2 = Gather(links, jnp.concatenate([weights["two"], affine]))
        self.g3 = Gather(links, weights["three"])
        g1, g2, g3 = self.g1, self.g2, self.g3
        g1.far()
        g1.near()
        g2.far(g1.seen)
        g1.first()
        g2.near(g1.seen)
        g1.second()
        g1.finish()
        g3.far(g2.seen)
        g2.first(g1.seen)
        self.shards = lax.all_gather(tied(self.rest_packed, g1.seen), AXES)
        g3.near(g2.seen)
        g2.second()
        g2.busy()
        self.mats = {"one": g1.pieces(self.lone["one"])}
        self.grads, self.buffer, self.pending = {}, None, {}

    def get(self, name):
        if name in self.mats:
            return self.mats[name]
        if name == "two":
            self.g2.finish()
            rows = self.lone["two"].rows
            self.mats[name] = self.g2.pieces(self.lone["two"])
            flat = collect(self.g2.pieces(FlatMember(rows, 16)))
            parts = flat.reshape(32, 2048)[:, :960].astype(F32).reshape(32, 3, 2, 160)
            self.affine = (parts[:, 0] + parts[:, 1] + parts[:, 2]).transpose(1, 0, 2).reshape(2, 1, -1)
        elif name == "three":
            self.g3.finish()
            self.mats[name] = self.g3.pieces(self.lone["three"])
        else:
            self.mats[name] = Pieces(self.rest[name], [(0, self.rest_rows, None)], self.me, [self.shards])
        return self.mats[name]

    def put(self, name, matrix):
        self.mats[name] = matrix

    def during(self, point):
        if point == 1:

            def start(x):
                self.g3.first(x)
                self.g3.second()
                self.g3.busy()

            return {Y: [start]}
        if point == 12 and "three" in self.pending:

            def start(x):
                self.pending["three"].first(x)
                self.pending["three"].second()

            return {Y: [start]}
        return {}

    def add(self, name, act, low):
        if name in self.rest:
            self.buffer = weight_blocks(self.geom, self.me, act, low, self.rest[name], self.rest_rows, False, self.buffer)
            if name == "four":
                out = lax.psum_scatter(self.buffer, AXES, tiled=False)
                for n, m in self.rest.items():
                    value = unpack(out[m.at : m.at + m.rows], m.blocks)
                    self.grads[n] = (columns_of_core(value) if m.split else value).astype(F32)
        else:
            m = self.lone[name]
            blocks = weight_blocks(self.geom, self.me, act, low, m, m.rows, True)
            self.pending[name] = Scatter(self.links, blocks)

    def step(self, point, value=None):
        if point == "last":
            for name in ("two", "one"):
                s = self.pending[name]
                s.first()
                s.second()
            for name in ("three", "two", "one"):
                s = self.pending[name]
                s.along_z()
                self.grads[name] = s.out


class FlatMember:
    def __init__(self, at, rows):
        self.at, self.vr, self.rows, self.blocks, self.shape = at, rows, rows, 1, (32 * rows, LANES)

    def spots(self, i, j):
        yield self.at, (i * 4 + j) * self.vr, 0


def body(
    frames_in,
    domain,
    kernel_one,
    kernel_two,
    kernel_three,
    attn_enc,
    kernel_four,
    kernel_five,
    kernel_six,
    attn_dec,
    gains,
    biases,
    enc_cot,
    dec_cot,
):
    frames, rows, cols, _ = frames_in.shape
    total_frames = frames * lax.axis_size(AXES)
    first = total_frames * 5 // 8
    counts = (float(first * rows * cols), float((total_frames - first) * rows * cols))
    geom = (frames, rows, cols, counts)
    pix = frames * rows * cols
    source = frames_in.reshape(pix, C_IN)
    enc_cot = enc_cot.transpose(0, 1, 3, 2, 4)
    dec_cot = dec_cot.reshape(pix, TASKS, C_DEC).transpose(1, 0, 2)
    weights = dict(
        one=kernel_one, two=kernel_two, three=kernel_three, attend=attn_enc,
        four=kernel_four, five=kernel_five, six=kernel_six, gating=attn_dec,
    )
    links = Links()
    this = lax.axis_size("dp") == 8 and lax.axis_size("fsdp") == 4
    w = (ThisMesh if this else AnyMesh)(links, geom, weights, gains, biases)

    def forward(name, source, norm=None):
        got = forward_layer(geom, domain, source, w.get(name), norm)
        w.put(name, got[-1])
        return got[:3] if norm is not None else got[:2]

    def point(name, act):
        got = point_layer(geom, domain, act, w.get(name))
        w.put(name, got[-1])
        return got[:2]

    pre_1, local = forward("one", source)
    st_1 = links.total(local, w.during(1))
    w.get("two")
    widths = (C_MID, C_MID, C_MID, TASKS * C_MID, C_MID, C_MID, C_DEC, TASKS * C_DEC)
    gain, bias, at = [], [], 0
    for width in widths:
        gain.append(w.affine[0, :, at : at + width])
        bias.append(w.affine[1, :, at : at + width])
        at += width
    pre_2, local, act_1 = forward("two", pre_1, (st_1, gain[0], bias[0]))
    st_2 = links.total(local)
    pre_3, local, act_2 = forward("three", pre_2, (st_2, gain[1], bias[1]))
    st_3 = links.total(local)
    unpooled = pool_layer(geom, domain, pre_3, st_3, gain[2], bias[2])
    pre_4, local = forward("four", unpooled)
    st_4 = links.total(local)
    pre_5, local, act_4 = forward("five", pre_4, (st_4, gain[4], bias[4]))
    st_5 = links.total(local)
    pre_g, local_g = point("gating", act_4)
    pre_a, local_a = point("attend", act_2)
    pre_6, local, act_5 = forward("six", pre_5, (st_5, gain[5], bias[5]))
    both = links.total(jnp.concatenate([local, local_g, local_a], 1))
    st_6, st_g, st_a = both[:, :C_DEC], both[:, C_DEC : 4 * C_DEC], both[:, 4 * C_DEC :]
    task_maps, g_6, g_g, local = head_layer(
        geom, domain, pre_6, st_6, pre_g, st_g, gain[6], bias[6], gain[7], bias[7], dec_cot
    )
    both = links.total(local)
    sm_6, sm_g = both[:, :C_DEC], both[:, C_DEC:]
    pool_args = (geom, domain, pre_3, st_3, pre_a, st_a, gain[2], bias[2], gain[3], bias[3])
    mix, g_a, sums_a = pool_early(*pool_args, enc_cot)
    task_features = task_layer(*pool_args)

    win_6, g_5, local = backward_layer(
        geom, domain, (g_6, pre_6, st_6, sm_6, gain[6]), w.get("six"), lower=(pre_5, st_5, gain[5], bias[5])
    )
    both = links.total(jnp.concatenate([local, sums_a], 1))
    sm_5, sm_a = both[:, :C_MID], both[:, C_MID:]
    w.add("six", act_5, win_6)
    low_g, add_4 = point_back(geom, domain, g_g, pre_g, st_g, sm_g, gain[7], w.get("gating"))
    w.add("gating", act_4, low_g)
    win_5, g_4, local = backward_layer(
        geom, domain, (g_5, pre_5, st_5, sm_5, gain[5]), w.get("five"), added=add_4, lower=(pre_4, st_4, gain[4], bias[4])
    )
    sm_4 = links.total(local)
    low_a, add_2 = point_back(geom, domain, g_a, pre_a, st_a, sm_a, gain[3], w.get("attend"))
    w.add("attend", act_2, low_a)
    w.add("five", act_4, win_5)
    win_4, g_3, local = backward_layer(
        geom, domain, (g_4, pre_4, st_4, sm_4, gain[4]), w.get("four"), lower=(pre_3, st_3, gain[2], bias[2]), mix=mix
    )
    sm_3 = links.total(local)
    w.add("four", unpooled, win_4)
    win_3, g_2, local = backward_layer(
        geom, domain, (g_3, pre_3, st_3, sm_3, gain[2]), w.get("three"), added=add_2, lower=(pre_2, st_2, gain[1], bias[1])
    )
    sm_2 = links.total(local)
    w.add("three", act_2, win_3)
    win_2, g_1, local = backward_layer(
        geom, domain, (g_2, pre_2, st_2, sm_2, gain[1]), w.get("two"), lower=(pre_1, st_1, gain[0], bias[0])
    )
    sm_1 = links.total(local, w.during(12))
    w.add("two", act_1, win_2)
    win_1, frames_grad = backward_layer(geom, domain, (g_1, pre_1, st_1, sm_1, gain[0]), w.get("one"))
    w.add("one", source, win_1)
    w.step("last")

    sums = jnp.concatenate([sm_1, sm_2, sm_3, sm_a, sm_4, sm_5, sm_6, sm_g], 1)
    shard = gains.shape[0]
    mine = lax.dynamic_slice_in_dim(sums, lax.axis_index(AXES) * shard, shard, 1)
    return (
        task_features.transpose(0, 1, 3, 2, 4),
        task_maps.transpose(1, 0, 2).reshape(frames, rows, cols, TASKS, C_DEC),
        frames_grad.reshape(frames, rows, cols, C_IN),
        *(w.grads[n] for n in ("one", "two", "three", "attend", "four", "five", "six", "gating")),
        mine[2] + mine[3],
        mine[0] + mine[1],
    )


def solution(mesh):
    whole_split = P(AXES)
    matrix = P("dp", "fsdp")
    return jax.shard_map(
        body,
        mesh=mesh,
        in_specs=(whole_split, whole_split) + (matrix,) * 8 + (whole_split,) * 4,
        out_specs=(whole_split,) * 3 + (matrix,) * 8 + (whole_split,) * 2,
        check_vma=False,
    )
```

```python
import functools

import jax
import jax.numpy as jnp
from jax import lax
from jax.experimental import pallas as pl
from jax.experimental.pallas import tpu as pltpu
from jax.sharding import PartitionSpec as P

C_IN = 256
C_MID = 512
C_DEC = 256
TASKS = 3
EPS = 1e-05
LANES = 128
F32 = jnp.float32
BF16 = jnp.bfloat16
COST = 0.1
VMEM_LIMIT = 20 * 1024 * 1024


def params(grid_dims=0):
    return pltpu.CompilerParams(
        vmem_limit_bytes=VMEM_LIMIT,
        dimension_semantics=("arbitrary",) * grid_dims if grid_dims else None,
    )


def cost(flops, size):
    return pl.CostEstimate(flops=int(flops * COST), bytes_accessed=int(size * COST), transcendentals=0)


def whole(shape):
    zeros = (0,) * len(shape)
    return pl.BlockSpec(shape, lambda *_: zeros, pipeline_mode=pl.Buffered(1))


SCALARS = pl.BlockSpec(memory_space=pltpu.SMEM)


def sds(shape, dtype):
    return jax.ShapeDtypeStruct(shape, dtype)


def sigmoid(v):
    return 0.5 * jnp.tanh(0.5 * v) + 0.5


def frame_tables(stats, domain_at, counts):
    first = domain_at == 0
    share = jnp.where(first, 1.0 / counts[0], 1.0 / counts[1])
    average = jnp.where(first, stats[0:1], stats[1:2]) * share
    square = jnp.where(first, stats[2:3], stats[3:4]) * share
    return average, lax.rsqrt(square - average * average + EPS)


def grad_tables(sums, domain_at, counts):
    first = domain_at == 0
    share = jnp.where(first, 1.0 / counts[0], 1.0 / counts[1])
    return (
        jnp.where(first, sums[0:1], sums[1:2]) * share,
        jnp.where(first, sums[2:3], sums[3:4]) * share,
    )


def by_domain(first, second, domain_ref):
    rows = []
    for per_frame in (first, second):
        for d in (0, 1):
            total = None
            for f, value in enumerate(per_frame):
                term = jnp.where(domain_ref[f] == d, value, jnp.zeros_like(value))
                total = term if total is None else total + term
            rows.append(total)
    return jnp.concatenate(rows, 0)


def fold(x):
    return jnp.sum(x.reshape(-1, 8, x.shape[-1]), 0)


def put_windows(win_ref, f, row, value, cols):
    col = lax.broadcasted_iota(jnp.int32, value.shape, 0)
    left = jnp.where(col == 0, 0.0, pltpu.roll(value, 1, 0))
    right = jnp.where(col == cols - 1, 0.0, pltpu.roll(value, cols - 1, 0))
    win_ref[0, f, row + 1] = left.astype(BF16)
    win_ref[1, f, row + 1] = value.astype(BF16)
    win_ref[2, f, row + 1] = right.astype(BF16)


def clear_edges(win_ref, rows):
    shape = win_ref.shape
    for b in range(3):
        for f in range(shape[1]):
            win_ref[b, f, 0] = jnp.zeros(shape[3:], BF16)
            win_ref[b, f, rows + 1] = jnp.zeros(shape[3:], BF16)


def window(win_ref, b, row_at, rows):
    part = win_ref[b, :, pl.ds(row_at, rows)]
    return part.reshape(-1, part.shape[-1])


def column_sums(ref, f, pixels, lanes, step=64):
    def add(i, carry):
        part = ref[pl.ds(f * pixels + i * step, step), lanes]
        return carry[0] + fold(part), carry[1] + fold(part * part)

    width = lanes.stop - lanes.start
    zero = jnp.zeros((8, width), F32)
    one, two = lax.fori_loop(0, pixels // step, add, (zero, zero), unroll=2)
    return jnp.sum(one, 0, keepdims=True), jnp.sum(two, 0, keepdims=True)


def in_hbm(x):
    return pltpu.with_memory_space_constraint(x, pltpu.HBM)


class Pieces:
    def __init__(self, member, parts, me, sources):
        self.member, self.parts, self.me = member, parts, me
        self.sources = [in_hbm(x) for x in sources]
        self.shape = member.shape


def span(start, size):
    return pl.ds(start if isinstance(start, int) else pl.multiple_of(start, size & -size), size)


def fetch(member, parts, me_ref, sources, dst_ref, sem):
    me = me_ref[0]
    for (first, size, masks), src in zip(parts, sources):
        for q in range(src.shape[0]):
            d = q if masks is None else me ^ masks[q]
            for at, row, col in member.spots(d >> 2, d & 3):
                low, high = max(at, first), min(at + member.vr, first + size)
                if low < high:
                    pltpu.make_async_copy(
                        src.at[q, pl.ds(low - first, high - low)],
                        dst_ref.at[span(row + (low - at), high - low), span(col, LANES)],
                        sem,
                    ).start()


def arrived(ref, sem):
    pltpu.make_async_copy(ref, ref, sem).wait()


def forward_kernel(geom, normed, pieces, *refs):
    frames, rows, cols, counts = geom
    pixels = rows * cols
    refs = list(refs)
    domain_ref = refs.pop(0)
    source_ref = refs.pop(0)
    if normed:
        stats_ref, gain_ref, bias_ref = refs.pop(0), refs.pop(0), refs.pop(0)
    if pieces:
        me_ref = refs.pop(0)
        sources = [refs.pop(0) for _ in pieces[1]]
    else:
        kernel_ref = refs.pop(0)
    out_ref = refs.pop(0)
    sums_ref = refs.pop(0)
    act_ref = refs.pop(0) if normed else None
    if pieces:
        matrix_ref = refs.pop(0)
    win_ref = refs.pop(0)
    if pieces:
        held_ref, sem = refs.pop(0), refs.pop(0)
    step = pl.program_id(0)
    chans = win_ref.shape[-1]

    @pl.when(step == 0)
    def _():
        if pieces:
            fetch(*pieces, me_ref, sources, held_ref, sem.at[0])
        clear_edges(win_ref, rows)
        for f in range(frames):
            if normed:
                average, inverse = frame_tables(stats_ref[...], domain_ref[f], counts)
                scale = inverse * gain_ref[...]
                shift = bias_ref[...] - average * scale

            def one_row(r, _):
                at = pl.multiple_of(f * pixels + r * cols, cols)
                value = source_ref[pl.ds(at, cols), :].astype(F32)
                if normed:
                    act = value * scale + shift
                    value = act * sigmoid(act)
                    act_ref[pl.ds(at, cols), :] = value.astype(BF16)
                put_windows(win_ref, f, r, value, cols)
                return 0

            lax.fori_loop(0, rows, one_row, 0, unroll=2)
        if pieces:
            arrived(held_ref, sem.at[0])
            pltpu.make_async_copy(held_ref, matrix_ref, sem.at[1]).start()

    source = jnp.concatenate([window(win_ref, b, step, rows) for b in range(3)], 1)
    if pieces:
        matrix = held_ref[pl.ds(pl.multiple_of(step * 3 * chans, 3 * chans), 3 * chans), :]
    else:
        matrix = kernel_ref[...]
    part = jnp.dot(source, matrix, preferred_element_type=F32)

    @pl.when(step == 0)
    def _():
        out_ref[...] = part

    @pl.when(step > 0)
    def _():
        out_ref[...] += part

    @pl.when(step == 2)
    def _():
        for lane in range(0, out_ref.shape[-1], 256):
            lanes = slice(lane, lane + 256)
            pairs = [column_sums(out_ref, f, pixels, lanes) for f in range(frames)]
            sums_ref[:, lanes] = by_domain([p[0] for p in pairs], [p[1] for p in pairs], domain_ref)
        if pieces:
            pltpu.make_async_copy(held_ref, matrix_ref, sem.at[1]).wait()


ANYWHERE = pl.BlockSpec(memory_space=pl.ANY)


def forward_layer(geom, domain, source, kernel, norm=None):
    frames, rows, cols, _ = geom
    pix, chans = source.shape
    width = kernel.shape[1]
    pieces = isinstance(kernel, Pieces)
    args, specs = [domain, source], [SCALARS, whole(source.shape)]
    if norm is not None:
        args += list(norm)
        specs += [whole(x.shape) for x in norm]
    if pieces:
        args += [kernel.me, *kernel.sources]
        specs += [SCALARS] + [ANYWHERE] * len(kernel.sources)
    else:
        args.append(kernel)
        specs.append(pl.BlockSpec((3 * chans, width), lambda a: (a, 0)))
    outs, out_specs = [sds((pix, width), F32)], [whole((pix, width))]
    outs.append(sds((4, width), F32))
    out_specs.append(whole((4, width)))
    if norm is not None:
        outs.append(sds((pix, chans), BF16))
        out_specs.append(whole((pix, chans)))
    scratch = [pltpu.VMEM((3, frames, rows + 2, cols, chans), BF16)]
    if pieces:
        outs.append(pltpu.HBM(kernel.shape, BF16))
        out_specs.append(ANYWHERE)
        scratch += [pltpu.VMEM(kernel.shape, BF16), pltpu.SemaphoreType.DMA((2,))]
    size = kernel.shape[0] * kernel.shape[1]
    return pl.pallas_call(
        functools.partial(forward_kernel, geom, norm is not None, (kernel.member, kernel.parts) if pieces else None),
        grid=(3,),
        in_specs=specs,
        out_specs=out_specs,
        out_shape=outs,
        scratch_shapes=scratch,
        compiler_params=params(1),
        cost_estimate=cost(2 * pix * size, size * 2 + pix * 4096),
    )(*args)


def pair_sum(x, cols):
    even = lax.broadcasted_iota(jnp.int32, x.shape, 0) % 2 == 0
    return x + jnp.where(even, pltpu.roll(x, cols - 1, 0), pltpu.roll(x, 1, 0))


def softmax_window(top, cols):
    exps = [jnp.exp(t) for t in top]
    share = 1.0 / pair_sum(exps[0] + exps[1], cols)
    return [e * share for e in exps]


def spread_cols(scr_ref, x):
    half = x.shape[0]
    scr_ref[pl.ds(0, half, stride=2), :] = x
    scr_ref[pl.ds(1, half, stride=2), :] = x
    return scr_ref[...]


def top_rows(top_ref, at, cols, lanes, scale, shift):
    top = []
    for a in at:
        act = top_ref[pl.ds(a, cols), lanes] * scale + shift
        top.append(act * sigmoid(act))
    return top


def pool_kernel(geom, domain_ref, top_ref, top_st, gain_t, bias_t, un_ref):
    frames, rows, cols, counts = geom
    pixels = rows * cols
    for f in range(frames):
        for lane in range(0, top_ref.shape[-1], LANES):
            lanes = slice(lane, lane + LANES)
            average, inverse = frame_tables(top_st[:, lanes], domain_ref[f], counts)
            scale = inverse * gain_t[:, lanes]
            shift = bias_t[:, lanes] - average * scale

            def one(i, _):
                at = [pl.multiple_of(f * pixels + (2 * i + h) * cols, cols) for h in (0, 1)]
                top = top_rows(top_ref, at, cols, lanes, scale, shift)
                weight = softmax_window(top, cols)
                pooled = pair_sum(weight[0] * top[0] + weight[1] * top[1], cols)
                for h in (0, 1):
                    un_ref[pl.ds(at[h], cols), lanes] = (weight[h] * pooled).astype(BF16)
                return 0

            lax.fori_loop(0, rows // 2, one, 0, unroll=2)


def pool_layer(geom, domain, top, top_st, gain_t, bias_t):
    pix, chans = top.shape
    args = (domain, top, top_st, gain_t, bias_t)
    return pl.pallas_call(
        functools.partial(pool_kernel, geom),
        in_specs=[SCALARS] + [whole(x.shape) for x in args[1:]],
        out_specs=whole((pix, chans)),
        out_shape=sds((pix, chans), BF16),
        compiler_params=params(),
        cost_estimate=cost(pix * chans * 20, pix * chans * 6),
    )(*args)


def task_kernel(geom, domain_ref, top_ref, top_st, gain_t, bias_t, *refs):
    frames, rows, cols, counts = geom
    pixels = rows * cols
    masks = [refs[4 * k : 4 * k + 4] for k in range(TASKS)]
    task_ref, scr_ref = refs[-2:]
    for f in range(frames):
        for lane in range(0, top_ref.shape[-1], LANES):
            lanes = slice(lane, lane + LANES)

            def table(st, gain, bias):
                average, inverse = frame_tables(st[:, lanes], domain_ref[f], counts)
                scale = inverse * gain[:, lanes]
                return scale, bias[:, lanes] - average * scale

            t_scale, t_shift = table(top_st, gain_t, bias_t)
            wide = [table(*mask[1:]) for mask in masks]

            def one(i, _):
                at = [pl.multiple_of(f * pixels + (2 * i + h) * cols, cols) for h in (0, 1)]
                top = top_rows(top_ref, at, cols, lanes, t_scale, t_shift)
                weight = softmax_window(top, cols)
                held = [w * t for w, t in zip(weight, top)]
                for k in range(TASKS):
                    scale, shift = wide[k]
                    total = None
                    for h in (0, 1):
                        term = sigmoid(masks[k][0][pl.ds(at[h], cols), lanes] * scale + shift) * held[h]
                        total = term if total is None else total + term
                    scr_ref[k] = total
                    even = scr_ref[k, pl.ds(0, cols // 2, stride=2), :]
                    odd = scr_ref[k, pl.ds(1, cols // 2, stride=2), :]
                    task_ref[f, i, k, :, lanes] = even + odd
                return 0

            lax.fori_loop(0, rows // 2, one, 0, unroll=2)


def task_layer(geom, domain, top, top_st, gain_t, bias_t, masks):
    frames, rows, cols, _ = geom
    pix, chans = top.shape
    task_shape = (frames, rows // 2, TASKS, cols // 2, chans)
    args = (domain, top, top_st, gain_t, bias_t, *(x for mask in masks for x in mask))
    return pl.pallas_call(
        functools.partial(task_kernel, geom),
        in_specs=[SCALARS] + [whole(x.shape) for x in args[1:]],
        out_specs=whole(task_shape),
        out_shape=sds(task_shape, F32),
        scratch_shapes=[pltpu.VMEM((TASKS, cols, LANES), F32)],
        compiler_params=params(),
        cost_estimate=cost(pix * chans * 60, pix * chans * 28),
    )(*args)


def pool_early_kernel(geom, first, domain_ref, top_ref, top_st, gain_t, bias_t, wide_ref, wide_st, gain_w, bias_w, cot_ref, *refs):
    frames, rows, cols, counts = geom
    pixels = rows * cols
    mix_ref, gw_ref, sums_ref, scr_ref = refs[-4:]
    for lane in range(0, top_ref.shape[-1], LANES):
        lanes = slice(lane, lane + LANES)
        sums = []
        for f in range(frames):
            average, inverse = frame_tables(top_st[:, lanes], domain_ref[f], counts)
            t_scale = inverse * gain_t[:, lanes]
            t_shift = bias_t[:, lanes] - average * t_scale
            w_mean, w_inv = frame_tables(wide_st[:, lanes], domain_ref[f], counts)

            def one(i, carry):
                at = [pl.multiple_of(f * pixels + (2 * i + h) * cols, cols) for h in (0, 1)]
                top = top_rows(top_ref, at, cols, lanes, t_scale, t_shift)
                weight = softmax_window(top, cols)
                cot = spread_cols(scr_ref, cot_ref[f, i, :, lanes].astype(F32))
                one_sum, two_sum = carry
                for h in (0, 1):
                    xhat = (wide_ref[pl.ds(at[h], cols), lanes] - w_mean) * w_inv
                    mask = sigmoid(xhat * gain_w[:, lanes] + bias_w[:, lanes])
                    part = cot * mask
                    mix = part if first else refs[0][pl.ds(at[h], cols), lanes] + part
                    mix_ref[pl.ds(at[h], cols), lanes] = mix
                    g = part * (weight[h] * top[h]) * (1.0 - mask)
                    gw_ref[pl.ds(at[h], cols), lanes] = g
                    one_sum = one_sum + fold(g)
                    two_sum = two_sum + fold(g * xhat)
                return one_sum, two_sum

            zero = jnp.zeros((8, LANES), F32)
            sums.append(lax.fori_loop(0, rows // 2, one, (zero, zero), unroll=2))
        sums_ref[:, lanes] = by_domain(
            [jnp.sum(s[0], 0, keepdims=True) for s in sums], [jnp.sum(s[1], 0, keepdims=True) for s in sums], domain_ref
        )


def pool_early(geom, domain, _, top_st, gain_t, bias_t, wide, wide_st, gain_w, bias_w, cot, top, mix=None):
    cols = geom[2]
    pix, chans = top.shape
    args = (domain, top, top_st, gain_t, bias_t, wide, wide_st, gain_w, bias_w, cot) + (() if mix is None else (mix,))
    outs = [sds((pix, chans), F32)] * 2 + [sds((4, chans), F32)]
    return pl.pallas_call(
        functools.partial(pool_early_kernel, geom, mix is None),
        in_specs=[SCALARS] + [whole(x.shape) for x in args[1:]],
        out_specs=[whole(o.shape) for o in outs],
        out_shape=outs,
        scratch_shapes=[pltpu.VMEM((cols, LANES), F32)],
        compiler_params=params(),
        cost_estimate=cost(pix * chans * 40, pix * chans * 20),
    )(*args)


def head_kernel(geom, domain_ref, bot_ref, bot_st, gate_ref, gate_st, gain_b, bias_b, gain_g, bias_g, cot_ref,
                maps_ref, gb_ref, gg_ref, sums_ref):
    frames, rows, cols, counts = geom
    pixels = rows * cols
    chans = bot_ref.shape[-1]
    for lane in range(0, chans, LANES):
        lanes = slice(lane, lane + LANES)
        sums = []
        for f in range(frames):
            b_mean, b_inv = frame_tables(bot_st[:, lanes], domain_ref[f], counts)
            gate = []
            for k in range(TASKS):
                sl = slice(k * chans + lane, k * chans + lane + LANES)
                gate.append((sl, *frame_tables(gate_st[:, sl], domain_ref[f], counts)))

            def one(r, carry):
                at = pl.multiple_of(f * pixels + r * cols, cols)
                b_hat = (bot_ref[pl.ds(at, cols), lanes] - b_mean) * b_inv
                act = b_hat * gain_b[:, lanes] + bias_b[:, lanes]
                s = sigmoid(act)
                bottom = act * s
                back = None
                new = []
                for k in range(TASKS):
                    sl, mean, inv = gate[k]
                    xhat = (gate_ref[pl.ds(at, cols), sl] - mean) * inv
                    value = sigmoid(xhat * gain_g[:, sl] + bias_g[:, sl])
                    maps_ref[k, pl.ds(at, cols), lanes] = value * bottom
                    cot = cot_ref[k, pl.ds(at, cols), lanes].astype(F32)
                    part = cot * value
                    back = part if back is None else back + part
                    g = part * bottom * (1.0 - value)
                    gg_ref[pl.ds(at, cols), sl] = g
                    new += [carry[2 * k] + fold(g), carry[2 * k + 1] + fold(g * xhat)]
                g = back * (s * (1.0 + act * (1.0 - s)))
                gb_ref[pl.ds(at, cols), lanes] = g
                new += [carry[-2] + fold(g), carry[-1] + fold(g * b_hat)]
                return tuple(new)

            zero = jnp.zeros((8, LANES), F32)
            sums.append(lax.fori_loop(0, rows, one, (zero,) * (2 * TASKS + 2), unroll=2))
        for k in range(TASKS + 1):
            first = [jnp.sum(s[2 * k], 0, keepdims=True) for s in sums]
            second = [jnp.sum(s[2 * k + 1], 0, keepdims=True) for s in sums]
            at = chans + k * chans + lane if k < TASKS else lane
            sums_ref[:, at : at + LANES] = by_domain(first, second, domain_ref)


def head_layer(geom, domain, bot, bot_st, gate, gate_st, gain_b, bias_b, gain_g, bias_g, cot):
    pix, chans = bot.shape
    args = (domain, bot, bot_st, gate, gate_st, gain_b, bias_b, gain_g, bias_g, cot)
    outs = [sds((TASKS, pix, chans), F32), sds((pix, chans), F32), sds((pix, TASKS * chans), F32),
            sds((4, (TASKS + 1) * chans), F32)]
    return pl.pallas_call(
        functools.partial(head_kernel, geom),
        in_specs=[SCALARS] + [whole(x.shape) for x in args[1:]],
        out_specs=[whole(o.shape) for o in outs],
        out_shape=outs,
        compiler_params=params(),
        cost_estimate=cost(pix * chans * 80, pix * chans * 44),
    )(*args)


def norm_back_rows(g, pre, tables):
    mean, inv, scale, g_mean, g_cross = tables
    xhat = (pre - mean) * inv
    return scale * (g - g_mean - xhat * g_cross)


def back_tables(stats_ref, sums_ref, gain_ref, domain_at, counts):
    mean, inv = frame_tables(stats_ref[...], domain_at, counts)
    g_mean, g_cross = grad_tables(sums_ref[...], domain_at, counts)
    return mean, inv, inv * gain_ref[...], g_mean, g_cross


def backward_kernel(geom, added, epilogue, *refs):
    frames, rows, cols, counts = geom
    pixels = rows * cols
    refs = list(refs)
    domain_ref = refs.pop(0)
    g_ref, pre_ref, st_ref, sm_ref, gain_ref = (refs.pop(0) for _ in range(5))
    kernel_ref = refs.pop(0)
    add_ref = refs.pop(0) if added else None
    if epilogue in ("silu", "pool"):
        lpre_ref, lst_ref, lgain_ref, lbias_ref = (refs.pop(0) for _ in range(4))
    if epilogue == "pool":
        mix_ref = refs.pop(0)
    win_ref = refs.pop(0)
    out_ref = refs.pop(0)
    if epilogue != "none":
        sums_ref = refs.pop(0)
    step = pl.program_id(0)
    chans = kernel_ref.shape[0] // 3

    @pl.when(step == 0)
    def _():
        clear_edges(win_ref, rows)
        for f in range(frames):
            tables = back_tables(st_ref, sm_ref, gain_ref, domain_ref[f], counts)

            def one_row(r, _):
                at = pl.multiple_of(f * pixels + r * cols, cols)
                low = norm_back_rows(g_ref[pl.ds(at, cols), :], pre_ref[pl.ds(at, cols), :], tables)
                put_windows(win_ref, f, r, low, cols)
                return 0

            lax.fori_loop(0, rows, one_row, 0, unroll=2)

    source = jnp.concatenate([window(win_ref, 2 - b, 2 - step, rows) for b in range(3)], 1)
    weight = jnp.concatenate([kernel_ref[b * chans : (b + 1) * chans, :] for b in range(3)], 1)
    nt = (((1,), (1,)), ((), ()))
    part = lax.dot_general(source, weight, nt, preferred_element_type=F32)

    @pl.when(step == 0)
    def _():
        out_ref[...] = part + add_ref[...] if added else part

    @pl.when(step > 0)
    def _():
        out_ref[...] += part

    if epilogue == "none":
        return

    @pl.when(step == 2)
    def _():
        for lane in range(0, chans, LANES):
            lanes = slice(lane, lane + LANES)
            sums = []
            for f in range(frames):
                mean, inv = frame_tables(lst_ref[:, lanes], domain_ref[f], counts)

                def slope(at):
                    xhat = (lpre_ref[pl.ds(at, cols), lanes] - mean) * inv
                    act = xhat * lgain_ref[:, lanes] + lbias_ref[:, lanes]
                    s = sigmoid(act)
                    return xhat, act * s, s * (1.0 + act * (1.0 - s))

                def finish(at, g, xhat, carry):
                    out_ref[pl.ds(at, cols), lanes] = g
                    return carry[0] + fold(g), carry[1] + fold(g * xhat)

                def one_row(r, carry):
                    at = pl.multiple_of(f * pixels + r * cols, cols)
                    xhat, _, steep = slope(at)
                    return finish(at, out_ref[pl.ds(at, cols), lanes] * steep, xhat, carry)

                def one_pair(i, carry):
                    at = [pl.multiple_of(f * pixels + (2 * i + h) * cols, cols) for h in (0, 1)]
                    xhat, top, steep = zip(*(slope(a) for a in at))
                    weight = softmax_window(top, cols)
                    up = [out_ref[pl.ds(a, cols), lanes] for a in at]
                    mix = [mix_ref[pl.ds(a, cols), lanes] for a in at]
                    pooled = pair_sum(weight[0] * top[0] + weight[1] * top[1], cols)
                    d_pool = pair_sum(weight[0] * up[0] + weight[1] * up[1], cols)
                    flow = [m + d_pool for m in mix]
                    d_w = [u * pooled + fl * t for u, fl, t in zip(up, flow, top)]
                    centre = pair_sum(weight[0] * d_w[0] + weight[1] * d_w[1], cols)
                    for h in (0, 1):
                        d_top = weight[h] * (flow[h] + d_w[h] - centre)
                        carry = finish(at[h], d_top * steep[h], xhat[h], carry)
                    return carry

                zero = jnp.zeros((8, LANES), F32)
                if epilogue == "silu":
                    sums.append(lax.fori_loop(0, rows, one_row, (zero, zero), unroll=2))
                else:
                    sums.append(lax.fori_loop(0, rows // 2, one_pair, (zero, zero)))
            sums_ref[:, lanes] = by_domain(
                [jnp.sum(s[0], 0, keepdims=True) for s in sums],
                [jnp.sum(s[1], 0, keepdims=True) for s in sums],
                domain_ref,
            )


def backward_layer(geom, domain, top, kernel, added=None, lower=None, mix=None):
    frames, rows, cols, _ = geom
    pix, width = top[0].shape
    chans = kernel.shape[0] // 9
    args = [domain, *top, in_hbm(kernel)]
    specs = [SCALARS] + [whole(x.shape) for x in top] + [pl.BlockSpec((3 * chans, width), lambda a: (a, 0))]
    win = (3, frames, rows + 2, cols, width)
    outs = [sds(win, BF16), sds((pix, chans), F32)]
    extra = [] if added is None else [added]
    epilogue = "none"
    if lower is not None:
        epilogue = "silu" if mix is None else "pool"
        extra += list(lower) + ([] if mix is None else [mix])
        outs.append(sds((4, chans), F32))
    return pl.pallas_call(
        functools.partial(backward_kernel, geom, added is not None, epilogue),
        grid=(3,),
        in_specs=specs + [whole(x.shape) for x in extra],
        out_specs=[whole(o.shape) for o in outs],
        out_shape=outs,
        compiler_params=params(1),
        cost_estimate=cost(2 * pix * kernel.size, kernel.size * 2 + pix * 10240),
    )(*args, *extra)


def low_kernel(geom, domain_ref, g_ref, pre_ref, st_ref, sm_ref, gain_ref, win_ref):
    frames, rows, cols, counts = geom
    pixels = rows * cols
    clear_edges(win_ref, rows)
    for f in range(frames):
        tables = back_tables(st_ref, sm_ref, gain_ref, domain_ref[f], counts)

        def one_row(r, _):
            at = pl.multiple_of(f * pixels + r * cols, cols)
            low = norm_back_rows(g_ref[pl.ds(at, cols), :], pre_ref[pl.ds(at, cols), :], tables)
            put_windows(win_ref, f, r, low, cols)
            return 0

        lax.fori_loop(0, rows, one_row, 0, unroll=2)


def low_layer(geom, domain, top):
    frames, rows, cols, _ = geom
    pix, width = top[0].shape
    out = sds((3, frames, rows + 2, cols, width), BF16)
    return pl.pallas_call(
        functools.partial(low_kernel, geom),
        grid=(1,),
        in_specs=[SCALARS] + [whole(x.shape) for x in top],
        out_specs=whole(out.shape),
        out_shape=out,
        compiler_params=params(1),
        cost_estimate=cost(pix * width * 20, pix * width * 14),
    )(domain, *top)


def input_kernel(geom, win_ref, kernel_ref, out_ref):
    rows = geom[1]
    step = pl.program_id(0)
    chans = kernel_ref.shape[0] // 3
    source = jnp.concatenate([window(win_ref, 2 - b, 2 - step, rows) for b in range(3)], 1)
    weight = jnp.concatenate([kernel_ref[b * chans : (b + 1) * chans, :] for b in range(3)], 1)
    part = lax.dot_general(source, weight, (((1,), (1,)), ((), ())), preferred_element_type=F32)

    @pl.when(step == 0)
    def _():
        out_ref[...] = part

    @pl.when(step > 0)
    def _():
        out_ref[...] += part


def input_layer(geom, win, kernel):
    frames, rows, cols, _ = geom
    pix = frames * rows * cols
    chans, width = kernel.shape[0] // 9, kernel.shape[1]
    return pl.pallas_call(
        functools.partial(input_kernel, geom),
        grid=(3,),
        in_specs=[whole(win.shape), pl.BlockSpec((3 * chans, width), lambda a: (a, 0))],
        out_specs=whole((pix, chans)),
        out_shape=sds((pix, chans), F32),
        compiler_params=params(1),
        cost_estimate=cost(2 * pix * kernel.size, kernel.size * 2 + pix * 4096),
    )(win, in_hbm(kernel))


class Member:
    def __init__(self, at, shape, dp, fsdp, split=False):
        self.at, self.shape, self.split = at, shape, split
        self.vr = shape[0] // dp // (2 if split else 1)
        self.blocks = shape[1] // fsdp * (2 if split else 1) // LANES
        self.rows = self.vr * self.blocks

    def spots(self, i, j):
        if self.split:
            row, col = i * 2 * self.vr + (j & 1) * self.vr, (j >> 1) * self.blocks * LANES
        else:
            row, col = i * self.vr, j * self.blocks * LANES
        for k in range(self.blocks):
            yield self.at + k * self.vr, row, col + k * LANES


def collect_kernel(member, parts, me_ref, *refs):
    out_ref, sem = refs[-2:]
    fetch(member, parts, me_ref, refs[:-2], out_ref, sem)
    arrived(out_ref, sem)


def collect(pieces):
    return pl.pallas_call(
        functools.partial(collect_kernel, pieces.member, pieces.parts),
        in_specs=[SCALARS] + [ANYWHERE] * len(pieces.sources),
        out_specs=whole(pieces.shape),
        out_shape=sds(pieces.shape, BF16),
        scratch_shapes=[pltpu.SemaphoreType.DMA],
        grid=(1,),
        compiler_params=params(1),
        cost_estimate=cost(0, 4 * pieces.shape[0] * pieces.shape[1]),
    )(pieces.me, *pieces.sources)


def affine_kernel(member, parts, me_ref, *refs):
    out_ref, rows_ref, sem = refs[-3:]
    fetch(member, parts, me_ref, refs[:-3], rows_ref, sem)
    arrived(rows_ref, sem)
    width = out_ref.shape[1] // 32
    for d in range(32):
        rows = rows_ref[16 * d : 16 * d + 16].astype(F32)
        both = jnp.concatenate([rows[:8], rows[8:]], 1)
        out_ref[:, d * width : (d + 1) * width] = (both[0:2] + both[2:4] + both[4:6])[:, :width]


def collect_affine(pieces):
    return pl.pallas_call(
        functools.partial(affine_kernel, pieces.member, pieces.parts),
        in_specs=[SCALARS] + [ANYWHERE] * len(pieces.sources),
        out_specs=whole((2, 5120)),
        out_shape=sds((2, 5120), F32),
        scratch_shapes=[pltpu.VMEM((512, LANES), BF16), pltpu.SemaphoreType.DMA],
        grid=(1,),
        compiler_params=params(1),
        cost_estimate=cost(10000000, 1000000),
    )(pieces.me, *pieces.sources)


def weight_parts(geom, step, act_ref, low_ref, tr_ref):
    rows = geom[1]

    @pl.when(step == 0)
    def _():
        tr_ref[...] = act_ref[...].astype(F32).T.astype(BF16)

    if len(low_ref.shape) == 5:
        for b in range(3):
            yield jnp.dot(tr_ref[...], window(low_ref, 2 - b, 2 - step, rows), preferred_element_type=F32)
    else:
        yield jnp.dot(tr_ref[...], low_ref[...], preferred_element_type=F32)


def weight_kernel(geom, act_ref, low_ref, out_ref, tr_ref):
    chans = tr_ref.shape[0]
    for b, part in enumerate(weight_parts(geom, pl.program_id(0), act_ref, low_ref, tr_ref)):
        out_ref[b * chans : (b + 1) * chans, :] = part.astype(BF16)


def weight_layer(geom, act, low):
    pix, chans = act.shape
    win = low.ndim == 5
    width = low.shape[-1]
    steps = 3 if win else 1
    out = sds((9 * chans if win else chans, width), BF16)
    return pl.pallas_call(
        functools.partial(weight_kernel, geom),
        grid=(steps,),
        in_specs=[whole(act.shape), whole(low.shape)],
        out_specs=pl.BlockSpec((out.shape[0] // steps, width), lambda a: (a, 0)),
        out_shape=out,
        scratch_shapes=[pltpu.VMEM((chans, pix), BF16)],
        compiler_params=params(1),
        cost_estimate=cost(2 * pix * out.size, out.size * 2 + pix * 4096),
    )(act, low)


def weight_blocks_kernel(geom, member, steps, held, *refs):
    refs = list(refs)
    me_ref, act_ref, low_ref = (refs.pop(0) for _ in range(3))
    if held:
        del refs[:3]
    near_ref, far_ref, send_ref, scr_ref, tr_ref, sem = refs
    step = pl.program_id(0)
    chans = tr_ref.shape[0]
    for b, part in enumerate(weight_parts(geom, step, act_ref, low_ref, tr_ref)):
        scr_ref[pl.ds(pl.multiple_of(step * 3 * chans, chans) + b * chans, chans), :] = part.astype(BF16)
    me = me_ref[0]
    share = member.shape[0] // 8
    done = 0
    for s in range(steps):
        ready = member.shape[0] * (s + 1) // steps // share

        @pl.when(step == s)
        def _(done=done, ready=ready):
            for i in range(done, ready):
                e = i ^ (me >> 2)
                q = ((e & 1) << 2) | (e & 2) | (e >> 2)
                for jd in range(4):
                    dst = send_ref.at[jd >> 1, q] if jd & 1 else (near_ref, far_ref)[jd >> 1].at[q]
                    for at, row, col in member.spots(i, (me & 3) ^ jd):
                        pltpu.make_async_copy(
                            scr_ref.at[span(row, member.vr), span(col, LANES)], dst.at[pl.ds(at, member.vr)], sem
                        ).start()

        done = ready

    @pl.when(step == steps - 1)
    def _():
        pltpu.make_async_copy(scr_ref, scr_ref, sem).wait()


def weight_blocks(geom, me, act, low, member, rows, held=None):
    pix, chans = act.shape
    win = low.ndim == 5
    steps = 3 if win else 1
    shard = (rows, LANES)
    outs = [pltpu.HBM((8, *shard), BF16)] * 2 + [pltpu.HBM((2, 8, *shard), BF16)]
    args = [me, act, low] + [in_hbm(x) for x in held or ()]
    size = member.shape[0] * member.shape[1]
    return pl.pallas_call(
        functools.partial(weight_blocks_kernel, geom, member, steps, held is not None),
        grid=(steps,),
        in_specs=[SCALARS, whole(act.shape), whole(low.shape)] + [ANYWHERE] * len(held or ()),
        out_specs=[ANYWHERE] * 3,
        out_shape=outs,
        scratch_shapes=[pltpu.VMEM(member.shape, BF16), pltpu.VMEM((chans, pix), BF16), pltpu.SemaphoreType.DMA],
        input_output_aliases={} if held is None else {3: 0, 4: 1, 5: 2},
        compiler_params=params(1),
        cost_estimate=cost(2 * pix * size, size * 2 + pix * 4096),
    )(*args)


def weight_piece_kernel(geom, member, step, held, *refs):
    rows = geom[1]
    refs = list(refs)
    me_ref, act_ref, low_ref = (refs.pop(0) for _ in range(3))
    if held:
        del refs[:3]
    near_ref, far_ref, send_ref = (refs.pop(0) for _ in range(3))
    if step == 0:
        tr_ref = refs.pop(0)
        tr_ref[...] = act_ref[...].astype(F32).T.astype(BF16)
    else:
        tr_ref = act_ref
    scr_ref, sem = refs
    chans = tr_ref.shape[0]
    for b in range(3):
        part = jnp.dot(tr_ref[...], window(low_ref, 2 - b, 2 - step, rows), preferred_element_type=F32)
        scr_ref[b * chans : (b + 1) * chans, :] = part.astype(BF16)
    me = me_ref[0]
    start, stop = 3 * chans * step, 3 * chans * (step + 1)
    for i in range(8):
        first, last = max(start, i * member.vr), min(stop, (i + 1) * member.vr)
        if first >= last:
            continue
        e = i ^ (me >> 2)
        q = ((e & 1) << 2) | (e & 2) | (e >> 2)
        for jd in range(4):
            dst = send_ref.at[jd >> 1, q] if jd & 1 else (near_ref, far_ref)[jd >> 1].at[q]
            col = ((me & 3) ^ jd) * LANES
            pltpu.make_async_copy(
                scr_ref.at[pl.ds(first - start, last - first), span(col, LANES)],
                dst.at[pl.ds(member.at + first - i * member.vr, last - first)],
                sem,
            ).start()
    arrived(scr_ref, sem)


def weight_piece(geom, me, act, low, member, rows, step, held=None):
    chans = member.shape[0] // 9
    pix, width = low.shape[1] * geom[1] * geom[2], low.shape[-1]
    shard = (rows, LANES)
    outs = [pltpu.HBM((8, *shard), BF16)] * 2 + [pltpu.HBM((2, 8, *shard), BF16)]
    out_specs = [ANYWHERE] * 3
    if step == 0:
        outs.append(sds((chans, pix), BF16))
        out_specs.append(whole((chans, pix)))
    args = [me, act, low] + [in_hbm(x) for x in held or ()]
    return pl.pallas_call(
        functools.partial(weight_piece_kernel, geom, member, step, held is not None),
        grid=(1,),
        in_specs=[SCALARS, whole(act.shape), whole(low.shape)] + [ANYWHERE] * len(held or ()),
        out_specs=out_specs,
        out_shape=outs,
        scratch_shapes=[pltpu.VMEM((3 * chans, width), BF16), pltpu.SemaphoreType.DMA],
        input_output_aliases={} if held is None else {3: 0, 4: 1, 5: 2},
        compiler_params=params(1),
        cost_estimate=cost(2 * pix * 3 * chans * width, chans * width * 6),
    )(*args)


def point_kernel(geom, pieces, *refs):
    frames, rows, cols, _ = geom
    pixels = rows * cols
    refs = list(refs)
    domain_ref, act_ref = refs.pop(0), refs.pop(0)
    if pieces:
        out_ref, sums_ref, matrix_ref, sem = refs[-4:]
        fetch(*pieces, refs[0], refs[1:-4], matrix_ref, sem)
        arrived(matrix_ref, sem)
    else:
        matrix_ref, out_ref, sums_ref = refs
    for lane in range(0, out_ref.shape[-1], 256):
        lanes = slice(lane, lane + 256)
        out_ref[:, lanes] = jnp.dot(act_ref[...], matrix_ref[:, lanes], preferred_element_type=F32)
        pairs = [column_sums(out_ref, f, pixels, lanes) for f in range(frames)]
        sums_ref[:, lanes] = by_domain([p[0] for p in pairs], [p[1] for p in pairs], domain_ref)


def point_layer(geom, domain, act, mat):
    pix, chans = act.shape
    width = mat.shape[1]
    pieces = isinstance(mat, Pieces)
    outs = [sds((pix, width), F32), sds((4, width), F32)] + [sds(mat.shape, BF16)] * pieces
    args = [domain, act] + ([mat.me, *mat.sources] if pieces else [mat])
    specs = [SCALARS, whole(act.shape)]
    specs += [SCALARS] + [ANYWHERE] * len(mat.sources) if pieces else [whole(mat.shape)]
    return pl.pallas_call(
        functools.partial(point_kernel, geom, (mat.member, mat.parts) if pieces else None),
        in_specs=specs,
        out_specs=[whole(o.shape) for o in outs],
        out_shape=outs,
        scratch_shapes=[pltpu.SemaphoreType.DMA] * pieces,
        grid=(1,),
        compiler_params=params(1),
        cost_estimate=cost(2 * pix * chans * width, chans * width * 2 + pix * width * 4),
    )(*args)


def point_back_kernel(geom, added, domain_ref, g_ref, pre_ref, st_ref, sm_ref, gain_ref, mat_ref, *refs):
    frames, rows, cols, counts = geom
    pixels = rows * cols
    low_ref, out_ref = refs[-2:]
    for f in range(frames):
        tables = back_tables(st_ref, sm_ref, gain_ref, domain_ref[f], counts)

        def one_row(r, _):
            at = pl.multiple_of(f * pixels + r * cols, cols)
            low = norm_back_rows(g_ref[pl.ds(at, cols), :], pre_ref[pl.ds(at, cols), :], tables)
            low_ref[pl.ds(at, cols), :] = low.astype(BF16)
            return 0

        lax.fori_loop(0, rows, one_row, 0, unroll=2)
    part = lax.dot_general(low_ref[...], mat_ref[...], (((1,), (1,)), ((), ())), preferred_element_type=F32)
    out_ref[...] = part + refs[0][...] if added else part


def point_back(geom, domain, g, pre, stats, sums, gain, mat, added=None):
    pix, width = g.shape
    chans = mat.shape[0]
    args = (domain, g, pre, stats, sums, gain, mat) + (() if added is None else (added,))
    outs = [sds((pix, width), BF16), sds((pix, chans), F32)]
    return pl.pallas_call(
        functools.partial(point_back_kernel, geom, added is not None),
        grid=(1,),
        in_specs=[SCALARS] + [whole(x.shape) for x in args[1:]],
        out_specs=[whole(o.shape) for o in outs],
        out_shape=outs,
        compiler_params=params(1),
        cost_estimate=cost(2 * pix * mat.size, mat.size * 2 + pix * width * 10),
    )(*args)


AXES = ("dp", "fsdp")
CORE, X, Y, Z_NEAR, Z_FAR = range(5)
ORDER = (CORE, Z_NEAR, Z_FAR, X, Y)


def swap(x, bit):
    n = lax.axis_size(AXES)
    return lax.ppermute(x, AXES, [(i, i ^ (1 << bit)) for i in range(n)])


def bit_of(bit):
    return (lax.axis_index(AXES) >> bit) & 1


def all_bits():
    return range(lax.axis_size(AXES).bit_length() - 1)


def tied(value, to):
    return value if to is None else lax.optimization_barrier((value, to))[0]


class Links:
    def __init__(self):
        self.under_way = {}

    def busy(self, bit, *values):
        self.under_way.setdefault(bit, []).extend(values)

    def total(self, x, after=None, order=None, fill=()):
        bits = order if order and len(all_bits()) == 5 else all_bits()
        fill = list(fill)
        for bit in bits:
            for value in self.under_way.pop(bit, ()):
                x = tied(x, value)
            got = swap(x, bit)
            if fill and (bit != CORE or len(bits) != 5):
                got = tied(got, fill.pop(0)(x))
            x = x + got
            for start in (after or {}).get(bit, ()):
                start(x)
        for work in fill:
            work(x)
        return x


def half_rows(rows):
    return rows // 32 * 16


class Gather:
    def __init__(self, links, shard):
        self.links, self.shard, self.cut = links, shard, half_rows(shard.shape[0])
        self.sources = None

    def far(self, to=None):
        self.z = tied(self.shard, to)
        self.got = swap(self.z, Z_FAR)

    def near(self, to=None):
        self.z = jnp.stack(tied((self.z, self.got), to))
        self.got = swap(self.z, Z_NEAR)

    def first(self, to=None):
        z = jnp.concatenate(tied((self.z, self.got), to))
        self.a, self.b = z[:, : self.cut], z[:, self.cut :]
        self.got = swap(self.a, Y), swap(self.b, X)

    def second(self, to=None):
        a, b, (got_a, got_b) = tied((self.a, self.b, self.got), to)
        self.a, self.b = jnp.concatenate([a, got_a]), jnp.concatenate([b, got_b])
        self.got = swap(self.a, X), swap(self.b, Y)

    def busy(self):
        if isinstance(self.got, tuple):
            self.links.busy(X, self.got[0])
            self.links.busy(Y, self.got[1])
        else:
            self.links.busy(CORE, self.got)

    def finish(self, to=None):
        rows = self.shard.shape[0]
        self.a, self.b, self.got = tied((self.a, self.b, self.got), to)
        self.sources, self.parts = [], []
        for core in (0, 1):
            for n, value in enumerate((self.a, self.got[0], self.b, self.got[1])):
                z = [8 * (k >> 1) + 16 * (k & 1) for k in range(4)]
                if n < 2:
                    masks = [core + 2 * n + 4 * y + m for y in (0, 1) for m in z]
                else:
                    masks = [core + 4 * (n - 2) + 2 * x + m for x in (0, 1) for m in z]
                self.parts.append((0, self.cut, masks) if n < 2 else (self.cut, rows - self.cut, masks))
                self.sources.append(swap(value, CORE) if core else value)

    def pieces(self, member):
        return Pieces(member, self.parts, number(1), self.sources)


def number(entries):
    return jnp.full((entries,), lax.axis_index(AXES), jnp.int32)


def plus(a, b):
    return (a.astype(F32) + b.astype(F32)).astype(BF16)


class Scatter:
    def __init__(self, links, blocks):
        self.links = links
        self.near_blocks, self.far_blocks, send = blocks
        self.cut = half_rows(self.near_blocks.shape[1])
        self.got = swap(send, CORE)

    def first(self, to=None):
        cut = self.cut
        near, far, got = tied((self.near_blocks, self.far_blocks, self.got), to)
        self.a, send_a = plus(near[:, :cut], got[0, :, :cut]), plus(far[:, :cut], got[1, :, :cut])
        self.b, send_b = (
            jnp.stack([plus(near[s, cut:], got[0, s, cut:]), plus(far[s, cut:], got[1, s, cut:])])
            for s in (slice(0, 4), slice(4, 8))
        )
        self.got = swap(send_a, X), swap(send_b, Y)

    def second(self, to=None):
        a, b, (got_a, got_b) = tied((self.a, self.b, self.got), to)
        self.a, self.b = plus(a[:4], got_a[:4]), plus(b[0], got_b[0])
        self.got = swap(plus(a[4:], got_a[4:]), Y), swap(plus(b[1], got_b[1]), X)

    def near_sums(self, to=None):
        a, b, (got_a, got_b) = tied((self.a, self.b, self.got), to)
        self.z, self.send = (
            jnp.concatenate([plus(a[s], got_a[s]), plus(b[s], got_b[s])], 1) for s in (slice(0, 2), slice(2, 4))
        )

    def near(self, to=None):
        self.got = swap(tied(self.send, to), Z_NEAR)

    def far(self, to=None):
        z, got = tied((self.z, self.got), to)
        self.z = plus(z[0], got[0])
        self.got = swap(plus(z[1], got[1]), Z_FAR)

    def finish(self, to=None):
        z, got = tied((self.z, self.got), to)
        self.out = z.astype(F32) + got.astype(F32)

    def busy(self):
        if isinstance(self.got, tuple):
            self.links.busy(X, *self.got)
        else:
            self.links.busy(CORE, self.got)


def rows_of_chip(shard):
    half = shard.shape[0] // 2
    odd = bit_of(CORE) == 1
    mine = jnp.where(odd, shard[half:], shard[:half])
    got = swap(jnp.where(odd, shard[:half], shard[half:]), CORE)
    return jnp.concatenate([jnp.where(odd, got, mine), jnp.where(odd, mine, got)], 1)


def columns_of_core(rows):
    half = rows.shape[1] // 2
    odd = bit_of(CORE) == 1
    mine = jnp.where(odd, rows[:, half:], rows[:, :half])
    got = swap(jnp.where(odd, rows[:, :half], rows[:, half:]), CORE)
    return jnp.concatenate([jnp.where(odd, got, mine), jnp.where(odd, mine, got)], 0)


def pack(x):
    return jnp.concatenate([x[:, k : k + LANES] for k in range(0, x.shape[1], LANES)], 0)


def unpack(x, blocks):
    rows = x.shape[0] // blocks
    return jnp.concatenate([x[k * rows : (k + 1) * rows] for k in range(blocks)], 1)


def in_three(x):
    high = lax.reduce_precision(x, 8, 7)
    middle = lax.reduce_precision(x - high, 8, 7)
    return jnp.stack([high, middle, x - high - middle]).astype(BF16)


def gather(x):
    x = x[None]
    for bit in all_bits():
        other = swap(x, bit)
        high = bit_of(bit) == 1
        x = jnp.concatenate([jnp.where(high, other, x), jnp.where(high, x, other)], 0)
    return x


def scatter(x):
    for bit in reversed(all_bits()):
        half = x.shape[0] // 2
        high = bit_of(bit) == 1
        send = jnp.where(high, x[:half], x[half:])
        keep = jnp.where(high, x[half:], x[:half])
        x = plus(keep, swap(send, bit))
    return x[0]


def gather_matrix(shard):
    dp, fsdp = lax.axis_size("dp"), lax.axis_size("fsdp")
    rows, cols = shard.shape
    full = gather(shard).reshape(dp, fsdp, rows, cols)
    return full.transpose(0, 2, 1, 3).reshape(dp * rows, fsdp * cols)


def scatter_matrix(full):
    dp, fsdp = lax.axis_size("dp"), lax.axis_size("fsdp")
    rows, cols = full.shape[0] // dp, full.shape[1] // fsdp
    parts = full.reshape(dp, rows, fsdp, cols).transpose(0, 2, 1, 3)
    return scatter(parts.reshape(dp * fsdp, rows, cols)).astype(F32)


class AnyMesh:
    def __init__(self, links, geom, weights, gains, biases):
        self.geom = geom
        self.mats = {name: gather_matrix(w) for name, w in weights.items()}
        self.affine = gather(jnp.stack([gains, biases])).transpose(1, 0, 2).reshape(2, 1, -1)
        self.grads, self.ready = {}, None

    def get(self, name):
        return self.mats[name]

    def whole(self, name):
        return self.mats[name]

    def put(self, name, matrix):
        pass

    def layer_done(self, n, local):
        pass

    def during(self, point):
        return {}

    def add(self, name, act, low):
        got = weight_layer(self.geom, act, low)
        self.grads[name] = scatter_matrix(got)
        return got

    def pieces(self, name, act, low):
        return [lambda x: self.add(name, act, low)]

    def send(self, n):
        pass

    def after_layer(self, n, local):
        pass

    def tail(self, blocks, kernels):
        return [kernel(None) for kernel in kernels]


class ThisMesh:
    def __init__(self, links, geom, weights, gains, biases):
        self.geom, self.links = geom, links
        self.me = number(1)
        sizes = (8, 4)
        full = {n: (w.shape[0] * 8, w.shape[1] * 4) for n, w in weights.items()}
        splits = ("six", "gating")
        g1 = Gather(links, weights["one"])
        g1.far()
        packed = {n: pack(rows_of_chip(tied(w, g1.got)) if n in splits else w) for n, w in weights.items()}
        gains, biases = tied((gains, biases), g1.got)
        affine = in_three(jnp.stack([gains, biases])).reshape(6, -1)
        affine = jnp.pad(affine, ((0, 2), (0, 2 * LANES - affine.shape[1])))
        affine = jnp.concatenate([affine[:, :LANES], affine[:, LANES:]])
        groups = (("one",), ("two",), ("three",), ("four",), ("five",), ("six", "gating", "attend"))
        self.g, self.members, self.group = [], {}, {}
        for names in groups:
            at = 0
            for name in names:
                self.members[name] = Member(at, full[name], *sizes, split=name in splits)
                at += self.members[name].rows
            if names == ("one",):
                group = g1
            else:
                group = Gather(links, jnp.concatenate([packed[n] for n in names] + [affine] * (names == ("two",))))
            self.g.append(group)
            self.group.update((n, group) for n in names)
        g2 = self.g[1]
        g1.near()
        g2.far(g1.got)
        g1.first()
        g2.near(g1.got)
        g1.second()
        g1.finish()
        self.g[2].far(g2.got)
        g2.first(g1.got)
        self.ready = self.g[5].shard
        self.mats = {}
        self.grads, self.blocks, self.sums = {}, {}, {}
        self.homes, self.rows = {}, {}
        for names in (("six", "gating"), ("five",), ("four",), ("three", "attend"), ("two",), ("one",)):
            at = 0
            for name in names:
                self.homes[name] = Member(at, full[name], *sizes, split=name in splits)
                at += self.homes[name].rows
            self.rows.update((name, at) for name in names)

    def layer_done(self, n, local):
        if n < 6:
            self.g[n].second((local, self.g[n + 1].got) if n < 5 else local)
            self.g[n].busy()

    def get(self, name):
        if name in self.mats:
            return self.mats[name]
        group = self.group[name]
        self.mats[name] = group.pieces(self.members[name])
        if name == "two":
            self.affine = collect_affine(group.pieces(FlatMember(self.members["two"].rows, 16)))[:, None]
        return self.mats[name]

    def whole(self, name):
        self.mats[name] = collect(self.get(name))
        return self.mats[name]

    def put(self, name, matrix):
        self.mats[name] = matrix

    def during(self, point):
        if point <= 5:

            def x_done(x):
                self.g[point].finish(x)

            if point == 5:
                return {X: [x_done]}
            group = self.g[point + 1]

            def z_done(x):
                group.near(x)

            def y_done(x):
                group.first(x)
                if point < 4:
                    self.g[point + 2].far(x)

            return {Z_FAR: [z_done], X: [x_done], Y: [y_done]}
        n = 14 - point

        def z_done(x):
            self.sums[n + 2].near(x)

        def y_done(x):
            self.sums[n + 1].second(x)
            if n < 5:
                self.sums[n + 2].far(x)

        return {Y: [y_done], Z_FAR: [z_done] if n < 5 else []}

    def add(self, name, act, low):
        n = NUMBER[name]
        self.blocks[n] = weight_blocks(
            self.geom, self.me, act, low, self.homes[name], self.rows[name], self.blocks.get(n)
        )
        return self.blocks[n][0]

    def pieces(self, name, act, low):
        def piece(step):
            def work(x):
                n = NUMBER[name]
                if step == 0:
                    *self.blocks[n], self.turned = weight_piece(
                        self.geom, self.me, tied(act, x), low, self.homes[name], self.rows[name], 0
                    )
                else:
                    self.blocks[n] = weight_piece(
                        self.geom, self.me, tied(self.turned, x), low, self.homes[name], self.rows[name], step, self.blocks[n]
                    )
                return self.blocks[n][0]

            return work

        return [piece(step) for step in range(3)]

    def send(self, n):
        self.sums[n] = Scatter(self.links, self.blocks[n])

    def after_layer(self, n, local):
        if n < 4:
            self.sums[n + 3].finish(local)
            local = (local, self.sums[n + 3].out)
        if n < 5:
            self.sums[n + 2].near_sums(local)
            local = self.sums[n + 2].send
        self.sums[n + 1].first(local)
        self.sums[n + 1].busy()

    def tail(self, blocks, kernels):
        self.send(1)
        one, two, three, four = (self.sums[n] for n in (1, 2, 3, 4))
        four.finish(blocks)
        two.first((blocks, four.out))
        three.near_sums(two.b)
        three.near(two.b)
        outs = [kernels[0]((two.b, three.z))]
        one.first(outs[0])
        three.far(one.b)
        outs.append(kernels[1]((one.b, three.z)))
        two.second(outs[1])
        one.second(two.b)
        three.finish(two.b)
        two.near_sums((one.b, three.out))
        two.near()
        one.near_sums(two.z)
        one.near()
        two.far(one.z)
        one.far(two.z)
        two.finish(one.z)
        one.finish()
        for name, m in self.homes.items():
            out = unpack(self.sums[NUMBER[name]].out[m.at : m.at + m.rows], m.blocks)
            self.grads[name] = columns_of_core(out) if m.split else out
        return outs


NUMBER = dict(one=1, two=2, three=3, attend=3, four=4, five=5, six=6, gating=6)


class FlatMember:
    def __init__(self, at, rows):
        self.at, self.vr, self.rows, self.blocks, self.shape = at, rows, rows, 1, (32 * rows, LANES)

    def spots(self, i, j):
        yield self.at, (i * 4 + j) * self.vr, 0


def body(
    frames_in,
    domain,
    kernel_one,
    kernel_two,
    kernel_three,
    attn_enc,
    kernel_four,
    kernel_five,
    kernel_six,
    attn_dec,
    gains,
    biases,
    enc_cot,
    dec_cot,
):
    frames, rows, cols, _ = frames_in.shape
    total_frames = frames * lax.axis_size(AXES)
    first = total_frames * 5 // 8
    counts = (float(first * rows * cols), float((total_frames - first) * rows * cols))
    geom = (frames, rows, cols, counts)
    pix = frames * rows * cols
    source = frames_in.reshape(pix, C_IN)
    enc_cot = enc_cot.transpose(0, 1, 3, 2, 4)
    dec_cot = dec_cot.reshape(pix, TASKS, C_DEC).transpose(1, 0, 2)
    weights = dict(
        one=kernel_one, two=kernel_two, three=kernel_three, attend=attn_enc,
        four=kernel_four, five=kernel_five, six=kernel_six, gating=attn_dec,
    )
    links = Links()
    this = lax.axis_size("dp") == 8 and lax.axis_size("fsdp") == 4
    w = (ThisMesh if this else AnyMesh)(links, geom, weights, gains, biases)

    def forward(name, source, norm=None):
        got = forward_layer(geom, domain, source, w.get(name), norm)
        w.put(name, got[-1])
        return got[:3] if norm is not None else got[:2]

    def point(name, act):
        got = point_layer(geom, domain, act, w.get(name))
        w.put(name, got[-1])
        return got[:2]

    pre_1, local = forward("one", tied(source, w.ready))
    w.layer_done(1, local)
    st_1 = links.total(local, w.during(1), ORDER)
    w.get("two")
    widths = (C_MID, C_MID, C_MID, TASKS * C_MID, C_MID, C_MID, C_DEC, TASKS * C_DEC)
    gain, bias, at = [], [], 0
    for width in widths:
        gain.append(w.affine[0, :, at : at + width])
        bias.append(w.affine[1, :, at : at + width])
        at += width
    pre_2, local, act_1 = forward("two", pre_1, (st_1, gain[0], bias[0]))
    w.layer_done(2, local)
    st_2 = links.total(local, w.during(2), ORDER)
    pre_3, local, act_2 = forward("three", pre_2, (st_2, gain[1], bias[1]))
    w.layer_done(3, local)
    st_3 = links.total(local, w.during(3), ORDER)
    unpooled = pool_layer(geom, domain, pre_3, st_3, gain[2], bias[2])
    pre_4, local = forward("four", unpooled)
    w.layer_done(4, local)
    st_4 = links.total(local, w.during(4), ORDER)
    pre_5, local, act_4 = forward("five", pre_4, (st_4, gain[4], bias[4]))
    w.layer_done(5, local)
    st_5 = links.total(local, w.during(5), ORDER)
    pre_g, local_g = point("gating", act_4)
    pre_6, local, act_5 = forward("six", pre_5, (st_5, gain[5], bias[5]))
    attend = w.whole("attend")
    wide = []

    def attend_part(k):
        def work(x):
            wide.append(point_layer(geom, domain, tied(act_2, x), attend[:, k * C_MID : (k + 1) * C_MID]))
            return wide[-1][0]

        return work

    both = links.total(jnp.concatenate([local, local_g], 1), None, ORDER, [attend_part(k) for k in range(TASKS)])
    st_6, st_g = both[:, :C_DEC], both[:, C_DEC:]
    pre_a = [p for p, _ in wide]
    task_maps, g_6, g_g, local = head_layer(
        geom, domain, pre_6, st_6, pre_g, st_g, gain[6], bias[6], gain[7], bias[7], dec_cot
    )
    out_maps = []

    def place_maps(x):
        out_maps.append(tied(task_maps, x).transpose(1, 0, 2).reshape(frames, rows, cols, TASKS, C_DEC))
        return out_maps[0]

    both = links.total(jnp.concatenate([local] + [s for _, s in wide], 1), None, ORDER, [place_maps])
    sm_6, sm_g, st_a = both[:, :C_DEC], both[:, C_DEC : 4 * C_DEC], both[:, 4 * C_DEC :]
    st_a = [st_a[:, k * C_MID : (k + 1) * C_MID] for k in range(TASKS)]
    pool_args = (geom, domain, pre_3, st_3, gain[2], bias[2])
    masks = [(pre_a[k], st_a[k], gain[3][:, k * C_MID : (k + 1) * C_MID], bias[3][:, k * C_MID : (k + 1) * C_MID]) for k in range(TASKS)]

    win_6, g_5, local = backward_layer(
        geom, domain, (g_6, pre_6, st_6, sm_6, gain[6]), w.get("six"), lower=(pre_5, st_5, gain[5], bias[5])
    )
    early, gate_back = [], []

    def early_part(k):
        def work(x):
            early.append(pool_early(*pool_args, *masks[k], enc_cot[:, :, k], tied(pre_3, x), early[-1][0] if early else None))
            return early[-1][0]

        return work

    def gate_part(x):
        gate_back.extend(point_back(geom, domain, tied(g_g, x), pre_g, st_g, sm_g, gain[7], w.get("gating")))
        return gate_back[0]

    sm_5 = links.total(
        local, None, ORDER, [lambda x: w.add("six", act_5, tied(win_6, x)), gate_part, early_part(0), early_part(1)]
    )
    early_part(2)(sm_5)
    mix = early[-1][0]
    low_g, add_4 = gate_back
    blocks = w.add("gating", act_4, low_g)
    w.send(6)
    win_5, g_4, local = backward_layer(
        geom,
        domain,
        (tied(g_5, blocks), pre_5, st_5, sm_5, gain[5]),
        w.get("five"),
        added=add_4,
        lower=(pre_4, st_4, gain[4], bias[4]),
    )
    w.after_layer(5, local)
    both = links.total(
        jnp.concatenate([local] + [e[2] for e in early], 1), w.during(9), ORDER, w.pieces("five", act_4, win_5)
    )
    w.send(5)
    sm_4 = both[:, :C_MID]
    sm_a = [both[:, (k + 1) * C_MID : (k + 2) * C_MID] for k in range(TASKS)]
    win_4, g_3, local = backward_layer(
        geom,
        domain,
        (g_4, pre_4, st_4, sm_4, gain[4]),
        w.get("four"),
        lower=(pre_3, st_3, gain[2], bias[2]),
        mix=mix,
    )
    w.after_layer(4, local)
    backs = []

    def attend_back(k):
        def work(x):
            backs.append(
                point_back(
                    geom, domain, tied(early[k][1], x), pre_a[k], st_a[k], sm_a[k], masks[k][2],
                    attend[:, k * C_MID : (k + 1) * C_MID], backs[-1][1] if backs else None,
                )
            )
            return backs[-1][1]

        return work

    sm_3 = links.total(local, w.during(10), ORDER, w.pieces("four", unpooled, win_4) + [attend_back(0)])
    w.send(4)
    attend_back(1)(sm_3)
    attend_back(2)(backs[-1][1])
    low_a = jnp.concatenate([low for low, _ in backs], 1)
    win_3, g_2, local = backward_layer(
        geom,
        domain,
        (g_3, pre_3, st_3, sm_3, gain[2]),
        w.get("three"),
        added=backs[-1][1],
        lower=(pre_2, st_2, gain[1], bias[1]),
    )
    w.after_layer(3, local)
    sm_2 = links.total(
        local, w.during(11), ORDER, w.pieces("three", act_2, win_3) + [lambda x: w.add("attend", act_2, tied(low_a, x))]
    )
    w.send(3)
    win_2, g_1, local = backward_layer(
        geom,
        domain,
        (g_2, pre_2, st_2, sm_2, gain[1]),
        w.get("two"),
        lower=(pre_1, st_1, gain[0], bias[0]),
    )
    w.after_layer(2, local)
    sm_1 = links.total(local, w.during(12), ORDER, w.pieces("two", act_1, win_2))
    w.send(2)
    win_1 = low_layer(geom, domain, (g_1, pre_1, st_1, sm_1, gain[0]))
    blocks = w.add("one", source, win_1)
    frames_grad, task_features = w.tail(
        blocks,
        (
            lambda to: input_layer(geom, tied(win_1, to), w.get("one")),
            lambda to: task_layer(geom, domain, tied(pre_3, to), *pool_args[3:], masks),
        ),
    )

    sums = jnp.concatenate([sm_1, sm_2, sm_3, *sm_a, sm_4, sm_5, sm_6, sm_g], 1)
    shard = gains.shape[0]
    mine = lax.dynamic_slice_in_dim(sums, lax.axis_index(AXES) * shard, shard, 1)
    return (
        task_features.transpose(0, 1, 3, 2, 4),
        out_maps[0],
        frames_grad.reshape(frames, rows, cols, C_IN),
        *(w.grads[n] for n in ("one", "two", "three", "attend", "four", "five", "six", "gating")),
        mine[2] + mine[3],
        mine[0] + mine[1],
    )


def solution(mesh):
    whole_split = P(AXES)
    matrix = P("dp", "fsdp")
    return jax.shard_map(
        body,
        mesh=mesh,
        in_specs=(whole_split, whole_split) + (matrix,) * 8 + (whole_split,) * 4,
        out_specs=(whole_split,) * 3 + (matrix,) * 8 + (whole_split,) * 2,
        check_vma=False,
    )
```

```python
import functools

import jax
import jax.numpy as jnp
from jax import lax
from jax.experimental import pallas as pl
from jax.experimental.pallas import tpu as pltpu
from jax.sharding import PartitionSpec as P

C_IN = 256
C_MID = 512
C_DEC = 256
TASKS = 3
EPS = 1e-05
LANES = 128
F32 = jnp.float32
BF16 = jnp.bfloat16
COST = 0.1
VMEM_LIMIT = 12 * 1024 * 1024


def params(grid_dims=0):
    return pltpu.CompilerParams(
        vmem_limit_bytes=VMEM_LIMIT,
        dimension_semantics=("arbitrary",) * grid_dims if grid_dims else None,
    )


def cost(flops, size):
    return pl.CostEstimate(flops=int(flops * COST), bytes_accessed=int(size * COST), transcendentals=0)


def whole(shape):
    zeros = (0,) * len(shape)
    return pl.BlockSpec(shape, lambda *_: zeros, pipeline_mode=pl.Buffered(1))


SCALARS = pl.BlockSpec(memory_space=pltpu.SMEM)


def sds(shape, dtype):
    return jax.ShapeDtypeStruct(shape, dtype)


def sigmoid(v):
    return 0.5 * jnp.tanh(0.5 * v) + 0.5


def frame_tables(stats, domain_at, counts):
    first = domain_at == 0
    share = jnp.where(first, 1.0 / counts[0], 1.0 / counts[1])
    average = jnp.where(first, stats[0:1], stats[1:2]) * share
    square = jnp.where(first, stats[2:3], stats[3:4]) * share
    return average, lax.rsqrt(square - average * average + EPS)


def grad_tables(sums, domain_at, counts):
    first = domain_at == 0
    share = jnp.where(first, 1.0 / counts[0], 1.0 / counts[1])
    return (
        jnp.where(first, sums[0:1], sums[1:2]) * share,
        jnp.where(first, sums[2:3], sums[3:4]) * share,
    )


def by_domain(first, second, domain_ref):
    rows = []
    for per_frame in (first, second):
        for d in (0, 1):
            total = None
            for f, value in enumerate(per_frame):
                term = jnp.where(domain_ref[f] == d, value, jnp.zeros_like(value))
                total = term if total is None else total + term
            rows.append(total)
    return jnp.concatenate(rows, 0)


def fold(x):
    return jnp.sum(x.reshape(-1, 8, x.shape[-1]), 0)


def put_windows(win_ref, f, row, value, cols):
    col = lax.broadcasted_iota(jnp.int32, value.shape, 0)
    left = jnp.where(col == 0, 0.0, pltpu.roll(value, 1, 0))
    right = jnp.where(col == cols - 1, 0.0, pltpu.roll(value, cols - 1, 0))
    win_ref[0, f, row + 1] = left.astype(BF16)
    win_ref[1, f, row + 1] = value.astype(BF16)
    win_ref[2, f, row + 1] = right.astype(BF16)


def clear_edges(win_ref, rows):
    shape = win_ref.shape
    for b in range(3):
        for f in range(shape[1]):
            win_ref[b, f, 0] = jnp.zeros(shape[3:], BF16)
            win_ref[b, f, rows + 1] = jnp.zeros(shape[3:], BF16)


def window(win_ref, b, row_at, rows):
    part = win_ref[b, :, pl.ds(row_at, rows)]
    return part.reshape(-1, part.shape[-1])


def column_sums(ref, f, pixels, lanes, step=64):
    def add(i, carry):
        part = ref[pl.ds(f * pixels + i * step, step), lanes]
        return carry[0] + fold(part), carry[1] + fold(part * part)

    width = lanes.stop - lanes.start
    zero = jnp.zeros((8, width), F32)
    one, two = lax.fori_loop(0, pixels // step, add, (zero, zero), unroll=2)
    return jnp.sum(one, 0, keepdims=True), jnp.sum(two, 0, keepdims=True)


def in_hbm(x):
    return pltpu.with_memory_space_constraint(x, pltpu.HBM)


class Pieces:
    def __init__(self, member, parts, me, sources):
        self.member, self.parts, self.me = member, parts, me
        self.sources = [in_hbm(x) for x in sources]
        self.shape = member.shape


def span(start, size):
    return pl.ds(start if isinstance(start, int) else pl.multiple_of(start, size & -size), size)


def fetch(member, parts, me_ref, sources, dst_ref, sem):
    me = me_ref[0]
    for (first, size, masks), src in zip(parts, sources):
        for q in range(src.shape[0]):
            d = q if masks is None else me ^ masks[q]
            for at, row, col in member.spots(d >> 2, d & 3):
                low, high = max(at, first), min(at + member.vr, first + size)
                if low < high:
                    pltpu.make_async_copy(
                        src.at[q, pl.ds(low - first, high - low)],
                        dst_ref.at[span(row + (low - at), high - low), span(col, LANES)],
                        sem,
                    ).start()


def arrived(ref, sem):
    pltpu.make_async_copy(ref, ref, sem).wait()


def forward_kernel(geom, normed, pieces, *refs):
    frames, rows, cols, counts = geom
    pixels = rows * cols
    refs = list(refs)
    domain_ref = refs.pop(0)
    source_ref = refs.pop(0)
    if normed:
        stats_ref, gain_ref, bias_ref = refs.pop(0), refs.pop(0), refs.pop(0)
    if pieces:
        me_ref = refs.pop(0)
        sources = [refs.pop(0) for _ in pieces[1]]
    else:
        kernel_ref = refs.pop(0)
    out_ref = refs.pop(0)
    sums_ref = refs.pop(0)
    act_ref = refs.pop(0) if normed else None
    if pieces:
        matrix_ref = refs.pop(0)
    win_ref, held_ref, sem = refs

    if pieces:
        fetch(*pieces, me_ref, sources, held_ref, sem.at[0])
    else:
        pltpu.make_async_copy(kernel_ref, held_ref, sem.at[0]).start()
    clear_edges(win_ref, rows)
    for f in range(frames):
        if normed:
            average, inverse = frame_tables(stats_ref[...], domain_ref[f], counts)
            scale = inverse * gain_ref[...]
            shift = bias_ref[...] - average * scale

        def one_row(r, _):
            at = pl.multiple_of(f * pixels + r * cols, cols)
            value = source_ref[pl.ds(at, cols), :].astype(F32)
            if normed:
                act = value * scale + shift
                value = act * sigmoid(act)
                act_ref[pl.ds(at, cols), :] = value.astype(BF16)
            put_windows(win_ref, f, r, value, cols)
            return 0

        lax.fori_loop(0, rows, one_row, 0, unroll=2)
    arrived(held_ref, sem.at[0])
    if pieces:
        pltpu.make_async_copy(held_ref, matrix_ref, sem.at[1]).start()
    source = jnp.concatenate([window(win_ref, b, a, rows) for a in range(3) for b in range(3)], 1)
    out = jnp.dot(source, held_ref[...], preferred_element_type=F32)
    out_ref[...] = out
    parts = [out[f * pixels : (f + 1) * pixels] for f in range(frames)]
    sums_ref[...] = by_domain(
        [jnp.sum(fold(p), 0, keepdims=True) for p in parts],
        [jnp.sum(fold(p * p), 0, keepdims=True) for p in parts],
        domain_ref,
    )
    if pieces:
        pltpu.make_async_copy(held_ref, matrix_ref, sem.at[1]).wait()


ANYWHERE = pl.BlockSpec(memory_space=pl.ANY)


def forward_layer(geom, domain, source, kernel, norm=None):
    frames, rows, cols, _ = geom
    pix, chans = source.shape
    width = kernel.shape[1]
    pieces = isinstance(kernel, Pieces)
    args, specs = [domain, source], [SCALARS, whole(source.shape)]
    if norm is not None:
        args += list(norm)
        specs += [whole(x.shape) for x in norm]
    if pieces:
        args += [kernel.me, *kernel.sources]
        specs += [SCALARS] + [ANYWHERE] * len(kernel.sources)
    else:
        args.append(in_hbm(kernel))
        specs.append(ANYWHERE)
    outs, out_specs = [sds((pix, width), F32)], [whole((pix, width))]
    outs.append(sds((4, width), F32))
    out_specs.append(whole((4, width)))
    if norm is not None:
        outs.append(sds((pix, chans), BF16))
        out_specs.append(whole((pix, chans)))
    scratch = [pltpu.VMEM((3, frames, rows + 2, cols, chans), BF16)]
    scratch += [pltpu.VMEM(kernel.shape, BF16), pltpu.SemaphoreType.DMA((2,))]
    if pieces:
        outs.append(pltpu.HBM(kernel.shape, BF16))
        out_specs.append(ANYWHERE)
    size = kernel.shape[0] * kernel.shape[1]
    return pl.pallas_call(
        functools.partial(forward_kernel, geom, norm is not None, (kernel.member, kernel.parts) if pieces else None),
        grid=(1,),
        in_specs=specs,
        out_specs=out_specs,
        out_shape=outs,
        scratch_shapes=scratch,
        compiler_params=params(1),
        cost_estimate=cost(2 * pix * size, size * 2 + pix * 4096),
    )(*args)


def pair_sum(x, cols):
    even = lax.broadcasted_iota(jnp.int32, x.shape, 0) % 2 == 0
    return x + jnp.where(even, pltpu.roll(x, cols - 1, 0), pltpu.roll(x, 1, 0))


def softmax_window(top, cols):
    exps = [jnp.exp(t) for t in top]
    share = 1.0 / pair_sum(exps[0] + exps[1], cols)
    return [e * share for e in exps]


def spread_cols(scr_ref, x):
    half = x.shape[0]
    scr_ref[pl.ds(0, half, stride=2), :] = x
    scr_ref[pl.ds(1, half, stride=2), :] = x
    return scr_ref[...]


def top_rows(top_ref, at, cols, lanes, scale, shift):
    top = []
    for a in at:
        act = top_ref[pl.ds(a, cols), lanes] * scale + shift
        top.append(act * sigmoid(act))
    return top


def pool_kernel(geom, domain_ref, top_ref, top_st, gain_t, bias_t, un_ref):
    frames, rows, cols, counts = geom
    pixels = rows * cols
    for f in range(frames):
        for lane in range(0, top_ref.shape[-1], LANES):
            lanes = slice(lane, lane + LANES)
            average, inverse = frame_tables(top_st[:, lanes], domain_ref[f], counts)
            scale = inverse * gain_t[:, lanes]
            shift = bias_t[:, lanes] - average * scale

            def one(i, _):
                at = [pl.multiple_of(f * pixels + (2 * i + h) * cols, cols) for h in (0, 1)]
                top = top_rows(top_ref, at, cols, lanes, scale, shift)
                weight = softmax_window(top, cols)
                pooled = pair_sum(weight[0] * top[0] + weight[1] * top[1], cols)
                for h in (0, 1):
                    un_ref[pl.ds(at[h], cols), lanes] = (weight[h] * pooled).astype(BF16)
                return 0

            lax.fori_loop(0, rows // 2, one, 0, unroll=2)


def pool_layer(geom, domain, top, top_st, gain_t, bias_t):
    pix, chans = top.shape
    args = (domain, top, top_st, gain_t, bias_t)
    return pl.pallas_call(
        functools.partial(pool_kernel, geom),
        in_specs=[SCALARS] + [whole(x.shape) for x in args[1:]],
        out_specs=whole((pix, chans)),
        out_shape=sds((pix, chans), BF16),
        compiler_params=params(),
        cost_estimate=cost(pix * chans * 20, pix * chans * 6),
    )(*args)


def task_kernel(geom, domain_ref, top_ref, top_st, gain_t, bias_t, *refs):
    frames, rows, cols, counts = geom
    pixels = rows * cols
    masks = [refs[4 * k : 4 * k + 4] for k in range(TASKS)]
    task_ref, scr_ref = refs[-2:]
    for f in range(frames):
        for lane in range(0, top_ref.shape[-1], LANES):
            lanes = slice(lane, lane + LANES)

            def table(st, gain, bias):
                average, inverse = frame_tables(st[:, lanes], domain_ref[f], counts)
                scale = inverse * gain[:, lanes]
                return scale, bias[:, lanes] - average * scale

            t_scale, t_shift = table(top_st, gain_t, bias_t)
            wide = [table(*mask[1:]) for mask in masks]

            def one(i, _):
                at = [pl.multiple_of(f * pixels + (2 * i + h) * cols, cols) for h in (0, 1)]
                top = top_rows(top_ref, at, cols, lanes, t_scale, t_shift)
                weight = softmax_window(top, cols)
                held = [w * t for w, t in zip(weight, top)]
                for k in range(TASKS):
                    scale, shift = wide[k]
                    total = None
                    for h in (0, 1):
                        term = sigmoid(masks[k][0][pl.ds(at[h], cols), lanes] * scale + shift) * held[h]
                        total = term if total is None else total + term
                    scr_ref[k] = total
                    even = scr_ref[k, pl.ds(0, cols // 2, stride=2), :]
                    odd = scr_ref[k, pl.ds(1, cols // 2, stride=2), :]
                    task_ref[f, i, k, :, lanes] = even + odd
                return 0

            lax.fori_loop(0, rows // 2, one, 0, unroll=2)


def task_layer(geom, domain, top, top_st, gain_t, bias_t, masks):
    frames, rows, cols, _ = geom
    pix, chans = top.shape
    task_shape = (frames, rows // 2, TASKS, cols // 2, chans)
    args = (domain, top, top_st, gain_t, bias_t, *(x for mask in masks for x in mask))
    return pl.pallas_call(
        functools.partial(task_kernel, geom),
        in_specs=[SCALARS] + [whole(x.shape) for x in args[1:]],
        out_specs=whole(task_shape),
        out_shape=sds(task_shape, F32),
        scratch_shapes=[pltpu.VMEM((TASKS, cols, LANES), F32)],
        compiler_params=params(),
        cost_estimate=cost(pix * chans * 60, pix * chans * 28),
    )(*args)


def pool_early_kernel(geom, first, domain_ref, top_ref, top_st, gain_t, bias_t, wide_ref, wide_st, gain_w, bias_w, cot_ref, *refs):
    frames, rows, cols, counts = geom
    pixels = rows * cols
    mix_ref, gw_ref, sums_ref, scr_ref = refs[-4:]
    for lane in range(0, top_ref.shape[-1], LANES):
        lanes = slice(lane, lane + LANES)
        sums = []
        for f in range(frames):
            average, inverse = frame_tables(top_st[:, lanes], domain_ref[f], counts)
            t_scale = inverse * gain_t[:, lanes]
            t_shift = bias_t[:, lanes] - average * t_scale
            w_mean, w_inv = frame_tables(wide_st[:, lanes], domain_ref[f], counts)

            def one(i, carry):
                at = [pl.multiple_of(f * pixels + (2 * i + h) * cols, cols) for h in (0, 1)]
                top = top_rows(top_ref, at, cols, lanes, t_scale, t_shift)
                weight = softmax_window(top, cols)
                cot = spread_cols(scr_ref, cot_ref[f, i, :, lanes].astype(F32))
                one_sum, two_sum = carry
                for h in (0, 1):
                    xhat = (wide_ref[pl.ds(at[h], cols), lanes] - w_mean) * w_inv
                    mask = sigmoid(xhat * gain_w[:, lanes] + bias_w[:, lanes])
                    part = cot * mask
                    mix = part if first else refs[0][pl.ds(at[h], cols), lanes] + part
                    mix_ref[pl.ds(at[h], cols), lanes] = mix
                    g = part * (weight[h] * top[h]) * (1.0 - mask)
                    gw_ref[pl.ds(at[h], cols), lanes] = g
                    one_sum = one_sum + fold(g)
                    two_sum = two_sum + fold(g * xhat)
                return one_sum, two_sum

            zero = jnp.zeros((8, LANES), F32)
            sums.append(lax.fori_loop(0, rows // 2, one, (zero, zero), unroll=2))
        sums_ref[:, lanes] = by_domain(
            [jnp.sum(s[0], 0, keepdims=True) for s in sums], [jnp.sum(s[1], 0, keepdims=True) for s in sums], domain_ref
        )


def pool_early(geom, domain, _, top_st, gain_t, bias_t, wide, wide_st, gain_w, bias_w, cot, top, mix=None):
    cols = geom[2]
    pix, chans = top.shape
    args = (domain, top, top_st, gain_t, bias_t, wide, wide_st, gain_w, bias_w, cot) + (() if mix is None else (mix,))
    outs = [sds((pix, chans), F32)] * 2 + [sds((4, chans), F32)]
    return pl.pallas_call(
        functools.partial(pool_early_kernel, geom, mix is None),
        in_specs=[SCALARS] + [whole(x.shape) for x in args[1:]],
        out_specs=[whole(o.shape) for o in outs],
        out_shape=outs,
        scratch_shapes=[pltpu.VMEM((cols, LANES), F32)],
        compiler_params=params(),
        cost_estimate=cost(pix * chans * 40, pix * chans * 20),
    )(*args)


def head_kernel(geom, domain_ref, bot_ref, bot_st, gate_ref, gate_st, gain_b, bias_b, gain_g, bias_g, cot_ref,
                maps_ref, gb_ref, gg_ref, sums_ref):
    frames, rows, cols, counts = geom
    pixels = rows * cols
    chans = bot_ref.shape[-1]
    for lane in range(0, chans, LANES):
        lanes = slice(lane, lane + LANES)
        sums = []
        for f in range(frames):
            b_mean, b_inv = frame_tables(bot_st[:, lanes], domain_ref[f], counts)
            gate = []
            for k in range(TASKS):
                sl = slice(k * chans + lane, k * chans + lane + LANES)
                gate.append((sl, *frame_tables(gate_st[:, sl], domain_ref[f], counts)))

            def one(r, carry):
                at = pl.multiple_of(f * pixels + r * cols, cols)
                b_hat = (bot_ref[pl.ds(at, cols), lanes] - b_mean) * b_inv
                act = b_hat * gain_b[:, lanes] + bias_b[:, lanes]
                s = sigmoid(act)
                bottom = act * s
                back = None
                new = []
                for k in range(TASKS):
                    sl, mean, inv = gate[k]
                    xhat = (gate_ref[pl.ds(at, cols), sl] - mean) * inv
                    value = sigmoid(xhat * gain_g[:, sl] + bias_g[:, sl])
                    maps_ref[k, pl.ds(at, cols), lanes] = value * bottom
                    cot = cot_ref[k, pl.ds(at, cols), lanes].astype(F32)
                    part = cot * value
                    back = part if back is None else back + part
                    g = part * bottom * (1.0 - value)
                    gg_ref[pl.ds(at, cols), sl] = g
                    new += [carry[2 * k] + fold(g), carry[2 * k + 1] + fold(g * xhat)]
                g = back * (s * (1.0 + act * (1.0 - s)))
                gb_ref[pl.ds(at, cols), lanes] = g
                new += [carry[-2] + fold(g), carry[-1] + fold(g * b_hat)]
                return tuple(new)

            zero = jnp.zeros((8, LANES), F32)
            sums.append(lax.fori_loop(0, rows, one, (zero,) * (2 * TASKS + 2), unroll=2))
        for k in range(TASKS + 1):
            first = [jnp.sum(s[2 * k], 0, keepdims=True) for s in sums]
            second = [jnp.sum(s[2 * k + 1], 0, keepdims=True) for s in sums]
            at = chans + k * chans + lane if k < TASKS else lane
            sums_ref[:, at : at + LANES] = by_domain(first, second, domain_ref)


def head_layer(geom, domain, bot, bot_st, gate, gate_st, gain_b, bias_b, gain_g, bias_g, cot):
    pix, chans = bot.shape
    args = (domain, bot, bot_st, gate, gate_st, gain_b, bias_b, gain_g, bias_g, cot)
    outs = [sds((TASKS, pix, chans), F32), sds((pix, chans), F32), sds((pix, TASKS * chans), F32),
            sds((4, (TASKS + 1) * chans), F32)]
    return pl.pallas_call(
        functools.partial(head_kernel, geom),
        in_specs=[SCALARS] + [whole(x.shape) for x in args[1:]],
        out_specs=[whole(o.shape) for o in outs],
        out_shape=outs,
        compiler_params=params(),
        cost_estimate=cost(pix * chans * 80, pix * chans * 44),
    )(*args)


def norm_back_rows(g, pre, tables):
    mean, inv, scale, g_mean, g_cross = tables
    xhat = (pre - mean) * inv
    return scale * (g - g_mean - xhat * g_cross)


def back_tables(stats_ref, sums_ref, gain_ref, domain_at, counts):
    mean, inv = frame_tables(stats_ref[...], domain_at, counts)
    g_mean, g_cross = grad_tables(sums_ref[...], domain_at, counts)
    return mean, inv, inv * gain_ref[...], g_mean, g_cross


def backward_kernel(geom, added, epilogue, *refs):
    frames, rows, cols, counts = geom
    pixels = rows * cols
    refs = list(refs)
    domain_ref = refs.pop(0)
    g_ref, pre_ref, st_ref, sm_ref, gain_ref = (refs.pop(0) for _ in range(5))
    kernel_ref = refs.pop(0)
    add_ref = refs.pop(0) if added else None
    lpre_ref, lst_ref, lgain_ref, lbias_ref = (refs.pop(0) for _ in range(4))
    if epilogue == "pool":
        mix_ref = refs.pop(0)
    win_ref, out_ref, sums_ref, held_ref, sem = refs
    chans = kernel_ref.shape[0] // 9

    load = pltpu.make_async_copy(kernel_ref, held_ref, sem)
    load.start()
    clear_edges(win_ref, rows)
    for f in range(frames):
        tables = back_tables(st_ref, sm_ref, gain_ref, domain_ref[f], counts)

        def one_row(r, _):
            at = pl.multiple_of(f * pixels + r * cols, cols)
            low = norm_back_rows(g_ref[pl.ds(at, cols), :], pre_ref[pl.ds(at, cols), :], tables)
            put_windows(win_ref, f, r, low, cols)
            return 0

        lax.fori_loop(0, rows, one_row, 0, unroll=2)
    load.wait()
    source = jnp.concatenate([window(win_ref, 2 - b, 2 - a, rows) for a in range(3) for b in range(3)], 1)
    weight = jnp.concatenate([held_ref[k * chans : (k + 1) * chans, :] for k in range(9)], 1)
    out = lax.dot_general(source, weight, (((1,), (1,)), ((), ())), preferred_element_type=F32)
    out_ref[...] = out + add_ref[...] if added else out

    for lane in range(0, chans, LANES):
        lanes = slice(lane, lane + LANES)
        sums = []
        for f in range(frames):
            mean, inv = frame_tables(lst_ref[:, lanes], domain_ref[f], counts)

            def slope(at):
                xhat = (lpre_ref[pl.ds(at, cols), lanes] - mean) * inv
                act = xhat * lgain_ref[:, lanes] + lbias_ref[:, lanes]
                s = sigmoid(act)
                return xhat, act * s, s * (1.0 + act * (1.0 - s))

            def finish(at, g, xhat, carry):
                out_ref[pl.ds(at, cols), lanes] = g
                return carry[0] + fold(g), carry[1] + fold(g * xhat)

            def one_row(r, carry):
                at = pl.multiple_of(f * pixels + r * cols, cols)
                xhat, _, steep = slope(at)
                return finish(at, out_ref[pl.ds(at, cols), lanes] * steep, xhat, carry)

            def one_pair(i, carry):
                at = [pl.multiple_of(f * pixels + (2 * i + h) * cols, cols) for h in (0, 1)]
                xhat, top, steep = zip(*(slope(a) for a in at))
                weight = softmax_window(top, cols)
                up = [out_ref[pl.ds(a, cols), lanes] for a in at]
                mix = [mix_ref[pl.ds(a, cols), lanes] for a in at]
                pooled = pair_sum(weight[0] * top[0] + weight[1] * top[1], cols)
                d_pool = pair_sum(weight[0] * up[0] + weight[1] * up[1], cols)
                flow = [m + d_pool for m in mix]
                d_w = [u * pooled + fl * t for u, fl, t in zip(up, flow, top)]
                centre = pair_sum(weight[0] * d_w[0] + weight[1] * d_w[1], cols)
                for h in (0, 1):
                    d_top = weight[h] * (flow[h] + d_w[h] - centre)
                    carry = finish(at[h], d_top * steep[h], xhat[h], carry)
                return carry

            zero = jnp.zeros((8, LANES), F32)
            if epilogue == "silu":
                sums.append(lax.fori_loop(0, rows, one_row, (zero, zero), unroll=2))
            else:
                sums.append(lax.fori_loop(0, rows // 2, one_pair, (zero, zero)))
        sums_ref[:, lanes] = by_domain(
            [jnp.sum(s[0], 0, keepdims=True) for s in sums],
            [jnp.sum(s[1], 0, keepdims=True) for s in sums],
            domain_ref,
        )


def backward_layer(geom, domain, top, kernel, lower, added=None, mix=None):
    frames, rows, cols, _ = geom
    pix, width = top[0].shape
    chans = kernel.shape[0] // 9
    args = [domain, *top, in_hbm(kernel)]
    specs = [SCALARS] + [whole(x.shape) for x in top] + [ANYWHERE]
    win = (3, frames, rows + 2, cols, width)
    outs = [sds(win, BF16), sds((pix, chans), F32)]
    extra = ([] if added is None else [added]) + list(lower) + ([] if mix is None else [mix])
    epilogue = "silu" if mix is None else "pool"
    outs.append(sds((4, chans), F32))
    return pl.pallas_call(
        functools.partial(backward_kernel, geom, added is not None, epilogue),
        grid=(1,),
        in_specs=specs + [whole(x.shape) for x in extra],
        out_specs=[whole(o.shape) for o in outs],
        out_shape=outs,
        scratch_shapes=[pltpu.VMEM(kernel.shape, BF16), pltpu.SemaphoreType.DMA],
        compiler_params=params(1),
        cost_estimate=cost(2 * pix * kernel.size, kernel.size * 2 + pix * 10240),
    )(*args, *extra)


def low_kernel(geom, domain_ref, g_ref, pre_ref, st_ref, sm_ref, gain_ref, win_ref):
    frames, rows, cols, counts = geom
    pixels = rows * cols
    clear_edges(win_ref, rows)
    for f in range(frames):
        tables = back_tables(st_ref, sm_ref, gain_ref, domain_ref[f], counts)

        def one_row(r, _):
            at = pl.multiple_of(f * pixels + r * cols, cols)
            low = norm_back_rows(g_ref[pl.ds(at, cols), :], pre_ref[pl.ds(at, cols), :], tables)
            put_windows(win_ref, f, r, low, cols)
            return 0

        lax.fori_loop(0, rows, one_row, 0, unroll=2)


def low_layer(geom, domain, top):
    frames, rows, cols, _ = geom
    pix, width = top[0].shape
    out = sds((3, frames, rows + 2, cols, width), BF16)
    return pl.pallas_call(
        functools.partial(low_kernel, geom),
        grid=(1,),
        in_specs=[SCALARS] + [whole(x.shape) for x in top],
        out_specs=whole(out.shape),
        out_shape=out,
        compiler_params=params(1),
        cost_estimate=cost(pix * width * 20, pix * width * 14),
    )(domain, *top)


def input_kernel(geom, win_ref, kernel_ref, out_ref):
    rows = geom[1]
    step = pl.program_id(0)
    chans = kernel_ref.shape[0] // 3
    source = jnp.concatenate([window(win_ref, 2 - b, 2 - step, rows) for b in range(3)], 1)
    weight = jnp.concatenate([kernel_ref[b * chans : (b + 1) * chans, :] for b in range(3)], 1)
    part = lax.dot_general(source, weight, (((1,), (1,)), ((), ())), preferred_element_type=F32)

    @pl.when(step == 0)
    def _():
        out_ref[...] = part

    @pl.when(step > 0)
    def _():
        out_ref[...] += part


def input_layer(geom, win, kernel):
    frames, rows, cols, _ = geom
    pix = frames * rows * cols
    chans, width = kernel.shape[0] // 9, kernel.shape[1]
    return pl.pallas_call(
        functools.partial(input_kernel, geom),
        grid=(3,),
        in_specs=[whole(win.shape), pl.BlockSpec((3 * chans, width), lambda a: (a, 0))],
        out_specs=whole((pix, chans)),
        out_shape=sds((pix, chans), F32),
        compiler_params=params(1),
        cost_estimate=cost(2 * pix * kernel.size, kernel.size * 2 + pix * 4096),
    )(win, in_hbm(kernel))


class Member:
    def __init__(self, at, shape, dp, fsdp, split=False):
        self.at, self.shape, self.split = at, shape, split
        self.vr = shape[0] // dp // (2 if split else 1)
        self.blocks = shape[1] // fsdp * (2 if split else 1) // LANES
        self.rows = self.vr * self.blocks

    def spots(self, i, j):
        if self.split:
            row, col = i * 2 * self.vr + (j & 1) * self.vr, (j >> 1) * self.blocks * LANES
        else:
            row, col = i * self.vr, j * self.blocks * LANES
        for k in range(self.blocks):
            yield self.at + k * self.vr, row, col + k * LANES


def collect_kernel(member, parts, me_ref, *refs):
    out_ref, sem = refs[-2:]
    fetch(member, parts, me_ref, refs[:-2], out_ref, sem)
    arrived(out_ref, sem)


def collect(pieces):
    return pl.pallas_call(
        functools.partial(collect_kernel, pieces.member, pieces.parts),
        in_specs=[SCALARS] + [ANYWHERE] * len(pieces.sources),
        out_specs=whole(pieces.shape),
        out_shape=sds(pieces.shape, BF16),
        scratch_shapes=[pltpu.SemaphoreType.DMA],
        grid=(1,),
        compiler_params=params(1),
        cost_estimate=cost(0, 4 * pieces.shape[0] * pieces.shape[1]),
    )(pieces.me, *pieces.sources)


def affine_kernel(member, parts, me_ref, *refs):
    out_ref, rows_ref, sem = refs[-3:]
    fetch(member, parts, me_ref, refs[:-3], rows_ref, sem)
    arrived(rows_ref, sem)
    width = out_ref.shape[1] // 32
    for d in range(32):
        rows = rows_ref[16 * d : 16 * d + 16].astype(F32)
        both = jnp.concatenate([rows[:8], rows[8:]], 1)
        out_ref[:, d * width : (d + 1) * width] = (both[0:2] + both[2:4] + both[4:6])[:, :width]


def collect_affine(pieces):
    return pl.pallas_call(
        functools.partial(affine_kernel, pieces.member, pieces.parts),
        in_specs=[SCALARS] + [ANYWHERE] * len(pieces.sources),
        out_specs=whole((2, 5120)),
        out_shape=sds((2, 5120), F32),
        scratch_shapes=[pltpu.VMEM((512, LANES), BF16), pltpu.SemaphoreType.DMA],
        grid=(1,),
        compiler_params=params(1),
        cost_estimate=cost(10000000, 1000000),
    )(pieces.me, *pieces.sources)


def weight_parts(geom, step, act_ref, low_ref, tr_ref):
    rows = geom[1]

    @pl.when(step == 0)
    def _():
        tr_ref[...] = act_ref[...].astype(F32).T.astype(BF16)

    if len(low_ref.shape) == 5:
        for b in range(3):
            yield jnp.dot(tr_ref[...], window(low_ref, 2 - b, 2 - step, rows), preferred_element_type=F32)
    else:
        yield jnp.dot(tr_ref[...], low_ref[...], preferred_element_type=F32)


def weight_kernel(geom, act_ref, low_ref, out_ref, tr_ref):
    chans = tr_ref.shape[0]
    for b, part in enumerate(weight_parts(geom, pl.program_id(0), act_ref, low_ref, tr_ref)):
        out_ref[b * chans : (b + 1) * chans, :] = part.astype(BF16)


def weight_layer(geom, act, low):
    pix, chans = act.shape
    win = low.ndim == 5
    width = low.shape[-1]
    steps = 3 if win else 1
    out = sds((9 * chans if win else chans, width), BF16)
    return pl.pallas_call(
        functools.partial(weight_kernel, geom),
        grid=(steps,),
        in_specs=[whole(act.shape), whole(low.shape)],
        out_specs=pl.BlockSpec((out.shape[0] // steps, width), lambda a: (a, 0)),
        out_shape=out,
        scratch_shapes=[pltpu.VMEM((chans, pix), BF16)],
        compiler_params=params(1),
        cost_estimate=cost(2 * pix * out.size, out.size * 2 + pix * 4096),
    )(act, low)


def weight_blocks_kernel(geom, member, steps, held, *refs):
    refs = list(refs)
    me_ref, act_ref, low_ref = (refs.pop(0) for _ in range(3))
    if held:
        del refs[:3]
    near_ref, far_ref, send_ref, scr_ref, tr_ref, sem = refs
    step = pl.program_id(0)
    chans = tr_ref.shape[0]
    for b, part in enumerate(weight_parts(geom, step, act_ref, low_ref, tr_ref)):
        scr_ref[pl.ds(pl.multiple_of(step * 3 * chans, chans) + b * chans, chans), :] = part.astype(BF16)
    me = me_ref[0]
    share = member.shape[0] // 8
    done = 0
    for s in range(steps):
        ready = member.shape[0] * (s + 1) // steps // share

        @pl.when(step == s)
        def _(done=done, ready=ready):
            for i in range(done, ready):
                e = i ^ (me >> 2)
                q = ((e & 1) << 2) | (e & 2) | (e >> 2)
                for jd in range(4):
                    dst = send_ref.at[jd >> 1, q] if jd & 1 else (near_ref, far_ref)[jd >> 1].at[q]
                    for at, row, col in member.spots(i, (me & 3) ^ jd):
                        pltpu.make_async_copy(
                            scr_ref.at[span(row, member.vr), span(col, LANES)], dst.at[pl.ds(at, member.vr)], sem
                        ).start()

        done = ready

    @pl.when(step == steps - 1)
    def _():
        pltpu.make_async_copy(scr_ref, scr_ref, sem).wait()


def weight_blocks(geom, me, act, low, member, rows, held=None):
    pix, chans = act.shape
    win = low.ndim == 5
    steps = 3 if win else 1
    shard = (rows, LANES)
    outs = [pltpu.HBM((8, *shard), BF16)] * 2 + [pltpu.HBM((2, 8, *shard), BF16)]
    args = [me, act, low] + [in_hbm(x) for x in held or ()]
    size = member.shape[0] * member.shape[1]
    return pl.pallas_call(
        functools.partial(weight_blocks_kernel, geom, member, steps, held is not None),
        grid=(steps,),
        in_specs=[SCALARS, whole(act.shape), whole(low.shape)] + [ANYWHERE] * len(held or ()),
        out_specs=[ANYWHERE] * 3,
        out_shape=outs,
        scratch_shapes=[pltpu.VMEM(member.shape, BF16), pltpu.VMEM((chans, pix), BF16), pltpu.SemaphoreType.DMA],
        input_output_aliases={} if held is None else {3: 0, 4: 1, 5: 2},
        compiler_params=params(1),
        cost_estimate=cost(2 * pix * size, size * 2 + pix * 4096),
    )(*args)


def weight_piece_kernel(geom, member, step, held, *refs):
    rows = geom[1]
    refs = list(refs)
    me_ref, act_ref, low_ref = (refs.pop(0) for _ in range(3))
    if held:
        del refs[:3]
    near_ref, far_ref, send_ref = (refs.pop(0) for _ in range(3))
    if step == 0:
        tr_ref = refs.pop(0)
        tr_ref[...] = act_ref[...].astype(F32).T.astype(BF16)
    else:
        tr_ref = act_ref
    scr_ref, sem = refs
    chans = tr_ref.shape[0]
    for b in range(3):
        part = jnp.dot(tr_ref[...], window(low_ref, 2 - b, 2 - step, rows), preferred_element_type=F32)
        scr_ref[b * chans : (b + 1) * chans, :] = part.astype(BF16)
    me = me_ref[0]
    start, stop = 3 * chans * step, 3 * chans * (step + 1)
    for i in range(8):
        first, last = max(start, i * member.vr), min(stop, (i + 1) * member.vr)
        if first >= last:
            continue
        e = i ^ (me >> 2)
        q = ((e & 1) << 2) | (e & 2) | (e >> 2)
        for jd in range(4):
            dst = send_ref.at[jd >> 1, q] if jd & 1 else (near_ref, far_ref)[jd >> 1].at[q]
            col = ((me & 3) ^ jd) * LANES
            pltpu.make_async_copy(
                scr_ref.at[pl.ds(first - start, last - first), span(col, LANES)],
                dst.at[pl.ds(member.at + first - i * member.vr, last - first)],
                sem,
            ).start()
    arrived(scr_ref, sem)


def weight_piece(geom, me, act, low, member, rows, step, held=None):
    chans = member.shape[0] // 9
    pix, width = low.shape[1] * geom[1] * geom[2], low.shape[-1]
    shard = (rows, LANES)
    outs = [pltpu.HBM((8, *shard), BF16)] * 2 + [pltpu.HBM((2, 8, *shard), BF16)]
    out_specs = [ANYWHERE] * 3
    if step == 0:
        outs.append(sds((chans, pix), BF16))
        out_specs.append(whole((chans, pix)))
    args = [me, act, low] + [in_hbm(x) for x in held or ()]
    return pl.pallas_call(
        functools.partial(weight_piece_kernel, geom, member, step, held is not None),
        grid=(1,),
        in_specs=[SCALARS, whole(act.shape), whole(low.shape)] + [ANYWHERE] * len(held or ()),
        out_specs=out_specs,
        out_shape=outs,
        scratch_shapes=[pltpu.VMEM((3 * chans, width), BF16), pltpu.SemaphoreType.DMA],
        input_output_aliases={} if held is None else {3: 0, 4: 1, 5: 2},
        compiler_params=params(1),
        cost_estimate=cost(2 * pix * 3 * chans * width, chans * width * 6),
    )(*args)


def point_kernel(geom, pieces, *refs):
    frames, rows, cols, _ = geom
    pixels = rows * cols
    refs = list(refs)
    domain_ref, act_ref = refs.pop(0), refs.pop(0)
    if pieces:
        out_ref, sums_ref, matrix_ref, sem = refs[-4:]
        fetch(*pieces, refs[0], refs[1:-4], matrix_ref, sem)
        arrived(matrix_ref, sem)
    else:
        matrix_ref, out_ref, sums_ref = refs
    for lane in range(0, out_ref.shape[-1], 256):
        lanes = slice(lane, lane + 256)
        out_ref[:, lanes] = jnp.dot(act_ref[...], matrix_ref[:, lanes], preferred_element_type=F32)
        pairs = [column_sums(out_ref, f, pixels, lanes) for f in range(frames)]
        sums_ref[:, lanes] = by_domain([p[0] for p in pairs], [p[1] for p in pairs], domain_ref)


def point_layer(geom, domain, act, mat):
    pix, chans = act.shape
    width = mat.shape[1]
    pieces = isinstance(mat, Pieces)
    outs = [sds((pix, width), F32), sds((4, width), F32)] + [sds(mat.shape, BF16)] * pieces
    args = [domain, act] + ([mat.me, *mat.sources] if pieces else [mat])
    specs = [SCALARS, whole(act.shape)]
    specs += [SCALARS] + [ANYWHERE] * len(mat.sources) if pieces else [whole(mat.shape)]
    return pl.pallas_call(
        functools.partial(point_kernel, geom, (mat.member, mat.parts) if pieces else None),
        in_specs=specs,
        out_specs=[whole(o.shape) for o in outs],
        out_shape=outs,
        scratch_shapes=[pltpu.SemaphoreType.DMA] * pieces,
        grid=(1,),
        compiler_params=params(1),
        cost_estimate=cost(2 * pix * chans * width, chans * width * 2 + pix * width * 4),
    )(*args)


def point_back_kernel(geom, added, domain_ref, g_ref, pre_ref, st_ref, sm_ref, gain_ref, mat_ref, *refs):
    frames, rows, cols, counts = geom
    pixels = rows * cols
    low_ref, out_ref = refs[-2:]
    for f in range(frames):
        tables = back_tables(st_ref, sm_ref, gain_ref, domain_ref[f], counts)

        def one_row(r, _):
            at = pl.multiple_of(f * pixels + r * cols, cols)
            low = norm_back_rows(g_ref[pl.ds(at, cols), :], pre_ref[pl.ds(at, cols), :], tables)
            low_ref[pl.ds(at, cols), :] = low.astype(BF16)
            return 0

        lax.fori_loop(0, rows, one_row, 0, unroll=2)
    part = lax.dot_general(low_ref[...], mat_ref[...], (((1,), (1,)), ((), ())), preferred_element_type=F32)
    out_ref[...] = part + refs[0][...] if added else part


def point_back(geom, domain, g, pre, stats, sums, gain, mat, added=None):
    pix, width = g.shape
    chans = mat.shape[0]
    args = (domain, g, pre, stats, sums, gain, mat) + (() if added is None else (added,))
    outs = [sds((pix, width), BF16), sds((pix, chans), F32)]
    return pl.pallas_call(
        functools.partial(point_back_kernel, geom, added is not None),
        grid=(1,),
        in_specs=[SCALARS] + [whole(x.shape) for x in args[1:]],
        out_specs=[whole(o.shape) for o in outs],
        out_shape=outs,
        compiler_params=params(1),
        cost_estimate=cost(2 * pix * mat.size, mat.size * 2 + pix * width * 10),
    )(*args)


def share_kernel(widths, me_ref, *refs):
    *sums, gain_ref, bias_ref, flat_ref = refs
    at = 0
    for ref, width in zip(sums, widths):
        flat_ref[0:1, at : at + width] = ref[2:3, :] + ref[3:4, :]
        flat_ref[1:2, at : at + width] = ref[0:1, :] + ref[1:2, :]
        at += width
    share = gain_ref.shape[1]
    mine = pltpu.roll(flat_ref[...], at - me_ref[0] * share, 1)
    gain_ref[...] = mine[0:1, :share]
    bias_ref[...] = mine[1:2, :share]


def share_of(me, sums, share):
    widths = [x.shape[1] for x in sums]
    got = pl.pallas_call(
        functools.partial(share_kernel, widths),
        grid=(1,),
        in_specs=[SCALARS] + [whole(x.shape) for x in sums],
        out_specs=[whole((1, share))] * 2,
        out_shape=[sds((1, share), F32)] * 2,
        scratch_shapes=[pltpu.VMEM((8, sum(widths)), F32)],
        compiler_params=params(1),
        cost_estimate=cost(0, 100000),
    )(me, *(in_hbm(x) for x in sums))
    return [x[0] for x in got]


AXES = ("dp", "fsdp")
CORE, X, Y, Z_NEAR, Z_FAR = range(5)
ORDER = (CORE, Z_NEAR, Z_FAR, X, Y)


def swap(x, bit):
    n = lax.axis_size(AXES)
    return lax.ppermute(x, AXES, [(i, i ^ (1 << bit)) for i in range(n)])


def bit_of(bit):
    return (lax.axis_index(AXES) >> bit) & 1


def all_bits():
    return range(lax.axis_size(AXES).bit_length() - 1)


def tied(value, to):
    return value if to is None else lax.optimization_barrier((value, to))[0]


class Links:
    def __init__(self):
        self.under_way = {}

    def busy(self, bit, *values):
        self.under_way.setdefault(bit, []).extend(values)

    def total(self, x, after=None, order=None, fill=()):
        bits = order if order and len(all_bits()) == 5 else all_bits()
        fill = list(fill)
        for bit in bits:
            for value in self.under_way.pop(bit, ()):
                x = tied(x, value)
            got = swap(x, bit)
            if fill and (bit != CORE or len(bits) != 5):
                got = tied(got, fill.pop(0)(x))
            x = x + got
            for start in (after or {}).get(bit, ()):
                x = tied(x, start(x))
        for work in fill:
            work(x)
        return x


def half_rows(rows):
    return rows // 32 * 16


class Gather:
    def __init__(self, links, shard):
        self.links, self.shard, self.cut = links, shard, half_rows(shard.shape[0])
        self.sources = None

    def far(self, to=None):
        self.z = tied(self.shard, to)
        self.got = swap(self.z, Z_FAR)

    def near(self, to=None):
        self.z = jnp.stack(tied((self.z, self.got), to))
        self.got = swap(self.z, Z_NEAR)

    def first(self, to=None):
        z = jnp.concatenate(tied((self.z, self.got), to))
        self.a, self.b = z[:, : self.cut], z[:, self.cut :]
        self.got = swap(self.a, Y), swap(self.b, X)

    def second(self, to=None):
        a, b, (got_a, got_b) = tied((self.a, self.b, self.got), to)
        self.a, self.b = jnp.concatenate([a, got_a]), jnp.concatenate([b, got_b])
        self.got = swap(self.a, X), swap(self.b, Y)

    def busy(self):
        if isinstance(self.got, tuple):
            self.links.busy(X, self.got[0])
            self.links.busy(Y, self.got[1])
        else:
            self.links.busy(CORE, self.got)

    def finish(self, to=None):
        rows = self.shard.shape[0]
        self.a, self.b, self.got = tied((self.a, self.b, self.got), to)
        self.sources, self.parts = [], []
        for core in (0, 1):
            for n, value in enumerate((self.a, self.got[0], self.b, self.got[1])):
                z = [8 * (k >> 1) + 16 * (k & 1) for k in range(4)]
                if n < 2:
                    masks = [core + 2 * n + 4 * y + m for y in (0, 1) for m in z]
                else:
                    masks = [core + 4 * (n - 2) + 2 * x + m for x in (0, 1) for m in z]
                self.parts.append((0, self.cut, masks) if n < 2 else (self.cut, rows - self.cut, masks))
                self.sources.append(swap(value, CORE) if core else value)

    def pieces(self, member):
        return Pieces(member, self.parts, number(1), self.sources)


def number(entries):
    return jnp.full((entries,), lax.axis_index(AXES), jnp.int32)


def plus(a, b):
    return (a.astype(F32) + b.astype(F32)).astype(BF16)


def add_kernel(jobs, *refs):
    refs = list(refs)
    count = sum(n for _, n, _ in jobs)
    ins, outs = refs[:count], refs[count:]
    for work, n_in, n_out in jobs:
        work(*ins[:n_in], *outs[:n_out])
        del ins[:n_in], outs[:n_out]


def add_all(*jobs):
    ins = [x for _, job, _ in jobs for x in job]
    outs = [x for _, _, job in jobs for x in job]
    got = pl.pallas_call(
        functools.partial(add_kernel, [(work, len(i), len(o)) for work, i, o in jobs]),
        grid=(1,),
        in_specs=[whole(x.shape) for x in ins],
        out_specs=[whole(x.shape) for x in outs],
        out_shape=outs,
        compiler_params=params(1),
        cost_estimate=cost(0, sum(x.size * 2 for x in ins + outs)),
    )(*ins)
    result = []
    for _, _, job in jobs:
        result.append(got[: len(job)])
        got = got[len(job) :]
    return result


def first_work(cut, near, far, got, a, send_a, b, send_b):
    a[...] = plus(near[:, :cut], got[0, :, :cut])
    send_a[...] = plus(far[:, :cut], got[1, :, :cut])
    for half, out in enumerate((b, send_b)):
        s = slice(4 * half, 4 * half + 4)
        out[0] = plus(near[s, cut:], got[0, s, cut:])
        out[1] = plus(far[s, cut:], got[1, s, cut:])


def second_work(a, b, got_a, got_b, a_out, send_a, b_out, send_b):
    a_out[...] = plus(a[:4], got_a[:4])
    send_a[...] = plus(a[4:], got_a[4:])
    b_out[...] = plus(b[0], got_b[0])
    send_b[...] = plus(b[1], got_b[1])


def near_work(cut, a, b, got_a, got_b, z, send):
    for half, out in enumerate((z, send)):
        s = slice(2 * half, 2 * half + 2)
        out[:, :cut] = plus(a[s], got_a[s])
        out[:, cut:] = plus(b[s], got_b[s])


def far_work(z, got, z_out, send):
    z_out[...] = plus(z[0], got[0])
    send[...] = plus(z[1], got[1])


def finish_work(z, got, out):
    out[...] = z[...].astype(F32) + got[...].astype(F32)


class Scatter:
    def __init__(self, links, blocks):
        self.links, self.blocks = links, blocks
        self.rows = blocks[0].shape[1]
        self.cut = half_rows(self.rows)
        self.got = swap(blocks[2], CORE)

    def shape(self, *dims):
        return sds((*dims, LANES), BF16)

    def first_job(self):
        c, r = self.cut, self.rows - self.cut
        outs = [self.shape(8, c)] * 2 + [self.shape(2, 4, r)] * 2
        return functools.partial(first_work, c), [*self.blocks[:2], self.got], outs

    def first(self, a, send_a, b, send_b):
        self.a, self.b = a, b
        self.got = swap(send_a, X), swap(send_b, Y)

    def second_job(self):
        c, r = self.cut, self.rows - self.cut
        return second_work, [self.a, self.b, *self.got], [self.shape(4, c)] * 2 + [self.shape(4, r)] * 2

    def second(self, a, send_a, b, send_b):
        self.a, self.b = a, b
        self.got = swap(send_a, Y), swap(send_b, X)

    def near_job(self):
        return functools.partial(near_work, self.cut), [self.a, self.b, *self.got], [self.shape(2, self.rows)] * 2

    def near(self, to=None):
        self.got = swap(tied(self.send, to), Z_NEAR)

    def far_job(self):
        return far_work, [self.z, self.got], [self.shape(self.rows)] * 2

    def far(self, z, send):
        self.z = z
        self.got = swap(send, Z_FAR)

    def finish_job(self):
        return finish_work, [self.z, self.got], [sds((self.rows, LANES), F32)]


def add_after(to, *jobs):
    return add_all(*((work, tied(ins, to), outs) for work, ins, outs in jobs))


def rows_of_chip(shard):
    half = shard.shape[0] // 2
    odd = bit_of(CORE) == 1
    mine = jnp.where(odd, shard[half:], shard[:half])
    got = swap(jnp.where(odd, shard[:half], shard[half:]), CORE)
    return jnp.concatenate([jnp.where(odd, got, mine), jnp.where(odd, mine, got)], 1)


def columns_of_core(rows):
    half = rows.shape[1] // 2
    odd = bit_of(CORE) == 1
    mine = jnp.where(odd, rows[:, half:], rows[:, :half])
    got = swap(jnp.where(odd, rows[:, :half], rows[:, half:]), CORE)
    return jnp.concatenate([jnp.where(odd, got, mine), jnp.where(odd, mine, got)], 0)


def pack(x):
    return jnp.concatenate([x[:, k : k + LANES] for k in range(0, x.shape[1], LANES)], 0)


def unpack(x, blocks):
    rows = x.shape[0] // blocks
    return jnp.concatenate([x[k * rows : (k + 1) * rows] for k in range(blocks)], 1)


def in_three(x):
    high = lax.reduce_precision(x, 8, 7)
    middle = lax.reduce_precision(x - high, 8, 7)
    return jnp.stack([high, middle, x - high - middle]).astype(BF16)


def gather(x):
    x = x[None]
    for bit in all_bits():
        other = swap(x, bit)
        high = bit_of(bit) == 1
        x = jnp.concatenate([jnp.where(high, other, x), jnp.where(high, x, other)], 0)
    return x


def scatter(x):
    for bit in reversed(all_bits()):
        half = x.shape[0] // 2
        high = bit_of(bit) == 1
        send = jnp.where(high, x[:half], x[half:])
        keep = jnp.where(high, x[half:], x[:half])
        x = plus(keep, swap(send, bit))
    return x[0]


def gather_matrix(shard):
    dp, fsdp = lax.axis_size("dp"), lax.axis_size("fsdp")
    rows, cols = shard.shape
    full = gather(shard).reshape(dp, fsdp, rows, cols)
    return full.transpose(0, 2, 1, 3).reshape(dp * rows, fsdp * cols)


def scatter_matrix(full):
    dp, fsdp = lax.axis_size("dp"), lax.axis_size("fsdp")
    rows, cols = full.shape[0] // dp, full.shape[1] // fsdp
    parts = full.reshape(dp, rows, fsdp, cols).transpose(0, 2, 1, 3)
    return scatter(parts.reshape(dp * fsdp, rows, cols)).astype(F32)


class AnyMesh:
    def __init__(self, links, geom, weights, gains, biases):
        self.geom = geom
        self.mats = {name: gather_matrix(w) for name, w in weights.items()}
        self.affine = gather(jnp.stack([gains, biases])).transpose(1, 0, 2).reshape(2, 1, -1)
        self.grads, self.ready = {}, None

    def get(self, name):
        return self.mats[name]

    def whole(self, name):
        return self.mats[name]

    def put(self, name, matrix):
        pass

    def layer_done(self, n, local):
        pass

    def during(self, point):
        return {}

    def add(self, name, act, low):
        got = weight_layer(self.geom, act, low)
        self.grads[name] = scatter_matrix(got)
        return got

    def pieces(self, name, act, low):
        return [lambda x: self.add(name, act, low)]

    def send(self, n, to=None):
        pass

    def after_layer(self, n, local):
        pass

    def now(self):
        return None

    def tail(self, blocks, kernels):
        return [kernel(None) for kernel in kernels]


class ThisMesh:
    def __init__(self, links, geom, weights, gains, biases):
        self.geom, self.links = geom, links
        self.me = number(1)
        sizes = (8, 4)
        full = {n: (w.shape[0] * 8, w.shape[1] * 4) for n, w in weights.items()}
        splits = ("six", "gating")
        g1 = Gather(links, weights["one"])
        g1.far()
        packed = {n: pack(rows_of_chip(tied(w, g1.got)) if n in splits else w) for n, w in weights.items()}
        gains, biases = tied((gains, biases), g1.got)
        affine = in_three(jnp.stack([gains, biases])).reshape(6, -1)
        affine = jnp.pad(affine, ((0, 2), (0, 2 * LANES - affine.shape[1])))
        affine = jnp.concatenate([affine[:, :LANES], affine[:, LANES:]])
        groups = (("one",), ("two",), ("three",), ("four",), ("five",), ("six", "gating", "attend"))
        self.g, self.members, self.group = [], {}, {}
        for names in groups:
            at = 0
            for name in names:
                self.members[name] = Member(at, full[name], *sizes, split=name in splits)
                at += self.members[name].rows
            if names == ("one",):
                group = g1
            else:
                group = Gather(links, jnp.concatenate([packed[n] for n in names] + [affine] * (names == ("two",))))
            self.g.append(group)
            self.group.update((n, group) for n in names)
        g2 = self.g[1]
        g1.near()
        g2.far(g1.got)
        g1.first()
        g2.near(g1.got)
        g1.second()
        g1.finish()
        self.g[2].far(g2.got)
        g2.first(g1.got)
        self.ready = self.g[5].shard
        self.mats = {}
        self.grads, self.blocks, self.sums = {}, {}, {}
        self.homes, self.rows = {}, {}
        for names in (("six", "gating"), ("five",), ("four", "attend"), ("three",), ("two",), ("one",)):
            at = 0
            for name in names:
                self.homes[name] = Member(at, full[name], *sizes, split=name in splits)
                at += self.homes[name].rows
            self.rows.update((name, at) for name in names)

    def layer_done(self, n, local):
        if n < 6:
            self.g[n].second((local, self.g[n + 1].got) if n < 5 else local)
            self.g[n].busy()

    def get(self, name):
        if name in self.mats:
            return self.mats[name]
        group = self.group[name]
        self.mats[name] = group.pieces(self.members[name])
        if name == "two":
            self.affine = collect_affine(group.pieces(FlatMember(self.members["two"].rows, 16)))[:, None]
        return self.mats[name]

    def whole(self, name):
        self.mats[name] = collect(self.get(name))
        return self.mats[name]

    def put(self, name, matrix):
        self.mats[name] = matrix

    def during(self, point):
        if point <= 5:

            def x_done(x):
                self.g[point].finish(x)

            if point == 5:
                return {X: [x_done]}
            group = self.g[point + 1]

            def z_done(x):
                group.near(x)

            def y_done(x):
                group.first(x)
                if point < 4:
                    self.g[point + 2].far(x)

            return {Z_FAR: [z_done], X: [x_done], Y: [y_done]}
        n = 14 - point

        def z_done(x):
            self.sums[n + 2].near(x)

        def x_done(x):
            (got,) = add_after(x, self.sums[n + 2].far_job())
            if n == 2:
                self.late = got
            else:
                self.sums[n + 2].far(*got)
            return got[0]

        def y_done(x):
            jobs = [self.sums[n + 1].second_job()]
            if n == 2:
                self.send(2)
                jobs.append(self.sums[2].first_job())
            got = add_after(x, *jobs)
            self.sums[n + 1].second(*got[0])
            if n == 2:
                self.sums[2].first(*got[1])

        return {Z_FAR: [z_done], X: [x_done], Y: [y_done]} if n < 5 else {Y: [y_done]}

    def add(self, name, act, low):
        n = NUMBER[name]
        self.blocks[n] = weight_blocks(
            self.geom, self.me, act, low, self.homes[name], self.rows[name], self.blocks.get(n)
        )
        return self.blocks[n][0]

    def pieces(self, name, act, low):
        def piece(step):
            def work(x):
                n = NUMBER[name]
                if step == 0:
                    *self.blocks[n], self.turned = weight_piece(
                        self.geom, self.me, tied(act, x), low, self.homes[name], self.rows[name], 0
                    )
                else:
                    self.blocks[n] = weight_piece(
                        self.geom, self.me, tied(self.turned, x), low, self.homes[name], self.rows[name], step, self.blocks[n]
                    )
                return self.blocks[n][0]

            return work

        return [piece(step) for step in range(3)]

    def send(self, n, to=None):
        near, far, away = self.blocks[n]
        self.sums[n] = Scatter(self.links, (near, far, tied(away, to)))

    def after_layer(self, n, local):
        jobs = [self.sums[n + 1].first_job()]
        if n < 5:
            jobs.append(self.sums[n + 2].near_job())
        if n < 4:
            jobs.append(self.sums[n + 3].finish_job())
        got = add_after(local, *jobs)
        self.sums[n + 1].first(*got[0])
        self.links.busy(X, *self.sums[n + 1].got)
        if n < 5:
            s = self.sums[n + 2]
            s.z, s.send = got[1]
        if n < 4:
            (self.sums[n + 3].out,) = got[2]

    def now(self):
        return self.sums[3].a

    def tail(self, blocks, kernels):
        two, three, four = (self.sums[n] for n in (2, 3, 4))
        outs = [kernels[0](blocks)]
        got = add_after(outs[0], two.second_job(), three.near_job())
        two.second(*got[0])
        three.z, three.send = got[1]
        three.near()
        self.send(1, got[0][0])
        one = self.sums[1]
        got = add_after(got[0][0], one.first_job(), two.near_job(), three.far_job())
        one.first(*got[0])
        two.z, two.send = got[1]
        two.near()
        three.far(*got[2])
        outs.append(kernels[1](got[0][0]))
        (got,) = add_after(got[0][0], one.second_job())
        one.second(*got)
        (got,) = add_after(got[0], two.far_job())
        two.far(*got)
        got = add_after(got[0], one.near_job(), three.finish_job())
        one.z, one.send = got[0]
        one.near()
        (three.out,) = got[1]
        four.far(*tied(tuple(self.late), one.z))
        got = add_after(one.z, one.far_job(), two.finish_job())
        one.far(*got[0])
        (two.out,) = got[1]
        ((four.out,),) = add_after(got[0][0], four.finish_job())
        ((one.out,),) = add_after(four.out, one.finish_job())
        for name, m in self.homes.items():
            out = unpack(self.sums[NUMBER[name]].out[m.at : m.at + m.rows], m.blocks)
            self.grads[name] = columns_of_core(out) if m.split else out
        return outs


NUMBER = dict(one=1, two=2, three=3, attend=4, four=4, five=5, six=6, gating=6)


class FlatMember:
    def __init__(self, at, rows):
        self.at, self.vr, self.rows, self.blocks, self.shape = at, rows, rows, 1, (32 * rows, LANES)

    def spots(self, i, j):
        yield self.at, (i * 4 + j) * self.vr, 0


def body(
    frames_in,
    domain,
    kernel_one,
    kernel_two,
    kernel_three,
    attn_enc,
    kernel_four,
    kernel_five,
    kernel_six,
    attn_dec,
    gains,
    biases,
    enc_cot,
    dec_cot,
):
    frames, rows, cols, _ = frames_in.shape
    total_frames = frames * lax.axis_size(AXES)
    first = total_frames * 5 // 8
    counts = (float(first * rows * cols), float((total_frames - first) * rows * cols))
    geom = (frames, rows, cols, counts)
    pix = frames * rows * cols
    source = frames_in.reshape(pix, C_IN)
    enc_cot = enc_cot.transpose(0, 1, 3, 2, 4)
    dec_cot = dec_cot.reshape(pix, TASKS, C_DEC).transpose(1, 0, 2)
    weights = dict(
        one=kernel_one, two=kernel_two, three=kernel_three, attend=attn_enc,
        four=kernel_four, five=kernel_five, six=kernel_six, gating=attn_dec,
    )
    links = Links()
    this = lax.axis_size("dp") == 8 and lax.axis_size("fsdp") == 4
    w = (ThisMesh if this else AnyMesh)(links, geom, weights, gains, biases)

    def forward(name, source, norm=None):
        got = forward_layer(geom, domain, source, w.get(name), norm)
        w.put(name, got[-1])
        return got[:3] if norm is not None else got[:2]

    def point(name, act):
        got = point_layer(geom, domain, act, w.get(name))
        w.put(name, got[-1])
        return got[:2]

    pre_1, local = forward("one", tied(source, w.ready))
    w.layer_done(1, local)
    st_1 = links.total(local, w.during(1), ORDER)
    w.get("two")
    widths = (C_MID, C_MID, C_MID, TASKS * C_MID, C_MID, C_MID, C_DEC, TASKS * C_DEC)
    gain, bias, at = [], [], 0
    for width in widths:
        gain.append(w.affine[0, :, at : at + width])
        bias.append(w.affine[1, :, at : at + width])
        at += width
    pre_2, local, act_1 = forward("two", pre_1, (st_1, gain[0], bias[0]))
    w.layer_done(2, local)
    st_2 = links.total(local, w.during(2), ORDER)
    pre_3, local, act_2 = forward("three", pre_2, (st_2, gain[1], bias[1]))
    w.layer_done(3, local)
    st_3 = links.total(local, w.during(3), ORDER)
    unpooled = pool_layer(geom, domain, pre_3, st_3, gain[2], bias[2])
    pre_4, local = forward("four", unpooled)
    w.layer_done(4, local)
    st_4 = links.total(local, w.during(4), ORDER)
    pre_5, local, act_4 = forward("five", pre_4, (st_4, gain[4], bias[4]))
    w.layer_done(5, local)
    st_5 = links.total(local, w.during(5), ORDER)
    pre_g, local_g = point("gating", act_4)
    pre_6, local, act_5 = forward("six", pre_5, (st_5, gain[5], bias[5]))
    attend = w.whole("attend")
    wide = []

    def attend_part(k):
        def work(x):
            wide.append(point_layer(geom, domain, tied(act_2, x), attend[:, k * C_MID : (k + 1) * C_MID]))
            return wide[-1][0]

        return work

    both = links.total(jnp.concatenate([local, local_g], 1), None, ORDER, [attend_part(k) for k in range(TASKS)])
    st_6, st_g = both[:, :C_DEC], both[:, C_DEC:]
    pre_a = [p for p, _ in wide]
    task_maps, g_6, g_g, local = head_layer(
        geom, domain, pre_6, st_6, pre_g, st_g, gain[6], bias[6], gain[7], bias[7], dec_cot
    )
    both = links.total(jnp.concatenate([local] + [s for _, s in wide], 1), None, ORDER)
    sm_6, sm_g, st_a = both[:, :C_DEC], both[:, C_DEC : 4 * C_DEC], both[:, 4 * C_DEC :]
    st_a = [st_a[:, k * C_MID : (k + 1) * C_MID] for k in range(TASKS)]
    pool_args = (geom, domain, pre_3, st_3, gain[2], bias[2])
    masks = [(pre_a[k], st_a[k], gain[3][:, k * C_MID : (k + 1) * C_MID], bias[3][:, k * C_MID : (k + 1) * C_MID]) for k in range(TASKS)]

    win_6, g_5, local = backward_layer(
        geom, domain, (g_6, pre_6, st_6, sm_6, gain[6]), w.get("six"), lower=(pre_5, st_5, gain[5], bias[5])
    )
    early, gate_back = [], []

    def early_part(k):
        def work(x):
            early.append(pool_early(*pool_args, *masks[k], enc_cot[:, :, k], tied(pre_3, x), early[-1][0] if early else None))
            return early[-1][0]

        return work

    def gate_part(x):
        gate_back.extend(point_back(geom, domain, tied(g_g, x), pre_g, st_g, sm_g, gain[7], w.get("gating")))
        return gate_back[0]

    sm_5 = links.total(
        local, None, ORDER, [lambda x: w.add("six", act_5, tied(win_6, x)), gate_part, early_part(0), early_part(1)]
    )
    early_part(2)(sm_5)
    mix = early[-1][0]
    low_g, add_4 = gate_back
    blocks = w.add("gating", act_4, low_g)
    w.send(6, sm_5)
    win_5, g_4, local = backward_layer(
        geom,
        domain,
        (tied(g_5, blocks), pre_5, st_5, sm_5, gain[5]),
        w.get("five"),
        added=add_4,
        lower=(pre_4, st_4, gain[4], bias[4]),
    )
    w.after_layer(5, local)
    both = links.total(
        jnp.concatenate([local] + [e[2] for e in early], 1), w.during(9), ORDER, w.pieces("five", act_4, win_5)
    )
    w.send(5, both)
    sm_4 = both[:, :C_MID]
    sm_a = [both[:, (k + 1) * C_MID : (k + 2) * C_MID] for k in range(TASKS)]
    win_4, g_3, local = backward_layer(
        geom,
        domain,
        (g_4, pre_4, st_4, sm_4, gain[4]),
        w.get("four"),
        lower=(pre_3, st_3, gain[2], bias[2]),
        mix=mix,
    )
    w.after_layer(4, local)
    backs = []

    def attend_back(k):
        def work(x):
            backs.append(
                point_back(
                    geom, domain, tied(early[k][1], x), pre_a[k], st_a[k], sm_a[k], masks[k][2],
                    attend[:, k * C_MID : (k + 1) * C_MID], backs[-1][1] if backs else None,
                )
            )
            return backs[-1][1]

        return work

    sm_3 = links.total(local, w.during(10), ORDER, w.pieces("four", unpooled, win_4) + [attend_back(0)])
    attend_back(1)(sm_3)
    attend_back(2)(backs[-1][1])
    low_a = jnp.concatenate([low for low, _ in backs], 1)
    blocks = w.add("attend", act_2, low_a)
    w.send(4)
    win_3, g_2, local = backward_layer(
        geom,
        domain,
        (tied(g_3, blocks), pre_3, st_3, sm_3, gain[2]),
        w.get("three"),
        added=backs[-1][1],
        lower=(pre_2, st_2, gain[1], bias[1]),
    )
    w.after_layer(3, local)
    tasks = []

    def task_part(x):
        tasks.append(task_layer(geom, domain, tied(pre_3, x), *pool_args[3:], masks))
        return tasks[0]

    sm_2 = links.total(local, w.during(11), ORDER, w.pieces("three", act_2, win_3) + [task_part])
    w.send(3, sm_2)
    win_2, g_1, local = backward_layer(
        geom,
        domain,
        (g_2, pre_2, st_2, sm_2, gain[1]),
        w.get("two"),
        lower=(pre_1, st_1, gain[0], bias[0]),
    )
    w.after_layer(2, local)
    sm_1 = links.total(local, w.during(12), ORDER, w.pieces("two", act_1, win_2))
    win_1 = low_layer(geom, domain, (tied(g_1, w.now()), pre_1, st_1, sm_1, gain[0]))
    blocks = w.add("one", source, win_1)
    frames_grad, task_maps = w.tail(
        blocks,
        (
            lambda to: input_layer(geom, tied(win_1, to), w.get("one")),
            lambda to: tied(task_maps, to).transpose(1, 0, 2).reshape(frames, rows, cols, TASKS, C_DEC),
        ),
    )
    gains_grad, biases_grad = share_of(number(1), [sm_1, sm_2, sm_3, *sm_a, sm_4, sm_5, sm_6, sm_g], gains.shape[0])
    return (
        tasks[0].transpose(0, 1, 3, 2, 4),
        task_maps,
        frames_grad.reshape(frames, rows, cols, C_IN),
        *(w.grads[n] for n in ("one", "two", "three", "attend", "four", "five", "six", "gating")),
        gains_grad,
        biases_grad,
    )


def solution(mesh):
    whole_split = P(AXES)
    matrix = P("dp", "fsdp")
    return jax.shard_map(
        body,
        mesh=mesh,
        in_specs=(whole_split, whole_split) + (matrix,) * 8 + (whole_split,) * 4,
        out_specs=(whole_split,) * 3 + (matrix,) * 8 + (whole_split,) * 2,
        check_vma=False,
    )
```

```python
import functools

import jax
import jax.numpy as jnp
from jax import lax
from jax.experimental import pallas as pl
from jax.experimental.pallas import tpu as pltpu
from jax.sharding import PartitionSpec as P

C_IN = 256
C_MID = 512
C_DEC = 256
TASKS = 3
EPS = 1e-05
LANES = 128
F32 = jnp.float32
BF16 = jnp.bfloat16
COST = 0.1
VMEM_LIMIT = 12 * 1024 * 1024


def params(grid_dims=0):
    return pltpu.CompilerParams(
        vmem_limit_bytes=VMEM_LIMIT,
        dimension_semantics=("arbitrary",) * grid_dims if grid_dims else None,
    )


def cost(flops, size):
    return pl.CostEstimate(flops=int(flops * COST), bytes_accessed=int(size * COST), transcendentals=0)


def whole(shape):
    zeros = (0,) * len(shape)
    return pl.BlockSpec(shape, lambda *_: zeros, pipeline_mode=pl.Buffered(1))


SCALARS = pl.BlockSpec(memory_space=pltpu.SMEM)


def sds(shape, dtype):
    return jax.ShapeDtypeStruct(shape, dtype)


def sigmoid(v):
    return 0.5 * jnp.tanh(0.5 * v) + 0.5


def frame_tables(stats, domain_at, counts):
    first = domain_at == 0
    share = jnp.where(first, 1.0 / counts[0], 1.0 / counts[1])
    average = jnp.where(first, stats[0:1], stats[1:2]) * share
    square = jnp.where(first, stats[2:3], stats[3:4]) * share
    return average, lax.rsqrt(square - average * average + EPS)


def grad_tables(sums, domain_at, counts):
    first = domain_at == 0
    share = jnp.where(first, 1.0 / counts[0], 1.0 / counts[1])
    return (
        jnp.where(first, sums[0:1], sums[1:2]) * share,
        jnp.where(first, sums[2:3], sums[3:4]) * share,
    )


def by_domain(first, second, domain_ref):
    rows = []
    for per_frame in (first, second):
        for d in (0, 1):
            total = None
            for f, value in enumerate(per_frame):
                term = jnp.where(domain_ref[f] == d, value, jnp.zeros_like(value))
                total = term if total is None else total + term
            rows.append(total)
    return jnp.concatenate(rows, 0)


def fold(x):
    return jnp.sum(x.reshape(-1, 8, x.shape[-1]), 0)


def value_sums(parts, domain_ref, others=None):
    others = parts if others is None else others
    return by_domain(
        [jnp.sum(fold(p), 0, keepdims=True) for p in parts],
        [jnp.sum(fold(p * o), 0, keepdims=True) for p, o in zip(parts, others)],
        domain_ref,
    )


def put_windows(win_ref, f, row, value, cols):
    col = lax.broadcasted_iota(jnp.int32, value.shape, 0)
    left = jnp.where(col == 0, 0.0, pltpu.roll(value, 1, 0))
    right = jnp.where(col == cols - 1, 0.0, pltpu.roll(value, cols - 1, 0))
    win_ref[0, f, row + 1] = left.astype(BF16)
    win_ref[1, f, row + 1] = value.astype(BF16)
    win_ref[2, f, row + 1] = right.astype(BF16)


def clear_edges(win_ref, rows):
    shape = win_ref.shape
    for b in range(3):
        for f in range(shape[1]):
            win_ref[b, f, 0] = jnp.zeros(shape[3:], BF16)
            win_ref[b, f, rows + 1] = jnp.zeros(shape[3:], BF16)


def window(win_ref, b, row_at, rows):
    part = win_ref[b, :, pl.ds(row_at, rows)]
    return part.reshape(-1, part.shape[-1])


def column_sums(ref, f, pixels, lanes, step=64):
    def add(i, carry):
        part = ref[pl.ds(f * pixels + i * step, step), lanes]
        return carry[0] + fold(part), carry[1] + fold(part * part)

    width = lanes.stop - lanes.start
    zero = jnp.zeros((8, width), F32)
    one, two = lax.fori_loop(0, pixels // step, add, (zero, zero), unroll=2)
    return jnp.sum(one, 0, keepdims=True), jnp.sum(two, 0, keepdims=True)


def in_hbm(x):
    return pltpu.with_memory_space_constraint(x, pltpu.HBM)


class Pieces:
    def __init__(self, member, parts, me, sources):
        self.member, self.parts, self.me = member, parts, me
        self.sources = list(sources)
        self.shape = member.shape


def span(start, size):
    return pl.ds(start if isinstance(start, int) else pl.multiple_of(start, size & -size), size)


def fetch(member, parts, me_ref, sources, dst_ref, sem):
    me = me_ref[0]
    for (first, size, masks), src in zip(parts, sources):
        for q in range(src.shape[0]):
            d = q if masks is None else me ^ masks[q]
            for at, row, col in member.spots(d >> 2, d & 3):
                low, high = max(at, first), min(at + member.vr, first + size)
                if low < high:
                    pltpu.make_async_copy(
                        src.at[q, pl.ds(low - first, high - low)],
                        dst_ref.at[span(row + (low - at), high - low), span(col, LANES)],
                        sem,
                    ).start()


def arrived(ref, sem):
    pltpu.make_async_copy(ref, ref, sem).wait()


def forward_kernel(geom, normed, pieces, *refs):
    frames, rows, cols, counts = geom
    pixels = rows * cols
    refs = list(refs)
    domain_ref = refs.pop(0)
    source_ref = refs.pop(0)
    if normed:
        stats_ref, gain_ref, bias_ref = refs.pop(0), refs.pop(0), refs.pop(0)
    if pieces:
        me_ref = refs.pop(0)
        sources = [refs.pop(0) for _ in pieces[1]]
    else:
        kernel_ref = refs.pop(0)
    out_ref = refs.pop(0)
    sums_ref = refs.pop(0)
    act_ref = refs.pop(0) if normed else None
    if pieces:
        matrix_ref = refs.pop(0)
    win_ref, held_ref, sem = refs

    if pieces:
        fetch(*pieces, me_ref, sources, held_ref, sem.at[0])
    else:
        pltpu.make_async_copy(kernel_ref, held_ref, sem.at[0]).start()
    clear_edges(win_ref, rows)
    for f in range(frames):
        if normed:
            average, inverse = frame_tables(stats_ref[...], domain_ref[f], counts)
            scale = inverse * gain_ref[...]
            shift = bias_ref[...] - average * scale

        def one_row(r, _):
            at = pl.multiple_of(f * pixels + r * cols, cols)
            value = source_ref[pl.ds(at, cols), :].astype(F32)
            if normed:
                act = value * scale + shift
                value = act * sigmoid(act)
                act_ref[pl.ds(at, cols), :] = value.astype(BF16)
            put_windows(win_ref, f, r, value, cols)
            return 0

        lax.fori_loop(0, rows, one_row, 0, unroll=2)
    arrived(held_ref, sem.at[0])
    if pieces:
        pltpu.make_async_copy(held_ref, matrix_ref, sem.at[1]).start()
    source = jnp.concatenate([window(win_ref, b, a, rows) for a in range(3) for b in range(3)], 1)
    out = jnp.dot(source, held_ref[...], preferred_element_type=F32)
    out_ref[...] = out
    parts = [out[f * pixels : (f + 1) * pixels] for f in range(frames)]
    sums_ref[...] = by_domain(
        [jnp.sum(fold(p), 0, keepdims=True) for p in parts],
        [jnp.sum(fold(p * p), 0, keepdims=True) for p in parts],
        domain_ref,
    )
    if pieces:
        pltpu.make_async_copy(held_ref, matrix_ref, sem.at[1]).wait()


ANYWHERE = pl.BlockSpec(memory_space=pl.ANY)


def forward_layer(geom, domain, source, kernel, norm=None):
    frames, rows, cols, _ = geom
    pix, chans = source.shape
    width = kernel.shape[1]
    pieces = isinstance(kernel, Pieces)
    args, specs = [domain, source], [SCALARS, whole(source.shape)]
    if norm is not None:
        args += list(norm)
        specs += [whole(x.shape) for x in norm]
    if pieces:
        args += [kernel.me, *kernel.sources]
        specs += [SCALARS] + [ANYWHERE] * len(kernel.sources)
    else:
        args.append(in_hbm(kernel))
        specs.append(ANYWHERE)
    outs, out_specs = [sds((pix, width), F32)], [whole((pix, width))]
    outs.append(sds((4, width), F32))
    out_specs.append(whole((4, width)))
    if norm is not None:
        outs.append(sds((pix, chans), BF16))
        out_specs.append(whole((pix, chans)))
    scratch = [pltpu.VMEM((3, frames, rows + 2, cols, chans), BF16)]
    scratch += [pltpu.VMEM(kernel.shape, BF16), pltpu.SemaphoreType.DMA((2,))]
    if pieces:
        outs.append(pltpu.HBM(kernel.shape, BF16))
        out_specs.append(ANYWHERE)
    size = kernel.shape[0] * kernel.shape[1]
    return pl.pallas_call(
        functools.partial(forward_kernel, geom, norm is not None, (kernel.member, kernel.parts) if pieces else None),
        grid=(1,),
        in_specs=specs,
        out_specs=out_specs,
        out_shape=outs,
        scratch_shapes=scratch,
        compiler_params=params(1),
        cost_estimate=cost(2 * pix * size, size * 2 + pix * 4096),
    )(*args)


def pair_sum(x, cols):
    even = lax.broadcasted_iota(jnp.int32, x.shape, 0) % 2 == 0
    return x + jnp.where(even, pltpu.roll(x, cols - 1, 0), pltpu.roll(x, 1, 0))


def softmax_window(top, cols):
    exps = [jnp.exp(t) for t in top]
    share = 1.0 / pair_sum(exps[0] + exps[1], cols)
    return [e * share for e in exps]


def spread_cols(scr_ref, x):
    half = x.shape[0]
    scr_ref[pl.ds(0, half, stride=2), :] = x
    scr_ref[pl.ds(1, half, stride=2), :] = x
    return scr_ref[...]


def top_rows(top_ref, at, cols, lanes, scale, shift):
    top = []
    for a in at:
        act = top_ref[pl.ds(a, cols), lanes] * scale + shift
        top.append(act * sigmoid(act))
    return top


def row_pairs(x, cols):
    x = x.reshape(-1, 2, cols, x.shape[-1])
    return x[:, 0], x[:, 1]


def pair_sums(x):
    cols = x.shape[1]
    even = lax.broadcasted_iota(jnp.int32, x.shape, 1) % 2 == 0
    return x + jnp.where(even, pltpu.roll(x, cols - 1, 1), pltpu.roll(x, 1, 1))


def window_weights(top):
    exps = [jnp.exp(t) for t in top]
    share = 1.0 / pair_sums(exps[0] + exps[1])
    return [e * share for e in exps]


def pool_kernel(geom, domain_ref, top_ref, top_st, gain_t, bias_t, un_ref):
    frames, rows, cols, counts = geom
    pixels = rows * cols
    for f in range(frames):
        at = slice(f * pixels, (f + 1) * pixels)
        for lane in range(0, top_ref.shape[-1], LANES):
            lanes = slice(lane, lane + LANES)
            average, inverse = frame_tables(top_st[:, lanes], domain_ref[f], counts)
            scale = inverse * gain_t[:, lanes]
            act = top_ref[at, lanes] * scale + (bias_t[:, lanes] - average * scale)
            top = row_pairs(act * sigmoid(act), cols)
            weight = window_weights(top)
            pooled = pair_sums(weight[0] * top[0] + weight[1] * top[1])
            un_ref[at, lanes] = jnp.stack([w * pooled for w in weight], 1).reshape(pixels, LANES).astype(BF16)


def pool_layer(geom, domain, top, top_st, gain_t, bias_t):
    pix, chans = top.shape
    args = (domain, top, top_st, gain_t, bias_t)
    return pl.pallas_call(
        functools.partial(pool_kernel, geom),
        in_specs=[SCALARS] + [whole(x.shape) for x in args[1:]],
        out_specs=whole((pix, chans)),
        out_shape=sds((pix, chans), BF16),
        compiler_params=params(),
        cost_estimate=cost(pix * chans * 20, pix * chans * 6),
    )(*args)


def task_kernel(geom, domain_ref, top_ref, top_st, gain_t, bias_t, *refs):
    frames, rows, cols, counts = geom
    pixels = rows * cols
    masks = [refs[4 * k : 4 * k + 4] for k in range(TASKS)]
    task_ref, scr_ref = refs[-2:]
    for f in range(frames):
        for lane in range(0, top_ref.shape[-1], LANES):
            lanes = slice(lane, lane + LANES)

            def table(st, gain, bias):
                average, inverse = frame_tables(st[:, lanes], domain_ref[f], counts)
                scale = inverse * gain[:, lanes]
                return scale, bias[:, lanes] - average * scale

            t_scale, t_shift = table(top_st, gain_t, bias_t)
            wide = [table(*mask[1:]) for mask in masks]

            def one(i, _):
                at = [pl.multiple_of(f * pixels + (2 * i + h) * cols, cols) for h in (0, 1)]
                top = top_rows(top_ref, at, cols, lanes, t_scale, t_shift)
                weight = softmax_window(top, cols)
                held = [w * t for w, t in zip(weight, top)]
                for k in range(TASKS):
                    scale, shift = wide[k]
                    total = None
                    for h in (0, 1):
                        term = sigmoid(masks[k][0][pl.ds(at[h], cols), lanes] * scale + shift) * held[h]
                        total = term if total is None else total + term
                    scr_ref[k] = total
                    even = scr_ref[k, pl.ds(0, cols // 2, stride=2), :]
                    odd = scr_ref[k, pl.ds(1, cols // 2, stride=2), :]
                    task_ref[f, i, k, :, lanes] = even + odd
                return 0

            lax.fori_loop(0, rows // 2, one, 0, unroll=2)


def task_layer(geom, domain, top, top_st, gain_t, bias_t, masks):
    frames, rows, cols, _ = geom
    pix, chans = top.shape
    task_shape = (frames, rows // 2, TASKS, cols // 2, chans)
    args = (domain, top, top_st, gain_t, bias_t, *(x for mask in masks for x in mask))
    return pl.pallas_call(
        functools.partial(task_kernel, geom),
        in_specs=[SCALARS] + [whole(x.shape) for x in args[1:]],
        out_specs=whole(task_shape),
        out_shape=sds(task_shape, F32),
        scratch_shapes=[pltpu.VMEM((TASKS, cols, LANES), F32)],
        compiler_params=params(),
        cost_estimate=cost(pix * chans * 60, pix * chans * 28),
    )(*args)


def pool_early_kernel(geom, first, domain_ref, top_ref, top_st, gain_t, bias_t, wide_ref, wide_st, gain_w, bias_w, cot_ref, *refs):
    frames, rows, cols, counts = geom
    pixels = rows * cols
    mix_ref, gw_ref, sums_ref, scr_ref = refs[-4:]
    for lane in range(0, top_ref.shape[-1], LANES):
        lanes = slice(lane, lane + LANES)
        sums = []
        for f in range(frames):
            average, inverse = frame_tables(top_st[:, lanes], domain_ref[f], counts)
            t_scale = inverse * gain_t[:, lanes]
            t_shift = bias_t[:, lanes] - average * t_scale
            w_mean, w_inv = frame_tables(wide_st[:, lanes], domain_ref[f], counts)

            def one(i, carry):
                at = [pl.multiple_of(f * pixels + (2 * i + h) * cols, cols) for h in (0, 1)]
                top = top_rows(top_ref, at, cols, lanes, t_scale, t_shift)
                weight = softmax_window(top, cols)
                cot = spread_cols(scr_ref, cot_ref[f, i, :, lanes].astype(F32))
                one_sum, two_sum = carry
                for h in (0, 1):
                    xhat = (wide_ref[pl.ds(at[h], cols), lanes] - w_mean) * w_inv
                    mask = sigmoid(xhat * gain_w[:, lanes] + bias_w[:, lanes])
                    part = cot * mask
                    mix = part if first else refs[0][pl.ds(at[h], cols), lanes] + part
                    mix_ref[pl.ds(at[h], cols), lanes] = mix
                    g = part * (weight[h] * top[h]) * (1.0 - mask)
                    gw_ref[pl.ds(at[h], cols), lanes] = g
                    one_sum = one_sum + fold(g)
                    two_sum = two_sum + fold(g * xhat)
                return one_sum, two_sum

            zero = jnp.zeros((8, LANES), F32)
            sums.append(lax.fori_loop(0, rows // 2, one, (zero, zero), unroll=2))
        sums_ref[:, lanes] = by_domain(
            [jnp.sum(s[0], 0, keepdims=True) for s in sums], [jnp.sum(s[1], 0, keepdims=True) for s in sums], domain_ref
        )


def pool_early(geom, domain, _, top_st, gain_t, bias_t, wide, wide_st, gain_w, bias_w, cot, top, mix=None):
    cols = geom[2]
    pix, chans = top.shape
    args = (domain, top, top_st, gain_t, bias_t, wide, wide_st, gain_w, bias_w, cot) + (() if mix is None else (mix,))
    outs = [sds((pix, chans), F32)] * 2 + [sds((4, chans), F32)]
    return pl.pallas_call(
        functools.partial(pool_early_kernel, geom, mix is None),
        in_specs=[SCALARS] + [whole(x.shape) for x in args[1:]],
        out_specs=[whole(o.shape) for o in outs],
        out_shape=outs,
        scratch_shapes=[pltpu.VMEM((cols, LANES), F32)],
        compiler_params=params(),
        cost_estimate=cost(pix * chans * 40, pix * chans * 20),
    )(*args)


def head_kernel(geom, domain_ref, bot_ref, bot_st, gate_ref, gate_st, gain_b, bias_b, gain_g, bias_g, cot_ref,
                maps_ref, gb_ref, gg_ref, sums_ref):
    frames, rows, cols, counts = geom
    pixels = rows * cols
    chans = bot_ref.shape[-1]
    for lane in range(0, chans, LANES):
        lanes = slice(lane, lane + LANES)
        grads, hats = ([[] for _ in range(TASKS + 1)] for _ in range(2))
        for f in range(frames):
            at = slice(f * pixels, (f + 1) * pixels)
            mean, inv = frame_tables(bot_st[:, lanes], domain_ref[f], counts)
            b_hat = (bot_ref[at, lanes] - mean) * inv
            act = b_hat * gain_b[:, lanes] + bias_b[:, lanes]
            s = sigmoid(act)
            bottom = act * s
            back = None
            for k in range(TASKS):
                sl = slice(k * chans + lane, k * chans + lane + LANES)
                mean, inv = frame_tables(gate_st[:, sl], domain_ref[f], counts)
                xhat = (gate_ref[at, sl] - mean) * inv
                value = sigmoid(xhat * gain_g[:, sl] + bias_g[:, sl])
                maps_ref[k, at, lanes] = value * bottom
                part = cot_ref[k, at, lanes].astype(F32) * value
                back = part if back is None else back + part
                g = part * bottom * (1.0 - value)
                gg_ref[at, sl] = g
                grads[k].append(g)
                hats[k].append(xhat)
            g = back * (s * (1.0 + act * (1.0 - s)))
            gb_ref[at, lanes] = g
            grads[-1].append(g)
            hats[-1].append(b_hat)
        for k in range(TASKS + 1):
            to = chans + k * chans + lane if k < TASKS else lane
            sums_ref[:, to : to + LANES] = value_sums(grads[k], domain_ref, hats[k])


def head_layer(geom, domain, bot, bot_st, gate, gate_st, gain_b, bias_b, gain_g, bias_g, cot):
    pix, chans = bot.shape
    args = (domain, bot, bot_st, gate, gate_st, gain_b, bias_b, gain_g, bias_g, cot)
    outs = [sds((TASKS, pix, chans), F32), sds((pix, chans), F32), sds((pix, TASKS * chans), F32),
            sds((4, (TASKS + 1) * chans), F32)]
    return pl.pallas_call(
        functools.partial(head_kernel, geom),
        in_specs=[SCALARS] + [whole(x.shape) for x in args[1:]],
        out_specs=[whole(o.shape) for o in outs],
        out_shape=outs,
        compiler_params=params(),
        cost_estimate=cost(pix * chans * 80, pix * chans * 44),
    )(*args)


def norm_back_rows(g, pre, tables):
    mean, inv, scale, g_mean, g_cross = tables
    xhat = (pre - mean) * inv
    return scale * (g - g_mean - xhat * g_cross)


def back_tables(stats_ref, sums_ref, gain_ref, domain_at, counts):
    mean, inv = frame_tables(stats_ref[...], domain_at, counts)
    g_mean, g_cross = grad_tables(sums_ref[...], domain_at, counts)
    return mean, inv, inv * gain_ref[...], g_mean, g_cross


def backward_kernel(geom, added, epilogue, *refs):
    frames, rows, cols, counts = geom
    pixels = rows * cols
    refs = list(refs)
    domain_ref = refs.pop(0)
    g_ref, pre_ref, st_ref, sm_ref, gain_ref = (refs.pop(0) for _ in range(5))
    kernel_ref = refs.pop(0)
    add_ref = refs.pop(0) if added else None
    lpre_ref, lst_ref, lgain_ref, lbias_ref = (refs.pop(0) for _ in range(4))
    if epilogue == "pool":
        mix_ref = refs.pop(0)
    win_ref, out_ref, sums_ref, held_ref, sem = refs
    chans = kernel_ref.shape[0] // 9

    load = pltpu.make_async_copy(kernel_ref, held_ref, sem)
    load.start()
    clear_edges(win_ref, rows)
    for f in range(frames):
        tables = back_tables(st_ref, sm_ref, gain_ref, domain_ref[f], counts)

        def one_row(r, _):
            at = pl.multiple_of(f * pixels + r * cols, cols)
            low = norm_back_rows(g_ref[pl.ds(at, cols), :], pre_ref[pl.ds(at, cols), :], tables)
            put_windows(win_ref, f, r, low, cols)
            return 0

        lax.fori_loop(0, rows, one_row, 0, unroll=2)
    load.wait()
    source = jnp.concatenate([window(win_ref, 2 - b, 2 - a, rows) for a in range(3) for b in range(3)], 1)
    weight = jnp.concatenate([held_ref[k * chans : (k + 1) * chans, :] for k in range(9)], 1)
    out = lax.dot_general(source, weight, (((1,), (1,)), ((), ())), preferred_element_type=F32)
    if added:
        out = out + add_ref[...]
    if epilogue == "silu":
        first, second = [], []
        for f in range(frames):
            at = slice(f * pixels, (f + 1) * pixels)
            mean, inv = frame_tables(lst_ref[...], domain_ref[f], counts)
            xhat = (lpre_ref[at] - mean) * inv
            act = xhat * lgain_ref[...] + lbias_ref[...]
            s = sigmoid(act)
            g = out[at] * (s * (1.0 + act * (1.0 - s)))
            out_ref[at] = g
            first.append(jnp.sum(fold(g), 0, keepdims=True))
            second.append(jnp.sum(fold(g * xhat), 0, keepdims=True))
        sums_ref[...] = by_domain(first, second, domain_ref)
        return
    for lane in range(0, chans, LANES):
        lanes = slice(lane, lane + LANES)
        first, second = [], []
        for f in range(frames):
            at = slice(f * pixels, (f + 1) * pixels)
            mean, inv = frame_tables(lst_ref[:, lanes], domain_ref[f], counts)
            xhat = (lpre_ref[at, lanes] - mean) * inv
            act = xhat * lgain_ref[:, lanes] + lbias_ref[:, lanes]
            s = sigmoid(act)
            steep = s * (1.0 + act * (1.0 - s))
            top, up, mix = (row_pairs(x, cols) for x in (act * s, out[at, lanes], mix_ref[at, lanes]))
            weight = window_weights(top)
            pooled = pair_sums(weight[0] * top[0] + weight[1] * top[1])
            d_pool = pair_sums(weight[0] * up[0] + weight[1] * up[1])
            flow = [m + d_pool for m in mix]
            d_w = [u * pooled + fl * t for u, fl, t in zip(up, flow, top)]
            centre = pair_sums(weight[0] * d_w[0] + weight[1] * d_w[1])
            d_top = jnp.stack([w * (fl + d - centre) for w, fl, d in zip(weight, flow, d_w)], 1)
            g = d_top.reshape(pixels, LANES) * steep
            out_ref[at, lanes] = g
            first.append(jnp.sum(fold(g), 0, keepdims=True))
            second.append(jnp.sum(fold(g * xhat), 0, keepdims=True))
        sums_ref[:, lanes] = by_domain(first, second, domain_ref)


def backward_layer(geom, domain, top, kernel, lower, added=None, mix=None):
    frames, rows, cols, _ = geom
    pix, width = top[0].shape
    chans = kernel.shape[0] // 9
    args = [domain, *top, kernel]
    specs = [SCALARS] + [whole(x.shape) for x in top] + [ANYWHERE]
    win = (3, frames, rows + 2, cols, width)
    outs = [sds(win, BF16), sds((pix, chans), F32)]
    extra = ([] if added is None else [added]) + list(lower) + ([] if mix is None else [mix])
    epilogue = "silu" if mix is None else "pool"
    outs.append(sds((4, chans), F32))
    return pl.pallas_call(
        functools.partial(backward_kernel, geom, added is not None, epilogue),
        grid=(1,),
        in_specs=specs + [whole(x.shape) for x in extra],
        out_specs=[whole(o.shape) for o in outs],
        out_shape=outs,
        scratch_shapes=[pltpu.VMEM(kernel.shape, BF16), pltpu.SemaphoreType.DMA],
        compiler_params=params(1),
        cost_estimate=cost(2 * pix * kernel.size, kernel.size * 2 + pix * 10240),
    )(*args, *extra)


def low_kernel(geom, domain_ref, g_ref, pre_ref, st_ref, sm_ref, gain_ref, win_ref):
    frames, rows, cols, counts = geom
    pixels = rows * cols
    clear_edges(win_ref, rows)
    for f in range(frames):
        tables = back_tables(st_ref, sm_ref, gain_ref, domain_ref[f], counts)

        def one_row(r, _):
            at = pl.multiple_of(f * pixels + r * cols, cols)
            low = norm_back_rows(g_ref[pl.ds(at, cols), :], pre_ref[pl.ds(at, cols), :], tables)
            put_windows(win_ref, f, r, low, cols)
            return 0

        lax.fori_loop(0, rows, one_row, 0, unroll=2)


def low_layer(geom, domain, top):
    frames, rows, cols, _ = geom
    pix, width = top[0].shape
    out = sds((3, frames, rows + 2, cols, width), BF16)
    return pl.pallas_call(
        functools.partial(low_kernel, geom),
        grid=(1,),
        in_specs=[SCALARS] + [whole(x.shape) for x in top],
        out_specs=whole(out.shape),
        out_shape=out,
        compiler_params=params(1),
        cost_estimate=cost(pix * width * 20, pix * width * 14),
    )(domain, *top)


def input_kernel(geom, win_ref, kernel_ref, out_ref):
    rows = geom[1]
    step = pl.program_id(0)
    chans = kernel_ref.shape[0] // 3
    source = jnp.concatenate([window(win_ref, 2 - b, 2 - step, rows) for b in range(3)], 1)
    weight = jnp.concatenate([kernel_ref[b * chans : (b + 1) * chans, :] for b in range(3)], 1)
    part = lax.dot_general(source, weight, (((1,), (1,)), ((), ())), preferred_element_type=F32)

    @pl.when(step == 0)
    def _():
        out_ref[...] = part

    @pl.when(step > 0)
    def _():
        out_ref[...] += part


def input_layer(geom, win, kernel):
    frames, rows, cols, _ = geom
    pix = frames * rows * cols
    chans, width = kernel.shape[0] // 9, kernel.shape[1]
    return pl.pallas_call(
        functools.partial(input_kernel, geom),
        grid=(3,),
        in_specs=[whole(win.shape), pl.BlockSpec((3 * chans, width), lambda a: (a, 0))],
        out_specs=whole((pix, chans)),
        out_shape=sds((pix, chans), F32),
        compiler_params=params(1),
        cost_estimate=cost(2 * pix * kernel.size, kernel.size * 2 + pix * 4096),
    )(win, in_hbm(kernel))


class Member:
    def __init__(self, at, shape, dp, fsdp, split=False):
        self.at, self.shape, self.split = at, shape, split
        self.vr = shape[0] // dp // (2 if split else 1)
        self.blocks = shape[1] // fsdp * (2 if split else 1) // LANES
        self.rows = self.vr * self.blocks

    def spots(self, i, j):
        if self.split:
            row, col = i * 2 * self.vr + (j & 1) * self.vr, (j >> 1) * self.blocks * LANES
        else:
            row, col = i * self.vr, j * self.blocks * LANES
        for k in range(self.blocks):
            yield self.at + k * self.vr, row, col + k * LANES


def collect_kernel(member, parts, me_ref, *refs):
    out_ref, sem = refs[-2:]
    fetch(member, parts, me_ref, refs[:-2], out_ref, sem)
    arrived(out_ref, sem)


def collect(pieces):
    return pl.pallas_call(
        functools.partial(collect_kernel, pieces.member, pieces.parts),
        in_specs=[SCALARS] + [ANYWHERE] * len(pieces.sources),
        out_specs=whole(pieces.shape),
        out_shape=sds(pieces.shape, BF16),
        scratch_shapes=[pltpu.SemaphoreType.DMA],
        grid=(1,),
        compiler_params=params(1),
        cost_estimate=cost(0, 4 * pieces.shape[0] * pieces.shape[1]),
    )(pieces.me, *pieces.sources)


def affine_kernel(member, parts, me_ref, *refs):
    out_ref, rows_ref, sem = refs[-3:]
    fetch(member, parts, me_ref, refs[:-3], rows_ref, sem)
    arrived(rows_ref, sem)
    width = out_ref.shape[1] // 32
    for d in range(32):
        rows = rows_ref[16 * d : 16 * d + 16].astype(F32)
        both = jnp.concatenate([rows[:8], rows[8:]], 1)
        out_ref[:, d * width : (d + 1) * width] = (both[0:2] + both[2:4] + both[4:6])[:, :width]


def collect_affine(pieces):
    return pl.pallas_call(
        functools.partial(affine_kernel, pieces.member, pieces.parts),
        in_specs=[SCALARS] + [ANYWHERE] * len(pieces.sources),
        out_specs=whole((2, 5120)),
        out_shape=sds((2, 5120), F32),
        scratch_shapes=[pltpu.VMEM((512, LANES), BF16), pltpu.SemaphoreType.DMA],
        grid=(1,),
        compiler_params=params(1),
        cost_estimate=cost(10000000, 1000000),
    )(pieces.me, *pieces.sources)


def weight_parts(geom, step, act_ref, low_ref, tr_ref):
    rows = geom[1]

    @pl.when(step == 0)
    def _():
        tr_ref[...] = act_ref[...].astype(F32).T.astype(BF16)

    if len(low_ref.shape) == 5:
        for b in range(3):
            yield jnp.dot(tr_ref[...], window(low_ref, 2 - b, 2 - step, rows), preferred_element_type=F32)
    else:
        yield jnp.dot(tr_ref[...], low_ref[...], preferred_element_type=F32)


def weight_kernel(geom, act_ref, low_ref, out_ref, tr_ref):
    chans = tr_ref.shape[0]
    for b, part in enumerate(weight_parts(geom, pl.program_id(0), act_ref, low_ref, tr_ref)):
        out_ref[b * chans : (b + 1) * chans, :] = part.astype(BF16)


def weight_layer(geom, act, low):
    pix, chans = act.shape
    win = low.ndim == 5
    width = low.shape[-1]
    steps = 3 if win else 1
    out = sds((9 * chans if win else chans, width), BF16)
    return pl.pallas_call(
        functools.partial(weight_kernel, geom),
        grid=(steps,),
        in_specs=[whole(act.shape), whole(low.shape)],
        out_specs=pl.BlockSpec((out.shape[0] // steps, width), lambda a: (a, 0)),
        out_shape=out,
        scratch_shapes=[pltpu.VMEM((chans, pix), BF16)],
        compiler_params=params(1),
        cost_estimate=cost(2 * pix * out.size, out.size * 2 + pix * 4096),
    )(act, low)


def weight_blocks_kernel(geom, member, steps, held, *refs):
    refs = list(refs)
    me_ref, act_ref, low_ref = (refs.pop(0) for _ in range(3))
    if held:
        del refs[:3]
    near_ref, far_ref, send_ref, scr_ref, tr_ref, sem = refs
    step = pl.program_id(0)
    chans = tr_ref.shape[0]
    for b, part in enumerate(weight_parts(geom, step, act_ref, low_ref, tr_ref)):
        scr_ref[pl.ds(pl.multiple_of(step * 3 * chans, chans) + b * chans, chans), :] = part.astype(BF16)
    me = me_ref[0]
    share = member.shape[0] // 8
    done = 0
    for s in range(steps):
        ready = member.shape[0] * (s + 1) // steps // share

        @pl.when(step == s)
        def _(done=done, ready=ready):
            for i in range(done, ready):
                e = i ^ (me >> 2)
                q = ((e & 1) << 2) | (e & 2) | (e >> 2)
                for jd in range(4):
                    dst = send_ref.at[jd >> 1, q] if jd & 1 else (near_ref, far_ref)[jd >> 1].at[q]
                    for at, row, col in member.spots(i, (me & 3) ^ jd):
                        pltpu.make_async_copy(
                            scr_ref.at[span(row, member.vr), span(col, LANES)], dst.at[pl.ds(at, member.vr)], sem
                        ).start()

        done = ready

    @pl.when(step == steps - 1)
    def _():
        pltpu.make_async_copy(scr_ref, scr_ref, sem).wait()


def weight_blocks(geom, me, act, low, member, rows, held=None):
    pix, chans = act.shape
    win = low.ndim == 5
    steps = 3 if win else 1
    shard = (rows, LANES)
    outs = [sds((8, *shard), BF16)] * 2 + [sds((2, 8, *shard), BF16)]
    args = [me, act, low] + list(held or ())
    size = member.shape[0] * member.shape[1]
    return pl.pallas_call(
        functools.partial(weight_blocks_kernel, geom, member, steps, held is not None),
        grid=(steps,),
        in_specs=[SCALARS, whole(act.shape), whole(low.shape)] + [ANYWHERE] * len(held or ()),
        out_specs=[ANYWHERE] * 3,
        out_shape=outs,
        scratch_shapes=[pltpu.VMEM(member.shape, BF16), pltpu.VMEM((chans, pix), BF16), pltpu.SemaphoreType.DMA],
        input_output_aliases={} if held is None else {3: 0, 4: 1, 5: 2},
        compiler_params=params(1),
        cost_estimate=cost(2 * pix * size, size * 2 + pix * 4096),
    )(*args)


def weight_piece_kernel(geom, member, step, held, *refs):
    rows = geom[1]
    refs = list(refs)
    me_ref, act_ref, low_ref = (refs.pop(0) for _ in range(3))
    if held:
        del refs[:3]
    near_ref, far_ref, send_ref = (refs.pop(0) for _ in range(3))
    if step == 0:
        tr_ref = refs.pop(0)
        tr_ref[...] = act_ref[...].astype(F32).T.astype(BF16)
    else:
        tr_ref = act_ref
    scr_ref, sem = refs
    chans = tr_ref.shape[0]
    for b in range(3):
        part = jnp.dot(tr_ref[...], window(low_ref, 2 - b, 2 - step, rows), preferred_element_type=F32)
        scr_ref[b * chans : (b + 1) * chans, :] = part.astype(BF16)
    me = me_ref[0]
    start, stop = 3 * chans * step, 3 * chans * (step + 1)
    for i in range(8):
        first, last = max(start, i * member.vr), min(stop, (i + 1) * member.vr)
        if first >= last:
            continue
        e = i ^ (me >> 2)
        q = ((e & 1) << 2) | (e & 2) | (e >> 2)
        for jd in range(4):
            dst = send_ref.at[jd >> 1, q] if jd & 1 else (near_ref, far_ref)[jd >> 1].at[q]
            col = ((me & 3) ^ jd) * LANES
            pltpu.make_async_copy(
                scr_ref.at[pl.ds(first - start, last - first), span(col, LANES)],
                dst.at[pl.ds(member.at + first - i * member.vr, last - first)],
                sem,
            ).start()
    arrived(scr_ref, sem)


def weight_piece(geom, me, act, low, member, rows, step, held=None):
    chans = member.shape[0] // 9
    pix, width = low.shape[1] * geom[1] * geom[2], low.shape[-1]
    shard = (rows, LANES)
    outs = [sds((8, *shard), BF16)] * 2 + [sds((2, 8, *shard), BF16)]
    out_specs = [ANYWHERE] * 3
    if step == 0:
        outs.append(sds((chans, pix), BF16))
        out_specs.append(whole((chans, pix)))
    args = [me, act, low] + list(held or ())
    return pl.pallas_call(
        functools.partial(weight_piece_kernel, geom, member, step, held is not None),
        grid=(1,),
        in_specs=[SCALARS, whole(act.shape), whole(low.shape)] + [ANYWHERE] * len(held or ()),
        out_specs=out_specs,
        out_shape=outs,
        scratch_shapes=[pltpu.VMEM((3 * chans, width), BF16), pltpu.SemaphoreType.DMA],
        input_output_aliases={} if held is None else {3: 0, 4: 1, 5: 2},
        compiler_params=params(1),
        cost_estimate=cost(2 * pix * 3 * chans * width, chans * width * 6),
    )(*args)


def point_kernel(geom, pieces, *refs):
    frames, rows, cols, _ = geom
    pixels = rows * cols
    refs = list(refs)
    domain_ref, act_ref = refs.pop(0), refs.pop(0)
    if pieces:
        out_ref, sums_ref, matrix_ref, sem = refs[-4:]
        fetch(*pieces, refs[0], refs[1:-4], matrix_ref, sem)
        arrived(matrix_ref, sem)
    else:
        matrix_ref, out_ref, sums_ref = refs
    for lane in range(0, out_ref.shape[-1], 256):
        lanes = slice(lane, lane + 256)
        out = jnp.dot(act_ref[...], matrix_ref[:, lanes], preferred_element_type=F32)
        out_ref[:, lanes] = out
        sums_ref[:, lanes] = value_sums([out[f * pixels : (f + 1) * pixels] for f in range(frames)], domain_ref)


def point_layer(geom, domain, act, mat):
    pix, chans = act.shape
    width = mat.shape[1]
    pieces = isinstance(mat, Pieces)
    outs = [sds((pix, width), F32), sds((4, width), F32)] + [sds(mat.shape, BF16)] * pieces
    args = [domain, act] + ([mat.me, *mat.sources] if pieces else [mat])
    specs = [SCALARS, whole(act.shape)]
    specs += [SCALARS] + [ANYWHERE] * len(mat.sources) if pieces else [whole(mat.shape)]
    return pl.pallas_call(
        functools.partial(point_kernel, geom, (mat.member, mat.parts) if pieces else None),
        in_specs=specs,
        out_specs=[whole(o.shape) for o in outs],
        out_shape=outs,
        scratch_shapes=[pltpu.SemaphoreType.DMA] * pieces,
        grid=(1,),
        compiler_params=params(1),
        cost_estimate=cost(2 * pix * chans * width, chans * width * 2 + pix * width * 4),
    )(*args)


def point_back_kernel(geom, added, domain_ref, g_ref, pre_ref, st_ref, sm_ref, gain_ref, mat_ref, *refs):
    frames, rows, cols, counts = geom
    pixels = rows * cols
    low_ref, out_ref = refs[-2:]
    for f in range(frames):
        tables = back_tables(st_ref, sm_ref, gain_ref, domain_ref[f], counts)

        def one_row(r, _):
            at = pl.multiple_of(f * pixels + r * cols, cols)
            low = norm_back_rows(g_ref[pl.ds(at, cols), :], pre_ref[pl.ds(at, cols), :], tables)
            low_ref[pl.ds(at, cols), :] = low.astype(BF16)
            return 0

        lax.fori_loop(0, rows, one_row, 0, unroll=2)
    part = lax.dot_general(low_ref[...], mat_ref[...], (((1,), (1,)), ((), ())), preferred_element_type=F32)
    out_ref[...] = part + refs[0][...] if added else part


def point_back(geom, domain, g, pre, stats, sums, gain, mat, added=None):
    pix, width = g.shape
    chans = mat.shape[0]
    args = (domain, g, pre, stats, sums, gain, mat) + (() if added is None else (added,))
    outs = [sds((pix, width), BF16), sds((pix, chans), F32)]
    return pl.pallas_call(
        functools.partial(point_back_kernel, geom, added is not None),
        grid=(1,),
        in_specs=[SCALARS] + [whole(x.shape) for x in args[1:]],
        out_specs=[whole(o.shape) for o in outs],
        out_shape=outs,
        compiler_params=params(1),
        cost_estimate=cost(2 * pix * mat.size, mat.size * 2 + pix * width * 10),
    )(*args)


def share_kernel(widths, me_ref, *refs):
    *sums, gain_ref, bias_ref, flat_ref = refs
    at = 0
    for ref, width in zip(sums, widths):
        flat_ref[0:1, at : at + width] = ref[2:3, :] + ref[3:4, :]
        flat_ref[1:2, at : at + width] = ref[0:1, :] + ref[1:2, :]
        at += width
    share = gain_ref.shape[1]
    mine = pltpu.roll(flat_ref[...], at - me_ref[0] * share, 1)
    gain_ref[...] = mine[0:1, :share]
    bias_ref[...] = mine[1:2, :share]


def share_of(me, sums, share):
    widths = [x.shape[1] for x in sums]
    got = pl.pallas_call(
        functools.partial(share_kernel, widths),
        grid=(1,),
        in_specs=[SCALARS] + [whole(x.shape) for x in sums],
        out_specs=[whole((1, share))] * 2,
        out_shape=[sds((1, share), F32)] * 2,
        scratch_shapes=[pltpu.VMEM((8, sum(widths)), F32)],
        compiler_params=params(1),
        cost_estimate=cost(0, 100000),
    )(me, *(in_hbm(x) for x in sums))
    return [x[0] for x in got]


AXES = ("dp", "fsdp")
CORE, X, Y, Z_NEAR, Z_FAR = range(5)
ORDER = (CORE, Z_NEAR, Z_FAR, X, Y)


def swap(x, bit):
    n = lax.axis_size(AXES)
    return lax.ppermute(x, AXES, [(i, i ^ (1 << bit)) for i in range(n)])


def bit_of(bit):
    return (lax.axis_index(AXES) >> bit) & 1


def all_bits():
    return range(lax.axis_size(AXES).bit_length() - 1)


def tied(value, to):
    return value if to is None else lax.optimization_barrier((value, to))[0]


class Links:
    def __init__(self):
        self.under_way = {}

    def busy(self, bit, *values):
        self.under_way.setdefault(bit, []).extend(values)

    def total(self, x, after=None, order=None, fill=()):
        bits = order if order and len(all_bits()) == 5 else all_bits()
        fill = list(fill)
        for bit in bits:
            for value in self.under_way.pop(bit, ()):
                x = tied(x, value)
            got = swap(x, bit)
            if fill and (bit != CORE or len(bits) != 5):
                got = tied(got, fill.pop(0)(x))
            x = x + got
            for start in (after or {}).get(bit, ()):
                x = tied(x, start(x))
        for work in fill:
            work(x)
        return x


def half_rows(rows):
    return rows // 32 * 16


class Gather:
    def __init__(self, links, shard):
        self.links, self.shard, self.cut = links, shard, half_rows(shard.shape[0])
        self.sources = None

    def far(self, to=None):
        self.z = tied(self.shard, to)
        self.got = swap(self.z, Z_FAR)

    def near(self, to=None):
        self.z = jnp.stack(tied((self.z, self.got), to))
        self.got = swap(self.z, Z_NEAR)

    def first(self, to=None):
        z = jnp.concatenate(tied((self.z, self.got), to))
        self.a, self.b = z[:, : self.cut], z[:, self.cut :]
        self.got = swap(self.a, Y), swap(self.b, X)

    def second(self, to=None):
        a, b, (got_a, got_b) = tied((self.a, self.b, self.got), to)
        self.a, self.b = jnp.concatenate([a, got_a]), jnp.concatenate([b, got_b])
        self.got = swap(self.a, X), swap(self.b, Y)

    def busy(self):
        if isinstance(self.got, tuple):
            self.links.busy(X, self.got[0])
            self.links.busy(Y, self.got[1])
        else:
            self.links.busy(CORE, self.got)

    def finish(self, to=None):
        rows = self.shard.shape[0]
        self.a, self.b, self.got = tied((self.a, self.b, self.got), to)
        self.sources, self.parts = [], []
        for core in (0, 1):
            for n, value in enumerate((self.a, self.got[0], self.b, self.got[1])):
                z = [8 * (k >> 1) + 16 * (k & 1) for k in range(4)]
                if n < 2:
                    masks = [core + 2 * n + 4 * y + m for y in (0, 1) for m in z]
                else:
                    masks = [core + 4 * (n - 2) + 2 * x + m for x in (0, 1) for m in z]
                self.parts.append((0, self.cut, masks) if n < 2 else (self.cut, rows - self.cut, masks))
                self.sources.append(swap(value, CORE) if core else value)

    def pieces(self, member):
        return Pieces(member, self.parts, number(1), self.sources)


def number(entries):
    return jnp.full((entries,), lax.axis_index(AXES), jnp.int32)


def plus(a, b):
    return (a.astype(F32) + b.astype(F32)).astype(BF16)


def add_kernel(jobs, *refs):
    refs = list(refs)
    count = sum(n for _, n, _ in jobs)
    ins, outs = refs[:count], refs[count:]
    for work, n_in, n_out in jobs:
        work(*ins[:n_in], *outs[:n_out])
        del ins[:n_in], outs[:n_out]


def add_all(*jobs):
    ins = [x for _, job, _ in jobs for x in job]
    outs = [x for _, _, job in jobs for x in job]
    got = pl.pallas_call(
        functools.partial(add_kernel, [(work, len(i), len(o)) for work, i, o in jobs]),
        grid=(1,),
        in_specs=[whole(x.shape) for x in ins],
        out_specs=[whole(x.shape) for x in outs],
        out_shape=outs,
        compiler_params=params(1),
        cost_estimate=cost(0, sum(x.size * 2 for x in ins + outs)),
    )(*ins)
    result = []
    for _, _, job in jobs:
        result.append(got[: len(job)])
        got = got[len(job) :]
    return result


def first_work(cut, near, far, got, a, send_a, b, send_b):
    a[...] = plus(near[:, :cut], got[0, :, :cut])
    send_a[...] = plus(far[:, :cut], got[1, :, :cut])
    for half, out in enumerate((b, send_b)):
        s = slice(4 * half, 4 * half + 4)
        out[0] = plus(near[s, cut:], got[0, s, cut:])
        out[1] = plus(far[s, cut:], got[1, s, cut:])


def second_work(a, b, got_a, got_b, a_out, send_a, b_out, send_b):
    a_out[...] = plus(a[:4], got_a[:4])
    send_a[...] = plus(a[4:], got_a[4:])
    b_out[...] = plus(b[0], got_b[0])
    send_b[...] = plus(b[1], got_b[1])


def near_work(cut, a, b, got_a, got_b, z, send):
    for half, out in enumerate((z, send)):
        s = slice(2 * half, 2 * half + 2)
        out[:, :cut] = plus(a[s], got_a[s])
        out[:, cut:] = plus(b[s], got_b[s])


def far_work(z, got, z_out, send):
    z_out[...] = plus(z[0], got[0])
    send[...] = plus(z[1], got[1])


def finish_work(z, got, out):
    out[...] = z[...].astype(F32) + got[...].astype(F32)


class Scatter:
    def __init__(self, links, blocks):
        self.links, self.blocks = links, blocks
        self.rows = blocks[0].shape[1]
        self.cut = half_rows(self.rows)
        self.got = swap(blocks[2], CORE)

    def shape(self, *dims):
        return sds((*dims, LANES), BF16)

    def first_job(self):
        c, r = self.cut, self.rows - self.cut
        outs = [self.shape(8, c)] * 2 + [self.shape(2, 4, r)] * 2
        return functools.partial(first_work, c), [*self.blocks[:2], self.got], outs

    def first(self, a, send_a, b, send_b):
        self.a, self.b = a, b
        self.got = swap(send_a, X), swap(send_b, Y)

    def second_job(self):
        c, r = self.cut, self.rows - self.cut
        return second_work, [self.a, self.b, *self.got], [self.shape(4, c)] * 2 + [self.shape(4, r)] * 2

    def second(self, a, send_a, b, send_b):
        self.a, self.b = a, b
        self.got = swap(send_a, Y), swap(send_b, X)

    def near_job(self):
        return functools.partial(near_work, self.cut), [self.a, self.b, *self.got], [self.shape(2, self.rows)] * 2

    def near(self, to=None):
        self.got = swap(tied(self.send, to), Z_NEAR)

    def far_job(self):
        return far_work, [self.z, self.got], [self.shape(self.rows)] * 2

    def far(self, z, send):
        self.z = z
        self.got = swap(send, Z_FAR)

    def finish_job(self):
        return finish_work, [self.z, self.got], [sds((self.rows, LANES), F32)]


def add_after(to, *jobs):
    return add_all(*((work, tied(ins, to), outs) for work, ins, outs in jobs))


def rows_of_chip(shard):
    half = shard.shape[0] // 2
    odd = bit_of(CORE) == 1
    mine = jnp.where(odd, shard[half:], shard[:half])
    got = swap(jnp.where(odd, shard[:half], shard[half:]), CORE)
    return jnp.concatenate([jnp.where(odd, got, mine), jnp.where(odd, mine, got)], 1)


def columns_of_core(rows):
    half = rows.shape[1] // 2
    odd = bit_of(CORE) == 1
    mine = jnp.where(odd, rows[:, half:], rows[:, :half])
    got = swap(jnp.where(odd, rows[:, :half], rows[:, half:]), CORE)
    return jnp.concatenate([jnp.where(odd, got, mine), jnp.where(odd, mine, got)], 0)


def pack(x):
    return jnp.concatenate([x[:, k : k + LANES] for k in range(0, x.shape[1], LANES)], 0)


def unpack(x, blocks):
    rows = x.shape[0] // blocks
    return jnp.concatenate([x[k * rows : (k + 1) * rows] for k in range(blocks)], 1)


def in_three(x):
    high = lax.reduce_precision(x, 8, 7)
    middle = lax.reduce_precision(x - high, 8, 7)
    return jnp.stack([high, middle, x - high - middle]).astype(BF16)


def gather(x):
    x = x[None]
    for bit in all_bits():
        other = swap(x, bit)
        high = bit_of(bit) == 1
        x = jnp.concatenate([jnp.where(high, other, x), jnp.where(high, x, other)], 0)
    return x


def scatter(x):
    for bit in reversed(all_bits()):
        half = x.shape[0] // 2
        high = bit_of(bit) == 1
        send = jnp.where(high, x[:half], x[half:])
        keep = jnp.where(high, x[half:], x[:half])
        x = plus(keep, swap(send, bit))
    return x[0]


def gather_matrix(shard):
    dp, fsdp = lax.axis_size("dp"), lax.axis_size("fsdp")
    rows, cols = shard.shape
    full = gather(shard).reshape(dp, fsdp, rows, cols)
    return full.transpose(0, 2, 1, 3).reshape(dp * rows, fsdp * cols)


def scatter_matrix(full):
    dp, fsdp = lax.axis_size("dp"), lax.axis_size("fsdp")
    rows, cols = full.shape[0] // dp, full.shape[1] // fsdp
    parts = full.reshape(dp, rows, fsdp, cols).transpose(0, 2, 1, 3)
    return scatter(parts.reshape(dp * fsdp, rows, cols)).astype(F32)


class AnyMesh:
    def __init__(self, links, geom, weights, gains, biases):
        self.geom = geom
        self.mats = {name: gather_matrix(w) for name, w in weights.items()}
        self.affine = gather(jnp.stack([gains, biases])).transpose(1, 0, 2).reshape(2, 1, -1)
        self.grads, self.ready = {}, None

    def get(self, name):
        return self.mats[name]

    def whole(self, name):
        return self.mats[name]

    def put(self, name, matrix):
        pass

    def layer_done(self, n, local):
        pass

    def during(self, point):
        return {}

    def add(self, name, act, low):
        got = weight_layer(self.geom, act, low)
        self.grads[name] = scatter_matrix(got)
        return got

    def pieces(self, name, act, low):
        return [lambda x: self.add(name, act, low)]

    def send(self, n, to=None):
        pass

    def after_layer(self, n, local):
        pass

    def now(self):
        return None

    def tail(self, blocks, kernels):
        return [kernel(None) for kernel in kernels]


class ThisMesh:
    def __init__(self, links, geom, weights, gains, biases):
        self.geom, self.links = geom, links
        self.me = number(1)
        sizes = (8, 4)
        full = {n: (w.shape[0] * 8, w.shape[1] * 4) for n, w in weights.items()}
        splits = ("six", "gating")
        g1 = Gather(links, weights["one"])
        g1.far()
        packed = {n: pack(rows_of_chip(tied(w, g1.got)) if n in splits else w) for n, w in weights.items()}
        gains, biases = tied((gains, biases), g1.got)
        affine = in_three(jnp.stack([gains, biases])).reshape(6, -1)
        affine = jnp.pad(affine, ((0, 2), (0, 2 * LANES - affine.shape[1])))
        affine = jnp.concatenate([affine[:, :LANES], affine[:, LANES:]])
        groups = (("one",), ("two",), ("three",), ("four",), ("five",), ("six", "gating", "attend"))
        self.g, self.members, self.group = [], {}, {}
        for names in groups:
            at = 0
            for name in names:
                self.members[name] = Member(at, full[name], *sizes, split=name in splits)
                at += self.members[name].rows
            if names == ("one",):
                group = g1
            else:
                group = Gather(links, jnp.concatenate([packed[n] for n in names] + [affine] * (names == ("two",))))
            self.g.append(group)
            self.group.update((n, group) for n in names)
        g2 = self.g[1]
        g1.near()
        g2.far(g1.got)
        g1.first()
        g2.near(g1.got)
        g1.second()
        g1.finish()
        self.g[2].far(g2.got)
        g2.first(g1.got)
        self.ready = self.g[5].shard
        self.mats = {}
        self.grads, self.blocks, self.sums = {}, {}, {}
        self.homes, self.rows = {}, {}
        for names in (("six", "gating"), ("five",), ("four", "attend"), ("three",), ("two",), ("one",)):
            at = 0
            for name in names:
                self.homes[name] = Member(at, full[name], *sizes, split=name in splits)
                at += self.homes[name].rows
            self.rows.update((name, at) for name in names)

    def layer_done(self, n, local):
        if n < 6:
            self.g[n].second((local, self.g[n + 1].got) if n < 5 else local)
            self.g[n].busy()

    def get(self, name):
        if name in self.mats:
            return self.mats[name]
        group = self.group[name]
        self.mats[name] = group.pieces(self.members[name])
        if name == "two":
            self.affine = collect_affine(group.pieces(FlatMember(self.members["two"].rows, 16)))[:, None]
        return self.mats[name]

    def whole(self, name):
        self.mats[name] = collect(self.get(name))
        return self.mats[name]

    def put(self, name, matrix):
        self.mats[name] = matrix

    def during(self, point):
        if point <= 5:

            def x_done(x):
                self.g[point].finish(x)

            if point == 5:
                return {X: [x_done]}
            group = self.g[point + 1]

            def z_done(x):
                group.near(x)

            def y_done(x):
                group.first(x)
                if point < 4:
                    self.g[point + 2].far(x)

            return {Z_FAR: [z_done], X: [x_done], Y: [y_done]}
        n = 14 - point

        def z_done(x):
            self.sums[n + 2].near(x)

        def x_done(x):
            (got,) = add_after(x, self.sums[n + 2].far_job())
            self.sums[n + 2].far(*got)
            return got[0]

        def y_done(x):
            if n == 2:
                self.send(2)
                (got,) = add_after(x, self.sums[2].first_job())
                self.sums[2].first(*got)
            else:
                (got,) = add_after(x, self.sums[n + 1].second_job())
                self.sums[n + 1].second(*got)

        return {Z_FAR: [z_done], X: [x_done], Y: [y_done]} if n < 5 else {Y: [y_done]}

    def add(self, name, act, low):
        n = NUMBER[name]
        self.blocks[n] = weight_blocks(
            self.geom, self.me, act, low, self.homes[name], self.rows[name], self.blocks.get(n)
        )
        return self.blocks[n][0]

    def pieces(self, name, act, low):
        def piece(step):
            def work(x):
                n = NUMBER[name]
                if step == 0:
                    *self.blocks[n], self.turned = weight_piece(
                        self.geom, self.me, tied(act, x), low, self.homes[name], self.rows[name], 0
                    )
                else:
                    self.blocks[n] = weight_piece(
                        self.geom, self.me, tied(self.turned, x), low, self.homes[name], self.rows[name], step, self.blocks[n]
                    )
                return self.blocks[n][0]

            return work

        return [piece(step) for step in range(3)]

    def send(self, n, to=None):
        near, far, away = self.blocks[n]
        self.sums[n] = Scatter(self.links, (near, far, tied(away, to)))

    def after_layer(self, n, local):
        jobs = [self.sums[n + 1].first_job()]
        if n < 5:
            jobs.append(self.sums[n + 2].near_job())
        if n < 4:
            jobs.append(self.sums[n + 3].finish_job())
        got = add_after(local, *jobs)
        self.sums[n + 1].first(*got[0])
        self.links.busy(X, *self.sums[n + 1].got)
        if n < 5:
            s = self.sums[n + 2]
            s.z, s.send = got[1]
        if n < 4:
            (self.sums[n + 3].out,) = got[2]

    def now(self):
        return self.sums[3].a

    def tail(self, blocks, kernels):
        two, three, four = (self.sums[n] for n in (2, 3, 4))
        outs = [kernels[0](blocks)]
        got = add_after(outs[0], two.second_job(), three.second_job(), four.finish_job())
        two.second(*got[0])
        three.second(*got[1])
        (four.out,) = got[2]
        ((two.z, two.send),) = add_after(got[0][0], two.near_job())
        two.near()
        self.send(1, two.send)
        one = self.sums[1]
        (got,) = add_after(two.z, one.first_job())
        one.first(*got)
        outs.append(kernels[1](got[0]))
        got = add_after(got[0], two.far_job(), three.near_job())
        two.far(*got[0])
        three.z, three.send = got[1]
        three.near()
        (got,) = add_after(got[0][0], one.second_job())
        one.second(*got)
        got = add_after(got[0], one.near_job(), two.finish_job(), three.far_job())
        one.z, one.send = got[0]
        (two.out,) = got[1]
        one.near()
        three.far(*got[2])
        (got,) = add_after(one.z, one.far_job())
        one.far(*got)
        ((three.out,),) = add_after(got[0], three.finish_job())
        ((one.out,),) = add_after(three.out, one.finish_job())
        for name, m in self.homes.items():
            out = unpack(self.sums[NUMBER[name]].out[m.at : m.at + m.rows], m.blocks)
            self.grads[name] = columns_of_core(out) if m.split else out
        return outs


NUMBER = dict(one=1, two=2, three=3, attend=4, four=4, five=5, six=6, gating=6)


class FlatMember:
    def __init__(self, at, rows):
        self.at, self.vr, self.rows, self.blocks, self.shape = at, rows, rows, 1, (32 * rows, LANES)

    def spots(self, i, j):
        yield self.at, (i * 4 + j) * self.vr, 0


def body(
    frames_in,
    domain,
    kernel_one,
    kernel_two,
    kernel_three,
    attn_enc,
    kernel_four,
    kernel_five,
    kernel_six,
    attn_dec,
    gains,
    biases,
    enc_cot,
    dec_cot,
):
    frames, rows, cols, _ = frames_in.shape
    total_frames = frames * lax.axis_size(AXES)
    first = total_frames * 5 // 8
    counts = (float(first * rows * cols), float((total_frames - first) * rows * cols))
    geom = (frames, rows, cols, counts)
    pix = frames * rows * cols
    source = frames_in.reshape(pix, C_IN)
    enc_cot = enc_cot.transpose(0, 1, 3, 2, 4)
    dec_cot = dec_cot.reshape(pix, TASKS, C_DEC).transpose(1, 0, 2)
    weights = dict(
        one=kernel_one, two=kernel_two, three=kernel_three, attend=attn_enc,
        four=kernel_four, five=kernel_five, six=kernel_six, gating=attn_dec,
    )
    links = Links()
    this = lax.axis_size("dp") == 8 and lax.axis_size("fsdp") == 4
    w = (ThisMesh if this else AnyMesh)(links, geom, weights, gains, biases)

    def forward(name, source, norm=None):
        got = forward_layer(geom, domain, source, w.get(name), norm)
        w.put(name, got[-1])
        return got[:3] if norm is not None else got[:2]

    def point(name, act):
        got = point_layer(geom, domain, act, w.get(name))
        w.put(name, got[-1])
        return got[:2]

    pre_1, local = forward("one", tied(source, w.ready))
    w.layer_done(1, local)
    st_1 = links.total(local, w.during(1), ORDER)
    w.get("two")
    widths = (C_MID, C_MID, C_MID, TASKS * C_MID, C_MID, C_MID, C_DEC, TASKS * C_DEC)
    gain, bias, at = [], [], 0
    for width in widths:
        gain.append(w.affine[0, :, at : at + width])
        bias.append(w.affine[1, :, at : at + width])
        at += width
    pre_2, local, act_1 = forward("two", pre_1, (st_1, gain[0], bias[0]))
    w.layer_done(2, local)
    st_2 = links.total(local, w.during(2), ORDER)
    pre_3, local, act_2 = forward("three", pre_2, (st_2, gain[1], bias[1]))
    w.layer_done(3, local)
    st_3 = links.total(local, w.during(3), ORDER)
    unpooled = pool_layer(geom, domain, pre_3, st_3, gain[2], bias[2])
    pre_4, local = forward("four", unpooled)
    w.layer_done(4, local)
    st_4 = links.total(local, w.during(4), ORDER)
    pre_5, local, act_4 = forward("five", pre_4, (st_4, gain[4], bias[4]))
    w.layer_done(5, local)
    st_5 = links.total(local, w.during(5), ORDER)
    pre_g, local_g = point("gating", act_4)
    pre_6, local, act_5 = forward("six", pre_5, (st_5, gain[5], bias[5]))
    attend = w.whole("attend")
    wide = []

    def attend_part(k):
        def work(x):
            wide.append(point_layer(geom, domain, tied(act_2, x), attend[:, k * C_MID : (k + 1) * C_MID]))
            return wide[-1][0]

        return work

    both = links.total(jnp.concatenate([local, local_g], 1), None, ORDER, [attend_part(k) for k in range(TASKS)])
    st_6, st_g = both[:, :C_DEC], both[:, C_DEC:]
    pre_a = [p for p, _ in wide]
    task_maps, g_6, g_g, local = head_layer(
        geom, domain, pre_6, st_6, pre_g, st_g, gain[6], bias[6], gain[7], bias[7], dec_cot
    )
    both = links.total(jnp.concatenate([local] + [s for _, s in wide], 1), None, ORDER)
    sm_6, sm_g, st_a = both[:, :C_DEC], both[:, C_DEC : 4 * C_DEC], both[:, 4 * C_DEC :]
    st_a = [st_a[:, k * C_MID : (k + 1) * C_MID] for k in range(TASKS)]
    pool_args = (geom, domain, pre_3, st_3, gain[2], bias[2])
    masks = [(pre_a[k], st_a[k], gain[3][:, k * C_MID : (k + 1) * C_MID], bias[3][:, k * C_MID : (k + 1) * C_MID]) for k in range(TASKS)]

    win_6, g_5, local = backward_layer(
        geom, domain, (g_6, pre_6, st_6, sm_6, gain[6]), w.get("six"), lower=(pre_5, st_5, gain[5], bias[5])
    )
    early, gate_back = [], []

    def early_part(k):
        def work(x):
            early.append(pool_early(*pool_args, *masks[k], enc_cot[:, :, k], tied(pre_3, x), early[-1][0] if early else None))
            return early[-1][0]

        return work

    def gate_part(x):
        gate_back.extend(point_back(geom, domain, tied(g_g, x), pre_g, st_g, sm_g, gain[7], w.get("gating")))
        return gate_back[0]

    sm_5 = links.total(
        local, None, ORDER, [lambda x: w.add("six", act_5, tied(win_6, x)), gate_part, early_part(0), early_part(1)]
    )
    early_part(2)(sm_5)
    mix = early[-1][0]
    low_g, add_4 = gate_back
    blocks = w.add("gating", act_4, low_g)
    w.send(6, sm_5)
    win_5, g_4, local = backward_layer(
        geom,
        domain,
        (tied(g_5, blocks), pre_5, st_5, sm_5, gain[5]),
        w.get("five"),
        added=add_4,
        lower=(pre_4, st_4, gain[4], bias[4]),
    )
    w.after_layer(5, local)
    both = links.total(
        jnp.concatenate([local] + [e[2] for e in early], 1), w.during(9), ORDER, w.pieces("five", act_4, win_5)
    )
    w.send(5, both)
    sm_4 = both[:, :C_MID]
    sm_a = [both[:, (k + 1) * C_MID : (k + 2) * C_MID] for k in range(TASKS)]
    win_4, g_3, local = backward_layer(
        geom,
        domain,
        (g_4, pre_4, st_4, sm_4, gain[4]),
        w.get("four"),
        lower=(pre_3, st_3, gain[2], bias[2]),
        mix=mix,
    )
    w.after_layer(4, local)
    backs = []

    def attend_back(k):
        def work(x):
            backs.append(
                point_back(
                    geom, domain, tied(early[k][1], x), pre_a[k], st_a[k], sm_a[k], masks[k][2],
                    attend[:, k * C_MID : (k + 1) * C_MID], backs[-1][1] if backs else None,
                )
            )
            return backs[-1][1]

        return work

    sm_3 = links.total(local, w.during(10), ORDER, w.pieces("four", unpooled, win_4) + [attend_back(0)])
    attend_back(1)(sm_3)
    attend_back(2)(backs[-1][1])
    low_a = jnp.concatenate([low for low, _ in backs], 1)
    blocks = w.add("attend", act_2, low_a)
    w.send(4)
    win_3, g_2, local = backward_layer(
        geom,
        domain,
        (tied(g_3, blocks), pre_3, st_3, sm_3, gain[2]),
        w.get("three"),
        added=backs[-1][1],
        lower=(pre_2, st_2, gain[1], bias[1]),
    )
    w.after_layer(3, local)
    tasks = []

    def task_part(x):
        tasks.append(task_layer(geom, domain, tied(pre_3, x), *pool_args[3:], masks))
        return tasks[0]

    sm_2 = links.total(local, w.during(11), ORDER, w.pieces("three", act_2, win_3) + [task_part])
    w.send(3, sm_2)
    win_2, g_1, local = backward_layer(
        geom,
        domain,
        (g_2, pre_2, st_2, sm_2, gain[1]),
        w.get("two"),
        lower=(pre_1, st_1, gain[0], bias[0]),
    )
    w.after_layer(2, local)
    sm_1 = links.total(local, w.during(12), ORDER, w.pieces("two", act_1, win_2))
    win_1 = low_layer(geom, domain, (tied(g_1, w.now()), pre_1, st_1, sm_1, gain[0]))
    blocks = w.add("one", source, win_1)
    frames_grad, task_maps = w.tail(
        blocks,
        (
            lambda to: input_layer(geom, tied(win_1, to), w.get("one")),
            lambda to: tied(task_maps, to).transpose(1, 0, 2).reshape(frames, rows, cols, TASKS, C_DEC),
        ),
    )
    gains_grad, biases_grad = share_of(number(1), [sm_1, sm_2, sm_3, *sm_a, sm_4, sm_5, sm_6, sm_g], gains.shape[0])
    return (
        tasks[0].transpose(0, 1, 3, 2, 4),
        task_maps,
        frames_grad.reshape(frames, rows, cols, C_IN),
        *(w.grads[n] for n in ("one", "two", "three", "attend", "four", "five", "six", "gating")),
        gains_grad,
        biases_grad,
    )


def solution(mesh):
    whole_split = P(AXES)
    matrix = P("dp", "fsdp")
    return jax.shard_map(
        body,
        mesh=mesh,
        in_specs=(whole_split, whole_split) + (matrix,) * 8 + (whole_split,) * 4,
        out_specs=(whole_split,) * 3 + (matrix,) * 8 + (whole_split,) * 2,
        check_vma=False,
    )
```

```python
import functools

import jax
import jax.numpy as jnp
from jax import lax
from jax.experimental import pallas as pl
from jax.experimental.pallas import tpu as pltpu
from jax.sharding import PartitionSpec as P

C_IN = 256
C_MID = 512
C_DEC = 256
TASKS = 3
EPS = 1e-05
LANES = 128
F32 = jnp.float32
BF16 = jnp.bfloat16
COST = 0.1
VMEM_LIMIT = 12 * 1024 * 1024


def params(grid_dims=0):
    return pltpu.CompilerParams(
        vmem_limit_bytes=VMEM_LIMIT,
        dimension_semantics=("arbitrary",) * grid_dims if grid_dims else None,
    )


def cost(flops, size):
    return pl.CostEstimate(flops=int(flops * COST), bytes_accessed=int(size * COST), transcendentals=0)


def whole(shape):
    zeros = (0,) * len(shape)
    return pl.BlockSpec(shape, lambda *_: zeros, pipeline_mode=pl.Buffered(1))


SCALARS = pl.BlockSpec(memory_space=pltpu.SMEM)


def sds(shape, dtype):
    return jax.ShapeDtypeStruct(shape, dtype)


def sigmoid(v):
    return 0.5 * jnp.tanh(0.5 * v) + 0.5


def frame_tables(stats, domain_at, counts):
    first = domain_at == 0
    share = jnp.where(first, 1.0 / counts[0], 1.0 / counts[1])
    average = jnp.where(first, stats[0:1], stats[1:2]) * share
    square = jnp.where(first, stats[2:3], stats[3:4]) * share
    return average, lax.rsqrt(square - average * average + EPS)


def grad_tables(sums, domain_at, counts):
    first = domain_at == 0
    share = jnp.where(first, 1.0 / counts[0], 1.0 / counts[1])
    return (
        jnp.where(first, sums[0:1], sums[1:2]) * share,
        jnp.where(first, sums[2:3], sums[3:4]) * share,
    )


def by_domain(first, second, domain_ref):
    rows = []
    for per_frame in (first, second):
        for d in (0, 1):
            total = None
            for f, value in enumerate(per_frame):
                term = jnp.where(domain_ref[f] == d, value, jnp.zeros_like(value))
                total = term if total is None else total + term
            rows.append(total)
    return jnp.concatenate(rows, 0)


def fold(x):
    return jnp.sum(x.reshape(-1, 8, x.shape[-1]), 0)


def value_sums(parts, domain_ref, others=None):
    others = parts if others is None else others
    return by_domain(
        [jnp.sum(fold(p), 0, keepdims=True) for p in parts],
        [jnp.sum(fold(p * o), 0, keepdims=True) for p, o in zip(parts, others)],
        domain_ref,
    )


def put_windows(win_ref, f, row, value, cols):
    col = lax.broadcasted_iota(jnp.int32, value.shape, 0)
    left = jnp.where(col == 0, 0.0, pltpu.roll(value, 1, 0))
    right = jnp.where(col == cols - 1, 0.0, pltpu.roll(value, cols - 1, 0))
    win_ref[0, f, row + 1] = left.astype(BF16)
    win_ref[1, f, row + 1] = value.astype(BF16)
    win_ref[2, f, row + 1] = right.astype(BF16)


def clear_edges(win_ref, rows):
    shape = win_ref.shape
    for b in range(3):
        for f in range(shape[1]):
            win_ref[b, f, 0] = jnp.zeros(shape[3:], BF16)
            win_ref[b, f, rows + 1] = jnp.zeros(shape[3:], BF16)


def window(win_ref, b, row_at, rows):
    part = win_ref[b, :, pl.ds(row_at, rows)]
    return part.reshape(-1, part.shape[-1])


def column_sums(ref, f, pixels, lanes, step=64):
    def add(i, carry):
        part = ref[pl.ds(f * pixels + i * step, step), lanes]
        return carry[0] + fold(part), carry[1] + fold(part * part)

    width = lanes.stop - lanes.start
    zero = jnp.zeros((8, width), F32)
    one, two = lax.fori_loop(0, pixels // step, add, (zero, zero), unroll=2)
    return jnp.sum(one, 0, keepdims=True), jnp.sum(two, 0, keepdims=True)


def in_hbm(x):
    return pltpu.with_memory_space_constraint(x, pltpu.HBM)


class Pieces:
    def __init__(self, member, parts, me, sources):
        self.member, self.parts, self.me = member, parts, me
        self.sources = list(sources)
        self.shape = member.shape


def span(start, size):
    return pl.ds(start if isinstance(start, int) else pl.multiple_of(start, size & -size), size)


def fetch(member, parts, me_ref, sources, dst_ref, sem):
    me = me_ref[0]
    for (first, size, masks), src in zip(parts, sources):
        for q in range(src.shape[0]):
            d = q if masks is None else me ^ masks[q]
            for at, row, col in member.spots(d >> 2, d & 3):
                low, high = max(at, first), min(at + member.vr, first + size)
                if low < high:
                    pltpu.make_async_copy(
                        src.at[q, pl.ds(low - first, high - low)],
                        dst_ref.at[span(row + (low - at), high - low), span(col, LANES)],
                        sem,
                    ).start()


def arrived(ref, sem):
    pltpu.make_async_copy(ref, ref, sem).wait()


def forward_kernel(geom, normed, pieces, *refs):
    frames, rows, cols, counts = geom
    pixels = rows * cols
    refs = list(refs)
    domain_ref = refs.pop(0)
    source_ref = refs.pop(0)
    if normed:
        stats_ref, gain_ref, bias_ref = refs.pop(0), refs.pop(0), refs.pop(0)
    if pieces:
        me_ref = refs.pop(0)
        sources = [refs.pop(0) for _ in pieces[1]]
    else:
        kernel_ref = refs.pop(0)
    out_ref = refs.pop(0)
    sums_ref = refs.pop(0)
    act_ref = refs.pop(0) if normed else None
    if pieces:
        matrix_ref = refs.pop(0)
    *wins, held_ref, sem = refs

    if pieces:
        fetch(*pieces, me_ref, sources, held_ref, sem.at[0])
    else:
        pltpu.make_async_copy(kernel_ref, held_ref, sem.at[0]).start()

    def prepare(f, unrolled):
        clear_edges(wins[f], rows)
        if normed:
            average, inverse = frame_tables(stats_ref[...], domain_ref[f], counts)
            scale = inverse * gain_ref[...]
            shift = bias_ref[...] - average * scale

        def one_row(r, _):
            at = f * pixels + r * cols
            at = at if unrolled else pl.multiple_of(at, cols)
            value = source_ref[pl.ds(at, cols), :].astype(F32)
            if normed:
                act = value * scale + shift
                value = act * sigmoid(act)
                act_ref[pl.ds(at, cols), :] = value.astype(BF16)
            put_windows(wins[f], 0, r, value, cols)
            return 0

        if unrolled:
            for r in range(rows):
                one_row(r, 0)
        else:
            lax.fori_loop(0, rows, one_row, 0, unroll=2)

    def product(f):
        source = jnp.concatenate([window(wins[f], b, a, rows) for a in range(3) for b in range(3)], 1)
        out = jnp.dot(source, held_ref[...], preferred_element_type=F32)
        out_ref[f * pixels : (f + 1) * pixels, :] = out
        return out

    prepare(0, False)
    arrived(held_ref, sem.at[0])
    if pieces:
        pltpu.make_async_copy(held_ref, matrix_ref, sem.at[1]).start()
    parts = []
    for f in range(frames):
        if f + 1 < frames:
            prepare(f + 1, True)
        parts.append(product(f))
    sums_ref[...] = value_sums(parts, domain_ref)
    if pieces:
        pltpu.make_async_copy(held_ref, matrix_ref, sem.at[1]).wait()


ANYWHERE = pl.BlockSpec(memory_space=pl.ANY)


def forward_layer(geom, domain, source, kernel, norm=None):
    frames, rows, cols, _ = geom
    pix, chans = source.shape
    width = kernel.shape[1]
    pieces = isinstance(kernel, Pieces)
    args, specs = [domain, source], [SCALARS, whole(source.shape)]
    if norm is not None:
        args += list(norm)
        specs += [whole(x.shape) for x in norm]
    if pieces:
        args += [kernel.me, *kernel.sources]
        specs += [SCALARS] + [ANYWHERE] * len(kernel.sources)
    else:
        args.append(in_hbm(kernel))
        specs.append(ANYWHERE)
    outs, out_specs = [sds((pix, width), F32)], [whole((pix, width))]
    outs.append(sds((4, width), F32))
    out_specs.append(whole((4, width)))
    if norm is not None:
        outs.append(sds((pix, chans), BF16))
        out_specs.append(whole((pix, chans)))
    scratch = [pltpu.VMEM((3, 1, rows + 2, cols, chans), BF16)] * frames
    scratch += [pltpu.VMEM(kernel.shape, BF16), pltpu.SemaphoreType.DMA((2,))]
    if pieces:
        outs.append(pltpu.HBM(kernel.shape, BF16))
        out_specs.append(ANYWHERE)
    size = kernel.shape[0] * kernel.shape[1]
    return pl.pallas_call(
        functools.partial(forward_kernel, geom, norm is not None, (kernel.member, kernel.parts) if pieces else None),
        grid=(1,),
        in_specs=specs,
        out_specs=out_specs,
        out_shape=outs,
        scratch_shapes=scratch,
        compiler_params=params(1),
        cost_estimate=cost(2 * pix * size, size * 2 + pix * 4096),
    )(*args)


def pair_sum(x, cols):
    even = lax.broadcasted_iota(jnp.int32, x.shape, 0) % 2 == 0
    return x + jnp.where(even, pltpu.roll(x, cols - 1, 0), pltpu.roll(x, 1, 0))


def softmax_window(top, cols):
    exps = [jnp.exp(t) for t in top]
    share = 1.0 / pair_sum(exps[0] + exps[1], cols)
    return [e * share for e in exps]


def spread_cols(scr_ref, x):
    half = x.shape[0]
    scr_ref[pl.ds(0, half, stride=2), :] = x
    scr_ref[pl.ds(1, half, stride=2), :] = x
    return scr_ref[pl.ds(0, 2 * half), :]


def top_rows(top_ref, at, cols, lanes, scale, shift):
    top = []
    for a in at:
        act = top_ref[pl.ds(a, cols), lanes] * scale + shift
        top.append(act * sigmoid(act))
    return top


def row_pairs(x, cols):
    x = x.reshape(-1, 2, cols, x.shape[-1])
    return x[:, 0], x[:, 1]


def pair_sums(x):
    cols = x.shape[1]
    even = lax.broadcasted_iota(jnp.int32, x.shape, 1) % 2 == 0
    return x + jnp.where(even, pltpu.roll(x, cols - 1, 1), pltpu.roll(x, 1, 1))


def window_weights(top):
    exps = [jnp.exp(t) for t in top]
    share = 1.0 / pair_sums(exps[0] + exps[1])
    return [e * share for e in exps]


def pool_kernel(geom, domain_ref, top_ref, top_st, gain_t, bias_t, un_ref):
    frames, rows, cols, counts = geom
    pixels = rows * cols
    for f in range(frames):
        at = slice(f * pixels, (f + 1) * pixels)
        for lane in range(0, top_ref.shape[-1], LANES):
            lanes = slice(lane, lane + LANES)
            average, inverse = frame_tables(top_st[:, lanes], domain_ref[f], counts)
            scale = inverse * gain_t[:, lanes]
            act = top_ref[at, lanes] * scale + (bias_t[:, lanes] - average * scale)
            top = row_pairs(act * sigmoid(act), cols)
            weight = window_weights(top)
            pooled = pair_sums(weight[0] * top[0] + weight[1] * top[1])
            un_ref[at, lanes] = jnp.stack([w * pooled for w in weight], 1).reshape(pixels, LANES).astype(BF16)


def pool_layer(geom, domain, top, top_st, gain_t, bias_t):
    pix, chans = top.shape
    args = (domain, top, top_st, gain_t, bias_t)
    return pl.pallas_call(
        functools.partial(pool_kernel, geom),
        in_specs=[SCALARS] + [whole(x.shape) for x in args[1:]],
        out_specs=whole((pix, chans)),
        out_shape=sds((pix, chans), BF16),
        compiler_params=params(),
        cost_estimate=cost(pix * chans * 20, pix * chans * 6),
    )(*args)


def task_kernel(geom, domain_ref, top_ref, top_st, gain_t, bias_t, *refs):
    frames, rows, cols, counts = geom
    pixels = rows * cols
    masks = [refs[4 * k : 4 * k + 4] for k in range(TASKS)]
    task_ref, scr_ref = refs[-2:]
    for f in range(frames):
        for lane in range(0, top_ref.shape[-1], LANES):
            lanes = slice(lane, lane + LANES)

            def table(st, gain, bias):
                average, inverse = frame_tables(st[:, lanes], domain_ref[f], counts)
                scale = inverse * gain[:, lanes]
                return scale, bias[:, lanes] - average * scale

            t_scale, t_shift = table(top_st, gain_t, bias_t)
            wide = [table(*mask[1:]) for mask in masks]

            def one(i, _):
                at = [pl.multiple_of(f * pixels + (2 * i + h) * cols, cols) for h in (0, 1)]
                top = top_rows(top_ref, at, cols, lanes, t_scale, t_shift)
                weight = softmax_window(top, cols)
                held = [w * t for w, t in zip(weight, top)]
                for k in range(TASKS):
                    scale, shift = wide[k]
                    total = None
                    for h in (0, 1):
                        term = sigmoid(masks[k][0][pl.ds(at[h], cols), lanes] * scale + shift) * held[h]
                        total = term if total is None else total + term
                    scr_ref[k, pl.ds(0, cols), :] = total
                    even = scr_ref[k, pl.ds(0, cols // 2, stride=2), :]
                    odd = scr_ref[k, pl.ds(1, cols // 2, stride=2), :]
                    task_ref[f, i, k, :, lanes] = even + odd
                return 0

            lax.fori_loop(0, rows // 2, one, 0, unroll=2)


def task_layer(geom, domain, top, top_st, gain_t, bias_t, masks):
    frames, rows, cols, _ = geom
    pix, chans = top.shape
    task_shape = (frames, rows // 2, TASKS, cols // 2, chans)
    args = (domain, top, top_st, gain_t, bias_t, *(x for mask in masks for x in mask))
    return pl.pallas_call(
        functools.partial(task_kernel, geom),
        in_specs=[SCALARS] + [whole(x.shape) for x in args[1:]],
        out_specs=whole(task_shape),
        out_shape=sds(task_shape, F32),
        scratch_shapes=[pltpu.VMEM((TASKS, cols + 8, LANES), F32)],
        compiler_params=params(),
        cost_estimate=cost(pix * chans * 60, pix * chans * 28),
    )(*args)


def pool_early_kernel(geom, first, domain_ref, top_ref, top_st, gain_t, bias_t, wide_ref, wide_st, gain_w, bias_w, cot_ref, *refs):
    frames, rows, cols, counts = geom
    pixels = rows * cols
    mix_ref, gw_ref, sums_ref, scr_ref = refs[-4:]
    for lane in range(0, top_ref.shape[-1], LANES):
        lanes = slice(lane, lane + LANES)
        sums = []
        for f in range(frames):
            average, inverse = frame_tables(top_st[:, lanes], domain_ref[f], counts)
            t_scale = inverse * gain_t[:, lanes]
            t_shift = bias_t[:, lanes] - average * t_scale
            w_mean, w_inv = frame_tables(wide_st[:, lanes], domain_ref[f], counts)

            def one(i, carry):
                at = [pl.multiple_of(f * pixels + (2 * i + h) * cols, cols) for h in (0, 1)]
                top = top_rows(top_ref, at, cols, lanes, t_scale, t_shift)
                weight = softmax_window(top, cols)
                cot = spread_cols(scr_ref, cot_ref[f, i, :, lanes].astype(F32))
                one_sum, two_sum = carry
                for h in (0, 1):
                    xhat = (wide_ref[pl.ds(at[h], cols), lanes] - w_mean) * w_inv
                    mask = sigmoid(xhat * gain_w[:, lanes] + bias_w[:, lanes])
                    part = cot * mask
                    mix = part if first else refs[0][pl.ds(at[h], cols), lanes] + part
                    mix_ref[pl.ds(at[h], cols), lanes] = mix
                    g = part * (weight[h] * top[h]) * (1.0 - mask)
                    gw_ref[pl.ds(at[h], cols), lanes] = g
                    one_sum = one_sum + fold(g)
                    two_sum = two_sum + fold(g * xhat)
                return one_sum, two_sum

            zero = jnp.zeros((8, LANES), F32)
            sums.append(lax.fori_loop(0, rows // 2, one, (zero, zero), unroll=2))
        sums_ref[:, lanes] = by_domain(
            [jnp.sum(s[0], 0, keepdims=True) for s in sums], [jnp.sum(s[1], 0, keepdims=True) for s in sums], domain_ref
        )


def pool_early(geom, domain, _, top_st, gain_t, bias_t, wide, wide_st, gain_w, bias_w, cot, top, mix=None):
    cols = geom[2]
    pix, chans = top.shape
    args = (domain, top, top_st, gain_t, bias_t, wide, wide_st, gain_w, bias_w, cot) + (() if mix is None else (mix,))
    outs = [sds((pix, chans), F32)] * 2 + [sds((4, chans), F32)]
    return pl.pallas_call(
        functools.partial(pool_early_kernel, geom, mix is None),
        in_specs=[SCALARS] + [whole(x.shape) for x in args[1:]],
        out_specs=[whole(o.shape) for o in outs],
        out_shape=outs,
        scratch_shapes=[pltpu.VMEM((cols + 8, LANES), F32)],
        compiler_params=params(),
        cost_estimate=cost(pix * chans * 40, pix * chans * 20),
    )(*args)


def head_kernel(geom, domain_ref, bot_ref, bot_st, gate_ref, gate_st, gain_b, bias_b, gain_g, bias_g, cot_ref,
                maps_ref, gb_ref, gg_ref, sums_ref):
    frames, rows, cols, counts = geom
    pixels = rows * cols
    chans = bot_ref.shape[-1]
    for lane in range(0, chans, LANES):
        lanes = slice(lane, lane + LANES)
        grads, hats = ([[] for _ in range(TASKS + 1)] for _ in range(2))
        for f in range(frames):
            at = slice(f * pixels, (f + 1) * pixels)
            mean, inv = frame_tables(bot_st[:, lanes], domain_ref[f], counts)
            b_hat = (bot_ref[at, lanes] - mean) * inv
            act = b_hat * gain_b[:, lanes] + bias_b[:, lanes]
            s = sigmoid(act)
            bottom = act * s
            back = None
            for k in range(TASKS):
                sl = slice(k * chans + lane, k * chans + lane + LANES)
                mean, inv = frame_tables(gate_st[:, sl], domain_ref[f], counts)
                xhat = (gate_ref[at, sl] - mean) * inv
                value = sigmoid(xhat * gain_g[:, sl] + bias_g[:, sl])
                maps_ref[k, at, lanes] = value * bottom
                part = cot_ref[k, at, lanes].astype(F32) * value
                back = part if back is None else back + part
                g = part * bottom * (1.0 - value)
                gg_ref[at, sl] = g
                grads[k].append(g)
                hats[k].append(xhat)
            g = back * (s * (1.0 + act * (1.0 - s)))
            gb_ref[at, lanes] = g
            grads[-1].append(g)
            hats[-1].append(b_hat)
        for k in range(TASKS + 1):
            to = chans + k * chans + lane if k < TASKS else lane
            sums_ref[:, to : to + LANES] = value_sums(grads[k], domain_ref, hats[k])


def head_layer(geom, domain, bot, bot_st, gate, gate_st, gain_b, bias_b, gain_g, bias_g, cot):
    pix, chans = bot.shape
    args = (domain, bot, bot_st, gate, gate_st, gain_b, bias_b, gain_g, bias_g, cot)
    outs = [sds((TASKS, pix, chans), F32), sds((pix, chans), F32), sds((pix, TASKS * chans), F32),
            sds((4, (TASKS + 1) * chans), F32)]
    return pl.pallas_call(
        functools.partial(head_kernel, geom),
        in_specs=[SCALARS] + [whole(x.shape) for x in args[1:]],
        out_specs=[whole(o.shape) for o in outs],
        out_shape=outs,
        compiler_params=params(),
        cost_estimate=cost(pix * chans * 80, pix * chans * 44),
    )(*args)


def norm_back_rows(g, pre, tables):
    mean, inv, scale, g_mean, g_cross = tables
    xhat = (pre - mean) * inv
    return scale * (g - g_mean - xhat * g_cross)


def back_tables(stats_ref, sums_ref, gain_ref, domain_at, counts):
    mean, inv = frame_tables(stats_ref[...], domain_at, counts)
    g_mean, g_cross = grad_tables(sums_ref[...], domain_at, counts)
    return mean, inv, inv * gain_ref[...], g_mean, g_cross


def backward_kernel(geom, added, epilogue, *refs):
    frames, rows, cols, counts = geom
    pixels = rows * cols
    refs = list(refs)
    domain_ref = refs.pop(0)
    g_ref, pre_ref, st_ref, sm_ref, gain_ref = (refs.pop(0) for _ in range(5))
    kernel_ref = refs.pop(0)
    add_ref = refs.pop(0) if added else None
    lpre_ref, lst_ref, lgain_ref, lbias_ref = (refs.pop(0) for _ in range(4))
    if epilogue == "pool":
        mix_ref = refs.pop(0)
    win_ref, out_ref, sums_ref, held_ref, sem = refs
    chans = kernel_ref.shape[0] // 9

    load = pltpu.make_async_copy(kernel_ref, held_ref, sem)
    load.start()
    clear_edges(win_ref, rows)
    for f in range(frames):
        tables = back_tables(st_ref, sm_ref, gain_ref, domain_ref[f], counts)

        def one_row(r, _):
            at = pl.multiple_of(f * pixels + r * cols, cols)
            low = norm_back_rows(g_ref[pl.ds(at, cols), :], pre_ref[pl.ds(at, cols), :], tables)
            put_windows(win_ref, f, r, low, cols)
            return 0

        lax.fori_loop(0, rows, one_row, 0, unroll=2)
    load.wait()
    source = jnp.concatenate([window(win_ref, 2 - b, 2 - a, rows) for a in range(3) for b in range(3)], 1)
    weight = jnp.concatenate([held_ref[k * chans : (k + 1) * chans, :] for k in range(9)], 1)
    out = lax.dot_general(source, weight, (((1,), (1,)), ((), ())), preferred_element_type=F32)
    if added:
        out = out + add_ref[...]
    if epilogue == "silu":
        first, second = [], []
        for f in range(frames):
            at = slice(f * pixels, (f + 1) * pixels)
            mean, inv = frame_tables(lst_ref[...], domain_ref[f], counts)
            xhat = (lpre_ref[at] - mean) * inv
            act = xhat * lgain_ref[...] + lbias_ref[...]
            s = sigmoid(act)
            g = out[at] * (s * (1.0 + act * (1.0 - s)))
            out_ref[at] = g
            first.append(jnp.sum(fold(g), 0, keepdims=True))
            second.append(jnp.sum(fold(g * xhat), 0, keepdims=True))
        sums_ref[...] = by_domain(first, second, domain_ref)
        return
    for lane in range(0, chans, LANES):
        lanes = slice(lane, lane + LANES)
        first, second = [], []
        for f in range(frames):
            at = slice(f * pixels, (f + 1) * pixels)
            mean, inv = frame_tables(lst_ref[:, lanes], domain_ref[f], counts)
            xhat = (lpre_ref[at, lanes] - mean) * inv
            act = xhat * lgain_ref[:, lanes] + lbias_ref[:, lanes]
            s = sigmoid(act)
            steep = s * (1.0 + act * (1.0 - s))
            top, up, mix = (row_pairs(x, cols) for x in (act * s, out[at, lanes], mix_ref[at, lanes]))
            weight = window_weights(top)
            pooled = pair_sums(weight[0] * top[0] + weight[1] * top[1])
            d_pool = pair_sums(weight[0] * up[0] + weight[1] * up[1])
            flow = [m + d_pool for m in mix]
            d_w = [u * pooled + fl * t for u, fl, t in zip(up, flow, top)]
            centre = pair_sums(weight[0] * d_w[0] + weight[1] * d_w[1])
            d_top = jnp.stack([w * (fl + d - centre) for w, fl, d in zip(weight, flow, d_w)], 1)
            g = d_top.reshape(pixels, LANES) * steep
            out_ref[at, lanes] = g
            first.append(jnp.sum(fold(g), 0, keepdims=True))
            second.append(jnp.sum(fold(g * xhat), 0, keepdims=True))
        sums_ref[:, lanes] = by_domain(first, second, domain_ref)


def backward_layer(geom, domain, top, kernel, lower, added=None, mix=None):
    frames, rows, cols, _ = geom
    pix, width = top[0].shape
    chans = kernel.shape[0] // 9
    args = [domain, *top, kernel]
    specs = [SCALARS] + [whole(x.shape) for x in top] + [ANYWHERE]
    win = (3, frames, rows + 2, cols, width)
    outs = [sds(win, BF16), sds((pix, chans), F32)]
    extra = ([] if added is None else [added]) + list(lower) + ([] if mix is None else [mix])
    epilogue = "silu" if mix is None else "pool"
    outs.append(sds((4, chans), F32))
    return pl.pallas_call(
        functools.partial(backward_kernel, geom, added is not None, epilogue),
        grid=(1,),
        in_specs=specs + [whole(x.shape) for x in extra],
        out_specs=[whole(o.shape) for o in outs],
        out_shape=outs,
        scratch_shapes=[pltpu.VMEM(kernel.shape, BF16), pltpu.SemaphoreType.DMA],
        compiler_params=params(1),
        cost_estimate=cost(2 * pix * kernel.size, kernel.size * 2 + pix * 10240),
    )(*args, *extra)


def low_kernel(geom, domain_ref, g_ref, pre_ref, st_ref, sm_ref, gain_ref, win_ref):
    frames, rows, cols, counts = geom
    pixels = rows * cols
    clear_edges(win_ref, rows)
    for f in range(frames):
        tables = back_tables(st_ref, sm_ref, gain_ref, domain_ref[f], counts)

        def one_row(r, _):
            at = pl.multiple_of(f * pixels + r * cols, cols)
            low = norm_back_rows(g_ref[pl.ds(at, cols), :], pre_ref[pl.ds(at, cols), :], tables)
            put_windows(win_ref, f, r, low, cols)
            return 0

        lax.fori_loop(0, rows, one_row, 0, unroll=2)


def low_layer(geom, domain, top):
    frames, rows, cols, _ = geom
    pix, width = top[0].shape
    out = sds((3, frames, rows + 2, cols, width), BF16)
    return pl.pallas_call(
        functools.partial(low_kernel, geom),
        grid=(1,),
        in_specs=[SCALARS] + [whole(x.shape) for x in top],
        out_specs=whole(out.shape),
        out_shape=out,
        compiler_params=params(1),
        cost_estimate=cost(pix * width * 20, pix * width * 14),
    )(domain, *top)


def input_kernel(geom, win_ref, kernel_ref, out_ref):
    rows = geom[1]
    step = pl.program_id(0)
    chans = kernel_ref.shape[0] // 3
    source = jnp.concatenate([window(win_ref, 2 - b, 2 - step, rows) for b in range(3)], 1)
    weight = jnp.concatenate([kernel_ref[b * chans : (b + 1) * chans, :] for b in range(3)], 1)
    part = lax.dot_general(source, weight, (((1,), (1,)), ((), ())), preferred_element_type=F32)

    @pl.when(step == 0)
    def _():
        out_ref[...] = part

    @pl.when(step > 0)
    def _():
        out_ref[...] += part


def input_layer(geom, win, kernel):
    frames, rows, cols, _ = geom
    pix = frames * rows * cols
    chans, width = kernel.shape[0] // 9, kernel.shape[1]
    return pl.pallas_call(
        functools.partial(input_kernel, geom),
        grid=(3,),
        in_specs=[whole(win.shape), pl.BlockSpec((3 * chans, width), lambda a: (a, 0))],
        out_specs=whole((pix, chans)),
        out_shape=sds((pix, chans), F32),
        compiler_params=params(1),
        cost_estimate=cost(2 * pix * kernel.size, kernel.size * 2 + pix * 4096),
    )(win, in_hbm(kernel))


class Member:
    def __init__(self, at, shape, dp, fsdp, split=False):
        self.at, self.shape, self.split = at, shape, split
        self.vr = shape[0] // dp // (2 if split else 1)
        self.blocks = shape[1] // fsdp * (2 if split else 1) // LANES
        self.rows = self.vr * self.blocks

    def spots(self, i, j):
        if self.split:
            row, col = i * 2 * self.vr + (j & 1) * self.vr, (j >> 1) * self.blocks * LANES
        else:
            row, col = i * self.vr, j * self.blocks * LANES
        for k in range(self.blocks):
            yield self.at + k * self.vr, row, col + k * LANES


def collect_kernel(member, parts, me_ref, *refs):
    out_ref, sem = refs[-2:]
    fetch(member, parts, me_ref, refs[:-2], out_ref, sem)
    arrived(out_ref, sem)


def collect(pieces):
    return pl.pallas_call(
        functools.partial(collect_kernel, pieces.member, pieces.parts),
        in_specs=[SCALARS] + [ANYWHERE] * len(pieces.sources),
        out_specs=whole(pieces.shape),
        out_shape=sds(pieces.shape, BF16),
        scratch_shapes=[pltpu.SemaphoreType.DMA],
        grid=(1,),
        compiler_params=params(1),
        cost_estimate=cost(0, 4 * pieces.shape[0] * pieces.shape[1]),
    )(pieces.me, *pieces.sources)


def affine_kernel(member, parts, me_ref, *refs):
    out_ref, rows_ref, sem = refs[-3:]
    fetch(member, parts, me_ref, refs[:-3], rows_ref, sem)
    arrived(rows_ref, sem)
    width = out_ref.shape[1] // 32
    for d in range(32):
        rows = rows_ref[16 * d : 16 * d + 16].astype(F32)
        both = jnp.concatenate([rows[:8], rows[8:]], 1)
        out_ref[:, d * width : (d + 1) * width] = (both[0:2] + both[2:4] + both[4:6])[:, :width]


def collect_affine(pieces):
    return pl.pallas_call(
        functools.partial(affine_kernel, pieces.member, pieces.parts),
        in_specs=[SCALARS] + [ANYWHERE] * len(pieces.sources),
        out_specs=whole((2, 5120)),
        out_shape=sds((2, 5120), F32),
        scratch_shapes=[pltpu.VMEM((512, LANES), BF16), pltpu.SemaphoreType.DMA],
        grid=(1,),
        compiler_params=params(1),
        cost_estimate=cost(10000000, 1000000),
    )(pieces.me, *pieces.sources)


def weight_parts(geom, step, act_ref, low_ref, tr_ref):
    rows = geom[1]

    @pl.when(step == 0)
    def _():
        tr_ref[...] = act_ref[...].astype(F32).T.astype(BF16)

    if len(low_ref.shape) == 5:
        for b in range(3):
            yield jnp.dot(tr_ref[...], window(low_ref, 2 - b, 2 - step, rows), preferred_element_type=F32)
    else:
        yield jnp.dot(tr_ref[...], low_ref[...], preferred_element_type=F32)


def weight_kernel(geom, act_ref, low_ref, out_ref, tr_ref):
    chans = tr_ref.shape[0]
    for b, part in enumerate(weight_parts(geom, pl.program_id(0), act_ref, low_ref, tr_ref)):
        out_ref[b * chans : (b + 1) * chans, :] = part.astype(BF16)


def weight_layer(geom, act, low):
    pix, chans = act.shape
    win = low.ndim == 5
    width = low.shape[-1]
    steps = 3 if win else 1
    out = sds((9 * chans if win else chans, width), BF16)
    return pl.pallas_call(
        functools.partial(weight_kernel, geom),
        grid=(steps,),
        in_specs=[whole(act.shape), whole(low.shape)],
        out_specs=pl.BlockSpec((out.shape[0] // steps, width), lambda a: (a, 0)),
        out_shape=out,
        scratch_shapes=[pltpu.VMEM((chans, pix), BF16)],
        compiler_params=params(1),
        cost_estimate=cost(2 * pix * out.size, out.size * 2 + pix * 4096),
    )(act, low)


def weight_blocks_kernel(geom, member, steps, held, *refs):
    refs = list(refs)
    me_ref, act_ref, low_ref = (refs.pop(0) for _ in range(3))
    if held:
        del refs[:3]
    near_ref, far_ref, send_ref, scr_ref, tr_ref, sem = refs
    step = pl.program_id(0)
    chans = tr_ref.shape[0]
    for b, part in enumerate(weight_parts(geom, step, act_ref, low_ref, tr_ref)):
        scr_ref[pl.ds(pl.multiple_of(step * 3 * chans, chans) + b * chans, chans), :] = part.astype(BF16)
    me = me_ref[0]
    share = member.shape[0] // 8
    done = 0
    for s in range(steps):
        ready = member.shape[0] * (s + 1) // steps // share

        @pl.when(step == s)
        def _(done=done, ready=ready):
            for i in range(done, ready):
                e = i ^ (me >> 2)
                q = ((e & 1) << 2) | (e & 2) | (e >> 2)
                for jd in range(4):
                    dst = send_ref.at[jd >> 1, q] if jd & 1 else (near_ref, far_ref)[jd >> 1].at[q]
                    for at, row, col in member.spots(i, (me & 3) ^ jd):
                        pltpu.make_async_copy(
                            scr_ref.at[span(row, member.vr), span(col, LANES)], dst.at[pl.ds(at, member.vr)], sem
                        ).start()

        done = ready

    @pl.when(step == steps - 1)
    def _():
        pltpu.make_async_copy(scr_ref, scr_ref, sem).wait()


def weight_blocks(geom, me, act, low, member, rows, held=None):
    pix, chans = act.shape
    win = low.ndim == 5
    steps = 3 if win else 1
    shard = (rows, LANES)
    outs = [sds((8, *shard), BF16)] * 2 + [sds((2, 8, *shard), BF16)]
    args = [me, act, low] + list(held or ())
    size = member.shape[0] * member.shape[1]
    return pl.pallas_call(
        functools.partial(weight_blocks_kernel, geom, member, steps, held is not None),
        grid=(steps,),
        in_specs=[SCALARS, whole(act.shape), whole(low.shape)] + [ANYWHERE] * len(held or ()),
        out_specs=[ANYWHERE] * 3,
        out_shape=outs,
        scratch_shapes=[pltpu.VMEM(member.shape, BF16), pltpu.VMEM((chans, pix), BF16), pltpu.SemaphoreType.DMA],
        input_output_aliases={} if held is None else {3: 0, 4: 1, 5: 2},
        compiler_params=params(1),
        cost_estimate=cost(2 * pix * size, size * 2 + pix * 4096),
    )(*args)


def weight_piece_kernel(geom, member, step, held, *refs):
    rows = geom[1]
    refs = list(refs)
    me_ref, act_ref, low_ref = (refs.pop(0) for _ in range(3))
    if held:
        del refs[:3]
    near_ref, far_ref, send_ref = (refs.pop(0) for _ in range(3))
    if step == 0:
        tr_ref = refs.pop(0)
        tr_ref[...] = act_ref[...].astype(F32).T.astype(BF16)
    else:
        tr_ref = act_ref
    scr_ref, sem = refs
    chans = tr_ref.shape[0]
    for b in range(3):
        part = jnp.dot(tr_ref[...], window(low_ref, 2 - b, 2 - step, rows), preferred_element_type=F32)
        scr_ref[b * chans : (b + 1) * chans, :] = part.astype(BF16)
    me = me_ref[0]
    start, stop = 3 * chans * step, 3 * chans * (step + 1)
    for i in range(8):
        first, last = max(start, i * member.vr), min(stop, (i + 1) * member.vr)
        if first >= last:
            continue
        e = i ^ (me >> 2)
        q = ((e & 1) << 2) | (e & 2) | (e >> 2)
        for jd in range(4):
            dst = send_ref.at[jd >> 1, q] if jd & 1 else (near_ref, far_ref)[jd >> 1].at[q]
            col = ((me & 3) ^ jd) * LANES
            pltpu.make_async_copy(
                scr_ref.at[pl.ds(first - start, last - first), span(col, LANES)],
                dst.at[pl.ds(member.at + first - i * member.vr, last - first)],
                sem,
            ).start()
    arrived(scr_ref, sem)


def weight_piece(geom, me, act, low, member, rows, step, held=None):
    chans = member.shape[0] // 9
    pix, width = low.shape[1] * geom[1] * geom[2], low.shape[-1]
    shard = (rows, LANES)
    outs = [sds((8, *shard), BF16)] * 2 + [sds((2, 8, *shard), BF16)]
    out_specs = [ANYWHERE] * 3
    if step == 0:
        outs.append(sds((chans, pix), BF16))
        out_specs.append(whole((chans, pix)))
    args = [me, act, low] + list(held or ())
    return pl.pallas_call(
        functools.partial(weight_piece_kernel, geom, member, step, held is not None),
        grid=(1,),
        in_specs=[SCALARS, whole(act.shape), whole(low.shape)] + [ANYWHERE] * len(held or ()),
        out_specs=out_specs,
        out_shape=outs,
        scratch_shapes=[pltpu.VMEM((3 * chans, width), BF16), pltpu.SemaphoreType.DMA],
        input_output_aliases={} if held is None else {3: 0, 4: 1, 5: 2},
        compiler_params=params(1),
        cost_estimate=cost(2 * pix * 3 * chans * width, chans * width * 6),
    )(*args)


def point_kernel(geom, pieces, *refs):
    frames, rows, cols, _ = geom
    pixels = rows * cols
    refs = list(refs)
    domain_ref, act_ref = refs.pop(0), refs.pop(0)
    if pieces:
        out_ref, sums_ref, matrix_ref, sem = refs[-4:]
        fetch(*pieces, refs[0], refs[1:-4], matrix_ref, sem)
        arrived(matrix_ref, sem)
    else:
        matrix_ref, out_ref, sums_ref = refs
    for lane in range(0, out_ref.shape[-1], 256):
        lanes = slice(lane, lane + 256)
        out = jnp.dot(act_ref[...], matrix_ref[:, lanes], preferred_element_type=F32)
        out_ref[:, lanes] = out
        sums_ref[:, lanes] = value_sums([out[f * pixels : (f + 1) * pixels] for f in range(frames)], domain_ref)


def point_layer(geom, domain, act, mat):
    pix, chans = act.shape
    width = mat.shape[1]
    pieces = isinstance(mat, Pieces)
    outs = [sds((pix, width), F32), sds((4, width), F32)] + [sds(mat.shape, BF16)] * pieces
    args = [domain, act] + ([mat.me, *mat.sources] if pieces else [mat])
    specs = [SCALARS, whole(act.shape)]
    specs += [SCALARS] + [ANYWHERE] * len(mat.sources) if pieces else [whole(mat.shape)]
    return pl.pallas_call(
        functools.partial(point_kernel, geom, (mat.member, mat.parts) if pieces else None),
        in_specs=specs,
        out_specs=[whole(o.shape) for o in outs],
        out_shape=outs,
        scratch_shapes=[pltpu.SemaphoreType.DMA] * pieces,
        grid=(1,),
        compiler_params=params(1),
        cost_estimate=cost(2 * pix * chans * width, chans * width * 2 + pix * width * 4),
    )(*args)


def point_back_kernel(geom, added, domain_ref, g_ref, pre_ref, st_ref, sm_ref, gain_ref, mat_ref, *refs):
    frames, rows, cols, counts = geom
    pixels = rows * cols
    low_ref, out_ref = refs[-2:]
    for f in range(frames):
        tables = back_tables(st_ref, sm_ref, gain_ref, domain_ref[f], counts)

        def one_row(r, _):
            at = pl.multiple_of(f * pixels + r * cols, cols)
            low = norm_back_rows(g_ref[pl.ds(at, cols), :], pre_ref[pl.ds(at, cols), :], tables)
            low_ref[pl.ds(at, cols), :] = low.astype(BF16)
            return 0

        lax.fori_loop(0, rows, one_row, 0, unroll=2)
    part = lax.dot_general(low_ref[...], mat_ref[...], (((1,), (1,)), ((), ())), preferred_element_type=F32)
    out_ref[...] = part + refs[0][...] if added else part


def point_back(geom, domain, g, pre, stats, sums, gain, mat, added=None):
    pix, width = g.shape
    chans = mat.shape[0]
    args = (domain, g, pre, stats, sums, gain, mat) + (() if added is None else (added,))
    outs = [sds((pix, width), BF16), sds((pix, chans), F32)]
    return pl.pallas_call(
        functools.partial(point_back_kernel, geom, added is not None),
        grid=(1,),
        in_specs=[SCALARS] + [whole(x.shape) for x in args[1:]],
        out_specs=[whole(o.shape) for o in outs],
        out_shape=outs,
        compiler_params=params(1),
        cost_estimate=cost(2 * pix * mat.size, mat.size * 2 + pix * width * 10),
    )(*args)


def share_kernel(widths, me_ref, *refs):
    *sums, gain_ref, bias_ref, flat_ref = refs
    at = 0
    for ref, width in zip(sums, widths):
        flat_ref[0:1, at : at + width] = ref[2:3, :] + ref[3:4, :]
        flat_ref[1:2, at : at + width] = ref[0:1, :] + ref[1:2, :]
        at += width
    share = gain_ref.shape[1]
    mine = pltpu.roll(flat_ref[...], at - me_ref[0] * share, 1)
    gain_ref[...] = mine[0:1, :share]
    bias_ref[...] = mine[1:2, :share]


def share_of(me, sums, share):
    widths = [x.shape[1] for x in sums]
    got = pl.pallas_call(
        functools.partial(share_kernel, widths),
        grid=(1,),
        in_specs=[SCALARS] + [whole(x.shape) for x in sums],
        out_specs=[whole((1, share))] * 2,
        out_shape=[sds((1, share), F32)] * 2,
        scratch_shapes=[pltpu.VMEM((8, sum(widths)), F32)],
        compiler_params=params(1),
        cost_estimate=cost(0, 100000),
    )(me, *(in_hbm(x) for x in sums))
    return [x[0] for x in got]


AXES = ("dp", "fsdp")
CORE, X, Y, Z_NEAR, Z_FAR = range(5)
ORDER = (CORE, Z_NEAR, Z_FAR, X, Y)


def swap(x, bit):
    n = lax.axis_size(AXES)
    return lax.ppermute(x, AXES, [(i, i ^ (1 << bit)) for i in range(n)])


def bit_of(bit):
    return (lax.axis_index(AXES) >> bit) & 1


def all_bits():
    return range(lax.axis_size(AXES).bit_length() - 1)


def tied(value, to):
    return value if to is None else lax.optimization_barrier((value, to))[0]


class Links:
    def __init__(self):
        self.under_way = {}

    def busy(self, bit, *values):
        self.under_way.setdefault(bit, []).extend(values)

    def total(self, x, after=None, order=None, fill=()):
        bits = order if order and len(all_bits()) == 5 else all_bits()
        fill = list(fill)
        for bit in bits:
            for value in self.under_way.pop(bit, ()):
                x = tied(x, value)
            got = swap(x, bit)
            if fill and (bit != CORE or len(bits) != 5):
                got = tied(got, fill.pop(0)(x))
            x = x + got
            for start in (after or {}).get(bit, ()):
                x = tied(x, start(x))
        for work in fill:
            work(x)
        return x


def half_rows(rows):
    return rows // 32 * 16


class Gather:
    def __init__(self, links, shard):
        self.links, self.shard, self.cut = links, shard, half_rows(shard.shape[0])
        self.sources = None

    def far(self, to=None):
        self.z = tied(self.shard, to)
        self.got = swap(self.z, Z_FAR)

    def near(self, to=None):
        self.z = jnp.stack(tied((self.z, self.got), to))
        self.got = swap(self.z, Z_NEAR)

    def first(self, to=None):
        z = jnp.concatenate(tied((self.z, self.got), to))
        self.a, self.b = z[:, : self.cut], z[:, self.cut :]
        self.got = swap(self.a, Y), swap(self.b, X)

    def second(self, to=None):
        a, b, (got_a, got_b) = tied((self.a, self.b, self.got), to)
        self.a, self.b = jnp.concatenate([a, got_a]), jnp.concatenate([b, got_b])
        self.got = swap(self.a, X), swap(self.b, Y)

    def busy(self):
        if isinstance(self.got, tuple):
            self.links.busy(X, self.got[0])
            self.links.busy(Y, self.got[1])
        else:
            self.links.busy(CORE, self.got)

    def finish(self, to=None):
        rows = self.shard.shape[0]
        self.a, self.b, self.got = tied((self.a, self.b, self.got), to)
        self.sources, self.parts = [], []
        for core in (0, 1):
            for n, value in enumerate((self.a, self.got[0], self.b, self.got[1])):
                z = [8 * (k >> 1) + 16 * (k & 1) for k in range(4)]
                if n < 2:
                    masks = [core + 2 * n + 4 * y + m for y in (0, 1) for m in z]
                else:
                    masks = [core + 4 * (n - 2) + 2 * x + m for x in (0, 1) for m in z]
                self.parts.append((0, self.cut, masks) if n < 2 else (self.cut, rows - self.cut, masks))
                self.sources.append(swap(value, CORE) if core else value)

    def pieces(self, member):
        return Pieces(member, self.parts, number(1), self.sources)


def number(entries):
    return jnp.full((entries,), lax.axis_index(AXES), jnp.int32)


def plus(a, b):
    return (a.astype(F32) + b.astype(F32)).astype(BF16)


def add_kernel(jobs, *refs):
    refs = list(refs)
    count = sum(n for _, n, _ in jobs)
    ins, outs = refs[:count], refs[count:]
    for work, n_in, n_out in jobs:
        work(*ins[:n_in], *outs[:n_out])
        del ins[:n_in], outs[:n_out]


def add_all(*jobs):
    ins = [x for _, job, _ in jobs for x in job]
    outs = [x for _, _, job in jobs for x in job]
    got = pl.pallas_call(
        functools.partial(add_kernel, [(work, len(i), len(o)) for work, i, o in jobs]),
        grid=(1,),
        in_specs=[whole(x.shape) for x in ins],
        out_specs=[whole(x.shape) for x in outs],
        out_shape=outs,
        compiler_params=params(1),
        cost_estimate=cost(0, sum(x.size * 2 for x in ins + outs)),
    )(*ins)
    result = []
    for _, _, job in jobs:
        result.append(got[: len(job)])
        got = got[len(job) :]
    return result


def first_work(cut, near, far, got, a, send_a, b, send_b):
    a[...] = plus(near[:, :cut], got[0, :, :cut])
    send_a[...] = plus(far[:, :cut], got[1, :, :cut])
    for half, out in enumerate((b, send_b)):
        s = slice(4 * half, 4 * half + 4)
        out[0] = plus(near[s, cut:], got[0, s, cut:])
        out[1] = plus(far[s, cut:], got[1, s, cut:])


def second_work(a, b, got_a, got_b, a_out, send_a, b_out, send_b):
    a_out[...] = plus(a[:4], got_a[:4])
    send_a[...] = plus(a[4:], got_a[4:])
    b_out[...] = plus(b[0], got_b[0])
    send_b[...] = plus(b[1], got_b[1])


def near_work(cut, a, b, got_a, got_b, z, send):
    for half, out in enumerate((z, send)):
        s = slice(2 * half, 2 * half + 2)
        out[:, :cut] = plus(a[s], got_a[s])
        out[:, cut:] = plus(b[s], got_b[s])


def far_work(z, got, z_out, send):
    z_out[...] = plus(z[0], got[0])
    send[...] = plus(z[1], got[1])


def finish_work(z, got, out):
    out[...] = z[...].astype(F32) + got[...].astype(F32)


class Scatter:
    def __init__(self, links, blocks):
        self.links, self.blocks = links, blocks
        self.rows = blocks[0].shape[1]
        self.cut = half_rows(self.rows)
        self.got = swap(blocks[2], CORE)

    def shape(self, *dims):
        return sds((*dims, LANES), BF16)

    def first_job(self):
        c, r = self.cut, self.rows - self.cut
        outs = [self.shape(8, c)] * 2 + [self.shape(2, 4, r)] * 2
        return functools.partial(first_work, c), [*self.blocks[:2], self.got], outs

    def first(self, a, send_a, b, send_b):
        self.a, self.b = a, b
        self.got = swap(send_a, X), swap(send_b, Y)

    def second_job(self):
        c, r = self.cut, self.rows - self.cut
        return second_work, [self.a, self.b, *self.got], [self.shape(4, c)] * 2 + [self.shape(4, r)] * 2

    def second(self, a, send_a, b, send_b):
        self.a, self.b = a, b
        self.got = swap(send_a, Y), swap(send_b, X)

    def near_job(self):
        return functools.partial(near_work, self.cut), [self.a, self.b, *self.got], [self.shape(2, self.rows)] * 2

    def near(self, to=None):
        self.got = swap(tied(self.send, to), Z_NEAR)

    def far_job(self):
        return far_work, [self.z, self.got], [self.shape(self.rows)] * 2

    def far(self, z, send):
        self.z = z
        self.got = swap(send, Z_FAR)

    def finish_job(self):
        return finish_work, [self.z, self.got], [sds((self.rows, LANES), F32)]


def add_after(to, *jobs):
    return add_all(*((work, tied(ins, to), outs) for work, ins, outs in jobs))


def rows_of_chip(shard):
    half = shard.shape[0] // 2
    odd = bit_of(CORE) == 1
    mine = jnp.where(odd, shard[half:], shard[:half])
    got = swap(jnp.where(odd, shard[:half], shard[half:]), CORE)
    return jnp.concatenate([jnp.where(odd, got, mine), jnp.where(odd, mine, got)], 1)


def columns_of_core(rows):
    half = rows.shape[1] // 2
    odd = bit_of(CORE) == 1
    mine = jnp.where(odd, rows[:, half:], rows[:, :half])
    got = swap(jnp.where(odd, rows[:, :half], rows[:, half:]), CORE)
    return jnp.concatenate([jnp.where(odd, got, mine), jnp.where(odd, mine, got)], 0)


def pack(x):
    return jnp.concatenate([x[:, k : k + LANES] for k in range(0, x.shape[1], LANES)], 0)


def unpack(x, blocks):
    rows = x.shape[0] // blocks
    return jnp.concatenate([x[k * rows : (k + 1) * rows] for k in range(blocks)], 1)


def in_three(x):
    high = lax.reduce_precision(x, 8, 7)
    middle = lax.reduce_precision(x - high, 8, 7)
    return jnp.stack([high, middle, x - high - middle]).astype(BF16)


def gather(x):
    x = x[None]
    for bit in all_bits():
        other = swap(x, bit)
        high = bit_of(bit) == 1
        x = jnp.concatenate([jnp.where(high, other, x), jnp.where(high, x, other)], 0)
    return x


def scatter(x):
    for bit in reversed(all_bits()):
        half = x.shape[0] // 2
        high = bit_of(bit) == 1
        send = jnp.where(high, x[:half], x[half:])
        keep = jnp.where(high, x[half:], x[:half])
        x = plus(keep, swap(send, bit))
    return x[0]


def gather_matrix(shard):
    dp, fsdp = lax.axis_size("dp"), lax.axis_size("fsdp")
    rows, cols = shard.shape
    full = gather(shard).reshape(dp, fsdp, rows, cols)
    return full.transpose(0, 2, 1, 3).reshape(dp * rows, fsdp * cols)


def scatter_matrix(full):
    dp, fsdp = lax.axis_size("dp"), lax.axis_size("fsdp")
    rows, cols = full.shape[0] // dp, full.shape[1] // fsdp
    parts = full.reshape(dp, rows, fsdp, cols).transpose(0, 2, 1, 3)
    return scatter(parts.reshape(dp * fsdp, rows, cols)).astype(F32)


class AnyMesh:
    def __init__(self, links, geom, weights, gains, biases):
        self.geom = geom
        self.mats = {name: gather_matrix(w) for name, w in weights.items()}
        self.affine = gather(jnp.stack([gains, biases])).transpose(1, 0, 2).reshape(2, 1, -1)
        self.grads, self.ready = {}, None

    def get(self, name):
        return self.mats[name]

    def whole(self, name):
        return self.mats[name]

    def put(self, name, matrix):
        pass

    def layer_done(self, n, local):
        pass

    def during(self, point):
        return {}

    def add(self, name, act, low):
        got = weight_layer(self.geom, act, low)
        self.grads[name] = scatter_matrix(got)
        return got

    def pieces(self, name, act, low):
        return [lambda x: self.add(name, act, low)]

    def send(self, n, to=None):
        pass

    def after_layer(self, n, local):
        pass

    def now(self):
        return None

    def tail(self, blocks, kernels):
        return [kernel(None) for kernel in kernels]


class ThisMesh:
    def __init__(self, links, geom, weights, gains, biases):
        self.geom, self.links = geom, links
        self.me = number(1)
        sizes = (8, 4)
        full = {n: (w.shape[0] * 8, w.shape[1] * 4) for n, w in weights.items()}
        splits = ("six", "gating")
        g1 = Gather(links, weights["one"])
        g1.far()
        g1.near()
        packed = {n: pack(rows_of_chip(tied(w, g1.got)) if n in splits else w) for n, w in weights.items()}
        gains, biases = tied((gains, biases), g1.z)
        affine = in_three(jnp.stack([gains, biases])).reshape(6, -1)
        affine = jnp.pad(affine, ((0, 2), (0, 2 * LANES - affine.shape[1])))
        affine = jnp.concatenate([affine[:, :LANES], affine[:, LANES:]])
        groups = (("one",), ("two",), ("three",), ("four",), ("five",), ("six", "gating", "attend"))
        self.g, self.members, self.group = [], {}, {}
        for names in groups:
            at = 0
            for name in names:
                self.members[name] = Member(at, full[name], *sizes, split=name in splits)
                at += self.members[name].rows
            if names == ("one",):
                group = g1
            else:
                group = Gather(links, jnp.concatenate([packed[n] for n in names] + [affine] * (names == ("two",))))
            self.g.append(group)
            self.group.update((n, group) for n in names)
        g2 = self.g[1]
        g2.far()
        g1.first()
        g2.near(g1.got)
        g1.second()
        g1.finish()
        self.g[2].far(g2.got)
        g2.first(g1.got)
        self.ready = self.g[5].shard
        self.mats = {}
        self.grads, self.blocks, self.sums = {}, {}, {}
        self.homes, self.rows = {}, {}
        for names in (("six", "gating"), ("five",), ("four", "attend"), ("three",), ("two",), ("one",)):
            at = 0
            for name in names:
                self.homes[name] = Member(at, full[name], *sizes, split=name in splits)
                at += self.homes[name].rows
            self.rows.update((name, at) for name in names)

    def layer_done(self, n, local):
        if n < 6:
            self.g[n].second((local, self.g[n + 1].got) if n < 5 else local)
            self.g[n].busy()

    def get(self, name):
        if name in self.mats:
            return self.mats[name]
        group = self.group[name]
        self.mats[name] = group.pieces(self.members[name])
        if name == "two":
            self.affine = collect_affine(group.pieces(FlatMember(self.members["two"].rows, 16)))[:, None]
        return self.mats[name]

    def whole(self, name):
        self.mats[name] = collect(self.get(name))
        return self.mats[name]

    def put(self, name, matrix):
        self.mats[name] = matrix

    def during(self, point):
        if point <= 5:

            def x_done(x):
                self.g[point].finish(x)

            if point == 5:
                return {X: [x_done]}
            group = self.g[point + 1]

            def z_done(x):
                group.near(x)

            def y_done(x):
                group.first(x)
                if point < 4:
                    self.g[point + 2].far(x)

            return {Z_FAR: [z_done], X: [x_done], Y: [y_done]}
        n = 14 - point

        def z_done(x):
            self.sums[n + 2].near(x)

        def x_done(x):
            (got,) = add_after(x, self.sums[n + 2].far_job())
            self.sums[n + 2].far(*got)
            return got[0]

        def y_done(x):
            if n == 2:
                self.send(2)
                got = add_after(x, self.sums[2].first_job(), self.sums[4].far_job())
                self.sums[2].first(*got[0])
                self.sums[4].far(*got[1])
            else:
                (got,) = add_after(x, self.sums[n + 1].second_job())
                self.sums[n + 1].second(*got)

        if n == 2:
            return {Z_FAR: [z_done], Y: [y_done]}
        return {Z_FAR: [z_done], X: [x_done], Y: [y_done]} if n < 5 else {Y: [y_done]}

    def add(self, name, act, low):
        n = NUMBER[name]
        self.blocks[n] = weight_blocks(
            self.geom, self.me, act, low, self.homes[name], self.rows[name], self.blocks.get(n)
        )
        return self.blocks[n][0]

    def pieces(self, name, act, low):
        def piece(step):
            def work(x):
                n = NUMBER[name]
                if step == 0:
                    *self.blocks[n], self.turned = weight_piece(
                        self.geom, self.me, tied(act, x), low, self.homes[name], self.rows[name], 0
                    )
                else:
                    self.blocks[n] = weight_piece(
                        self.geom, self.me, tied(self.turned, x), low, self.homes[name], self.rows[name], step, self.blocks[n]
                    )
                return self.blocks[n][0]

            return work

        return [piece(step) for step in range(3)]

    def send(self, n, to=None):
        near, far, away = self.blocks[n]
        self.sums[n] = Scatter(self.links, (near, far, tied(away, to)))

    def after_layer(self, n, local):
        jobs = [self.sums[n + 1].first_job()]
        if n < 5:
            jobs.append(self.sums[n + 2].near_job())
        if n < 4:
            jobs.append(self.sums[n + 3].finish_job())
        got = add_after(local, *jobs)
        self.sums[n + 1].first(*got[0])
        self.links.busy(X, *self.sums[n + 1].got)
        if n < 5:
            s = self.sums[n + 2]
            s.z, s.send = got[1]
        if n < 4:
            (self.sums[n + 3].out,) = got[2]

    def now(self):
        return self.sums[3].a

    def tail(self, blocks, kernels):
        two, three, four = (self.sums[n] for n in (2, 3, 4))
        outs = [kernels[0](blocks)]
        got = add_after(outs[0], two.second_job(), three.second_job(), four.finish_job())
        two.second(*got[0])
        three.second(*got[1])
        (four.out,) = got[2]
        ((two.z, two.send),) = add_after(got[0][0], two.near_job())
        two.near()
        self.send(1, two.send)
        one = self.sums[1]
        (got,) = add_after(two.z, one.first_job())
        one.first(*got)
        outs.append(kernels[1](got[0]))
        got = add_after(got[0], two.far_job(), three.near_job())
        two.far(*got[0])
        three.z, three.send = got[1]
        three.near()
        (got,) = add_after(got[0][0], one.second_job())
        one.second(*got)
        got = add_after(got[0], one.near_job(), two.finish_job(), three.far_job())
        one.z, one.send = got[0]
        (two.out,) = got[1]
        one.near()
        three.far(*got[2])
        (got,) = add_after(one.z, one.far_job())
        one.far(*got)
        ((three.out,),) = add_after(got[0], three.finish_job())
        ((one.out,),) = add_after(three.out, one.finish_job())
        for name, m in self.homes.items():
            out = unpack(self.sums[NUMBER[name]].out[m.at : m.at + m.rows], m.blocks)
            self.grads[name] = columns_of_core(out) if m.split else out
        return outs


NUMBER = dict(one=1, two=2, three=3, attend=4, four=4, five=5, six=6, gating=6)


class FlatMember:
    def __init__(self, at, rows):
        self.at, self.vr, self.rows, self.blocks, self.shape = at, rows, rows, 1, (32 * rows, LANES)

    def spots(self, i, j):
        yield self.at, (i * 4 + j) * self.vr, 0


def body(
    frames_in,
    domain,
    kernel_one,
    kernel_two,
    kernel_three,
    attn_enc,
    kernel_four,
    kernel_five,
    kernel_six,
    attn_dec,
    gains,
    biases,
    enc_cot,
    dec_cot,
):
    frames, rows, cols, _ = frames_in.shape
    total_frames = frames * lax.axis_size(AXES)
    first = total_frames * 5 // 8
    counts = (float(first * rows * cols), float((total_frames - first) * rows * cols))
    geom = (frames, rows, cols, counts)
    pix = frames * rows * cols
    source = frames_in.reshape(pix, C_IN)
    enc_cot = enc_cot.transpose(0, 1, 3, 2, 4)
    dec_cot = dec_cot.reshape(pix, TASKS, C_DEC).transpose(1, 0, 2)
    weights = dict(
        one=kernel_one, two=kernel_two, three=kernel_three, attend=attn_enc,
        four=kernel_four, five=kernel_five, six=kernel_six, gating=attn_dec,
    )
    links = Links()
    this = lax.axis_size("dp") == 8 and lax.axis_size("fsdp") == 4
    w = (ThisMesh if this else AnyMesh)(links, geom, weights, gains, biases)

    def forward(name, source, norm=None):
        got = forward_layer(geom, domain, source, w.get(name), norm)
        w.put(name, got[-1])
        return got[:3] if norm is not None else got[:2]

    def point(name, act):
        got = point_layer(geom, domain, act, w.get(name))
        w.put(name, got[-1])
        return got[:2]

    pre_1, local = forward("one", tied(source, w.ready))
    w.layer_done(1, local)
    st_1 = links.total(local, w.during(1), ORDER)
    w.get("two")
    widths = (C_MID, C_MID, C_MID, TASKS * C_MID, C_MID, C_MID, C_DEC, TASKS * C_DEC)
    gain, bias, at = [], [], 0
    for width in widths:
        gain.append(w.affine[0, :, at : at + width])
        bias.append(w.affine[1, :, at : at + width])
        at += width
    pre_2, local, act_1 = forward("two", pre_1, (st_1, gain[0], bias[0]))
    w.layer_done(2, local)
    st_2 = links.total(local, w.during(2), ORDER)
    pre_3, local, act_2 = forward("three", pre_2, (st_2, gain[1], bias[1]))
    w.layer_done(3, local)
    st_3 = links.total(local, w.during(3), ORDER)
    unpooled = pool_layer(geom, domain, pre_3, st_3, gain[2], bias[2])
    pre_4, local = forward("four", unpooled)
    w.layer_done(4, local)
    st_4 = links.total(local, w.during(4), ORDER)
    pre_5, local, act_4 = forward("five", pre_4, (st_4, gain[4], bias[4]))
    w.layer_done(5, local)
    st_5 = links.total(local, w.during(5), ORDER)
    pre_g, local_g = point("gating", act_4)
    pre_6, local, act_5 = forward("six", pre_5, (st_5, gain[5], bias[5]))
    attend = w.whole("attend")
    wide = []

    def attend_part(k):
        def work(x):
            wide.append(point_layer(geom, domain, tied(act_2, x), attend[:, k * C_MID : (k + 1) * C_MID]))
            return wide[-1][0]

        return work

    both = links.total(jnp.concatenate([local, local_g], 1), None, ORDER, [attend_part(k) for k in range(TASKS)])
    st_6, st_g = both[:, :C_DEC], both[:, C_DEC:]
    pre_a = [p for p, _ in wide]
    task_maps, g_6, g_g, local = head_layer(
        geom, domain, pre_6, st_6, pre_g, st_g, gain[6], bias[6], gain[7], bias[7], dec_cot
    )
    both = links.total(jnp.concatenate([local] + [s for _, s in wide], 1), None, ORDER)
    sm_6, sm_g, st_a = both[:, :C_DEC], both[:, C_DEC : 4 * C_DEC], both[:, 4 * C_DEC :]
    st_a = [st_a[:, k * C_MID : (k + 1) * C_MID] for k in range(TASKS)]
    pool_args = (geom, domain, pre_3, st_3, gain[2], bias[2])
    masks = [(pre_a[k], st_a[k], gain[3][:, k * C_MID : (k + 1) * C_MID], bias[3][:, k * C_MID : (k + 1) * C_MID]) for k in range(TASKS)]

    win_6, g_5, local = backward_layer(
        geom, domain, (g_6, pre_6, st_6, sm_6, gain[6]), w.get("six"), lower=(pre_5, st_5, gain[5], bias[5])
    )
    early, gate_back = [], []

    def early_part(k):
        def work(x):
            early.append(pool_early(*pool_args, *masks[k], enc_cot[:, :, k], tied(pre_3, x), early[-1][0] if early else None))
            return early[-1][0]

        return work

    def gate_part(x):
        gate_back.extend(point_back(geom, domain, tied(g_g, x), pre_g, st_g, sm_g, gain[7], w.get("gating")))
        return gate_back[0]

    sm_5 = links.total(
        local, None, ORDER, [lambda x: w.add("six", act_5, tied(win_6, x)), gate_part, early_part(0), early_part(1)]
    )
    early_part(2)(sm_5)
    mix = early[-1][0]
    low_g, add_4 = gate_back
    blocks = w.add("gating", act_4, low_g)
    w.send(6, sm_5)
    win_5, g_4, local = backward_layer(
        geom,
        domain,
        (tied(g_5, blocks), pre_5, st_5, sm_5, gain[5]),
        w.get("five"),
        added=add_4,
        lower=(pre_4, st_4, gain[4], bias[4]),
    )
    w.after_layer(5, local)
    both = links.total(
        jnp.concatenate([local] + [e[2] for e in early], 1), w.during(9), ORDER, w.pieces("five", act_4, win_5)
    )
    w.send(5, both)
    sm_4 = both[:, :C_MID]
    sm_a = [both[:, (k + 1) * C_MID : (k + 2) * C_MID] for k in range(TASKS)]
    win_4, g_3, local = backward_layer(
        geom,
        domain,
        (g_4, pre_4, st_4, sm_4, gain[4]),
        w.get("four"),
        lower=(pre_3, st_3, gain[2], bias[2]),
        mix=mix,
    )
    w.after_layer(4, local)
    backs = []

    def attend_back(k):
        def work(x):
            backs.append(
                point_back(
                    geom, domain, tied(early[k][1], x), pre_a[k], st_a[k], sm_a[k], masks[k][2],
                    attend[:, k * C_MID : (k + 1) * C_MID], backs[-1][1] if backs else None,
                )
            )
            return backs[-1][1]

        return work

    sm_3 = links.total(local, w.during(10), ORDER, w.pieces("four", unpooled, win_4) + [attend_back(0)])
    attend_back(1)(sm_3)
    attend_back(2)(backs[-1][1])
    low_a = jnp.concatenate([low for low, _ in backs], 1)
    blocks = w.add("attend", act_2, low_a)
    w.send(4)
    win_3, g_2, local = backward_layer(
        geom,
        domain,
        (tied(g_3, blocks), pre_3, st_3, sm_3, gain[2]),
        w.get("three"),
        added=backs[-1][1],
        lower=(pre_2, st_2, gain[1], bias[1]),
    )
    w.after_layer(3, local)
    tasks = []

    def task_part(x):
        tasks.append(task_layer(geom, domain, tied(pre_3, x), *pool_args[3:], masks))
        return tasks[0]

    sm_2 = links.total(local, w.during(11), ORDER, w.pieces("three", act_2, win_3) + [task_part])
    w.send(3, sm_2)
    win_2, g_1, local = backward_layer(
        geom,
        domain,
        (g_2, pre_2, st_2, sm_2, gain[1]),
        w.get("two"),
        lower=(pre_1, st_1, gain[0], bias[0]),
    )
    w.after_layer(2, local)
    sm_1 = links.total(local, w.during(12), ORDER, w.pieces("two", act_1, win_2))
    win_1 = low_layer(geom, domain, (tied(g_1, w.now()), pre_1, st_1, sm_1, gain[0]))
    blocks = w.add("one", source, win_1)
    frames_grad, task_maps = w.tail(
        blocks,
        (
            lambda to: input_layer(geom, tied(win_1, to), w.get("one")),
            lambda to: tied(task_maps, to).transpose(1, 0, 2).reshape(frames, rows, cols, TASKS, C_DEC),
        ),
    )
    gains_grad, biases_grad = share_of(number(1), [sm_1, sm_2, sm_3, *sm_a, sm_4, sm_5, sm_6, sm_g], gains.shape[0])
    return (
        tasks[0].transpose(0, 1, 3, 2, 4),
        task_maps,
        frames_grad.reshape(frames, rows, cols, C_IN),
        *(w.grads[n] for n in ("one", "two", "three", "attend", "four", "five", "six", "gating")),
        gains_grad,
        biases_grad,
    )


def solution(mesh):
    whole_split = P(AXES)
    matrix = P("dp", "fsdp")
    return jax.shard_map(
        body,
        mesh=mesh,
        in_specs=(whole_split, whole_split) + (matrix,) * 8 + (whole_split,) * 4,
        out_specs=(whole_split,) * 3 + (matrix,) * 8 + (whole_split,) * 2,
        check_vma=False,
    )
```

```python
import functools

import jax
import jax.numpy as jnp
from jax import lax
from jax.experimental import pallas as pl
from jax.experimental.pallas import tpu as pltpu
from jax.sharding import PartitionSpec as P

C_IN = 256
C_MID = 512
C_DEC = 256
TASKS = 3
EPS = 1e-05
LANES = 128
F32 = jnp.float32
BF16 = jnp.bfloat16
COST = 0.1
VMEM_LIMIT = 12 * 1024 * 1024


def params(grid_dims=0):
    return pltpu.CompilerParams(
        vmem_limit_bytes=VMEM_LIMIT,
        dimension_semantics=("arbitrary",) * grid_dims if grid_dims else None,
    )


def cost(flops, size):
    return pl.CostEstimate(flops=int(flops * COST), bytes_accessed=int(size * COST), transcendentals=0)


def whole(shape):
    zeros = (0,) * len(shape)
    return pl.BlockSpec(shape, lambda *_: zeros, pipeline_mode=pl.Buffered(1))


SCALARS = pl.BlockSpec(memory_space=pltpu.SMEM)


def sds(shape, dtype):
    return jax.ShapeDtypeStruct(shape, dtype)


def sigmoid(v):
    return 0.5 * jnp.tanh(0.5 * v) + 0.5


def frame_tables(stats, domain_at, counts):
    first = domain_at == 0
    share = jnp.where(first, 1.0 / counts[0], 1.0 / counts[1])
    average = jnp.where(first, stats[0:1], stats[1:2]) * share
    square = jnp.where(first, stats[2:3], stats[3:4]) * share
    return average, lax.rsqrt(square - average * average + EPS)


def grad_tables(sums, domain_at, counts):
    first = domain_at == 0
    share = jnp.where(first, 1.0 / counts[0], 1.0 / counts[1])
    return (
        jnp.where(first, sums[0:1], sums[1:2]) * share,
        jnp.where(first, sums[2:3], sums[3:4]) * share,
    )


def by_domain(first, second, domain_ref):
    rows = []
    for per_frame in (first, second):
        for d in (0, 1):
            total = None
            for f, value in enumerate(per_frame):
                term = jnp.where(domain_ref[f] == d, value, jnp.zeros_like(value))
                total = term if total is None else total + term
            rows.append(total)
    return jnp.concatenate(rows, 0)


def fold(x):
    return jnp.sum(x.reshape(-1, 8, x.shape[-1]), 0)


def value_sums(parts, domain_ref, others=None):
    others = parts if others is None else others
    return by_domain(
        [jnp.sum(fold(p), 0, keepdims=True) for p in parts],
        [jnp.sum(fold(p * o), 0, keepdims=True) for p, o in zip(parts, others)],
        domain_ref,
    )


def put_windows(win_ref, f, row, value, cols):
    col = lax.broadcasted_iota(jnp.int32, value.shape, 0)
    left = jnp.where(col == 0, 0.0, pltpu.roll(value, 1, 0))
    right = jnp.where(col == cols - 1, 0.0, pltpu.roll(value, cols - 1, 0))
    win_ref[0, f, row + 1] = left.astype(BF16)
    win_ref[1, f, row + 1] = value.astype(BF16)
    win_ref[2, f, row + 1] = right.astype(BF16)


def clear_edges(win_ref, rows):
    shape = win_ref.shape
    for b in range(3):
        for f in range(shape[1]):
            win_ref[b, f, 0] = jnp.zeros(shape[3:], BF16)
            win_ref[b, f, rows + 1] = jnp.zeros(shape[3:], BF16)


def window(win_ref, b, row_at, rows):
    part = win_ref[b, :, pl.ds(row_at, rows)]
    return part.reshape(-1, part.shape[-1])


def column_sums(ref, f, pixels, lanes, step=64):
    def add(i, carry):
        part = ref[pl.ds(f * pixels + i * step, step), lanes]
        return carry[0] + fold(part), carry[1] + fold(part * part)

    width = lanes.stop - lanes.start
    zero = jnp.zeros((8, width), F32)
    one, two = lax.fori_loop(0, pixels // step, add, (zero, zero), unroll=2)
    return jnp.sum(one, 0, keepdims=True), jnp.sum(two, 0, keepdims=True)


def in_hbm(x):
    return pltpu.with_memory_space_constraint(x, pltpu.HBM)


class Pieces:
    def __init__(self, member, parts, me, sources):
        self.member, self.parts, self.me = member, parts, me
        self.sources = list(sources)
        self.shape = member.shape


def span(start, size):
    return pl.ds(start if isinstance(start, int) else pl.multiple_of(start, size & -size), size)


def fetch(member, parts, me_ref, sources, dst_ref, sem):
    me = me_ref[0]
    for (first, size, masks), src in zip(parts, sources):
        for q in range(src.shape[0]):
            d = q if masks is None else me ^ masks[q]
            for at, row, col in member.spots(d >> 2, d & 3):
                low, high = max(at, first), min(at + member.vr, first + size)
                if low < high:
                    pltpu.make_async_copy(
                        src.at[q, pl.ds(low - first, high - low)],
                        dst_ref.at[span(row + (low - at), high - low), span(col, LANES)],
                        sem,
                    ).start()


def arrived(ref, sem):
    pltpu.make_async_copy(ref, ref, sem).wait()


def forward_kernel(geom, normed, pieces, *refs):
    frames, rows, cols, counts = geom
    pixels = rows * cols
    refs = list(refs)
    domain_ref = refs.pop(0)
    source_ref = refs.pop(0)
    if normed:
        stats_ref, gain_ref, bias_ref = refs.pop(0), refs.pop(0), refs.pop(0)
    if pieces:
        me_ref = refs.pop(0)
        sources = [refs.pop(0) for _ in pieces[1]]
    else:
        kernel_ref = refs.pop(0)
    out_ref = refs.pop(0)
    sums_ref = refs.pop(0)
    act_ref = refs.pop(0) if normed else None
    if pieces:
        matrix_ref = refs.pop(0)
    *wins, held_ref, sem = refs

    if pieces:
        fetch(*pieces, me_ref, sources, held_ref, sem.at[0])
    else:
        pltpu.make_async_copy(kernel_ref, held_ref, sem.at[0]).start()

    def prepare(f, unrolled):
        clear_edges(wins[f], rows)
        if normed:
            average, inverse = frame_tables(stats_ref[...], domain_ref[f], counts)
            scale = inverse * gain_ref[...]
            shift = bias_ref[...] - average * scale

        def one_row(r, _):
            at = f * pixels + r * cols
            at = at if unrolled else pl.multiple_of(at, cols)
            value = source_ref[pl.ds(at, cols), :].astype(F32)
            if normed:
                act = value * scale + shift
                value = act * sigmoid(act)
                act_ref[pl.ds(at, cols), :] = value.astype(BF16)
            put_windows(wins[f], 0, r, value, cols)
            return 0

        if unrolled:
            for r in range(rows):
                one_row(r, 0)
        else:
            lax.fori_loop(0, rows, one_row, 0, unroll=2)

    def product(f):
        source = jnp.concatenate([window(wins[f], b, a, rows) for a in range(3) for b in range(3)], 1)
        out = jnp.dot(source, held_ref[...], preferred_element_type=F32)
        out_ref[f * pixels : (f + 1) * pixels, :] = out
        return out

    prepare(0, False)
    arrived(held_ref, sem.at[0])
    if pieces:
        pltpu.make_async_copy(held_ref, matrix_ref, sem.at[1]).start()
    parts = []
    for f in range(frames):
        if f + 1 < frames:
            prepare(f + 1, True)
        parts.append(product(f))
    sums_ref[...] = value_sums(parts, domain_ref)
    if pieces:
        pltpu.make_async_copy(held_ref, matrix_ref, sem.at[1]).wait()


ANYWHERE = pl.BlockSpec(memory_space=pl.ANY)


def forward_layer(geom, domain, source, kernel, norm=None):
    frames, rows, cols, _ = geom
    pix, chans = source.shape
    width = kernel.shape[1]
    pieces = isinstance(kernel, Pieces)
    args, specs = [domain, source], [SCALARS, whole(source.shape)]
    if norm is not None:
        args += list(norm)
        specs += [whole(x.shape) for x in norm]
    if pieces:
        args += [kernel.me, *kernel.sources]
        specs += [SCALARS] + [ANYWHERE] * len(kernel.sources)
    else:
        args.append(in_hbm(kernel))
        specs.append(ANYWHERE)
    outs, out_specs = [sds((pix, width), F32)], [whole((pix, width))]
    outs.append(sds((4, width), F32))
    out_specs.append(whole((4, width)))
    if norm is not None:
        outs.append(sds((pix, chans), BF16))
        out_specs.append(whole((pix, chans)))
    scratch = [pltpu.VMEM((3, 1, rows + 2, cols, chans), BF16)] * frames
    scratch += [pltpu.VMEM(kernel.shape, BF16), pltpu.SemaphoreType.DMA((2,))]
    if pieces:
        outs.append(pltpu.HBM(kernel.shape, BF16))
        out_specs.append(ANYWHERE)
    size = kernel.shape[0] * kernel.shape[1]
    return pl.pallas_call(
        functools.partial(forward_kernel, geom, norm is not None, (kernel.member, kernel.parts) if pieces else None),
        grid=(1,),
        in_specs=specs,
        out_specs=out_specs,
        out_shape=outs,
        scratch_shapes=scratch,
        compiler_params=params(1),
        cost_estimate=cost(2 * pix * size, size * 2 + pix * 4096),
    )(*args)


def pair_sum(x, cols):
    even = lax.broadcasted_iota(jnp.int32, x.shape, 0) % 2 == 0
    return x + jnp.where(even, pltpu.roll(x, cols - 1, 0), pltpu.roll(x, 1, 0))


def softmax_window(top, cols):
    exps = [jnp.exp(t) for t in top]
    share = 1.0 / pair_sum(exps[0] + exps[1], cols)
    return [e * share for e in exps]


def spread_cols(scr_ref, x):
    half = x.shape[0]
    scr_ref[pl.ds(0, half, stride=2), :] = x
    scr_ref[pl.ds(1, half, stride=2), :] = x
    return scr_ref[pl.ds(0, 2 * half), :]


def top_rows(top_ref, at, cols, lanes, scale, shift):
    top = []
    for a in at:
        act = top_ref[pl.ds(a, cols), lanes] * scale + shift
        top.append(act * sigmoid(act))
    return top


def row_pairs(x, cols):
    x = x.reshape(-1, 2, cols, x.shape[-1])
    return x[:, 0], x[:, 1]


def pair_sums(x):
    cols = x.shape[1]
    even = lax.broadcasted_iota(jnp.int32, x.shape, 1) % 2 == 0
    return x + jnp.where(even, pltpu.roll(x, cols - 1, 1), pltpu.roll(x, 1, 1))


def window_weights(top):
    exps = [jnp.exp(t) for t in top]
    share = 1.0 / pair_sums(exps[0] + exps[1])
    return [e * share for e in exps]


def pool_kernel(geom, domain_ref, top_ref, top_st, gain_t, bias_t, un_ref):
    frames, rows, cols, counts = geom
    pixels = rows * cols
    for f in range(frames):
        at = slice(f * pixels, (f + 1) * pixels)
        for lane in range(0, top_ref.shape[-1], LANES):
            lanes = slice(lane, lane + LANES)
            average, inverse = frame_tables(top_st[:, lanes], domain_ref[f], counts)
            scale = inverse * gain_t[:, lanes]
            act = top_ref[at, lanes] * scale + (bias_t[:, lanes] - average * scale)
            top = row_pairs(act * sigmoid(act), cols)
            weight = window_weights(top)
            pooled = pair_sums(weight[0] * top[0] + weight[1] * top[1])
            un_ref[at, lanes] = jnp.stack([w * pooled for w in weight], 1).reshape(pixels, LANES).astype(BF16)


def pool_layer(geom, domain, top, top_st, gain_t, bias_t):
    pix, chans = top.shape
    args = (domain, top, top_st, gain_t, bias_t)
    return pl.pallas_call(
        functools.partial(pool_kernel, geom),
        in_specs=[SCALARS] + [whole(x.shape) for x in args[1:]],
        out_specs=whole((pix, chans)),
        out_shape=sds((pix, chans), BF16),
        compiler_params=params(),
        cost_estimate=cost(pix * chans * 20, pix * chans * 6),
    )(*args)


def task_kernel(geom, domain_ref, top_ref, top_st, gain_t, bias_t, *refs):
    frames, rows, cols, counts = geom
    pixels = rows * cols
    masks = [refs[4 * k : 4 * k + 4] for k in range(TASKS)]
    task_ref, scr_ref = refs[-2:]
    for f in range(frames):
        for lane in range(0, top_ref.shape[-1], LANES):
            lanes = slice(lane, lane + LANES)

            def table(st, gain, bias):
                average, inverse = frame_tables(st[:, lanes], domain_ref[f], counts)
                scale = inverse * gain[:, lanes]
                return scale, bias[:, lanes] - average * scale

            t_scale, t_shift = table(top_st, gain_t, bias_t)
            wide = [table(*mask[1:]) for mask in masks]

            def one(i, _):
                at = [pl.multiple_of(f * pixels + (2 * i + h) * cols, cols) for h in (0, 1)]
                top = top_rows(top_ref, at, cols, lanes, t_scale, t_shift)
                weight = softmax_window(top, cols)
                held = [w * t for w, t in zip(weight, top)]
                for k in range(TASKS):
                    scale, shift = wide[k]
                    total = None
                    for h in (0, 1):
                        term = sigmoid(masks[k][0][pl.ds(at[h], cols), lanes] * scale + shift) * held[h]
                        total = term if total is None else total + term
                    scr_ref[k, pl.ds(0, cols), :] = total
                    even = scr_ref[k, pl.ds(0, cols // 2, stride=2), :]
                    odd = scr_ref[k, pl.ds(1, cols // 2, stride=2), :]
                    task_ref[f, i, k, :, lanes] = even + odd
                return 0

            lax.fori_loop(0, rows // 2, one, 0, unroll=2)


def task_layer(geom, domain, top, top_st, gain_t, bias_t, masks):
    frames, rows, cols, _ = geom
    pix, chans = top.shape
    task_shape = (frames, rows // 2, TASKS, cols // 2, chans)
    args = (domain, top, top_st, gain_t, bias_t, *(x for mask in masks for x in mask))
    return pl.pallas_call(
        functools.partial(task_kernel, geom),
        in_specs=[SCALARS] + [whole(x.shape) for x in args[1:]],
        out_specs=whole(task_shape),
        out_shape=sds(task_shape, F32),
        scratch_shapes=[pltpu.VMEM((TASKS, cols + 8, LANES), F32)],
        compiler_params=params(),
        cost_estimate=cost(pix * chans * 60, pix * chans * 28),
    )(*args)


def pool_early_kernel(geom, first, domain_ref, top_ref, top_st, gain_t, bias_t, wide_ref, wide_st, gain_w, bias_w, cot_ref, *refs):
    frames, rows, cols, counts = geom
    pixels = rows * cols
    mix_ref, gw_ref, sums_ref, scr_ref = refs[-4:]
    for lane in range(0, top_ref.shape[-1], LANES):
        lanes = slice(lane, lane + LANES)
        sums = []
        for f in range(frames):
            average, inverse = frame_tables(top_st[:, lanes], domain_ref[f], counts)
            t_scale = inverse * gain_t[:, lanes]
            t_shift = bias_t[:, lanes] - average * t_scale
            w_mean, w_inv = frame_tables(wide_st[:, lanes], domain_ref[f], counts)

            def one(i, carry):
                at = [pl.multiple_of(f * pixels + (2 * i + h) * cols, cols) for h in (0, 1)]
                top = top_rows(top_ref, at, cols, lanes, t_scale, t_shift)
                weight = softmax_window(top, cols)
                cot = spread_cols(scr_ref, cot_ref[f, i, :, lanes].astype(F32))
                one_sum, two_sum = carry
                for h in (0, 1):
                    xhat = (wide_ref[pl.ds(at[h], cols), lanes] - w_mean) * w_inv
                    mask = sigmoid(xhat * gain_w[:, lanes] + bias_w[:, lanes])
                    part = cot * mask
                    mix = part if first else refs[0][pl.ds(at[h], cols), lanes] + part
                    mix_ref[pl.ds(at[h], cols), lanes] = mix
                    g = part * (weight[h] * top[h]) * (1.0 - mask)
                    gw_ref[pl.ds(at[h], cols), lanes] = g
                    one_sum = one_sum + fold(g)
                    two_sum = two_sum + fold(g * xhat)
                return one_sum, two_sum

            zero = jnp.zeros((8, LANES), F32)
            sums.append(lax.fori_loop(0, rows // 2, one, (zero, zero), unroll=2))
        sums_ref[:, lanes] = by_domain(
            [jnp.sum(s[0], 0, keepdims=True) for s in sums], [jnp.sum(s[1], 0, keepdims=True) for s in sums], domain_ref
        )


def pool_early(geom, domain, _, top_st, gain_t, bias_t, wide, wide_st, gain_w, bias_w, cot, top, mix=None):
    cols = geom[2]
    pix, chans = top.shape
    args = (domain, top, top_st, gain_t, bias_t, wide, wide_st, gain_w, bias_w, cot) + (() if mix is None else (mix,))
    outs = [sds((pix, chans), F32)] * 2 + [sds((4, chans), F32)]
    return pl.pallas_call(
        functools.partial(pool_early_kernel, geom, mix is None),
        in_specs=[SCALARS] + [whole(x.shape) for x in args[1:]],
        out_specs=[whole(o.shape) for o in outs],
        out_shape=outs,
        scratch_shapes=[pltpu.VMEM((cols + 8, LANES), F32)],
        compiler_params=params(),
        cost_estimate=cost(pix * chans * 40, pix * chans * 20),
    )(*args)


def head_kernel(geom, domain_ref, bot_ref, bot_st, gate_ref, gate_st, gain_b, bias_b, gain_g, bias_g, cot_ref,
                maps_ref, gb_ref, gg_ref, sums_ref):
    frames, rows, cols, counts = geom
    pixels = rows * cols
    chans = bot_ref.shape[-1]
    for lane in range(0, chans, LANES):
        lanes = slice(lane, lane + LANES)
        grads, hats = ([[] for _ in range(TASKS + 1)] for _ in range(2))
        for f in range(frames):
            at = slice(f * pixels, (f + 1) * pixels)
            mean, inv = frame_tables(bot_st[:, lanes], domain_ref[f], counts)
            b_hat = (bot_ref[at, lanes] - mean) * inv
            act = b_hat * gain_b[:, lanes] + bias_b[:, lanes]
            s = sigmoid(act)
            bottom = act * s
            back = None
            for k in range(TASKS):
                sl = slice(k * chans + lane, k * chans + lane + LANES)
                mean, inv = frame_tables(gate_st[:, sl], domain_ref[f], counts)
                xhat = (gate_ref[at, sl] - mean) * inv
                value = sigmoid(xhat * gain_g[:, sl] + bias_g[:, sl])
                maps_ref[k, at, lanes] = value * bottom
                part = cot_ref[k, at, lanes].astype(F32) * value
                back = part if back is None else back + part
                g = part * bottom * (1.0 - value)
                gg_ref[at, sl] = g
                grads[k].append(g)
                hats[k].append(xhat)
            g = back * (s * (1.0 + act * (1.0 - s)))
            gb_ref[at, lanes] = g
            grads[-1].append(g)
            hats[-1].append(b_hat)
        for k in range(TASKS + 1):
            to = chans + k * chans + lane if k < TASKS else lane
            sums_ref[:, to : to + LANES] = value_sums(grads[k], domain_ref, hats[k])


def head_layer(geom, domain, bot, bot_st, gate, gate_st, gain_b, bias_b, gain_g, bias_g, cot):
    pix, chans = bot.shape
    args = (domain, bot, bot_st, gate, gate_st, gain_b, bias_b, gain_g, bias_g, cot)
    outs = [sds((TASKS, pix, chans), F32), sds((pix, chans), F32), sds((pix, TASKS * chans), F32),
            sds((4, (TASKS + 1) * chans), F32)]
    return pl.pallas_call(
        functools.partial(head_kernel, geom),
        in_specs=[SCALARS] + [whole(x.shape) for x in args[1:]],
        out_specs=[whole(o.shape) for o in outs],
        out_shape=outs,
        compiler_params=params(),
        cost_estimate=cost(pix * chans * 80, pix * chans * 44),
    )(*args)


def norm_back_rows(g, pre, tables):
    mean, inv, scale, g_mean, g_cross = tables
    xhat = (pre - mean) * inv
    return scale * (g - g_mean - xhat * g_cross)


def back_tables(stats_ref, sums_ref, gain_ref, domain_at, counts):
    mean, inv = frame_tables(stats_ref[...], domain_at, counts)
    g_mean, g_cross = grad_tables(sums_ref[...], domain_at, counts)
    return mean, inv, inv * gain_ref[...], g_mean, g_cross


def backward_kernel(geom, added, epilogue, *refs):
    frames, rows, cols, counts = geom
    pixels = rows * cols
    refs = list(refs)
    domain_ref = refs.pop(0)
    g_ref, pre_ref, st_ref, sm_ref, gain_ref = (refs.pop(0) for _ in range(5))
    kernel_ref = refs.pop(0)
    add_ref = refs.pop(0) if added else None
    lpre_ref, lst_ref, lgain_ref, lbias_ref = (refs.pop(0) for _ in range(4))
    if epilogue == "pool":
        mix_ref = refs.pop(0)
    win_ref, out_ref, sums_ref, held_ref, sem = refs
    chans = kernel_ref.shape[0] // 9

    load = pltpu.make_async_copy(kernel_ref, held_ref, sem)
    load.start()
    clear_edges(win_ref, rows)
    for f in range(frames):
        tables = back_tables(st_ref, sm_ref, gain_ref, domain_ref[f], counts)

        def one_row(r, _):
            at = pl.multiple_of(f * pixels + r * cols, cols)
            low = norm_back_rows(g_ref[pl.ds(at, cols), :], pre_ref[pl.ds(at, cols), :], tables)
            put_windows(win_ref, f, r, low, cols)
            return 0

        lax.fori_loop(0, rows, one_row, 0, unroll=2)
    load.wait()
    source = jnp.concatenate([window(win_ref, 2 - b, 2 - a, rows) for a in range(3) for b in range(3)], 1)
    weight = jnp.concatenate([held_ref[k * chans : (k + 1) * chans, :] for k in range(9)], 1)
    out = lax.dot_general(source, weight, (((1,), (1,)), ((), ())), preferred_element_type=F32)
    if added:
        out = out + add_ref[...]
    if epilogue == "silu":
        first, second = [], []
        for f in range(frames):
            at = slice(f * pixels, (f + 1) * pixels)
            mean, inv = frame_tables(lst_ref[...], domain_ref[f], counts)
            xhat = (lpre_ref[at] - mean) * inv
            act = xhat * lgain_ref[...] + lbias_ref[...]
            s = sigmoid(act)
            g = out[at] * (s * (1.0 + act * (1.0 - s)))
            out_ref[at] = g
            first.append(jnp.sum(fold(g), 0, keepdims=True))
            second.append(jnp.sum(fold(g * xhat), 0, keepdims=True))
        sums_ref[...] = by_domain(first, second, domain_ref)
        return
    for lane in range(0, chans, LANES):
        lanes = slice(lane, lane + LANES)
        first, second = [], []
        for f in range(frames):
            at = slice(f * pixels, (f + 1) * pixels)
            mean, inv = frame_tables(lst_ref[:, lanes], domain_ref[f], counts)
            xhat = (lpre_ref[at, lanes] - mean) * inv
            act = xhat * lgain_ref[:, lanes] + lbias_ref[:, lanes]
            s = sigmoid(act)
            steep = s * (1.0 + act * (1.0 - s))
            top, up, mix = (row_pairs(x, cols) for x in (act * s, out[at, lanes], mix_ref[at, lanes]))
            weight = window_weights(top)
            pooled = pair_sums(weight[0] * top[0] + weight[1] * top[1])
            d_pool = pair_sums(weight[0] * up[0] + weight[1] * up[1])
            flow = [m + d_pool for m in mix]
            d_w = [u * pooled + fl * t for u, fl, t in zip(up, flow, top)]
            centre = pair_sums(weight[0] * d_w[0] + weight[1] * d_w[1])
            d_top = jnp.stack([w * (fl + d - centre) for w, fl, d in zip(weight, flow, d_w)], 1)
            g = d_top.reshape(pixels, LANES) * steep
            out_ref[at, lanes] = g
            first.append(jnp.sum(fold(g), 0, keepdims=True))
            second.append(jnp.sum(fold(g * xhat), 0, keepdims=True))
        sums_ref[:, lanes] = by_domain(first, second, domain_ref)


def backward_layer(geom, domain, top, kernel, lower, added=None, mix=None):
    frames, rows, cols, _ = geom
    pix, width = top[0].shape
    chans = kernel.shape[0] // 9
    args = [domain, *top, kernel]
    specs = [SCALARS] + [whole(x.shape) for x in top] + [ANYWHERE]
    win = (3, frames, rows + 2, cols, width)
    outs = [sds(win, BF16), sds((pix, chans), F32)]
    extra = ([] if added is None else [added]) + list(lower) + ([] if mix is None else [mix])
    epilogue = "silu" if mix is None else "pool"
    outs.append(sds((4, chans), F32))
    return pl.pallas_call(
        functools.partial(backward_kernel, geom, added is not None, epilogue),
        grid=(1,),
        in_specs=specs + [whole(x.shape) for x in extra],
        out_specs=[whole(o.shape) for o in outs],
        out_shape=outs,
        scratch_shapes=[pltpu.VMEM(kernel.shape, BF16), pltpu.SemaphoreType.DMA],
        compiler_params=params(1),
        cost_estimate=cost(2 * pix * kernel.size, kernel.size * 2 + pix * 10240),
    )(*args, *extra)


def low_kernel(geom, domain_ref, g_ref, pre_ref, st_ref, sm_ref, gain_ref, win_ref):
    frames, rows, cols, counts = geom
    pixels = rows * cols
    clear_edges(win_ref, rows)
    for f in range(frames):
        tables = back_tables(st_ref, sm_ref, gain_ref, domain_ref[f], counts)

        def one_row(r, _):
            at = pl.multiple_of(f * pixels + r * cols, cols)
            low = norm_back_rows(g_ref[pl.ds(at, cols), :], pre_ref[pl.ds(at, cols), :], tables)
            put_windows(win_ref, f, r, low, cols)
            return 0

        lax.fori_loop(0, rows, one_row, 0, unroll=2)


def low_layer(geom, domain, top):
    frames, rows, cols, _ = geom
    pix, width = top[0].shape
    out = sds((3, frames, rows + 2, cols, width), BF16)
    return pl.pallas_call(
        functools.partial(low_kernel, geom),
        grid=(1,),
        in_specs=[SCALARS] + [whole(x.shape) for x in top],
        out_specs=whole(out.shape),
        out_shape=out,
        compiler_params=params(1),
        cost_estimate=cost(pix * width * 20, pix * width * 14),
    )(domain, *top)


def input_kernel(geom, win_ref, kernel_ref, out_ref):
    rows = geom[1]
    step = pl.program_id(0)
    chans = kernel_ref.shape[0] // 3
    source = jnp.concatenate([window(win_ref, 2 - b, 2 - step, rows) for b in range(3)], 1)
    weight = jnp.concatenate([kernel_ref[b * chans : (b + 1) * chans, :] for b in range(3)], 1)
    part = lax.dot_general(source, weight, (((1,), (1,)), ((), ())), preferred_element_type=F32)

    @pl.when(step == 0)
    def _():
        out_ref[...] = part

    @pl.when(step > 0)
    def _():
        out_ref[...] += part


def input_layer(geom, win, kernel):
    frames, rows, cols, _ = geom
    pix = frames * rows * cols
    chans, width = kernel.shape[0] // 9, kernel.shape[1]
    return pl.pallas_call(
        functools.partial(input_kernel, geom),
        grid=(3,),
        in_specs=[whole(win.shape), pl.BlockSpec((3 * chans, width), lambda a: (a, 0))],
        out_specs=whole((pix, chans)),
        out_shape=sds((pix, chans), F32),
        compiler_params=params(1),
        cost_estimate=cost(2 * pix * kernel.size, kernel.size * 2 + pix * 4096),
    )(win, in_hbm(kernel))


class Member:
    def __init__(self, at, shape, dp, fsdp, split=False):
        self.at, self.shape, self.split = at, shape, split
        self.vr = shape[0] // dp // (2 if split else 1)
        self.blocks = shape[1] // fsdp * (2 if split else 1) // LANES
        self.rows = self.vr * self.blocks

    def spots(self, i, j):
        if self.split:
            row, col = i * 2 * self.vr + (j & 1) * self.vr, (j >> 1) * self.blocks * LANES
        else:
            row, col = i * self.vr, j * self.blocks * LANES
        for k in range(self.blocks):
            yield self.at + k * self.vr, row, col + k * LANES


def collect_kernel(member, parts, me_ref, *refs):
    out_ref, sem = refs[-2:]
    fetch(member, parts, me_ref, refs[:-2], out_ref, sem)
    arrived(out_ref, sem)


def collect(pieces):
    return pl.pallas_call(
        functools.partial(collect_kernel, pieces.member, pieces.parts),
        in_specs=[SCALARS] + [ANYWHERE] * len(pieces.sources),
        out_specs=whole(pieces.shape),
        out_shape=sds(pieces.shape, BF16),
        scratch_shapes=[pltpu.SemaphoreType.DMA],
        grid=(1,),
        compiler_params=params(1),
        cost_estimate=cost(0, 4 * pieces.shape[0] * pieces.shape[1]),
    )(pieces.me, *pieces.sources)


def affine_kernel(member, parts, me_ref, *refs):
    out_ref, rows_ref, sem = refs[-3:]
    fetch(member, parts, me_ref, refs[:-3], rows_ref, sem)
    arrived(rows_ref, sem)
    width = out_ref.shape[1] // 32
    for d in range(32):
        rows = rows_ref[16 * d : 16 * d + 16].astype(F32)
        both = jnp.concatenate([rows[:8], rows[8:]], 1)
        out_ref[:, d * width : (d + 1) * width] = (both[0:2] + both[2:4] + both[4:6])[:, :width]


def collect_affine(pieces):
    return pl.pallas_call(
        functools.partial(affine_kernel, pieces.member, pieces.parts),
        in_specs=[SCALARS] + [ANYWHERE] * len(pieces.sources),
        out_specs=whole((2, 5120)),
        out_shape=sds((2, 5120), F32),
        scratch_shapes=[pltpu.VMEM((512, LANES), BF16), pltpu.SemaphoreType.DMA],
        grid=(1,),
        compiler_params=params(1),
        cost_estimate=cost(10000000, 1000000),
    )(pieces.me, *pieces.sources)


def weight_parts(geom, step, act_ref, low_ref, tr_ref):
    rows = geom[1]

    @pl.when(step == 0)
    def _():
        tr_ref[...] = act_ref[...].astype(F32).T.astype(BF16)

    if len(low_ref.shape) == 5:
        for b in range(3):
            yield jnp.dot(tr_ref[...], window(low_ref, 2 - b, 2 - step, rows), preferred_element_type=F32)
    else:
        yield jnp.dot(tr_ref[...], low_ref[...], preferred_element_type=F32)


def weight_kernel(geom, act_ref, low_ref, out_ref, tr_ref):
    chans = tr_ref.shape[0]
    for b, part in enumerate(weight_parts(geom, pl.program_id(0), act_ref, low_ref, tr_ref)):
        out_ref[b * chans : (b + 1) * chans, :] = part.astype(BF16)


def weight_layer(geom, act, low):
    pix, chans = act.shape
    win = low.ndim == 5
    width = low.shape[-1]
    steps = 3 if win else 1
    out = sds((9 * chans if win else chans, width), BF16)
    return pl.pallas_call(
        functools.partial(weight_kernel, geom),
        grid=(steps,),
        in_specs=[whole(act.shape), whole(low.shape)],
        out_specs=pl.BlockSpec((out.shape[0] // steps, width), lambda a: (a, 0)),
        out_shape=out,
        scratch_shapes=[pltpu.VMEM((chans, pix), BF16)],
        compiler_params=params(1),
        cost_estimate=cost(2 * pix * out.size, out.size * 2 + pix * 4096),
    )(act, low)


def weight_blocks_kernel(geom, member, steps, held, *refs):
    refs = list(refs)
    me_ref, act_ref, low_ref = (refs.pop(0) for _ in range(3))
    if held:
        del refs[:3]
    near_ref, far_ref, send_ref, scr_ref, tr_ref, sem = refs
    step = pl.program_id(0)
    chans = tr_ref.shape[0]
    for b, part in enumerate(weight_parts(geom, step, act_ref, low_ref, tr_ref)):
        scr_ref[pl.ds(pl.multiple_of(step * 3 * chans, chans) + b * chans, chans), :] = part.astype(BF16)
    me = me_ref[0]
    share = member.shape[0] // 8
    done = 0
    for s in range(steps):
        ready = member.shape[0] * (s + 1) // steps // share

        @pl.when(step == s)
        def _(done=done, ready=ready):
            for i in range(done, ready):
                e = i ^ (me >> 2)
                q = ((e & 1) << 2) | (e & 2) | (e >> 2)
                for jd in range(4):
                    dst = send_ref.at[jd >> 1, q] if jd & 1 else (near_ref, far_ref)[jd >> 1].at[q]
                    for at, row, col in member.spots(i, (me & 3) ^ jd):
                        pltpu.make_async_copy(
                            scr_ref.at[span(row, member.vr), span(col, LANES)], dst.at[pl.ds(at, member.vr)], sem
                        ).start()

        done = ready

    @pl.when(step == steps - 1)
    def _():
        pltpu.make_async_copy(scr_ref, scr_ref, sem).wait()


def weight_blocks(geom, me, act, low, member, rows, held=None):
    pix, chans = act.shape
    win = low.ndim == 5
    steps = 3 if win else 1
    shard = (rows, LANES)
    outs = [sds((8, *shard), BF16)] * 2 + [sds((2, 8, *shard), BF16)]
    args = [me, act, low] + list(held or ())
    size = member.shape[0] * member.shape[1]
    return pl.pallas_call(
        functools.partial(weight_blocks_kernel, geom, member, steps, held is not None),
        grid=(steps,),
        in_specs=[SCALARS, whole(act.shape), whole(low.shape)] + [ANYWHERE] * len(held or ()),
        out_specs=[ANYWHERE] * 3,
        out_shape=outs,
        scratch_shapes=[pltpu.VMEM(member.shape, BF16), pltpu.VMEM((chans, pix), BF16), pltpu.SemaphoreType.DMA],
        input_output_aliases={} if held is None else {3: 0, 4: 1, 5: 2},
        compiler_params=params(1),
        cost_estimate=cost(2 * pix * size, size * 2 + pix * 4096),
    )(*args)


def weight_piece_kernel(geom, member, step, held, *refs):
    rows = geom[1]
    refs = list(refs)
    me_ref, act_ref, low_ref = (refs.pop(0) for _ in range(3))
    if held:
        del refs[:3]
    near_ref, far_ref, send_ref = (refs.pop(0) for _ in range(3))
    if step == 0:
        tr_ref = refs.pop(0)
        tr_ref[...] = act_ref[...].astype(F32).T.astype(BF16)
    else:
        tr_ref = act_ref
    scr_ref, sem = refs
    chans = tr_ref.shape[0]
    for b in range(3):
        part = jnp.dot(tr_ref[...], window(low_ref, 2 - b, 2 - step, rows), preferred_element_type=F32)
        scr_ref[b * chans : (b + 1) * chans, :] = part.astype(BF16)
    me = me_ref[0]
    start, stop = 3 * chans * step, 3 * chans * (step + 1)
    for i in range(8):
        first, last = max(start, i * member.vr), min(stop, (i + 1) * member.vr)
        if first >= last:
            continue
        e = i ^ (me >> 2)
        q = ((e & 1) << 2) | (e & 2) | (e >> 2)
        for jd in range(4):
            dst = send_ref.at[jd >> 1, q] if jd & 1 else (near_ref, far_ref)[jd >> 1].at[q]
            col = ((me & 3) ^ jd) * LANES
            pltpu.make_async_copy(
                scr_ref.at[pl.ds(first - start, last - first), span(col, LANES)],
                dst.at[pl.ds(member.at + first - i * member.vr, last - first)],
                sem,
            ).start()
    arrived(scr_ref, sem)


def weight_piece(geom, me, act, low, member, rows, step, held=None):
    chans = member.shape[0] // 9
    pix, width = low.shape[1] * geom[1] * geom[2], low.shape[-1]
    shard = (rows, LANES)
    outs = [sds((8, *shard), BF16)] * 2 + [sds((2, 8, *shard), BF16)]
    out_specs = [ANYWHERE] * 3
    if step == 0:
        outs.append(sds((chans, pix), BF16))
        out_specs.append(whole((chans, pix)))
    args = [me, act, low] + list(held or ())
    return pl.pallas_call(
        functools.partial(weight_piece_kernel, geom, member, step, held is not None),
        grid=(1,),
        in_specs=[SCALARS, whole(act.shape), whole(low.shape)] + [ANYWHERE] * len(held or ()),
        out_specs=out_specs,
        out_shape=outs,
        scratch_shapes=[pltpu.VMEM((3 * chans, width), BF16), pltpu.SemaphoreType.DMA],
        input_output_aliases={} if held is None else {3: 0, 4: 1, 5: 2},
        compiler_params=params(1),
        cost_estimate=cost(2 * pix * 3 * chans * width, chans * width * 6),
    )(*args)


def point_kernel(geom, pieces, *refs):
    frames, rows, cols, _ = geom
    pixels = rows * cols
    refs = list(refs)
    domain_ref, act_ref = refs.pop(0), refs.pop(0)
    if pieces:
        out_ref, sums_ref, matrix_ref, sem = refs[-4:]
        fetch(*pieces, refs[0], refs[1:-4], matrix_ref, sem)
        arrived(matrix_ref, sem)
    else:
        matrix_ref, out_ref, sums_ref = refs
    for lane in range(0, out_ref.shape[-1], 256):
        lanes = slice(lane, lane + 256)
        out = jnp.dot(act_ref[...], matrix_ref[:, lanes], preferred_element_type=F32)
        out_ref[:, lanes] = out
        sums_ref[:, lanes] = value_sums([out[f * pixels : (f + 1) * pixels] for f in range(frames)], domain_ref)


def point_layer(geom, domain, act, mat):
    pix, chans = act.shape
    width = mat.shape[1]
    pieces = isinstance(mat, Pieces)
    outs = [sds((pix, width), F32), sds((4, width), F32)] + [sds(mat.shape, BF16)] * pieces
    args = [domain, act] + ([mat.me, *mat.sources] if pieces else [mat])
    specs = [SCALARS, whole(act.shape)]
    specs += [SCALARS] + [ANYWHERE] * len(mat.sources) if pieces else [whole(mat.shape)]
    return pl.pallas_call(
        functools.partial(point_kernel, geom, (mat.member, mat.parts) if pieces else None),
        in_specs=specs,
        out_specs=[whole(o.shape) for o in outs],
        out_shape=outs,
        scratch_shapes=[pltpu.SemaphoreType.DMA] * pieces,
        grid=(1,),
        compiler_params=params(1),
        cost_estimate=cost(2 * pix * chans * width, chans * width * 2 + pix * width * 4),
    )(*args)


def point_back_kernel(geom, added, domain_ref, g_ref, pre_ref, st_ref, sm_ref, gain_ref, mat_ref, *refs):
    frames, rows, cols, counts = geom
    pixels = rows * cols
    low_ref, out_ref = refs[-2:]
    for f in range(frames):
        tables = back_tables(st_ref, sm_ref, gain_ref, domain_ref[f], counts)

        def one_row(r, _):
            at = pl.multiple_of(f * pixels + r * cols, cols)
            low = norm_back_rows(g_ref[pl.ds(at, cols), :], pre_ref[pl.ds(at, cols), :], tables)
            low_ref[pl.ds(at, cols), :] = low.astype(BF16)
            return 0

        lax.fori_loop(0, rows, one_row, 0, unroll=2)
    part = lax.dot_general(low_ref[...], mat_ref[...], (((1,), (1,)), ((), ())), preferred_element_type=F32)
    out_ref[...] = part + refs[0][...] if added else part


def point_back(geom, domain, g, pre, stats, sums, gain, mat, added=None):
    pix, width = g.shape
    chans = mat.shape[0]
    args = (domain, g, pre, stats, sums, gain, mat) + (() if added is None else (added,))
    outs = [sds((pix, width), BF16), sds((pix, chans), F32)]
    return pl.pallas_call(
        functools.partial(point_back_kernel, geom, added is not None),
        grid=(1,),
        in_specs=[SCALARS] + [whole(x.shape) for x in args[1:]],
        out_specs=[whole(o.shape) for o in outs],
        out_shape=outs,
        compiler_params=params(1),
        cost_estimate=cost(2 * pix * mat.size, mat.size * 2 + pix * width * 10),
    )(*args)


def share_kernel(widths, me_ref, *refs):
    *sums, gain_ref, bias_ref, flat_ref = refs
    at = 0
    for ref, width in zip(sums, widths):
        flat_ref[0:1, at : at + width] = ref[2:3, :] + ref[3:4, :]
        flat_ref[1:2, at : at + width] = ref[0:1, :] + ref[1:2, :]
        at += width
    share = gain_ref.shape[1]
    mine = pltpu.roll(flat_ref[...], at - me_ref[0] * share, 1)
    gain_ref[...] = mine[0:1, :share]
    bias_ref[...] = mine[1:2, :share]


def share_of(me, sums, share):
    widths = [x.shape[1] for x in sums]
    got = pl.pallas_call(
        functools.partial(share_kernel, widths),
        grid=(1,),
        in_specs=[SCALARS] + [whole(x.shape) for x in sums],
        out_specs=[whole((1, share))] * 2,
        out_shape=[sds((1, share), F32)] * 2,
        scratch_shapes=[pltpu.VMEM((8, sum(widths)), F32)],
        compiler_params=params(1),
        cost_estimate=cost(0, 100000),
    )(me, *(in_hbm(x) for x in sums))
    return [x[0] for x in got]


AXES = ("dp", "fsdp")
CORE, X, Y, Z_NEAR, Z_FAR = range(5)
ORDER = (CORE, Z_NEAR, Z_FAR, X, Y)


def swap(x, bit):
    n = lax.axis_size(AXES)
    return lax.ppermute(x, AXES, [(i, i ^ (1 << bit)) for i in range(n)])


def bit_of(bit):
    return (lax.axis_index(AXES) >> bit) & 1


def all_bits():
    return range(lax.axis_size(AXES).bit_length() - 1)


def tied(value, to):
    return value if to is None else lax.optimization_barrier((value, to))[0]


class Links:
    def __init__(self):
        self.under_way = {}

    def busy(self, bit, *values):
        self.under_way.setdefault(bit, []).extend(values)

    def total(self, x, after=None, order=None, fill=()):
        bits = order if order and len(all_bits()) == 5 else all_bits()
        fill = list(fill)
        for bit in bits:
            for value in self.under_way.pop(bit, ()):
                x = tied(x, value)
            got = swap(x, bit)
            if fill and (bit != CORE or len(bits) != 5):
                got = tied(got, fill.pop(0)(x))
            x = x + got
            for start in (after or {}).get(bit, ()):
                x = tied(x, start(x))
        for work in fill:
            work(x)
        return x


def half_rows(rows):
    return rows // 32 * 16


class Gather:
    def __init__(self, links, shard):
        self.links, self.shard, self.cut = links, shard, half_rows(shard.shape[0])
        self.sources = None

    def far(self, to=None):
        self.z = tied(self.shard, to)
        self.got = swap(self.z, Z_FAR)

    def near(self, to=None):
        self.z = jnp.stack(tied((self.z, self.got), to))
        self.got = swap(self.z, Z_NEAR)

    def first(self, to=None):
        z = jnp.concatenate(tied((self.z, self.got), to))
        self.a, self.b = z[:, : self.cut], z[:, self.cut :]
        self.got = swap(self.a, Y), swap(self.b, X)

    def second(self, to=None):
        a, b, (got_a, got_b) = tied((self.a, self.b, self.got), to)
        self.a, self.b = jnp.concatenate([a, got_a]), jnp.concatenate([b, got_b])
        self.got = swap(self.a, X), swap(self.b, Y)

    def busy(self):
        if isinstance(self.got, tuple):
            self.links.busy(X, self.got[0])
            self.links.busy(Y, self.got[1])
        else:
            self.links.busy(CORE, self.got)

    def finish(self, to=None):
        rows = self.shard.shape[0]
        self.a, self.b, self.got = tied((self.a, self.b, self.got), to)
        self.sources, self.parts = [], []
        for core in (0, 1):
            for n, value in enumerate((self.a, self.got[0], self.b, self.got[1])):
                z = [8 * (k >> 1) + 16 * (k & 1) for k in range(4)]
                if n < 2:
                    masks = [core + 2 * n + 4 * y + m for y in (0, 1) for m in z]
                else:
                    masks = [core + 4 * (n - 2) + 2 * x + m for x in (0, 1) for m in z]
                self.parts.append((0, self.cut, masks) if n < 2 else (self.cut, rows - self.cut, masks))
                self.sources.append(swap(value, CORE) if core else value)

    def pieces(self, member):
        return Pieces(member, self.parts, number(1), self.sources)


def number(entries):
    return jnp.full((entries,), lax.axis_index(AXES), jnp.int32)


def plus(a, b):
    return (a.astype(F32) + b.astype(F32)).astype(BF16)


def add_kernel(jobs, *refs):
    refs = list(refs)
    count = sum(n for _, n, _ in jobs)
    ins, outs = refs[:count], refs[count:]
    for work, n_in, n_out in jobs:
        work(*ins[:n_in], *outs[:n_out])
        del ins[:n_in], outs[:n_out]


def add_all(*jobs):
    ins = [x for _, job, _ in jobs for x in job]
    outs = [x for _, _, job in jobs for x in job]
    got = pl.pallas_call(
        functools.partial(add_kernel, [(work, len(i), len(o)) for work, i, o in jobs]),
        grid=(1,),
        in_specs=[whole(x.shape) for x in ins],
        out_specs=[whole(x.shape) for x in outs],
        out_shape=outs,
        compiler_params=params(1),
        cost_estimate=cost(0, sum(x.size * 2 for x in ins + outs)),
    )(*ins)
    result = []
    for _, _, job in jobs:
        result.append(got[: len(job)])
        got = got[len(job) :]
    return result


def first_work(cut, near, far, got, a, send_a, b, send_b):
    a[...] = plus(near[:, :cut], got[0, :, :cut])
    send_a[...] = plus(far[:, :cut], got[1, :, :cut])
    for half, out in enumerate((b, send_b)):
        s = slice(4 * half, 4 * half + 4)
        out[0] = plus(near[s, cut:], got[0, s, cut:])
        out[1] = plus(far[s, cut:], got[1, s, cut:])


def second_work(a, b, got_a, got_b, a_out, send_a, b_out, send_b):
    a_out[...] = plus(a[:4], got_a[:4])
    send_a[...] = plus(a[4:], got_a[4:])
    b_out[...] = plus(b[0], got_b[0])
    send_b[...] = plus(b[1], got_b[1])


def near_work(cut, a, b, got_a, got_b, z, send):
    for half, out in enumerate((z, send)):
        s = slice(2 * half, 2 * half + 2)
        out[:, :cut] = plus(a[s], got_a[s])
        out[:, cut:] = plus(b[s], got_b[s])


def far_work(z, got, z_out, send):
    z_out[...] = plus(z[0], got[0])
    send[...] = plus(z[1], got[1])


def finish_work(z, got, out):
    out[...] = z[...].astype(F32) + got[...].astype(F32)


class Scatter:
    def __init__(self, links, blocks):
        self.links, self.blocks = links, blocks
        self.rows = blocks[0].shape[1]
        self.cut = half_rows(self.rows)
        self.got = swap(blocks[2], CORE)

    def shape(self, *dims):
        return sds((*dims, LANES), BF16)

    def first_job(self):
        c, r = self.cut, self.rows - self.cut
        outs = [self.shape(8, c)] * 2 + [self.shape(2, 4, r)] * 2
        return functools.partial(first_work, c), [*self.blocks[:2], self.got], outs

    def first(self, a, send_a, b, send_b):
        self.a, self.b = a, b
        self.got = swap(send_a, X), swap(send_b, Y)

    def second_job(self):
        c, r = self.cut, self.rows - self.cut
        return second_work, [self.a, self.b, *self.got], [self.shape(4, c)] * 2 + [self.shape(4, r)] * 2

    def second(self, a, send_a, b, send_b):
        self.a, self.b = a, b
        self.got = swap(send_a, Y), swap(send_b, X)

    def near_job(self):
        return functools.partial(near_work, self.cut), [self.a, self.b, *self.got], [self.shape(2, self.rows)] * 2

    def near(self, to=None):
        self.got = swap(tied(self.send, to), Z_NEAR)

    def far_job(self):
        return far_work, [self.z, self.got], [self.shape(self.rows)] * 2

    def far(self, z, send):
        self.z = z
        self.got = swap(send, Z_FAR)

    def finish_job(self):
        return finish_work, [self.z, self.got], [sds((self.rows, LANES), F32)]


def add_after(to, *jobs):
    return add_all(*((work, tied(ins, to), outs) for work, ins, outs in jobs))


def rows_of_chip(shard):
    half = shard.shape[0] // 2
    odd = bit_of(CORE) == 1
    mine = jnp.where(odd, shard[half:], shard[:half])
    got = swap(jnp.where(odd, shard[:half], shard[half:]), CORE)
    return jnp.concatenate([jnp.where(odd, got, mine), jnp.where(odd, mine, got)], 1)


def columns_of_core(rows):
    half = rows.shape[1] // 2
    odd = bit_of(CORE) == 1
    mine = jnp.where(odd, rows[:, half:], rows[:, :half])
    got = swap(jnp.where(odd, rows[:, :half], rows[:, half:]), CORE)
    return jnp.concatenate([jnp.where(odd, got, mine), jnp.where(odd, mine, got)], 0)


def pack(x):
    return jnp.concatenate([x[:, k : k + LANES] for k in range(0, x.shape[1], LANES)], 0)


def unpack(x, blocks):
    rows = x.shape[0] // blocks
    return jnp.concatenate([x[k * rows : (k + 1) * rows] for k in range(blocks)], 1)


def in_three(x):
    high = lax.reduce_precision(x, 8, 7)
    middle = lax.reduce_precision(x - high, 8, 7)
    return jnp.stack([high, middle, x - high - middle]).astype(BF16)


def gather(x):
    x = x[None]
    for bit in all_bits():
        other = swap(x, bit)
        high = bit_of(bit) == 1
        x = jnp.concatenate([jnp.where(high, other, x), jnp.where(high, x, other)], 0)
    return x


def scatter(x):
    for bit in reversed(all_bits()):
        half = x.shape[0] // 2
        high = bit_of(bit) == 1
        send = jnp.where(high, x[:half], x[half:])
        keep = jnp.where(high, x[half:], x[:half])
        x = plus(keep, swap(send, bit))
    return x[0]


def gather_matrix(shard):
    dp, fsdp = lax.axis_size("dp"), lax.axis_size("fsdp")
    rows, cols = shard.shape
    full = gather(shard).reshape(dp, fsdp, rows, cols)
    return full.transpose(0, 2, 1, 3).reshape(dp * rows, fsdp * cols)


def scatter_matrix(full):
    dp, fsdp = lax.axis_size("dp"), lax.axis_size("fsdp")
    rows, cols = full.shape[0] // dp, full.shape[1] // fsdp
    parts = full.reshape(dp, rows, fsdp, cols).transpose(0, 2, 1, 3)
    return scatter(parts.reshape(dp * fsdp, rows, cols)).astype(F32)


class AnyMesh:
    def __init__(self, links, geom, weights, gains, biases):
        self.geom = geom
        self.mats = {name: gather_matrix(w) for name, w in weights.items()}
        self.affine = gather(jnp.stack([gains, biases])).transpose(1, 0, 2).reshape(2, 1, -1)
        self.grads, self.ready = {}, None

    def get(self, name):
        return self.mats[name]

    def whole(self, name):
        return self.mats[name]

    def put(self, name, matrix):
        pass

    def layer_done(self, n, local):
        pass

    def during(self, point):
        return {}

    def add(self, name, act, low):
        got = weight_layer(self.geom, act, low)
        self.grads[name] = scatter_matrix(got)
        return got

    def pieces(self, name, act, low):
        return [lambda x: self.add(name, act, low)]

    def send(self, n, to=None):
        pass

    def after_layer(self, n, local):
        pass

    def now(self):
        return None

    def tail(self, blocks, kernels):
        return [kernel(None) for kernel in kernels]


class ThisMesh:
    def __init__(self, links, geom, weights, gains, biases):
        self.geom, self.links = geom, links
        self.me = number(1)
        sizes = (8, 4)
        full = {n: (w.shape[0] * 8, w.shape[1] * 4) for n, w in weights.items()}
        splits = ("six", "gating")
        g1 = Gather(links, weights["one"])
        g1.far()
        g1.near()
        packed = {n: pack(rows_of_chip(tied(w, g1.got)) if n in splits else w) for n, w in weights.items()}
        gains, biases = tied((gains, biases), g1.z)
        affine = in_three(jnp.stack([gains, biases])).reshape(6, -1)
        affine = jnp.pad(affine, ((0, 2), (0, 2 * LANES - affine.shape[1])))
        affine = jnp.concatenate([affine[:, :LANES], affine[:, LANES:]])
        groups = (("one",), ("two",), ("three",), ("four",), ("five",), ("six", "gating", "attend"))
        self.g, self.members, self.group = [], {}, {}
        for names in groups:
            at = 0
            for name in names:
                self.members[name] = Member(at, full[name], *sizes, split=name in splits)
                at += self.members[name].rows
            if names == ("one",):
                group = g1
            else:
                group = Gather(links, jnp.concatenate([packed[n] for n in names] + [affine] * (names == ("two",))))
            self.g.append(group)
            self.group.update((n, group) for n in names)
        g2 = self.g[1]
        g2.far()
        g1.first()
        g2.near(g1.got)
        g1.second()
        g1.finish()
        self.g[2].far(g2.got)
        g2.first(g1.got)
        self.ready = self.g[5].shard
        self.mats = {}
        self.grads, self.blocks, self.sums = {}, {}, {}
        self.homes, self.rows = {}, {}
        for names in (("six", "gating"), ("five",), ("four", "attend"), ("three",), ("two",), ("one",)):
            at = 0
            for name in names:
                self.homes[name] = Member(at, full[name], *sizes, split=name in splits)
                at += self.homes[name].rows
            self.rows.update((name, at) for name in names)

    def layer_done(self, n, local):
        if n < 6:
            self.g[n].second((local, self.g[n + 1].got) if n < 5 else local)
            self.g[n].busy()

    def get(self, name):
        if name in self.mats:
            return self.mats[name]
        group = self.group[name]
        self.mats[name] = group.pieces(self.members[name])
        if name == "two":
            self.affine = collect_affine(group.pieces(FlatMember(self.members["two"].rows, 16)))[:, None]
        return self.mats[name]

    def whole(self, name):
        self.mats[name] = collect(self.get(name))
        return self.mats[name]

    def put(self, name, matrix):
        self.mats[name] = matrix

    def during(self, point):
        if point <= 5:

            def x_done(x):
                self.g[point].finish(x)

            if point == 5:
                return {X: [x_done]}
            group = self.g[point + 1]

            def z_done(x):
                group.near(x)

            def y_done(x):
                group.first(x)
                if point < 4:
                    self.g[point + 2].far(x)

            return {Z_FAR: [z_done], X: [x_done], Y: [y_done]}
        n = 14 - point

        def z_done(x):
            self.sums[n + 2].near(x)

        def x_done(x):
            (got,) = add_after(x, self.sums[n + 2].far_job())
            self.sums[n + 2].far(*got)
            return got[0]

        def y_done(x):
            if n == 2:
                self.send(2)
                got = add_after(x, self.sums[2].first_job(), self.sums[4].far_job())
                self.sums[2].first(*got[0])
                self.sums[4].far(*got[1])
            else:
                (got,) = add_after(x, self.sums[n + 1].second_job())
                self.sums[n + 1].second(*got)

        if n == 2:
            return {Z_FAR: [z_done], Y: [y_done]}
        return {Z_FAR: [z_done], X: [x_done], Y: [y_done]} if n < 5 else {Y: [y_done]}

    def add(self, name, act, low):
        n = NUMBER[name]
        self.blocks[n] = weight_blocks(
            self.geom, self.me, act, low, self.homes[name], self.rows[name], self.blocks.get(n)
        )
        return self.blocks[n][0]

    def pieces(self, name, act, low):
        def piece(step):
            def work(x):
                n = NUMBER[name]
                if step == 0:
                    *self.blocks[n], self.turned = weight_piece(
                        self.geom, self.me, tied(act, x), low, self.homes[name], self.rows[name], 0
                    )
                else:
                    self.blocks[n] = weight_piece(
                        self.geom, self.me, tied(self.turned, x), low, self.homes[name], self.rows[name], step, self.blocks[n]
                    )
                return self.blocks[n][0]

            return work

        return [piece(step) for step in range(3)]

    def send(self, n, to=None):
        near, far, away = self.blocks[n]
        self.sums[n] = Scatter(self.links, (near, far, tied(away, to)))

    def after_layer(self, n, local):
        jobs = [self.sums[n + 1].first_job()]
        if n < 5:
            jobs.append(self.sums[n + 2].near_job())
        if n < 4:
            jobs.append(self.sums[n + 3].finish_job())
        got = add_after(local, *jobs)
        self.sums[n + 1].first(*got[0])
        self.links.busy(X, *self.sums[n + 1].got)
        if n < 5:
            s = self.sums[n + 2]
            s.z, s.send = got[1]
        if n < 4:
            (self.sums[n + 3].out,) = got[2]

    def now(self):
        return self.sums[3].a

    def tail(self, blocks, kernels):
        two, three, four = (self.sums[n] for n in (2, 3, 4))
        outs = [kernels[0](blocks)]
        got = add_after(outs[0], two.second_job(), three.second_job(), four.finish_job())
        two.second(*got[0])
        three.second(*got[1])
        (four.out,) = got[2]
        ((two.z, two.send),) = add_after(got[0][0], two.near_job())
        two.near()
        self.send(1, two.send)
        one = self.sums[1]
        (got,) = add_after(two.z, one.first_job())
        one.first(*got)
        outs.append(kernels[1](got[0]))
        got = add_after(got[0], two.far_job(), three.near_job())
        two.far(*got[0])
        three.z, three.send = got[1]
        three.near()
        (got,) = add_after(got[0][0], one.second_job())
        one.second(*got)
        got = add_after(got[0], one.near_job(), two.finish_job(), three.far_job())
        one.z, one.send = got[0]
        (two.out,) = got[1]
        one.near()
        three.far(*got[2])
        (got,) = add_after(one.z, one.far_job())
        one.far(*got)
        ((three.out,),) = add_after(got[0], three.finish_job())
        ((one.out,),) = add_after(three.out, one.finish_job())
        for name, m in self.homes.items():
            out = unpack(self.sums[NUMBER[name]].out[m.at : m.at + m.rows], m.blocks)
            self.grads[name] = columns_of_core(out) if m.split else out
        return outs


NUMBER = dict(one=1, two=2, three=3, attend=4, four=4, five=5, six=6, gating=6)


class FlatMember:
    def __init__(self, at, rows):
        self.at, self.vr, self.rows, self.blocks, self.shape = at, rows, rows, 1, (32 * rows, LANES)

    def spots(self, i, j):
        yield self.at, (i * 4 + j) * self.vr, 0


def body(
    frames_in,
    domain,
    kernel_one,
    kernel_two,
    kernel_three,
    attn_enc,
    kernel_four,
    kernel_five,
    kernel_six,
    attn_dec,
    gains,
    biases,
    enc_cot,
    dec_cot,
):
    frames, rows, cols, _ = frames_in.shape
    total_frames = frames * lax.axis_size(AXES)
    first = total_frames * 5 // 8
    counts = (float(first * rows * cols), float((total_frames - first) * rows * cols))
    geom = (frames, rows, cols, counts)
    pix = frames * rows * cols
    source = frames_in.reshape(pix, C_IN)
    enc_cot = enc_cot.transpose(0, 1, 3, 2, 4)
    dec_cot = dec_cot.reshape(pix, TASKS, C_DEC).transpose(1, 0, 2)
    weights = dict(
        one=kernel_one, two=kernel_two, three=kernel_three, attend=attn_enc,
        four=kernel_four, five=kernel_five, six=kernel_six, gating=attn_dec,
    )
    links = Links()
    this = lax.axis_size("dp") == 8 and lax.axis_size("fsdp") == 4
    w = (ThisMesh if this else AnyMesh)(links, geom, weights, gains, biases)

    def forward(name, source, norm=None):
        got = forward_layer(geom, domain, source, w.get(name), norm)
        w.put(name, got[-1])
        return got[:3] if norm is not None else got[:2]

    def point(name, act):
        got = point_layer(geom, domain, act, w.get(name))
        w.put(name, got[-1])
        return got[:2]

    pre_1, local = forward("one", tied(source, w.ready))
    w.layer_done(1, local)
    st_1 = links.total(local, w.during(1), ORDER)
    w.get("two")
    widths = (C_MID, C_MID, C_MID, TASKS * C_MID, C_MID, C_MID, C_DEC, TASKS * C_DEC)
    gain, bias, at = [], [], 0
    for width in widths:
        gain.append(w.affine[0, :, at : at + width])
        bias.append(w.affine[1, :, at : at + width])
        at += width
    pre_2, local, act_1 = forward("two", pre_1, (st_1, gain[0], bias[0]))
    w.layer_done(2, local)
    st_2 = links.total(local, w.during(2), ORDER)
    pre_3, local, act_2 = forward("three", pre_2, (st_2, gain[1], bias[1]))
    w.layer_done(3, local)
    st_3 = links.total(local, w.during(3), ORDER)
    unpooled = pool_layer(geom, domain, pre_3, st_3, gain[2], bias[2])
    pre_4, local = forward("four", unpooled)
    w.layer_done(4, local)
    st_4 = links.total(local, w.during(4), ORDER)
    pre_5, local, act_4 = forward("five", pre_4, (st_4, gain[4], bias[4]))
    w.layer_done(5, local)
    st_5 = links.total(local, w.during(5), ORDER)
    pre_g, local_g = point("gating", act_4)
    pre_6, local, act_5 = forward("six", pre_5, (st_5, gain[5], bias[5]))
    attend = w.whole("attend")
    wide = []

    def attend_part(k):
        def work(x):
            wide.append(point_layer(geom, domain, tied(act_2, x), attend[:, k * C_MID : (k + 1) * C_MID]))
            return wide[-1][0]

        return work

    both = links.total(jnp.concatenate([local, local_g], 1), None, ORDER, [attend_part(k) for k in range(TASKS)])
    st_6, st_g = both[:, :C_DEC], both[:, C_DEC:]
    pre_a = [p for p, _ in wide]
    task_maps, g_6, g_g, local = head_layer(
        geom, domain, pre_6, st_6, pre_g, st_g, gain[6], bias[6], gain[7], bias[7], dec_cot
    )
    both = links.total(jnp.concatenate([local] + [s for _, s in wide], 1), None, ORDER)
    sm_6, sm_g, st_a = both[:, :C_DEC], both[:, C_DEC : 4 * C_DEC], both[:, 4 * C_DEC :]
    st_a = [st_a[:, k * C_MID : (k + 1) * C_MID] for k in range(TASKS)]
    pool_args = (geom, domain, pre_3, st_3, gain[2], bias[2])
    masks = [(pre_a[k], st_a[k], gain[3][:, k * C_MID : (k + 1) * C_MID], bias[3][:, k * C_MID : (k + 1) * C_MID]) for k in range(TASKS)]

    win_6, g_5, local = backward_layer(
        geom, domain, (g_6, pre_6, st_6, sm_6, gain[6]), w.get("six"), lower=(pre_5, st_5, gain[5], bias[5])
    )
    early, gate_back = [], []

    def early_part(k):
        def work(x):
            early.append(pool_early(*pool_args, *masks[k], enc_cot[:, :, k], tied(pre_3, x), early[-1][0] if early else None))
            return early[-1][0]

        return work

    def gate_part(x):
        gate_back.extend(point_back(geom, domain, tied(g_g, x), pre_g, st_g, sm_g, gain[7], w.get("gating")))
        return gate_back[0]

    sm_5 = links.total(
        local, None, ORDER, [lambda x: w.add("six", act_5, tied(win_6, x)), gate_part, early_part(0), early_part(1)]
    )
    early_part(2)(sm_5)
    mix = early[-1][0]
    low_g, add_4 = gate_back
    blocks = w.add("gating", act_4, low_g)
    w.send(6, sm_5)
    win_5, g_4, local = backward_layer(
        geom,
        domain,
        (tied(g_5, blocks), pre_5, st_5, sm_5, gain[5]),
        w.get("five"),
        added=add_4,
        lower=(pre_4, st_4, gain[4], bias[4]),
    )
    w.after_layer(5, local)
    both = links.total(
        jnp.concatenate([local] + [e[2] for e in early], 1), w.during(9), ORDER, w.pieces("five", act_4, win_5)
    )
    w.send(5, both)
    sm_4 = both[:, :C_MID]
    sm_a = [both[:, (k + 1) * C_MID : (k + 2) * C_MID] for k in range(TASKS)]
    win_4, g_3, local = backward_layer(
        geom,
        domain,
        (g_4, pre_4, st_4, sm_4, gain[4]),
        w.get("four"),
        lower=(pre_3, st_3, gain[2], bias[2]),
        mix=mix,
    )
    w.after_layer(4, local)
    backs = []

    def attend_back(k):
        def work(x):
            backs.append(
                point_back(
                    geom, domain, tied(early[k][1], x), pre_a[k], st_a[k], sm_a[k], masks[k][2],
                    attend[:, k * C_MID : (k + 1) * C_MID], backs[-1][1] if backs else None,
                )
            )
            return backs[-1][1]

        return work

    sm_3 = links.total(local, w.during(10), ORDER, w.pieces("four", unpooled, win_4) + [attend_back(0)])
    attend_back(1)(sm_3)
    attend_back(2)(backs[-1][1])
    low_a = jnp.concatenate([low for low, _ in backs], 1)
    blocks = w.add("attend", act_2, low_a)
    w.send(4)
    win_3, g_2, local = backward_layer(
        geom,
        domain,
        (tied(g_3, blocks), pre_3, st_3, sm_3, gain[2]),
        w.get("three"),
        added=backs[-1][1],
        lower=(pre_2, st_2, gain[1], bias[1]),
    )
    w.after_layer(3, local)
    tasks = []

    def task_part(x):
        tasks.append(task_layer(geom, domain, tied(pre_3, x), *pool_args[3:], masks))
        return tasks[0]

    sm_2 = links.total(local, w.during(11), ORDER, w.pieces("three", act_2, win_3))
    w.send(3, sm_2)
    win_2, g_1, local = backward_layer(
        geom,
        domain,
        (g_2, pre_2, st_2, sm_2, gain[1]),
        w.get("two"),
        lower=(pre_1, st_1, gain[0], bias[0]),
    )
    w.after_layer(2, local)
    sm_1 = links.total(local, w.during(12), ORDER, w.pieces("two", act_1, win_2) + [task_part])
    win_1 = low_layer(geom, domain, (tied(g_1, w.now()), pre_1, st_1, sm_1, gain[0]))
    blocks = w.add("one", source, win_1)
    frames_grad, task_maps = w.tail(
        blocks,
        (
            lambda to: input_layer(geom, tied(win_1, to), w.get("one")),
            lambda to: tied(task_maps, to).transpose(1, 0, 2).reshape(frames, rows, cols, TASKS, C_DEC),
        ),
    )
    gains_grad, biases_grad = share_of(number(1), [sm_1, sm_2, sm_3, *sm_a, sm_4, sm_5, sm_6, sm_g], gains.shape[0])
    return (
        tasks[0].transpose(0, 1, 3, 2, 4),
        task_maps,
        frames_grad.reshape(frames, rows, cols, C_IN),
        *(w.grads[n] for n in ("one", "two", "three", "attend", "four", "five", "six", "gating")),
        gains_grad,
        biases_grad,
    )


def solution(mesh):
    whole_split = P(AXES)
    matrix = P("dp", "fsdp")
    return jax.shard_map(
        body,
        mesh=mesh,
        in_specs=(whole_split, whole_split) + (matrix,) * 8 + (whole_split,) * 4,
        out_specs=(whole_split,) * 3 + (matrix,) * 8 + (whole_split,) * 2,
        check_vma=False,
    )
```
